256 devices in a mesh: grp: 4 (over x), grid: 64 (over y, z, core).
Axes of the slice: x: 4, y: 4, z: 8, core: 2. Of those that a mesh axis runs over, the one named last changes fastest.
Arguments:
- orbitals: float32 [512, 262144], P('grp', 'grid'), may hold values from -6 to 6
- anchors: int32 [512, 3], replicated, may hold values from 0 to 31
- pair_slots: int32 [256, 4, 2], replicated, may hold values from -1 to 511, as said below
Outputs:
- exchange_term: float32 [512, 262144], P('grp', 'grid')
The draws below stay inside these ranges and needn't reach their ends.
Inputs may be any that keep to these rules, and one draw needn't show every extreme that they name: `pair_slots`: row k lists the pairs of owner k, the device with index k in the order grp, grid; its first slots hold pairs of two different orbital numbers and its other slots hold -1 in both columns. Exactly 512 slots hold pairs in all, no row holds more than 4, and some row holds exactly 4.
All inputs are finite; a program needn't handle non-finite values.
Results may differ from the reference program's by a relative error of at most 0.0003.
Values sent between devices are 32-bit elements; how exact they have to be, the bound alone decides.
No kernel may reach another device: no remote copies, remote signals or barrier semaphores. Data moves between devices by JAX's collectives and lax.ppermute only.
A program may use at most 128 MiB of HBM per device.

```python
import jax
import jax.numpy as jnp
from jax import lax

B = 64
PAIR_DEV = 2
ITERS = 3
OWNERS = 256
NORB = 512
CAP = 4


def draw_pair_slots(key, part):
    order_key, first_key, gap_key = jax.random.split(jax.random.fold_in(key, 7), 3)
    position = jnp.argsort(jax.random.permutation(order_key, OWNERS))
    load = jnp.where(position < OWNERS // 4, CAP, jnp.where(position < 3 * OWNERS // 4, PAIR_DEV, 0))
    slot_idx = lax.broadcasted_iota(jnp.int32, (OWNERS, CAP), 1)
    filled = slot_idx < load[:, None]
    orbit_a = jax.random.randint(first_key, (OWNERS, CAP), 0, NORB)
    orbit_b = (orbit_a + jax.random.randint(gap_key, (OWNERS, CAP), 1, NORB)) % NORB
    paired = jnp.stack([orbit_a, orbit_b], -1)
    return jnp.where(filled[..., None], paired, -1).astype(jnp.int32)


def plant(drawn, stream_key, least, largest):
    place = [jax.random.randint(jax.random.fold_in(stream_key, axis), (), 0, length) for axis, length in enumerate(drawn.shape)]
    widest = drawn.shape.index(max(drawn.shape))
    next_to = place[:widest] + [(place[widest] + 1) % drawn.shape[widest]] + place[widest + 1:]
    return drawn.at[tuple(place)].set(least).at[tuple(next_to)].set(largest)


def block_scale(stream_key, dims, cuts, smallest, high):
    factor_of = 1.0
    for axis_at, parts in cuts:
        steps = jax.random.uniform(jax.random.fold_in(jax.random.fold_in(stream_key, 6), axis_at), (parts,), jnp.float32, smallest / len(cuts), high / len(cuts))
        factor_of = factor_of * jnp.repeat(jnp.exp(steps), dims[axis_at] // parts).reshape((-1,) + (1,) * (len(dims) - 1 - axis_at))
    return factor_of


def normal_values(key, shape, width, limit, cuts=(), kind=jnp.bfloat16):
    level = block_scale(key, shape, cuts, -0.22, 0.18) if cuts else 1.0
    values = jax.random.normal(key, shape, jnp.float32) * width * level
    return jnp.minimum(jnp.maximum(values, -limit), limit).astype(kind)


def setup_inputs(seed: int = 0) -> dict:
    keys = jax.random.split(jax.random.key(seed), 4)
    return {
        "orbitals": normal_values(keys[0], (NORB, B * B * B), 1.0, 6.0, ((0, 4), (1, 64)), jnp.float32),
        "anchors": plant(jax.random.randint(keys[1], (NORB, 3), 0, B // 2), jax.random.fold_in(keys[1], 1), 0, (B // 2) - 1).astype(jnp.int32),
        "pair_slots": draw_pair_slots(jax.random.fold_in(keys[3], 71), 0),
    }


def shift_field(field, offset, extent):
    plane_size = extent * extent
    padded_x = jnp.pad(field, ((extent, extent), (0, 0)))
    moved = lax.dynamic_slice_in_dim(padded_x, (extent - offset[0]).astype(jnp.int32), extent, 0)
    padded_yz = jnp.pad(moved, ((0, 0), (plane_size, plane_size)))
    linear = (offset[1] * extent + offset[2]).astype(jnp.int32)
    moved = lax.dynamic_slice_in_dim(padded_yz, (plane_size - linear).astype(jnp.int32), plane_size, 1)
    cells = lax.broadcasted_iota(jnp.int32, (1, plane_size), 1)
    coord_y = cells // extent - offset[1]
    coord_z = cells % extent - offset[2]
    inside = (coord_y >= 0) & (coord_y < extent) & (coord_z >= 0) & (coord_z < extent)
    return jnp.where(inside, moved, jnp.zeros_like(moved))


def operate(field, extent):
    padded_x = jnp.pad(field, ((1, 1), (0, 0)))
    beside = padded_x[2:] + padded_x[:-2]
    padded_y = jnp.pad(field, ((0, 0), (extent, extent)))
    beside = beside + padded_y[:, 2 * extent:] + padded_y[:, :-2 * extent]
    padded_z = jnp.pad(field, ((0, 0), (1, 1)))
    cells = lax.broadcasted_iota(jnp.int32, (1, field.shape[1]), 1) % extent
    upper_z = jnp.where(cells < extent - 1, padded_z[:, 2:], jnp.zeros_like(field))
    lower_z = jnp.where(cells > 0, padded_z[:, :-2], jnp.zeros_like(field))
    return 6.0 * field - beside - upper_z - lower_z


def conjugate(density, extent):
    potential = jnp.zeros_like(density)
    resid = density
    direction = density
    norm_now = jnp.sum(resid * resid)
    for turn in range(ITERS):
        image = operate(direction, extent)
        step_len = norm_now / jnp.sum(direction * image)
        potential = potential + step_len * direction
        resid = resid - step_len * image
        norm_next = jnp.sum(resid * resid)
        direction = resid + (norm_next / norm_now) * direction
        norm_now = norm_next
    return potential


def pair_terms(field_a, field_b, offset, extent):
    partner = shift_field(field_b, offset, extent)
    density = field_a * partner
    potential = conjugate(density, extent)
    term_a = potential * partner
    term_b = shift_field(potential * field_a, -offset, extent)
    return term_a, term_b


def reference(orbitals, anchors, pair_slots):
    extent = B
    slot_list = pair_slots.reshape(-1, 2)

    def add_pair(accum, slot_entry):
        filled = slot_entry[0] >= 0
        orbit_a = jnp.maximum(slot_entry[0], 0).astype(jnp.int32)
        orbit_b = jnp.maximum(slot_entry[1], 0).astype(jnp.int32)
        offset = anchors[orbit_b] - anchors[orbit_a]
        field_a = orbitals[orbit_a].reshape(extent, extent * extent)
        field_b = orbitals[orbit_b].reshape(extent, extent * extent)
        term_a, term_b = pair_terms(field_a, field_b, offset, extent)
        weight_flag = jnp.where(filled, 1.0, 0.0).astype(orbitals.dtype)
        accum = accum.at[orbit_a].add(weight_flag * term_a.reshape(-1))
        accum = accum.at[orbit_b].add(weight_flag * term_b.reshape(-1))
        return accum, None

    start = jnp.zeros(orbitals.shape, orbitals.dtype)
    accum, unused = lax.scan(add_pair, start, slot_list)
    return accum
```

```python
import jax
import jax.numpy as jnp
from jax import lax
from jax.sharding import PartitionSpec as P

B = 64
PAIR_DEV = 2
ITERS = 3


def shift_field(field, offset, extent):
    plane_size = extent * extent
    padded_x = jnp.pad(field, ((extent, extent), (0, 0)))
    moved = lax.dynamic_slice_in_dim(padded_x, extent - offset[0], extent, 0)
    padded_yz = jnp.pad(moved, ((0, 0), (plane_size, plane_size)))
    linear = offset[1] * extent + offset[2]
    moved = lax.dynamic_slice_in_dim(padded_yz, plane_size - linear, plane_size, 1)
    cells = lax.broadcasted_iota(jnp.int32, (1, plane_size), 1)
    coord_y = cells // extent - offset[1]
    coord_z = cells % extent - offset[2]
    inside = (coord_y >= 0) & (coord_y < extent) & (coord_z >= 0) & (coord_z < extent)
    return jnp.where(inside, moved, jnp.zeros_like(moved))


def operate(field, extent):
    padded_x = jnp.pad(field, ((1, 1), (0, 0)))
    beside = padded_x[2:] + padded_x[:-2]
    padded_y = jnp.pad(field, ((0, 0), (extent, extent)))
    beside = beside + padded_y[:, 2 * extent :] + padded_y[:, : -2 * extent]
    padded_z = jnp.pad(field, ((0, 0), (1, 1)))
    cells = lax.broadcasted_iota(jnp.int32, (1, field.shape[1]), 1) % extent
    upper_z = jnp.where(cells < extent - 1, padded_z[:, 2:], jnp.zeros_like(field))
    lower_z = jnp.where(cells > 0, padded_z[:, :-2], jnp.zeros_like(field))
    return 6.0 * field - beside - upper_z - lower_z


def conjugate(density, extent):
    potential = jnp.zeros_like(density)
    resid = density
    direction = density
    norm_now = jnp.sum(resid * resid)
    for turn in range(ITERS):
        image = operate(direction, extent)
        step_len = norm_now / jnp.sum(direction * image)
        potential = potential + step_len * direction
        resid = resid - step_len * image
        norm_next = jnp.sum(resid * resid)
        direction = resid + norm_next / norm_now * direction
        norm_now = norm_next
    return potential


def pair_terms(field_a, field_b, offset, extent):
    partner = shift_field(field_b, offset, extent)
    density = field_a * partner
    potential = conjugate(density, extent)
    term_a = potential * partner
    term_b = shift_field(potential * field_a, -offset, extent)
    return (term_a, term_b)


def deal_evenly(pair_slots, owner_count, each_owner):
    flat_slots = pair_slots.reshape(-1, 2)
    filled = (flat_slots[:, 0] >= 0).astype(jnp.int32)
    order = jnp.arange(flat_slots.shape[0], dtype=jnp.int32)
    position = jnp.sum(jnp.where(order[None, :] < order[:, None], filled[None, :], 0), axis=1)
    wanted = lax.broadcasted_iota(jnp.int32, (owner_count, each_owner), 1) * owner_count
    wanted = (wanted + lax.broadcasted_iota(jnp.int32, (owner_count, each_owner), 0)).reshape(-1)
    matched = (position[None, :] == wanted[:, None]) & (filled[None, :] == 1)
    picked = jnp.dot(matched.astype(jnp.int32), flat_slots)
    return picked.reshape(owner_count, each_owner, 2)


def body(orbitals, anchors, pair_slots):
    extent = B
    grid_count = lax.axis_size("grid")
    owner_count = lax.axis_size("grp") * grid_count
    group_idx = lax.axis_index("grp")
    place_idx = lax.axis_index("grid")
    assignment = deal_evenly(pair_slots, owner_count, PAIR_DEV)
    filled = assignment[..., 0] >= 0
    safe_ids = jnp.maximum(assignment, 0)
    pieces = lax.all_gather(orbitals, "grp", axis=0, tiled=True)
    group_table = lax.dynamic_slice_in_dim(safe_ids, group_idx * grid_count, grid_count, 0)
    gather_ids = jnp.transpose(group_table, (1, 2, 0))
    outgoing = pieces[gather_ids]
    arrived = lax.all_to_all(outgoing, "grid", split_axis=2, concat_axis=2, tiled=True)
    owner_idx = group_idx * grid_count + place_idx
    own_pairs = safe_ids[owner_idx]
    own_filled = filled[owner_idx]
    offsets = anchors[own_pairs[:, 1]] - anchors[own_pairs[:, 0]]

    def solve_slot(slot_item):
        boxes_pair, offset, flag = slot_item
        term_a, term_b = pair_terms(boxes_pair[0], boxes_pair[1], offset, extent)
        weight_flag = jnp.where(flag, 1.0, 0.0).astype(jnp.float32)
        return jnp.stack([term_a, term_b]) * weight_flag

    terms = lax.map(solve_slot, (arrived, offsets, own_filled))
    returned = lax.all_to_all(terms, "grid", split_axis=2, concat_axis=2, tiled=True)
    flat_terms = returned.reshape(-1, returned.shape[-1])
    summed = jax.ops.segment_sum(flat_terms, gather_ids.reshape(-1), num_segments=anchors.shape[0])
    return lax.psum_scatter(summed, "grp", scatter_dimension=0, tiled=True)


def solution(mesh):
    return jax.shard_map(
        body,
        mesh=mesh,
        in_specs=(P("grp", "grid"), P(), P()),
        out_specs=P("grp", "grid"),
        check_vma=False,
    )
```

```python
import functools

import jax
import jax.numpy as jnp
from jax import lax
from jax.experimental import pallas as pl
from jax.experimental.pallas import tpu as pltpu
from jax.sharding import PartitionSpec as P

B = 64
PAIR_DEV = 2
ITERS = 3
CHUNKS = 2
ROWS = B * B // 128
KEEP = 32


def shift_field(field, offset, extent):
    plane_size = extent * extent
    padded_x = jnp.pad(field, ((extent, extent), (0, 0)))
    moved = lax.dynamic_slice_in_dim(padded_x, extent - offset[0], extent, 0)
    padded_yz = jnp.pad(moved, ((0, 0), (plane_size, plane_size)))
    linear = offset[1] * extent + offset[2]
    moved = lax.dynamic_slice_in_dim(padded_yz, plane_size - linear, plane_size, 1)
    cells = lax.broadcasted_iota(jnp.int32, (1, plane_size), 1)
    coord_y = cells // extent - offset[1]
    coord_z = cells % extent - offset[2]
    inside = (coord_y >= 0) & (coord_y < extent) & (coord_z >= 0) & (coord_z < extent)
    return jnp.where(inside, moved, jnp.zeros_like(moved))


def operate(field, extent):
    padded_x = jnp.pad(field, ((1, 1), (0, 0)))
    beside = padded_x[2:] + padded_x[:-2]
    padded_y = jnp.pad(field, ((0, 0), (extent, extent)))
    beside = beside + padded_y[:, 2 * extent :] + padded_y[:, : -2 * extent]
    padded_z = jnp.pad(field, ((0, 0), (1, 1)))
    cells = lax.broadcasted_iota(jnp.int32, (1, field.shape[1]), 1) % extent
    upper_z = jnp.where(cells < extent - 1, padded_z[:, 2:], jnp.zeros_like(field))
    lower_z = jnp.where(cells > 0, padded_z[:, :-2], jnp.zeros_like(field))
    return 6.0 * field - beside - upper_z - lower_z


def conjugate(density, extent):
    potential = jnp.zeros_like(density)
    resid = density
    direction = density
    norm_now = jnp.sum(resid * resid)
    for turn in range(ITERS):
        image = operate(direction, extent)
        step_len = norm_now / jnp.sum(direction * image)
        potential = potential + step_len * direction
        resid = resid - step_len * image
        norm_next = jnp.sum(resid * resid)
        direction = resid + norm_next / norm_now * direction
        norm_now = norm_next
    return potential


def pair_terms(field_a, field_b, offset, extent):
    partner = shift_field(field_b, offset, extent)
    density = field_a * partner
    potential = conjugate(density, extent)
    term_a = potential * partner
    term_b = shift_field(potential * field_a, -offset, extent)
    return (term_a, term_b)


def deal_evenly(pair_slots, owner_count, each_owner):
    flat_slots = pair_slots.reshape(-1, 2)
    filled = (flat_slots[:, 0] >= 0).astype(jnp.int32)
    order = jnp.arange(flat_slots.shape[0], dtype=jnp.int32)
    position = jnp.sum(jnp.where(order[None, :] < order[:, None], filled[None, :], 0), axis=1)
    wanted = lax.broadcasted_iota(jnp.int32, (owner_count, each_owner), 1) * owner_count
    wanted = (wanted + lax.broadcasted_iota(jnp.int32, (owner_count, each_owner), 0)).reshape(-1)
    matched = (position[None, :] == wanted[:, None]) & (filled[None, :] == 1)
    picked = jnp.dot(matched.astype(jnp.int32), flat_slots)
    return picked.reshape(owner_count, each_owner, 2)


def general(orbitals, anchors, pair_slots):
    extent = B
    grid_count = lax.axis_size("grid")
    owner_count = lax.axis_size("grp") * grid_count
    group_idx = lax.axis_index("grp")
    place_idx = lax.axis_index("grid")
    assignment = deal_evenly(pair_slots, owner_count, PAIR_DEV)
    filled = assignment[..., 0] >= 0
    safe_ids = jnp.maximum(assignment, 0)
    pieces = lax.all_gather(orbitals, "grp", axis=0, tiled=True)
    group_table = lax.dynamic_slice_in_dim(safe_ids, group_idx * grid_count, grid_count, 0)
    gather_ids = jnp.transpose(group_table, (1, 2, 0))
    outgoing = pieces[gather_ids]
    arrived = lax.all_to_all(outgoing, "grid", split_axis=2, concat_axis=2, tiled=True)
    owner_idx = group_idx * grid_count + place_idx
    own_pairs = safe_ids[owner_idx]
    own_filled = filled[owner_idx]
    offsets = anchors[own_pairs[:, 1]] - anchors[own_pairs[:, 0]]

    def solve_slot(slot_item):
        boxes_pair, offset, flag = slot_item
        term_a, term_b = pair_terms(boxes_pair[0], boxes_pair[1], offset, extent)
        weight_flag = jnp.where(flag, 1.0, 0.0).astype(jnp.float32)
        return jnp.stack([term_a, term_b]) * weight_flag

    terms = lax.map(solve_slot, (arrived, offsets, own_filled))
    returned = lax.all_to_all(terms, "grid", split_axis=2, concat_axis=2, tiled=True)
    flat_terms = returned.reshape(-1, returned.shape[-1])
    summed = jax.ops.segment_sum(flat_terms, gather_ids.reshape(-1), num_segments=anchors.shape[0])
    return lax.psum_scatter(summed, "grp", scatter_dimension=0, tiled=True)


def route_kernel(me_ref, a_ref, b_ref, pos_ref, slot_ref, most_ref):
    me = me_ref[0]
    a, b = a_ref[...], b_ref[...]
    n = a.shape[0]
    f32, i32 = jnp.float32, jnp.int32

    def lanes(width):
        return lax.broadcasted_iota(i32, (n, width), 1)

    def row(x, width=128):
        return jnp.sum(x, axis=0, keepdims=True)

    def col(x):
        return jnp.sum(x, axis=1, keepdims=True)

    before = (lax.broadcasted_iota(i32, (n, n), 0) > lax.broadcasted_iota(i32, (n, n), 1))
    before = jnp.where(before, 1.0, 0.0).astype(jnp.bfloat16)

    def count_before(hot):
        return jnp.dot(before, hot.astype(jnp.bfloat16), preferred_element_type=f32)

    lane = lanes(128)
    valid = a >= 0
    ga, gb = a >> 7, b >> 7
    typ = jnp.where(valid, ga * 4 + gb, -1)
    hot = jnp.where(lane == typ, 1.0, 0.0)
    rank = col(count_before(hot) * hot).astype(i32)
    turn = (rank + ga + gb) & 3
    bin_no = jnp.where(valid, jnp.where((turn & 1) == 0, ga, gb) * CHUNKS + (turn >> 1), -1)
    hot = jnp.where(lane == bin_no, 1.0, 0.0)
    rank = col(count_before(hot) * hot)
    load = row(hot)
    over = jnp.maximum(load - B, 0.0)
    lane1 = lax.broadcasted_iota(i32, (1, 128), 1)
    room = jnp.where(lane1 < 4 * CHUNKS, jnp.maximum(B - load, 0.0), 0.0)
    upper = lax.broadcasted_iota(i32, (128, 128), 0) < lax.broadcasted_iota(i32, (128, 128), 1)
    upper = jnp.where(upper, 1.0, 0.0)
    both = jnp.where(lax.broadcasted_iota(i32, (8, 128), 0) == 0, over, room)
    sums = jnp.dot(both, upper, precision=lax.Precision.HIGHEST, preferred_element_type=f32)
    over_before, room_before = sums[0:1], sums[1:2]
    spilled = valid & (rank >= B)
    spill_no = rank - B + col(hot * over_before)
    lands = (spill_no >= room_before) & (spill_no < room_before + room)
    landed = jnp.where(lands, 1.0, 0.0)
    hot = jnp.where(spilled, landed, hot)
    place = jnp.where(spilled, col(landed * (load - room_before)) + spill_no, rank).astype(i32)
    bin_no = col(hot * lane.astype(f32)).astype(i32)
    group, chunk = bin_no >> 1, bin_no & 1

    from_a, from_b = valid & (ga != group), valid & (gb != group)
    key_a = jnp.where(from_a, (chunk * 4 + ga) * 4 + group, -1)
    key_b = jnp.where(from_b, (chunk * 4 + gb) * 4 + group, -1)
    hot_a = jnp.where(lane == key_a, 1.0, 0.0)
    hot_b = jnp.where((lane >= 32) & (lane - 32 == key_b), 1.0, 0.0)
    counts = count_before(hot_a + hot_b)
    all_a = row(hot_a)
    slot_a = col(hot_a * counts).astype(i32)
    slot_b = (col(hot_b * counts) + col(jnp.where(lane == key_b, all_a, 0.0))).astype(i32)
    highest = jnp.maximum(jnp.where(from_a, slot_a, 0), jnp.where(from_b, slot_b, 0))
    most_ref[...] = jnp.broadcast_to(jnp.max(highest, axis=0, keepdims=True), (8, 128))

    def exact(cols, mask):
        return lax.dot_general(
            cols, jnp.where(mask, 1.0, 0.0), (((0,), (0,)), ((), ())),
            precision=lax.Precision.HIGHEST, preferred_element_type=f32,
        )

    lane8 = lanes(8)

    def side(*columns):
        out = jnp.zeros((n, 8), f32)
        for at, column in enumerate(columns):
            out = jnp.where(lane8 == at, column.astype(f32), out)
        return out

    shift_a, shift_b = (group - ga) & 3, (group - gb) & 3
    put_a = (shift_a - 1) * KEEP + slot_a
    put_b = (shift_b - 1) * KEEP + slot_b
    local_a, local_b = a & 127, b & 127
    table_a = jnp.where(shift_a == 0, local_a, 128 + put_a)
    table_b = jnp.where(shift_b == 0, local_b, 128 + put_b)
    mine = valid & (group == me)
    pos = exact(side(table_a, table_b, a, b), mine & (lane == chunk * B + place))
    pos_ref[...] = pos.astype(i32)

    wide = lanes(slot_ref.shape[1])
    at_a, at_b = chunk * (3 * KEEP) + put_a, chunk * (3 * KEEP) + put_b
    fits_a, fits_b = from_a & (slot_a < KEEP), from_b & (slot_b < KEEP)
    one = jnp.ones_like(a)
    zero = jnp.zeros_like(a)
    slots = exact(side(local_a, zero, one), fits_a & (ga == me) & (wide == at_a))
    slots += exact(side(local_b, zero, one), fits_b & (gb == me) & (wide == at_b))
    slots += exact(side(zero, place * 2), fits_a & mine & (wide == at_a))
    slots += exact(side(zero, place * 2 + 1), fits_b & mine & (wide == at_b))
    slot_ref[...] = slots.astype(i32)


def route(me, pair_slots):
    flat = pair_slots.reshape(-1, 2)
    width = 128 * -(-(CHUNKS * 3 * KEEP) // 128)
    vmem = pl.BlockSpec(memory_space=pltpu.VMEM)
    return pl.pallas_call(
        route_kernel,
        out_shape=[
            jax.ShapeDtypeStruct((8, 128), jnp.int32),
            jax.ShapeDtypeStruct((8, width), jnp.int32),
            jax.ShapeDtypeStruct((8, 128), jnp.int32),
        ],
        in_specs=[pl.BlockSpec(memory_space=pltpu.SMEM), vmem, vmem],
        out_specs=[vmem, vmem, vmem],
        compiler_params=pltpu.CompilerParams(vmem_limit_bytes=40 << 20),
        cost_estimate=pl.CostEstimate(flops=10_000_000, bytes_accessed=1_000_000, transcendentals=0),
        name="route",
    )(me, flat[:, :1], flat[:, 1:])


def fetch_kernel(count, row_of, first, idx_ref, *refs):
    *tables, out_ref, sem = refs
    ends = []
    for table in tables:
        ends.append((ends[-1] if ends else 0) + table.shape[0])

    def start(i, carry):
        j = row_of(idx_ref, first, i)
        begin = 0
        for table, end in zip(tables, ends):
            if len(tables) == 1:
                pltpu.make_async_copy(table.at[j], out_ref.at[i], sem).start()
            else:
                @pl.when((j >= begin) & (j < end))
                def _(table=table, begin=begin):
                    pltpu.make_async_copy(table.at[j - begin], out_ref.at[i], sem).start()
            begin = end
        return carry

    lax.fori_loop(0, count, start, 0)
    pltpu.make_async_copy(out_ref, out_ref, sem).wait()


def fetch(idx, tables, count, row_of, first, name):
    return pl.pallas_call(
        functools.partial(fetch_kernel, count, row_of, first),
        out_shape=jax.ShapeDtypeStruct((count, ROWS, 128), jnp.float32),
        in_specs=[pl.BlockSpec(memory_space=pltpu.SMEM)] + [pl.BlockSpec(memory_space=pl.ANY)] * len(tables),
        out_specs=pl.BlockSpec(memory_space=pl.ANY),
        scratch_shapes=[pltpu.SemaphoreType.DMA],
        cost_estimate=pl.CostEstimate(flops=0, bytes_accessed=count * 32768, transcendentals=0),
        name=name,
    )(idx, *tables)


def pair_kernel(chunk, place_ref, pos_ref, anchor_ref, in_ref, out_ref, part, dens, resid, second, third, image):
    at = chunk * B + place_ref[0]
    orb_a, orb_b = pos_ref[2, at], pos_ref[3, at]
    ox, oy, oz = [anchor_ref[3 * orb_b + k] - anchor_ref[3 * orb_a + k] for k in range(3)]
    shape = (ROWS, 128)
    line = lax.broadcasted_iota(jnp.int32, shape, 0)
    lane = lax.broadcasted_iota(jnp.int32, shape, 1)
    cy = 2 * line + (lane >> 6)
    cz = lane & 63
    low = lane < 64
    no_y = ((cy == 0) | (cy == B - 1))
    no_up, no_down = cz == B - 1, cz == 0

    def shifter(sy, sz):
        flat = (sy * B + sz + B * B) & (B * B - 1)
        lines, steps = flat >> 7, flat & 127
        inside = (cy >= sy) & (cy < B + sy) & (cz >= sz) & (cz < B + sz)
        keep = lane >= steps

        def shift(plane):
            turned = pltpu.roll(plane, steps, axis=1)
            turned = jnp.where(keep, turned, pltpu.roll(turned, 1, axis=0))
            return jnp.where(inside, pltpu.roll(turned, lines, axis=0), 0.0)

        return shift

    def apply(ref, x):
        here = ref[x + 1]
        swapped = pltpu.roll(here, 64, axis=1)
        other = jnp.where(low, pltpu.roll(swapped, 1, axis=0), pltpu.roll(swapped, ROWS - 1, axis=0))
        beside = ref[x] + ref[x + 2] + swapped + jnp.where(no_y, 0.0, other)
        upper = jnp.where(no_up, 0.0, pltpu.roll(here, 127, axis=1))
        lower = jnp.where(no_down, 0.0, pltpu.roll(here, 1, axis=1))
        return here, 6.0 * here - beside - upper - lower

    zero = jnp.zeros(shape, jnp.float32)
    for ref in (dens, second, third):
        ref[0] = zero
        ref[B + 1] = zero

    def total(x):
        return jnp.sum(x, keepdims=True)

    def planes(step, init=None):
        return lax.fori_loop(0, B, step, zero if init is None else init, unroll=2)

    shift_on = shifter(oy, oz)
    shift_back = shifter(-oy, -oz)

    def begin(x, acc):
        src = x - ox
        inside = jnp.where((src >= 0) & (src < B), 1.0, 0.0)
        moved = shift_on(in_ref[jnp.clip(src, 0, B - 1), 1]) * inside
        density = in_ref[x, 0] * moved
        part[x] = moved
        dens[x + 1] = density
        return acc + density * density

    norm0 = total(planes(begin))

    def first(x, acc):
        here, img = apply(dens, x)
        image[x] = img
        return acc + here * img

    step0 = norm0 / total(planes(first))

    def rest0(x, acc):
        left = dens[x + 1] - step0 * image[x]
        resid[x] = left
        return acc + left * left

    norm1 = total(planes(rest0))
    ratio0 = norm1 / norm0

    def turn1(x, acc):
        second[x + 1] = resid[x] + ratio0 * dens[x + 1]
        return acc

    planes(turn1)

    def again(x, acc):
        here, img = apply(second, x)
        image[x] = img
        return acc + here * img

    step1 = norm1 / total(planes(again))

    def rest1(x, acc):
        left = resid[x] - step1 * image[x]
        resid[x] = left
        return acc + left * left

    norm2 = total(planes(rest1))
    ratio1 = norm2 / norm1

    def turn2(x, acc):
        third[x + 1] = resid[x] + ratio1 * second[x + 1]
        return acc

    planes(turn2)

    def last(x, acc):
        here, img = apply(third, x)
        return acc + here * img

    step2 = norm2 / total(planes(last))

    def finish(x, acc):
        potential = step0 * dens[x + 1] + step1 * second[x + 1] + step2 * third[x + 1]
        out_ref[x, 0] = potential * part[x]
        image[x] = potential * in_ref[x, 0]
        return acc

    planes(finish)

    def back(x, acc):
        src = x + ox
        inside = jnp.where((src >= 0) & (src < B), 1.0, 0.0)
        out_ref[x, 1] = shift_back(image[jnp.clip(src, 0, B - 1)]) * inside
        return acc

    planes(back)


def solve(chunk, place, pos, anchors, boxes):
    smem = pl.BlockSpec(memory_space=pltpu.SMEM)
    vmem = pl.BlockSpec(memory_space=pltpu.VMEM)
    field = pltpu.VMEM((B, ROWS, 128), jnp.float32)
    padded = pltpu.VMEM((B + 2, ROWS, 128), jnp.float32)
    return pl.pallas_call(
        functools.partial(pair_kernel, chunk),
        out_shape=jax.ShapeDtypeStruct((B, 2, ROWS, 128), jnp.float32),
        in_specs=[smem, smem, smem, vmem],
        out_specs=vmem,
        scratch_shapes=[field, padded, field, padded, padded, field],
        compiler_params=pltpu.CompilerParams(vmem_limit_bytes=24 << 20),
        cost_estimate=pl.CostEstimate(flops=60_000_000, bytes_accessed=30_000_000, transcendentals=0),
        name=f"solve{chunk}",
    )(place, pos, anchors, boxes)


def add_kernel(chunk, has_sum, is_last, pos_ref, slot_ref, *refs):
    if has_sum:
        sum_ref, terms_ref, far_ref, out_ref, acc = refs
    else:
        terms_ref, far_ref, out_ref, acc = refs
    total = acc if is_last else out_ref
    if has_sum:
        total[...] = sum_ref[...]
    else:
        total[...] = jnp.zeros(total.shape, jnp.float32)

    def near(p, carry):
        for r in range(2):
            j = pos_ref[r, chunk * B + p]

            @pl.when(j < 128)
            def _(j=j, r=r):
                total[j] = total[j] + terms_ref[p, r]

        return carry

    lax.fori_loop(0, B, near, 0)

    def far(k, carry):
        at = chunk * (3 * KEEP) + k

        @pl.when(slot_ref[2, at] == 1)
        def _():
            j = slot_ref[0, at]
            total[j] = total[j] + far_ref[k]

        return carry

    lax.fori_loop(0, 3 * KEEP, far, 0)
    if is_last:
        for j in range(ROWS):
            out_ref[:, j * 128 : (j + 1) * 128] = acc[:, j, :]


def add_up(chunk, pos, slot, summed, terms, far):
    is_last = chunk == CHUNKS - 1
    smem = pl.BlockSpec(memory_space=pltpu.SMEM)
    vmem = pl.BlockSpec(memory_space=pltpu.VMEM)
    args = ([] if summed is None else [summed]) + [terms, far]
    out = (128, ROWS * 128) if is_last else (128, ROWS, 128)
    return pl.pallas_call(
        functools.partial(add_kernel, chunk, summed is not None, is_last),
        out_shape=jax.ShapeDtypeStruct(out, jnp.float32),
        in_specs=[smem, smem] + [vmem] * len(args),
        out_specs=vmem,
        scratch_shapes=[pltpu.VMEM((128, ROWS, 128), jnp.float32)],
        compiler_params=pltpu.CompilerParams(vmem_limit_bytes=24 << 20),
        cost_estimate=pl.CostEstimate(flops=2_000_000, bytes_accessed=10_000_000, transcendentals=0),
        name=f"add{chunk}",
    )(pos, slot, *args)


def turned(x, shift):
    groups = lax.axis_size("grp")
    return lax.ppermute(x, "grp", [(g, (g + shift) % groups) for g in range(groups)])


def table_row(idx_ref, first, i):
    return idx_ref[i & 1, first + (i >> 1)]


def sent_row(idx_ref, first, i):
    return idx_ref[0, first + i]


def used_row(idx_ref, first, i):
    return idx_ref[1, first + i]


def fitting(orbitals, anchors, place, pos, slot):
    local = orbitals.reshape(128, ROWS, 128)
    anchor_list = anchors.reshape(-1)
    boxes = []
    for c in range(CHUNKS):
        arrived = []
        for d in (1, 2, 3):
            sent = fetch(slot, [local], KEEP, sent_row, (3 * c + d - 1) * KEEP, f"send{c}_{d}")
            arrived.append(turned(sent, d))
        outgoing = fetch(pos, [local] + arrived, 2 * B, table_row, c * B, f"deal{c}")
        boxes.append(lax.all_to_all(outgoing.reshape(B, 2, ROWS, 128), "grid", 0, 0, tiled=True))
    summed = None
    for c in range(CHUNKS):
        terms = solve(c, place, pos, anchor_list, boxes[c])
        terms = lax.all_to_all(terms, "grid", 0, 0, tiled=True)
        flat = terms.reshape(2 * B, ROWS, 128)
        far = []
        for d in (1, 2, 3):
            back = fetch(slot, [flat], KEEP, used_row, (3 * c + d - 1) * KEEP, f"back{c}_{d}")
            far.append(turned(back, -d))
        summed = add_up(c, pos, slot, summed, terms, jnp.concatenate(far))
    return summed


def body(orbitals, anchors, pair_slots):
    me = lax.axis_index("grp").astype(jnp.int32)[None]
    place = lax.axis_index("grid").astype(jnp.int32)[None]
    pos, slot, most = route(me, pair_slots)
    return lax.cond(
        most[0, 0] < KEEP,
        lambda: fitting(orbitals, anchors, place, pos, slot),
        lambda: general(orbitals, anchors, pair_slots),
    )


def solution(mesh):
    return jax.shard_map(
        body,
        mesh=mesh,
        in_specs=(P("grp", "grid"), P(), P()),
        out_specs=P("grp", "grid"),
        check_vma=False,
    )
```

```python
import functools

import jax
import jax.numpy as jnp
from jax import lax
from jax.experimental import pallas as pl
from jax.experimental.pallas import tpu as pltpu
from jax.sharding import PartitionSpec as P

B = 64
PAIR_DEV = 2
ITERS = 3
CHUNKS = 2
ROWS = B * B // 128
KEEP = 32


def shift_field(field, offset, extent):
    plane_size = extent * extent
    padded_x = jnp.pad(field, ((extent, extent), (0, 0)))
    moved = lax.dynamic_slice_in_dim(padded_x, extent - offset[0], extent, 0)
    padded_yz = jnp.pad(moved, ((0, 0), (plane_size, plane_size)))
    linear = offset[1] * extent + offset[2]
    moved = lax.dynamic_slice_in_dim(padded_yz, plane_size - linear, plane_size, 1)
    cells = lax.broadcasted_iota(jnp.int32, (1, plane_size), 1)
    coord_y = cells // extent - offset[1]
    coord_z = cells % extent - offset[2]
    inside = (coord_y >= 0) & (coord_y < extent) & (coord_z >= 0) & (coord_z < extent)
    return jnp.where(inside, moved, jnp.zeros_like(moved))


def operate(field, extent):
    padded_x = jnp.pad(field, ((1, 1), (0, 0)))
    beside = padded_x[2:] + padded_x[:-2]
    padded_y = jnp.pad(field, ((0, 0), (extent, extent)))
    beside = beside + padded_y[:, 2 * extent :] + padded_y[:, : -2 * extent]
    padded_z = jnp.pad(field, ((0, 0), (1, 1)))
    cells = lax.broadcasted_iota(jnp.int32, (1, field.shape[1]), 1) % extent
    upper_z = jnp.where(cells < extent - 1, padded_z[:, 2:], jnp.zeros_like(field))
    lower_z = jnp.where(cells > 0, padded_z[:, :-2], jnp.zeros_like(field))
    return 6.0 * field - beside - upper_z - lower_z


def conjugate(density, extent):
    potential = jnp.zeros_like(density)
    resid = density
    direction = density
    norm_now = jnp.sum(resid * resid)
    for turn in range(ITERS):
        image = operate(direction, extent)
        step_len = norm_now / jnp.sum(direction * image)
        potential = potential + step_len * direction
        resid = resid - step_len * image
        norm_next = jnp.sum(resid * resid)
        direction = resid + norm_next / norm_now * direction
        norm_now = norm_next
    return potential


def pair_terms(field_a, field_b, offset, extent):
    partner = shift_field(field_b, offset, extent)
    density = field_a * partner
    potential = conjugate(density, extent)
    term_a = potential * partner
    term_b = shift_field(potential * field_a, -offset, extent)
    return (term_a, term_b)


def deal_evenly(pair_slots, owner_count, each_owner):
    flat_slots = pair_slots.reshape(-1, 2)
    filled = (flat_slots[:, 0] >= 0).astype(jnp.int32)
    order = jnp.arange(flat_slots.shape[0], dtype=jnp.int32)
    position = jnp.sum(jnp.where(order[None, :] < order[:, None], filled[None, :], 0), axis=1)
    wanted = lax.broadcasted_iota(jnp.int32, (owner_count, each_owner), 1) * owner_count
    wanted = (wanted + lax.broadcasted_iota(jnp.int32, (owner_count, each_owner), 0)).reshape(-1)
    matched = (position[None, :] == wanted[:, None]) & (filled[None, :] == 1)
    picked = jnp.dot(matched.astype(jnp.int32), flat_slots)
    return picked.reshape(owner_count, each_owner, 2)


def general(orbitals, anchors, pair_slots):
    extent = B
    grid_count = lax.axis_size("grid")
    owner_count = lax.axis_size("grp") * grid_count
    group_idx = lax.axis_index("grp")
    place_idx = lax.axis_index("grid")
    assignment = deal_evenly(pair_slots, owner_count, PAIR_DEV)
    filled = assignment[..., 0] >= 0
    safe_ids = jnp.maximum(assignment, 0)
    pieces = lax.all_gather(orbitals, "grp", axis=0, tiled=True)
    group_table = lax.dynamic_slice_in_dim(safe_ids, group_idx * grid_count, grid_count, 0)
    gather_ids = jnp.transpose(group_table, (1, 2, 0))
    outgoing = pieces[gather_ids]
    arrived = lax.all_to_all(outgoing, "grid", split_axis=2, concat_axis=2, tiled=True)
    owner_idx = group_idx * grid_count + place_idx
    own_pairs = safe_ids[owner_idx]
    own_filled = filled[owner_idx]
    offsets = anchors[own_pairs[:, 1]] - anchors[own_pairs[:, 0]]

    def solve_slot(slot_item):
        boxes_pair, offset, flag = slot_item
        term_a, term_b = pair_terms(boxes_pair[0], boxes_pair[1], offset, extent)
        weight_flag = jnp.where(flag, 1.0, 0.0).astype(jnp.float32)
        return jnp.stack([term_a, term_b]) * weight_flag

    terms = lax.map(solve_slot, (arrived, offsets, own_filled))
    returned = lax.all_to_all(terms, "grid", split_axis=2, concat_axis=2, tiled=True)
    flat_terms = returned.reshape(-1, returned.shape[-1])
    summed = jax.ops.segment_sum(flat_terms, gather_ids.reshape(-1), num_segments=anchors.shape[0])
    return lax.psum_scatter(summed, "grp", scatter_dimension=0, tiled=True)


def route_kernel(me_ref, a_ref, b_ref, pos_ref, slot_ref, most_ref):
    me = me_ref[0]
    a, b = a_ref[...], b_ref[...]
    n = a.shape[0]
    f32, i32 = jnp.float32, jnp.int32

    def lanes(width):
        return lax.broadcasted_iota(i32, (n, width), 1)

    def row(x, width=128):
        return jnp.sum(x, axis=0, keepdims=True)

    def col(x):
        return jnp.sum(x, axis=1, keepdims=True)

    before = (lax.broadcasted_iota(i32, (n, n), 0) > lax.broadcasted_iota(i32, (n, n), 1))
    before = jnp.where(before, 1.0, 0.0).astype(jnp.bfloat16)

    def count_before(hot):
        return jnp.dot(before, hot.astype(jnp.bfloat16), preferred_element_type=f32)

    lane = lanes(128)
    valid = a >= 0
    ga, gb = a >> 7, b >> 7
    typ = jnp.where(valid, ga * 4 + gb, -1)
    hot = jnp.where(lane == typ, 1.0, 0.0)
    rank = col(count_before(hot) * hot).astype(i32)
    turn = (rank + ga + gb) & 3
    bin_no = jnp.where(valid, jnp.where((turn & 1) == 0, ga, gb) * CHUNKS + (turn >> 1), -1)
    hot = jnp.where(lane == bin_no, 1.0, 0.0)
    rank = col(count_before(hot) * hot)
    load = row(hot)
    over = jnp.maximum(load - B, 0.0)
    lane1 = lax.broadcasted_iota(i32, (1, 128), 1)
    room = jnp.where(lane1 < 4 * CHUNKS, jnp.maximum(B - load, 0.0), 0.0)
    upper = lax.broadcasted_iota(i32, (128, 128), 0) < lax.broadcasted_iota(i32, (128, 128), 1)
    upper = jnp.where(upper, 1.0, 0.0)
    both = jnp.where(lax.broadcasted_iota(i32, (8, 128), 0) == 0, over, room)
    sums = jnp.dot(both, upper, precision=lax.Precision.HIGHEST, preferred_element_type=f32)
    over_before, room_before = sums[0:1], sums[1:2]
    spilled = valid & (rank >= B)
    spill_no = rank - B + col(hot * over_before)
    lands = (spill_no >= room_before) & (spill_no < room_before + room)
    landed = jnp.where(lands, 1.0, 0.0)
    hot = jnp.where(spilled, landed, hot)
    place = jnp.where(spilled, col(landed * (load - room_before)) + spill_no, rank).astype(i32)
    bin_no = col(hot * lane.astype(f32)).astype(i32)
    group, chunk = bin_no >> 1, bin_no & 1

    from_a, from_b = valid & (ga != group), valid & (gb != group)
    key_a = jnp.where(from_a, (chunk * 4 + ga) * 4 + group, -1)
    key_b = jnp.where(from_b, (chunk * 4 + gb) * 4 + group, -1)
    hot_a = jnp.where(lane == key_a, 1.0, 0.0)
    hot_b = jnp.where((lane >= 32) & (lane - 32 == key_b), 1.0, 0.0)
    counts = count_before(hot_a + hot_b)
    all_a = row(hot_a)
    slot_a = col(hot_a * counts).astype(i32)
    slot_b = (col(hot_b * counts) + col(jnp.where(lane == key_b, all_a, 0.0))).astype(i32)
    highest = jnp.maximum(jnp.where(from_a, slot_a, 0), jnp.where(from_b, slot_b, 0))
    most_ref[...] = jnp.broadcast_to(jnp.max(highest, axis=0, keepdims=True), (8, 128))

    def exact(cols, mask):
        return lax.dot_general(
            cols, jnp.where(mask, 1.0, 0.0), (((0,), (0,)), ((), ())),
            precision=lax.Precision.HIGHEST, preferred_element_type=f32,
        )

    lane8 = lanes(8)

    def side(*columns):
        out = jnp.zeros((n, 8), f32)
        for at, column in enumerate(columns):
            out = jnp.where(lane8 == at, column.astype(f32), out)
        return out

    shift_a, shift_b = (group - ga) & 3, (group - gb) & 3
    put_a = (shift_a - 1) * KEEP + slot_a
    put_b = (shift_b - 1) * KEEP + slot_b
    local_a, local_b = a & 127, b & 127
    table_a = jnp.where(shift_a == 0, local_a, 128 + put_a)
    table_b = jnp.where(shift_b == 0, local_b, 128 + put_b)
    mine = valid & (group == me)
    pos = exact(side(table_a, table_b, a, b), mine & (lane == chunk * B + place))
    pos_ref[...] = pos.astype(i32)

    wide = lanes(slot_ref.shape[1])
    at_a, at_b = chunk * (3 * KEEP) + put_a, chunk * (3 * KEEP) + put_b
    fits_a, fits_b = from_a & (slot_a < KEEP), from_b & (slot_b < KEEP)
    one = jnp.ones_like(a)
    zero = jnp.zeros_like(a)
    slots = exact(side(local_a, zero, one), fits_a & (ga == me) & (wide == at_a))
    slots += exact(side(local_b, zero, one), fits_b & (gb == me) & (wide == at_b))
    slots += exact(side(zero, place * 2), fits_a & mine & (wide == at_a))
    slots += exact(side(zero, place * 2 + 1), fits_b & mine & (wide == at_b))
    slot_ref[...] = slots.astype(i32)


def route(me, pair_slots):
    flat = pair_slots.reshape(-1, 2)
    width = 128 * -(-(CHUNKS * 3 * KEEP) // 128)
    vmem = pl.BlockSpec(memory_space=pltpu.VMEM)
    return pl.pallas_call(
        route_kernel,
        out_shape=[
            jax.ShapeDtypeStruct((8, 128), jnp.int32),
            jax.ShapeDtypeStruct((8, width), jnp.int32),
            jax.ShapeDtypeStruct((8, 128), jnp.int32),
        ],
        in_specs=[pl.BlockSpec(memory_space=pltpu.SMEM), vmem, vmem],
        out_specs=[vmem, vmem, vmem],
        compiler_params=pltpu.CompilerParams(vmem_limit_bytes=40 << 20),
        cost_estimate=pl.CostEstimate(flops=10_000_000, bytes_accessed=1_000_000, transcendentals=0),
        name="route",
    )(me, flat[:, :1], flat[:, 1:])


def fetch_kernel(row_of, first, tables, idx_ref, *refs):
    parts, (*outs, table, sem) = refs[:tables], refs[tables:]
    copies, end = [], 0
    for k, part in enumerate(parts):
        copies.append(pltpu.make_async_copy(part, table.at[pl.ds(end, part.shape[0])], sem.at[k]))
        end += part.shape[0]
    for copy in copies:
        copy.start()
    for copy in copies:
        copy.wait()
    for k, out_ref in enumerate(outs):
        count = out_ref.shape[0]

        def move(i, carry, out_ref=out_ref, k=k, count=count):
            out_ref[i] = table[row_of(idx_ref, first + k * count, i)]
            return carry

        lax.fori_loop(0, count, move, 0, unroll=4)


def fetch(idx, tables, outs, count, row_of, first, name):
    rows = sum(t.shape[0] for t in tables)
    return pl.pallas_call(
        functools.partial(fetch_kernel, row_of, first, len(tables)),
        out_shape=[jax.ShapeDtypeStruct((count, ROWS, 128), jnp.float32)] * outs,
        in_specs=[pl.BlockSpec(memory_space=pltpu.SMEM)] + [pl.BlockSpec(memory_space=pl.ANY)] * len(tables),
        out_specs=[pl.BlockSpec(memory_space=pltpu.VMEM)] * outs,
        scratch_shapes=[pltpu.VMEM((rows, ROWS, 128), jnp.float32), pltpu.SemaphoreType.DMA((len(tables),))],
        compiler_params=pltpu.CompilerParams(vmem_limit_bytes=16 << 20),
        cost_estimate=pl.CostEstimate(flops=0, bytes_accessed=(rows + count * outs) * 16384, transcendentals=0),
        name=name,
    )(idx, *tables)


def pair_kernel(chunk, place_ref, pos_ref, anchor_ref, in_ref, out_ref, part, dens, resid, second, third, image):
    at = chunk * B + place_ref[0]
    orb_a, orb_b = pos_ref[2, at], pos_ref[3, at]
    ox, oy, oz = [anchor_ref[3 * orb_b + k] - anchor_ref[3 * orb_a + k] for k in range(3)]
    shape = (ROWS, 128)
    line = lax.broadcasted_iota(jnp.int32, shape, 0)
    lane = lax.broadcasted_iota(jnp.int32, shape, 1)
    cy = 2 * line + (lane >> 6)
    cz = lane & 63
    low = lane < 64
    no_y = ((cy == 0) | (cy == B - 1))
    no_up, no_down = cz == B - 1, cz == 0

    def shifter(sy, sz):
        flat = (sy * B + sz + B * B) & (B * B - 1)
        lines, steps = flat >> 7, flat & 127
        inside = (cy >= sy) & (cy < B + sy) & (cz >= sz) & (cz < B + sz)
        keep = lane >= steps

        def shift(plane):
            turned = pltpu.roll(plane, steps, axis=1)
            turned = jnp.where(keep, turned, pltpu.roll(turned, 1, axis=0))
            return jnp.where(inside, pltpu.roll(turned, lines, axis=0), 0.0)

        return shift

    def apply(ref, x):
        here = ref[x + 1]
        swapped = pltpu.roll(here, 64, axis=1)
        other = jnp.where(low, pltpu.roll(swapped, 1, axis=0), pltpu.roll(swapped, ROWS - 1, axis=0))
        beside = ref[x] + ref[x + 2] + swapped + jnp.where(no_y, 0.0, other)
        upper = jnp.where(no_up, 0.0, pltpu.roll(here, 127, axis=1))
        lower = jnp.where(no_down, 0.0, pltpu.roll(here, 1, axis=1))
        return here, 6.0 * here - beside - upper - lower

    zero = jnp.zeros(shape, jnp.float32)
    for ref in (dens, second, third):
        ref[0] = zero
        ref[B + 1] = zero

    def total(x):
        return jnp.sum(x, keepdims=True)

    def planes(step, init=None):
        return lax.fori_loop(0, B, step, zero if init is None else init, unroll=2)

    shift_on = shifter(oy, oz)
    shift_back = shifter(-oy, -oz)

    def begin(x, acc):
        src = x - ox
        inside = jnp.where((src >= 0) & (src < B), 1.0, 0.0)
        moved = shift_on(in_ref[jnp.clip(src, 0, B - 1), 1]) * inside
        density = in_ref[x, 0] * moved
        part[x] = moved
        dens[x + 1] = density
        return acc + density * density

    norm0 = total(planes(begin))

    def first(x, acc):
        here, img = apply(dens, x)
        image[x] = img
        return acc + here * img

    step0 = norm0 / total(planes(first))

    def rest0(x, acc):
        left = dens[x + 1] - step0 * image[x]
        resid[x] = left
        return acc + left * left

    norm1 = total(planes(rest0))
    ratio0 = norm1 / norm0

    def turn1(x, acc):
        second[x + 1] = resid[x] + ratio0 * dens[x + 1]
        return acc

    planes(turn1)

    def again(x, acc):
        here, img = apply(second, x)
        image[x] = img
        return acc + here * img

    step1 = norm1 / total(planes(again))

    def rest1(x, acc):
        left = resid[x] - step1 * image[x]
        resid[x] = left
        return acc + left * left

    norm2 = total(planes(rest1))
    ratio1 = norm2 / norm1

    def turn2(x, acc):
        third[x + 1] = resid[x] + ratio1 * second[x + 1]
        return acc

    planes(turn2)

    def last(x, acc):
        here, img = apply(third, x)
        return acc + here * img

    step2 = norm2 / total(planes(last))

    def finish(x, acc):
        potential = step0 * dens[x + 1] + step1 * second[x + 1] + step2 * third[x + 1]
        out_ref[x, 0] = potential * part[x]
        image[x] = potential * in_ref[x, 0]
        return acc

    planes(finish)

    def back(x, acc):
        src = x + ox
        inside = jnp.where((src >= 0) & (src < B), 1.0, 0.0)
        out_ref[x, 1] = shift_back(image[jnp.clip(src, 0, B - 1)]) * inside
        return acc

    planes(back)


def solve(chunk, place, pos, anchors, boxes):
    smem = pl.BlockSpec(memory_space=pltpu.SMEM)
    vmem = pl.BlockSpec(memory_space=pltpu.VMEM)
    field = pltpu.VMEM((B, ROWS, 128), jnp.float32)
    padded = pltpu.VMEM((B + 2, ROWS, 128), jnp.float32)
    return pl.pallas_call(
        functools.partial(pair_kernel, chunk),
        out_shape=jax.ShapeDtypeStruct((B, 2, ROWS, 128), jnp.float32),
        in_specs=[smem, smem, smem, vmem],
        out_specs=vmem,
        scratch_shapes=[field, padded, field, padded, padded, field],
        compiler_params=pltpu.CompilerParams(vmem_limit_bytes=24 << 20),
        cost_estimate=pl.CostEstimate(flops=60_000_000, bytes_accessed=30_000_000, transcendentals=0),
        name=f"solve{chunk}",
    )(place, pos, anchors, boxes)


def add_kernel(chunk, has_sum, is_last, pos_ref, slot_ref, *refs):
    if has_sum:
        sum_ref, terms_ref, *far_refs, out_ref, acc = refs
    else:
        terms_ref, *far_refs, out_ref, acc = refs
    total = acc if is_last else out_ref
    if has_sum:
        total[...] = sum_ref[...]
    else:
        total[...] = jnp.zeros(total.shape, jnp.float32)

    def near(p, carry):
        for r in range(2):
            j = pos_ref[r, chunk * B + p]

            @pl.when(j < 128)
            def _(j=j, r=r):
                total[j] = total[j] + terms_ref[p, r]

        return carry

    lax.fori_loop(0, B, near, 0)

    def far(k, carry):
        for d, far_ref in enumerate(far_refs):
            at = (3 * chunk + d) * KEEP + k

            @pl.when(slot_ref[2, at] == 1)
            def _(at=at, far_ref=far_ref):
                j = slot_ref[0, at]
                total[j] = total[j] + far_ref[k]

        return carry

    lax.fori_loop(0, KEEP, far, 0)
    if is_last:
        for j in range(ROWS):
            out_ref[:, j * 128 : (j + 1) * 128] = acc[:, j, :]


def add_up(chunk, pos, slot, summed, terms, far):
    is_last = chunk == CHUNKS - 1
    smem = pl.BlockSpec(memory_space=pltpu.SMEM)
    vmem = pl.BlockSpec(memory_space=pltpu.VMEM)
    args = ([] if summed is None else [summed]) + [terms, *far]
    out = (128, ROWS * 128) if is_last else (128, ROWS, 128)
    return pl.pallas_call(
        functools.partial(add_kernel, chunk, summed is not None, is_last),
        out_shape=jax.ShapeDtypeStruct(out, jnp.float32),
        in_specs=[smem, smem] + [vmem] * len(args),
        out_specs=vmem,
        scratch_shapes=[pltpu.VMEM((128, ROWS, 128), jnp.float32)],
        compiler_params=pltpu.CompilerParams(vmem_limit_bytes=24 << 20),
        cost_estimate=pl.CostEstimate(flops=2_000_000, bytes_accessed=10_000_000, transcendentals=0),
        name=f"add{chunk}",
    )(pos, slot, *args)


def turned(x, shift):
    groups = lax.axis_size("grp")
    return lax.ppermute(x, "grp", [(g, (g + shift) % groups) for g in range(groups)])


def table_row(idx_ref, first, i):
    return idx_ref[i & 1, first + (i >> 1)]


def sent_row(idx_ref, first, i):
    return idx_ref[0, first + i]


def used_row(idx_ref, first, i):
    return idx_ref[1, first + i]


def fitting(orbitals, anchors, place, pos, slot):
    local = orbitals.reshape(128, ROWS, 128)
    anchor_list = anchors.reshape(-1)
    boxes = []
    for c in range(CHUNKS):
        sent = fetch(slot, [local], 3, KEEP, sent_row, 3 * c * KEEP, f"send{c}")
        arrived = [turned(x, d) for d, x in enumerate(sent, 1)]
        [outgoing] = fetch(pos, [local] + arrived, 1, 2 * B, table_row, c * B, f"deal{c}")
        boxes.append(lax.all_to_all(outgoing.reshape(B, 2, ROWS, 128), "grid", 0, 0, tiled=True))
    summed = None
    for c in range(CHUNKS):
        terms = solve(c, place, pos, anchor_list, boxes[c])
        terms = lax.all_to_all(terms, "grid", 0, 0, tiled=True)
        flat = terms.reshape(2 * B, ROWS, 128)
        back = fetch(slot, [flat], 3, KEEP, used_row, 3 * c * KEEP, f"back{c}")
        far = [turned(x, -d) for d, x in enumerate(back, 1)]
        summed = add_up(c, pos, slot, summed, terms, far)
    return summed


def body(orbitals, anchors, pair_slots):
    me = lax.axis_index("grp").astype(jnp.int32)[None]
    place = lax.axis_index("grid").astype(jnp.int32)[None]
    pos, slot, most = route(me, pair_slots)
    return lax.cond(
        most[0, 0] < KEEP,
        lambda: fitting(orbitals, anchors, place, pos, slot),
        lambda: general(orbitals, anchors, pair_slots),
    )


def solution(mesh):
    return jax.shard_map(
        body,
        mesh=mesh,
        in_specs=(P("grp", "grid"), P(), P()),
        out_specs=P("grp", "grid"),
        check_vma=False,
    )
```

```python
import functools

import jax
import jax.numpy as jnp
from jax import lax
from jax.experimental import pallas as pl
from jax.experimental.pallas import tpu as pltpu
from jax.sharding import PartitionSpec as P

B = 64
PAIR_DEV = 2
ITERS = 3
ROWS = B * B // 128
KEEP = 48
UNROLL = 8


def shift_field(field, offset, extent):
    plane_size = extent * extent
    padded_x = jnp.pad(field, ((extent, extent), (0, 0)))
    moved = lax.dynamic_slice_in_dim(padded_x, extent - offset[0], extent, 0)
    padded_yz = jnp.pad(moved, ((0, 0), (plane_size, plane_size)))
    linear = offset[1] * extent + offset[2]
    moved = lax.dynamic_slice_in_dim(padded_yz, plane_size - linear, plane_size, 1)
    cells = lax.broadcasted_iota(jnp.int32, (1, plane_size), 1)
    coord_y = cells // extent - offset[1]
    coord_z = cells % extent - offset[2]
    inside = (coord_y >= 0) & (coord_y < extent) & (coord_z >= 0) & (coord_z < extent)
    return jnp.where(inside, moved, jnp.zeros_like(moved))


def operate(field, extent):
    padded_x = jnp.pad(field, ((1, 1), (0, 0)))
    beside = padded_x[2:] + padded_x[:-2]
    padded_y = jnp.pad(field, ((0, 0), (extent, extent)))
    beside = beside + padded_y[:, 2 * extent :] + padded_y[:, : -2 * extent]
    padded_z = jnp.pad(field, ((0, 0), (1, 1)))
    cells = lax.broadcasted_iota(jnp.int32, (1, field.shape[1]), 1) % extent
    upper_z = jnp.where(cells < extent - 1, padded_z[:, 2:], jnp.zeros_like(field))
    lower_z = jnp.where(cells > 0, padded_z[:, :-2], jnp.zeros_like(field))
    return 6.0 * field - beside - upper_z - lower_z


def conjugate(density, extent):
    potential = jnp.zeros_like(density)
    resid = density
    direction = density
    norm_now = jnp.sum(resid * resid)
    for turn in range(ITERS):
        image = operate(direction, extent)
        step_len = norm_now / jnp.sum(direction * image)
        potential = potential + step_len * direction
        resid = resid - step_len * image
        norm_next = jnp.sum(resid * resid)
        direction = resid + norm_next / norm_now * direction
        norm_now = norm_next
    return potential


def pair_terms(field_a, field_b, offset, extent):
    partner = shift_field(field_b, offset, extent)
    density = field_a * partner
    potential = conjugate(density, extent)
    term_a = potential * partner
    term_b = shift_field(potential * field_a, -offset, extent)
    return (term_a, term_b)


def deal_evenly(pair_slots, owner_count, each_owner):
    flat_slots = pair_slots.reshape(-1, 2)
    filled = (flat_slots[:, 0] >= 0).astype(jnp.int32)
    order = jnp.arange(flat_slots.shape[0], dtype=jnp.int32)
    position = jnp.sum(jnp.where(order[None, :] < order[:, None], filled[None, :], 0), axis=1)
    wanted = lax.broadcasted_iota(jnp.int32, (owner_count, each_owner), 1) * owner_count
    wanted = (wanted + lax.broadcasted_iota(jnp.int32, (owner_count, each_owner), 0)).reshape(-1)
    matched = (position[None, :] == wanted[:, None]) & (filled[None, :] == 1)
    picked = jnp.dot(matched.astype(jnp.int32), flat_slots)
    return picked.reshape(owner_count, each_owner, 2)


def general(orbitals, anchors, pair_slots):
    extent = B
    grid_count = lax.axis_size("grid")
    owner_count = lax.axis_size("grp") * grid_count
    group_idx = lax.axis_index("grp")
    place_idx = lax.axis_index("grid")
    assignment = deal_evenly(pair_slots, owner_count, PAIR_DEV)
    filled = assignment[..., 0] >= 0
    safe_ids = jnp.maximum(assignment, 0)
    pieces = lax.all_gather(orbitals, "grp", axis=0, tiled=True)
    group_table = lax.dynamic_slice_in_dim(safe_ids, group_idx * grid_count, grid_count, 0)
    gather_ids = jnp.transpose(group_table, (1, 2, 0))
    outgoing = pieces[gather_ids]
    arrived = lax.all_to_all(outgoing, "grid", split_axis=2, concat_axis=2, tiled=True)
    owner_idx = group_idx * grid_count + place_idx
    own_pairs = safe_ids[owner_idx]
    own_filled = filled[owner_idx]
    offsets = anchors[own_pairs[:, 1]] - anchors[own_pairs[:, 0]]

    def solve_slot(slot_item):
        boxes_pair, offset, flag = slot_item
        term_a, term_b = pair_terms(boxes_pair[0], boxes_pair[1], offset, extent)
        weight_flag = jnp.where(flag, 1.0, 0.0).astype(jnp.float32)
        return jnp.stack([term_a, term_b]) * weight_flag

    terms = lax.map(solve_slot, (arrived, offsets, own_filled))
    returned = lax.all_to_all(terms, "grid", split_axis=2, concat_axis=2, tiled=True)
    flat_terms = returned.reshape(-1, returned.shape[-1])
    summed = jax.ops.segment_sum(flat_terms, gather_ids.reshape(-1), num_segments=anchors.shape[0])
    return lax.psum_scatter(summed, "grp", scatter_dimension=0, tiled=True)


def route_kernel(me_ref, a_ref, b_ref, pos_ref, slot_ref, fits_ref):
    me = me_ref[0]
    a, b = a_ref[...], b_ref[...]
    n = a.shape[0]
    f32, i32 = jnp.float32, jnp.int32
    groups, each = 4, 2 * B

    def col(x):
        return jnp.sum(x, axis=1, keepdims=True)

    before = lax.broadcasted_iota(i32, (n, n), 0) > lax.broadcasted_iota(i32, (n, n), 1)
    before = jnp.where(before, 1.0, 0.0).astype(jnp.bfloat16)

    def rank_in(hot):
        return col(jnp.dot(before, hot.astype(jnp.bfloat16), preferred_element_type=f32) * hot).astype(i32)

    lane = lax.broadcasted_iota(i32, (n, 128), 1)
    valid = a >= 0
    ga, gb = a >> 7, b >> 7
    low, high = jnp.minimum(ga, gb), jnp.maximum(ga, gb)
    hot = jnp.where(valid & (lane == low * groups + high), 1.0, 0.0)
    rank = rank_in(hot)

    sums = jnp.sum(hot, axis=0, keepdims=True).astype(i32)
    lane1 = lax.broadcasted_iota(i32, (1, 128), 1)
    count, up = {}, {}
    for g in range(groups):
        for h in range(g, groups):
            count[g, h] = jnp.sum(jnp.where(lane1 == g * groups + h, sums, 0))
            up[g, h] = (count[g, h] >> 1) if h > g else 0

    def loads():
        load = [0] * groups
        for (g, h), c in count.items():
            load[g] = load[g] + (c - up[g, h])
            load[h] = load[h] + up[g, h]
        return load

    load = loads()
    for g, h in count:
        if h > g:
            up[g, h] = up[g, h] + ((load[g] - load[h] + 2) >> 2)
    load = loads()
    excess = 0
    for g in range(groups - 1):
        excess = excess + load[g] - each
        up[g, g + 1] = up[g, g + 1] + excess
    fits = 1
    goes_up = jnp.zeros((1, 128), i32)
    for (g, h), c in count.items():
        if h > g:
            u = up[g, h]
            fine = (u >= 0) & (u <= KEEP) & (c - u >= 0) & (c - u <= KEEP)
            fits = jnp.where(fine, fits, 0)
            goes_up = jnp.where(lane1 == g * groups + h, u, goes_up)
    fits_ref[0] = fits

    ups = col(hot * goes_up.astype(f32)).astype(i32)
    rises = rank < ups
    group = jnp.where(rises, high, low)
    source = low + high - group
    crosses = valid & (low != high)
    hot = jnp.where(valid & (lane == group), 1.0, 0.0)
    q = rank_in(hot)
    put = (((group - source) & 3) - 1) * KEEP + jnp.where(rises, rank, rank - ups)
    near_b = ga != group
    near = jnp.where(near_b, b, a) & 127
    far = jnp.where(near_b, a, b) & 127
    table = jnp.where(crosses, 128 + put, far)

    def side(*columns):
        at = lax.broadcasted_iota(i32, (n, 8), 1)
        out = jnp.zeros((n, 8), f32)
        for k, column in enumerate(columns):
            out = jnp.where(at == k, column.astype(f32), out)
        return out.astype(jnp.bfloat16)

    def spread(columns, mask):
        hot = jnp.where(mask, 1.0, 0.0).astype(jnp.bfloat16)
        out = lax.dot_general(columns, hot, (((0,), (0,)), ((), ())), preferred_element_type=f32)
        return out.astype(i32)

    mine = valid & (group == me)
    flag = jnp.where(near_b, 1, 0)
    columns = side(near, table & 255, a & 255, b & 255, flag, table >> 8, a >> 8, b >> 8)
    got = spread(columns, mine & (lane == q))
    pos_ref[...] = got
    pos_ref[1:4] = got[1:4] + 256 * got[5:8]
    wide = lax.broadcasted_iota(i32, (n, slot_ref.shape[1]), 1)
    here = wide == put
    zero = jnp.zeros_like(a)
    slots = spread(side(far, zero, zero + 1), crosses & (source == me) & here)
    slot_ref[...] = slots + spread(side(zero, q), crosses & mine & here)


def route(me, pair_slots):
    flat = pair_slots.reshape(-1, 2)
    width = 128 * -(-(3 * KEEP) // 128)
    vmem, smem = pl.BlockSpec(memory_space=pltpu.VMEM), pl.BlockSpec(memory_space=pltpu.SMEM)
    return pl.pallas_call(
        route_kernel,
        out_shape=[
            jax.ShapeDtypeStruct((8, 128), jnp.int32),
            jax.ShapeDtypeStruct((8, width), jnp.int32),
            jax.ShapeDtypeStruct((1,), jnp.int32),
        ],
        in_specs=[smem, vmem, vmem],
        out_specs=[vmem, vmem, smem],
        compiler_params=pltpu.CompilerParams(vmem_limit_bytes=40 << 20),
        cost_estimate=pl.CostEstimate(flops=10_000_000, bytes_accessed=1_000_000, transcendentals=0),
        name="route",
    )(me, flat[:, :1], flat[:, 1:])


def fetch_kernel(row_of, first, tables, idx_ref, *refs):
    parts, (*outs, table, sem) = refs[:tables], refs[tables:]
    copies, end = [], 0
    for k, part in enumerate(parts):
        copies.append(pltpu.make_async_copy(part, table.at[pl.ds(end, part.shape[0])], sem.at[k]))
        end += part.shape[0]
    for copy in copies:
        copy.start()
    for copy in copies:
        copy.wait()
    for k, out_ref in enumerate(outs):
        count = out_ref.shape[0]

        def move(i, carry, out_ref=out_ref, k=k, count=count):
            out_ref[i] = table[row_of(idx_ref, first + k * count, i)]
            return carry

        lax.fori_loop(0, count, move, 0, unroll=4)


def fetch(idx, tables, outs, count, row_of, first, name):
    rows = sum(t.shape[0] for t in tables)
    return pl.pallas_call(
        functools.partial(fetch_kernel, row_of, first, len(tables)),
        out_shape=[jax.ShapeDtypeStruct((count, ROWS, 128), jnp.float32)] * outs,
        in_specs=[pl.BlockSpec(memory_space=pltpu.SMEM)] + [pl.BlockSpec(memory_space=pl.ANY)] * len(tables),
        out_specs=[pl.BlockSpec(memory_space=pltpu.VMEM)] * outs,
        scratch_shapes=[pltpu.VMEM((rows, ROWS, 128), jnp.float32), pltpu.SemaphoreType.DMA((len(tables),))],
        compiler_params=pltpu.CompilerParams(vmem_limit_bytes=16 << 20),
        cost_estimate=pl.CostEstimate(flops=0, bytes_accessed=(rows + count * outs) * 16384, transcendentals=0),
        name=name,
    )(idx, *tables)


def solve_pair(orb_a, orb_b, anchor_ref, box_a, box_b, term_a, term_b, part, dens, resid, second, third, image):
    ox, oy, oz = [anchor_ref[3 * orb_b + k] - anchor_ref[3 * orb_a + k] for k in range(3)]
    shape = (ROWS, 128)
    line = lax.broadcasted_iota(jnp.int32, shape, 0)
    lane = lax.broadcasted_iota(jnp.int32, shape, 1)
    cy = 2 * line + (lane >> 6)
    cz = lane & 63
    low = lane < 64
    no_y = ((cy == 0) | (cy == B - 1))
    no_up, no_down = cz == B - 1, cz == 0

    def shifter(sy, sz):
        flat = (sy * B + sz + B * B) & (B * B - 1)
        lines, steps = flat >> 7, flat & 127
        inside = (cy >= sy) & (cy < B + sy) & (cz >= sz) & (cz < B + sz)
        keep = lane >= steps

        def shift(plane):
            turned = pltpu.roll(plane, steps, axis=1)
            turned = jnp.where(keep, turned, pltpu.roll(turned, 1, axis=0))
            return jnp.where(inside, pltpu.roll(turned, lines, axis=0), 0.0)

        return shift

    def apply(ref, x):
        here = ref[x + 1]
        swapped = pltpu.roll(here, 64, axis=1)
        other = jnp.where(low, pltpu.roll(swapped, 1, axis=0), pltpu.roll(swapped, ROWS - 1, axis=0))
        beside = ref[x] + ref[x + 2] + swapped + jnp.where(no_y, 0.0, other)
        upper = jnp.where(no_up, 0.0, pltpu.roll(here, 127, axis=1))
        lower = jnp.where(no_down, 0.0, pltpu.roll(here, 1, axis=1))
        return here, 6.0 * here - beside - upper - lower

    zero = jnp.zeros(shape, jnp.float32)
    for ref in (dens, second, third):
        ref[0] = zero
        ref[B + 1] = zero

    def total(x):
        return jnp.sum(x, keepdims=True)

    def planes(step, init=None):
        return lax.fori_loop(0, B, step, zero if init is None else init, unroll=UNROLL)

    shift_on = shifter(oy, oz)
    shift_back = shifter(-oy, -oz)

    def begin(x, acc):
        src = x - ox
        inside = jnp.where((src >= 0) & (src < B), 1.0, 0.0)
        moved = shift_on(box_b[jnp.clip(src, 0, B - 1)]) * inside
        density = box_a[x] * moved
        part[x] = moved
        dens[x + 1] = density
        return acc + density * density

    norm0 = total(planes(begin))

    def first(x, acc):
        here, img = apply(dens, x)
        image[x] = img
        return acc + here * img

    step0 = norm0 / total(planes(first))

    def rest0(x, acc):
        left = dens[x + 1] - step0 * image[x]
        resid[x] = left
        return acc + left * left

    norm1 = total(planes(rest0))
    ratio0 = norm1 / norm0

    def turn1(x, acc):
        second[x + 1] = resid[x] + ratio0 * dens[x + 1]
        return acc

    planes(turn1)

    def again(x, acc):
        here, img = apply(second, x)
        image[x] = img
        return acc + here * img

    step1 = norm1 / total(planes(again))

    def rest1(x, acc):
        left = resid[x] - step1 * image[x]
        resid[x] = left
        return acc + left * left

    norm2 = total(planes(rest1))
    ratio1 = norm2 / norm1

    def turn2(x, acc):
        third[x + 1] = resid[x] + ratio1 * second[x + 1]
        return acc

    planes(turn2)

    def last(x, acc):
        here, img = apply(third, x)
        return acc + here * img

    step2 = norm2 / total(planes(last))

    def finish(x, acc):
        potential = step0 * dens[x + 1] + step1 * second[x + 1] + step2 * third[x + 1]
        term_a[x] = potential * part[x]
        image[x] = potential * box_a[x]
        return acc

    planes(finish)

    def back(x, acc):
        src = x + ox
        inside = jnp.where((src >= 0) & (src < B), 1.0, 0.0)
        term_b[x] = shift_back(image[jnp.clip(src, 0, B - 1)]) * inside
        return acc

    planes(back)


def pair_kernel(place_ref, pos_ref, anchor_ref, near_ref, far_ref, near_out, far_out, boxes, terms, *rest):
    *fields, sem_in, sem_out = rest
    at = [s * B + place_ref[0] for s in range(PAIR_DEV)]
    flags = [pos_ref[4, k] for k in at]

    def pulls(s):
        return [
            pltpu.make_async_copy(near_ref.at[:, s], boxes.at[s, flags[s]], sem_in.at[s, 0]),
            pltpu.make_async_copy(far_ref.at[:, s], boxes.at[s, 1 - flags[s]], sem_in.at[s, 1]),
        ]

    def pushes(s):
        return [
            pltpu.make_async_copy(terms.at[s, flags[s]], near_out.at[:, s], sem_out.at[s, 0]),
            pltpu.make_async_copy(terms.at[s, 1 - flags[s]], far_out.at[:, s], sem_out.at[s, 1]),
        ]

    for s in range(PAIR_DEV):
        for copy in pulls(s):
            copy.start()
    for s in range(PAIR_DEV):
        for copy in pulls(s):
            copy.wait()
        solve_pair(
            pos_ref[2, at[s]], pos_ref[3, at[s]], anchor_ref,
            boxes.at[s, 0], boxes.at[s, 1], terms.at[s, 0], terms.at[s, 1], *fields,
        )
        for copy in pushes(s):
            copy.start()
    for s in range(PAIR_DEV):
        for copy in pushes(s):
            copy.wait()


def solve(place, pos, anchors, near, far):
    smem = pl.BlockSpec(memory_space=pltpu.SMEM)
    anywhere = pl.BlockSpec(memory_space=pl.ANY)
    field = pltpu.VMEM((B, ROWS, 128), jnp.float32)
    padded = pltpu.VMEM((B + 2, ROWS, 128), jnp.float32)
    two = pltpu.VMEM((PAIR_DEV, 2, B, ROWS, 128), jnp.float32)
    dma = pltpu.SemaphoreType.DMA((PAIR_DEV, 2))
    return pl.pallas_call(
        pair_kernel,
        out_shape=[jax.ShapeDtypeStruct((B, PAIR_DEV, ROWS, 128), jnp.float32)] * 2,
        in_specs=[smem, smem, smem, anywhere, anywhere],
        out_specs=[anywhere, anywhere],
        scratch_shapes=[two, two, field, padded, field, padded, padded, field, dma, dma],
        compiler_params=pltpu.CompilerParams(vmem_limit_bytes=32 << 20),
        cost_estimate=pl.CostEstimate(flops=100_000_000, bytes_accessed=30_000_000, transcendentals=0),
        name="solve",
    )(place, pos, anchors, near, far)


def add_far_kernel(pos_ref, slot_ref, terms_ref, *refs):
    *from_groups, out_ref = refs
    out_ref[...] = jnp.zeros(out_ref.shape, jnp.float32)

    def here(p, carry):
        for s in range(PAIR_DEV):
            j = pos_ref[1, s * B + p]

            @pl.when(j < 128)
            def _(j=j, s=s):
                out_ref[j] = out_ref[j] + terms_ref[p, s]

        return carry

    lax.fori_loop(0, B, here, 0)

    def there(k, carry):
        for d, ref in enumerate(from_groups):
            at = d * KEEP + k

            @pl.when(slot_ref[2, at] == 1)
            def _(at=at, ref=ref):
                j = slot_ref[0, at]
                out_ref[j] = out_ref[j] + ref[k]

        return carry

    lax.fori_loop(0, KEEP, there, 0)


def add_far(pos, slot, terms, from_groups):
    smem, vmem = pl.BlockSpec(memory_space=pltpu.SMEM), pl.BlockSpec(memory_space=pltpu.VMEM)
    return pl.pallas_call(
        add_far_kernel,
        out_shape=jax.ShapeDtypeStruct((128, ROWS, 128), jnp.float32),
        in_specs=[smem, smem] + [vmem] * 4,
        out_specs=vmem,
        compiler_params=pltpu.CompilerParams(vmem_limit_bytes=24 << 20),
        cost_estimate=pl.CostEstimate(flops=2_000_000, bytes_accessed=10_000_000, transcendentals=0),
        name="add_far",
    )(pos, slot, terms, *from_groups)


def add_near_kernel(pos_ref, sum_ref, terms_ref, out_ref, acc):
    acc[...] = sum_ref[...]

    def here(p, carry):
        for s in range(PAIR_DEV):
            j = pos_ref[0, s * B + p]
            acc[j] = acc[j] + terms_ref[p, s]
        return carry

    lax.fori_loop(0, B, here, 0)
    for j in range(ROWS):
        out_ref[:, j * 128 : (j + 1) * 128] = acc[:, j, :]


def add_near(pos, summed, terms):
    smem, vmem = pl.BlockSpec(memory_space=pltpu.SMEM), pl.BlockSpec(memory_space=pltpu.VMEM)
    return pl.pallas_call(
        add_near_kernel,
        out_shape=jax.ShapeDtypeStruct((128, ROWS * 128), jnp.float32),
        in_specs=[smem, vmem, vmem],
        out_specs=vmem,
        scratch_shapes=[pltpu.VMEM((128, ROWS, 128), jnp.float32)],
        compiler_params=pltpu.CompilerParams(vmem_limit_bytes=24 << 20),
        cost_estimate=pl.CostEstimate(flops=2_000_000, bytes_accessed=10_000_000, transcendentals=0),
        name="add_near",
    )(pos, summed, terms)


def turned(x, shift):
    groups = lax.axis_size("grp")
    return lax.ppermute(x, "grp", [(g, (g + shift) % groups) for g in range(groups)])


def near_row(pos, first, i):
    return pos[0, (i & 1) * B + (i >> 1)]


def far_row(pos, first, i):
    return pos[1, (i & 1) * B + (i >> 1)]


def sent_row(slot, first, i):
    return slot[0, first + i]


def used_row(slot, first, i):
    q = slot[1, first + i]
    return 2 * (q & (B - 1)) + (q >> 6)


def exchanged(planes):
    return lax.all_to_all(planes.reshape(B, PAIR_DEV, ROWS, 128), "grid", 0, 0, tiled=True)


def fitting(orbitals, anchors, place, pos, slot):
    local = orbitals.reshape(128, ROWS, 128)
    near = exchanged(*fetch(pos, [local], 1, 2 * B, near_row, 0, "deal_near"))
    sent = fetch(slot, [local], 3, KEEP, sent_row, 0, "send")
    arrived = [turned(x, d) for d, x in enumerate(sent, 1)]
    far = exchanged(*fetch(pos, [local] + arrived, 1, 2 * B, far_row, 0, "deal_far"))
    near_terms, far_terms = solve(place, pos, anchors.reshape(-1), near, far)
    far_terms = exchanged(far_terms)
    back = fetch(slot, [far_terms.reshape(2 * B, ROWS, 128)], 3, KEEP, used_row, 0, "back")
    from_groups = [turned(x, -d) for d, x in enumerate(back, 1)]
    near_terms = exchanged(near_terms)
    return add_near(pos, add_far(pos, slot, far_terms, from_groups), near_terms)


def body(orbitals, anchors, pair_slots):
    me = lax.axis_index("grp").astype(jnp.int32)[None]
    place = lax.axis_index("grid").astype(jnp.int32)[None]
    pos, slot, fits = route(me, pair_slots)
    return lax.cond(
        fits[0] == 1,
        lambda: fitting(orbitals, anchors, place, pos, slot),
        lambda: general(orbitals, anchors, pair_slots),
    )


def solution(mesh):
    return jax.shard_map(
        body,
        mesh=mesh,
        in_specs=(P("grp", "grid"), P(), P()),
        out_specs=P("grp", "grid"),
        check_vma=False,
    )
```

```python
import functools

import jax
import jax.numpy as jnp
from jax import lax
from jax.experimental import pallas as pl
from jax.experimental.pallas import tpu as pltpu
from jax.sharding import PartitionSpec as P

B = 64
PAIR_DEV = 2
ITERS = 3
ROWS = B * B // 128
KEEP = 48
UNROLL = 32
BLOCK = 8


def shift_field(field, offset, extent):
    plane_size = extent * extent
    padded_x = jnp.pad(field, ((extent, extent), (0, 0)))
    moved = lax.dynamic_slice_in_dim(padded_x, extent - offset[0], extent, 0)
    padded_yz = jnp.pad(moved, ((0, 0), (plane_size, plane_size)))
    linear = offset[1] * extent + offset[2]
    moved = lax.dynamic_slice_in_dim(padded_yz, plane_size - linear, plane_size, 1)
    cells = lax.broadcasted_iota(jnp.int32, (1, plane_size), 1)
    coord_y = cells // extent - offset[1]
    coord_z = cells % extent - offset[2]
    inside = (coord_y >= 0) & (coord_y < extent) & (coord_z >= 0) & (coord_z < extent)
    return jnp.where(inside, moved, jnp.zeros_like(moved))


def operate(field, extent):
    padded_x = jnp.pad(field, ((1, 1), (0, 0)))
    beside = padded_x[2:] + padded_x[:-2]
    padded_y = jnp.pad(field, ((0, 0), (extent, extent)))
    beside = beside + padded_y[:, 2 * extent :] + padded_y[:, : -2 * extent]
    padded_z = jnp.pad(field, ((0, 0), (1, 1)))
    cells = lax.broadcasted_iota(jnp.int32, (1, field.shape[1]), 1) % extent
    upper_z = jnp.where(cells < extent - 1, padded_z[:, 2:], jnp.zeros_like(field))
    lower_z = jnp.where(cells > 0, padded_z[:, :-2], jnp.zeros_like(field))
    return 6.0 * field - beside - upper_z - lower_z


def conjugate(density, extent):
    potential = jnp.zeros_like(density)
    resid = density
    direction = density
    norm_now = jnp.sum(resid * resid)
    for turn in range(ITERS):
        image = operate(direction, extent)
        step_len = norm_now / jnp.sum(direction * image)
        potential = potential + step_len * direction
        resid = resid - step_len * image
        norm_next = jnp.sum(resid * resid)
        direction = resid + norm_next / norm_now * direction
        norm_now = norm_next
    return potential


def pair_terms(field_a, field_b, offset, extent):
    partner = shift_field(field_b, offset, extent)
    density = field_a * partner
    potential = conjugate(density, extent)
    term_a = potential * partner
    term_b = shift_field(potential * field_a, -offset, extent)
    return (term_a, term_b)


def deal_evenly(pair_slots, owner_count, each_owner):
    flat_slots = pair_slots.reshape(-1, 2)
    filled = (flat_slots[:, 0] >= 0).astype(jnp.int32)
    order = jnp.arange(flat_slots.shape[0], dtype=jnp.int32)
    position = jnp.sum(jnp.where(order[None, :] < order[:, None], filled[None, :], 0), axis=1)
    wanted = lax.broadcasted_iota(jnp.int32, (owner_count, each_owner), 1) * owner_count
    wanted = (wanted + lax.broadcasted_iota(jnp.int32, (owner_count, each_owner), 0)).reshape(-1)
    matched = (position[None, :] == wanted[:, None]) & (filled[None, :] == 1)
    picked = jnp.dot(matched.astype(jnp.int32), flat_slots)
    return picked.reshape(owner_count, each_owner, 2)


def general(orbitals, anchors, pair_slots):
    extent = B
    grid_count = lax.axis_size("grid")
    owner_count = lax.axis_size("grp") * grid_count
    group_idx = lax.axis_index("grp")
    place_idx = lax.axis_index("grid")
    assignment = deal_evenly(pair_slots, owner_count, PAIR_DEV)
    filled = assignment[..., 0] >= 0
    safe_ids = jnp.maximum(assignment, 0)
    pieces = lax.all_gather(orbitals, "grp", axis=0, tiled=True)
    group_table = lax.dynamic_slice_in_dim(safe_ids, group_idx * grid_count, grid_count, 0)
    gather_ids = jnp.transpose(group_table, (1, 2, 0))
    outgoing = pieces[gather_ids]
    arrived = lax.all_to_all(outgoing, "grid", split_axis=2, concat_axis=2, tiled=True)
    owner_idx = group_idx * grid_count + place_idx
    own_pairs = safe_ids[owner_idx]
    own_filled = filled[owner_idx]
    offsets = anchors[own_pairs[:, 1]] - anchors[own_pairs[:, 0]]

    def solve_slot(slot_item):
        boxes_pair, offset, flag = slot_item
        term_a, term_b = pair_terms(boxes_pair[0], boxes_pair[1], offset, extent)
        weight_flag = jnp.where(flag, 1.0, 0.0).astype(jnp.float32)
        return jnp.stack([term_a, term_b]) * weight_flag

    terms = lax.map(solve_slot, (arrived, offsets, own_filled))
    returned = lax.all_to_all(terms, "grid", split_axis=2, concat_axis=2, tiled=True)
    flat_terms = returned.reshape(-1, returned.shape[-1])
    summed = jax.ops.segment_sum(flat_terms, gather_ids.reshape(-1), num_segments=anchors.shape[0])
    return lax.psum_scatter(summed, "grp", scatter_dimension=0, tiled=True)


def route_kernel(me_ref, a_ref, b_ref, pos_ref, slot_ref, fits_ref):
    me = me_ref[0]
    a, b = a_ref[...], b_ref[...]
    n = a.shape[0]
    f32, i32 = jnp.float32, jnp.int32
    groups, each = 4, 2 * B

    def col(x):
        return jnp.sum(x, axis=1, keepdims=True)

    before = lax.broadcasted_iota(i32, (n, n), 0) > lax.broadcasted_iota(i32, (n, n), 1)
    before = jnp.where(before, 1.0, 0.0).astype(jnp.bfloat16)

    def rank_in(hot):
        return col(jnp.dot(before, hot.astype(jnp.bfloat16), preferred_element_type=f32) * hot).astype(i32)

    lane = lax.broadcasted_iota(i32, (n, 128), 1)
    valid = a >= 0
    ga, gb = a >> 7, b >> 7
    low, high = jnp.minimum(ga, gb), jnp.maximum(ga, gb)
    hot = jnp.where(valid & (lane == low * groups + high), 1.0, 0.0)
    rank = rank_in(hot)

    sums = jnp.sum(hot, axis=0, keepdims=True).astype(i32)
    lane1 = lax.broadcasted_iota(i32, (1, 128), 1)
    count, up = {}, {}
    for g in range(groups):
        for h in range(g, groups):
            count[g, h] = jnp.sum(jnp.where(lane1 == g * groups + h, sums, 0))
            up[g, h] = (count[g, h] >> 1) if h > g else 0

    def loads():
        load = [0] * groups
        for (g, h), c in count.items():
            load[g] = load[g] + (c - up[g, h])
            load[h] = load[h] + up[g, h]
        return load

    load = loads()
    for g, h in count:
        if h > g:
            up[g, h] = up[g, h] + ((load[g] - load[h] + 2) >> 2)
    load = loads()
    excess = 0
    for g in range(groups - 1):
        excess = excess + load[g] - each
        up[g, g + 1] = up[g, g + 1] + excess
    fits = 1
    goes_up = jnp.zeros((1, 128), i32)
    for (g, h), c in count.items():
        if h > g:
            u = up[g, h]
            fine = (u >= 0) & (u <= KEEP) & (c - u >= 0) & (c - u <= KEEP)
            fits = jnp.where(fine, fits, 0)
            goes_up = jnp.where(lane1 == g * groups + h, u, goes_up)
    fits_ref[0] = fits

    ups = col(hot * goes_up.astype(f32)).astype(i32)
    rises = rank < ups
    group = jnp.where(rises, high, low)
    source = low + high - group
    crosses = valid & (low != high)
    hot = jnp.where(valid & (lane == group), 1.0, 0.0)
    q = rank_in(hot)
    put = (((group - source) & 3) - 1) * KEEP + jnp.where(rises, rank, rank - ups)
    near_b = ga != group
    near = jnp.where(near_b, b, a) & 127
    far = jnp.where(near_b, a, b) & 127
    table = jnp.where(crosses, 128 + put, far)

    def side(*columns):
        at = lax.broadcasted_iota(i32, (n, 8), 1)
        out = jnp.zeros((n, 8), f32)
        for k, column in enumerate(columns):
            out = jnp.where(at == k, column.astype(f32), out)
        return out.astype(jnp.bfloat16)

    def spread(columns, mask):
        hot = jnp.where(mask, 1.0, 0.0).astype(jnp.bfloat16)
        out = lax.dot_general(columns, hot, (((0,), (0,)), ((), ())), preferred_element_type=f32)
        return out.astype(i32)

    mine = valid & (group == me)
    flag = jnp.where(near_b, 1, 0)
    columns = side(near, table & 255, a & 255, b & 255, flag, table >> 8, a >> 8, b >> 8)
    got = spread(columns, mine & (lane == q))
    pos_ref[...] = got
    pos_ref[1:4] = got[1:4] + 256 * got[5:8]
    wide = lax.broadcasted_iota(i32, (n, slot_ref.shape[1]), 1)
    here = wide == put
    zero = jnp.zeros_like(a)
    slots = spread(side(far, zero, zero + 1), crosses & (source == me) & here)
    slot_ref[...] = slots + spread(side(zero, q), crosses & mine & here)


def route(me, pair_slots):
    flat = pair_slots.reshape(-1, 2)
    width = 128 * -(-(3 * KEEP) // 128)
    vmem, smem = pl.BlockSpec(memory_space=pltpu.VMEM), pl.BlockSpec(memory_space=pltpu.SMEM)
    return pl.pallas_call(
        route_kernel,
        out_shape=[
            jax.ShapeDtypeStruct((8, 128), jnp.int32),
            jax.ShapeDtypeStruct((8, width), jnp.int32),
            jax.ShapeDtypeStruct((1,), jnp.int32),
        ],
        in_specs=[smem, vmem, vmem],
        out_specs=[vmem, vmem, smem],
        compiler_params=pltpu.CompilerParams(vmem_limit_bytes=40 << 20),
        cost_estimate=pl.CostEstimate(flops=10_000_000, bytes_accessed=1_000_000, transcendentals=0),
        name="route",
    )(me, flat[:, :1], flat[:, 1:])


def fetch_kernel(row_of, first, tables, idx_ref, *refs):
    parts, (*outs, table, sem) = refs[:tables], refs[tables:]
    copies, end = [], 0
    for k, part in enumerate(parts):
        copies.append(pltpu.make_async_copy(part, table.at[pl.ds(end, part.shape[0])], sem.at[k]))
        end += part.shape[0]
    for copy in copies:
        copy.start()
    for copy in copies:
        copy.wait()
    for k, out_ref in enumerate(outs):
        count = out_ref.shape[0]

        def move(i, carry, out_ref=out_ref, k=k, count=count):
            out_ref[i] = table[row_of(idx_ref, first + k * count, i)]
            return carry

        lax.fori_loop(0, count, move, 0, unroll=4)


def fetch(idx, tables, outs, count, row_of, first, name):
    rows = sum(t.shape[0] for t in tables)
    return pl.pallas_call(
        functools.partial(fetch_kernel, row_of, first, len(tables)),
        out_shape=[jax.ShapeDtypeStruct((count, ROWS, 128), jnp.float32)] * outs,
        in_specs=[pl.BlockSpec(memory_space=pltpu.SMEM)] + [pl.BlockSpec(memory_space=pl.ANY)] * len(tables),
        out_specs=[pl.BlockSpec(memory_space=pltpu.VMEM)] * outs,
        scratch_shapes=[pltpu.VMEM((rows, ROWS, 128), jnp.float32), pltpu.SemaphoreType.DMA((len(tables),))],
        compiler_params=pltpu.CompilerParams(vmem_limit_bytes=16 << 20),
        cost_estimate=pl.CostEstimate(flops=0, bytes_accessed=(rows + count * outs) * 16384, transcendentals=0),
        name=name,
    )(idx, *tables)


def solve_pair(offset, box_a, box_b, term_a, term_b, part, dens, resid, second, third, image):
    ox, oy, oz = offset
    shape = (ROWS, 128)
    line = lax.broadcasted_iota(jnp.int32, shape, 0)
    lane = lax.broadcasted_iota(jnp.int32, shape, 1)
    cy = 2 * line + (lane >> 6)
    cz = lane & (B - 1)
    high = lane >= B
    ends = (high & (line == 0)) | (~high & (line == ROWS - 1))
    no_up, no_down = cz == B - 1, cz == 0

    def plane(ref, x):
        return ref[pl.ds(pl.multiple_of(x * ROWS, ROWS), ROWS)]

    def put(ref, x, value):
        ref[pl.ds(pl.multiple_of(x * ROWS, ROWS), ROWS)] = value

    def shifter(sy, sz):
        flat = sy * B + sz
        lines, steps = flat >> 7, flat & 127
        inside = (cy >= sy) & (cy < B + sy) & (cz >= sz) & (cz < B + sz)
        keep = lane < 128 - steps

        def shift(ref, x):
            at = x * ROWS - lines
            moved = jnp.where(keep, ref[pl.ds(at, ROWS)], ref[pl.ds(at - 1, ROWS)])
            return jnp.where(inside, pltpu.roll(moved, steps, axis=1), 0.0)

        return shift

    def apply(ref, x):
        here = plane(ref, x + 1)
        at = (x + 1) * ROWS
        other = jnp.where(high, ref[pl.ds(at - 1, ROWS)], ref[pl.ds(at + 1, ROWS)])
        other = here + jnp.where(ends, 0.0, other)
        beside = plane(ref, x) + plane(ref, x + 2) + pltpu.roll(other, B, axis=1)
        upper = jnp.where(no_up, 0.0, pltpu.roll(here, 127, axis=1))
        lower = jnp.where(no_down, 0.0, pltpu.roll(here, 1, axis=1))
        return here, 6.0 * here - beside - upper - lower

    zero = jnp.zeros(shape, jnp.float32)
    for ref in (dens, second, third):
        put(ref, 0, zero)
        put(ref, B + 1, zero)

    def total(x):
        return jnp.sum(x, keepdims=True)

    def planes(step):
        return lax.fori_loop(0, B, step, zero, unroll=UNROLL)

    shift_on = shifter(oy, oz)
    shift_back = shifter(-oy, -oz)

    def begin(x, acc):
        src = x - ox
        inside = jnp.where((src >= 0) & (src < B), 1.0, 0.0)
        moved = shift_on(box_b, jnp.clip(src, 0, B - 1) + 1) * inside
        density = plane(box_a, x + 1) * moved
        put(part, x, moved)
        put(dens, x + 1, density)
        return acc + density * density

    norm0 = total(planes(begin))

    def first(x, acc):
        here, img = apply(dens, x)
        put(image, x + 1, img)
        return acc + here * img

    step0 = norm0 / total(planes(first))

    def rest0(x, acc):
        left = plane(dens, x + 1) - step0 * plane(image, x + 1)
        put(resid, x, left)
        return acc + left * left

    norm1 = total(planes(rest0))
    ratio0 = norm1 / norm0

    def turn1(x, acc):
        put(second, x + 1, plane(resid, x) + ratio0 * plane(dens, x + 1))
        return acc

    planes(turn1)

    def again(x, acc):
        here, img = apply(second, x)
        put(image, x + 1, img)
        return acc + here * img

    step1 = norm1 / total(planes(again))

    def rest1(x, acc):
        left = plane(resid, x) - step1 * plane(image, x + 1)
        put(resid, x, left)
        return acc + left * left

    norm2 = total(planes(rest1))
    ratio1 = norm2 / norm1

    def turn2(x, acc):
        put(third, x + 1, plane(resid, x) + ratio1 * plane(second, x + 1))
        return acc

    planes(turn2)

    def last(x, acc):
        here, img = apply(third, x)
        return acc + here * img

    step2 = norm2 / total(planes(last))

    def finish(x, acc):
        potential = step0 * plane(dens, x + 1) + step1 * plane(second, x + 1) + step2 * plane(third, x + 1)
        put(term_a, x, potential * plane(part, x))
        put(image, x + 1, potential * plane(box_a, x + 1))
        return acc

    planes(finish)

    def back(x, acc):
        src = x + ox
        inside = jnp.where((src >= 0) & (src < B), 1.0, 0.0)
        put(term_b, x, shift_back(image, jnp.clip(src, 0, B - 1) + 1) * inside)
        return acc

    planes(back)


def pair_kernel(place_ref, pos_ref, anchor_ref, near_ref, far_ref, near_out, far_out, boxes, terms, *rest):
    *fields, sem_in, sem_out = rest

    def flat(ref):
        return ref.reshape(ref.shape[0] * ROWS, 128)

    at = [s * B + place_ref[0] for s in range(PAIR_DEV)]
    flags = [pos_ref[4, k] for k in at]

    def pulls(s):
        return [
            pltpu.make_async_copy(near_ref.at[:, s], boxes.at[s, flags[s], pl.ds(1, B)], sem_in.at[s, 0]),
            pltpu.make_async_copy(far_ref.at[:, s], boxes.at[s, 1 - flags[s], pl.ds(1, B)], sem_in.at[s, 1]),
        ]

    def pushes(s):
        return [
            pltpu.make_async_copy(terms.at[s, flags[s]], near_out.at[:, s], sem_out.at[s, 0]),
            pltpu.make_async_copy(terms.at[s, 1 - flags[s]], far_out.at[:, s], sem_out.at[s, 1]),
        ]

    for s in range(PAIR_DEV):
        for copy in pulls(s):
            copy.start()
    for s in range(PAIR_DEV):
        for copy in pulls(s):
            copy.wait()
        orb_a, orb_b = pos_ref[2, at[s]], pos_ref[3, at[s]]
        offset = [anchor_ref[3 * orb_b + k] - anchor_ref[3 * orb_a + k] for k in range(3)]
        solve_pair(offset, *[flat(ref.at[s, k]) for ref in (boxes, terms) for k in range(2)], *fields)
        for copy in pushes(s):
            copy.start()
    for s in range(PAIR_DEV):
        for copy in pushes(s):
            copy.wait()


def solve(place, pos, anchors, near, far):
    smem = pl.BlockSpec(memory_space=pltpu.SMEM)
    anywhere = pl.BlockSpec(memory_space=pl.ANY)
    field = pltpu.VMEM((B * ROWS, 128), jnp.float32)
    padded = pltpu.VMEM(((B + 2) * ROWS, 128), jnp.float32)
    boxes = pltpu.VMEM((PAIR_DEV, 2, B + 2, ROWS, 128), jnp.float32)
    terms = pltpu.VMEM((PAIR_DEV, 2, B, ROWS, 128), jnp.float32)
    dma = pltpu.SemaphoreType.DMA((PAIR_DEV, 2))
    return pl.pallas_call(
        pair_kernel,
        out_shape=[jax.ShapeDtypeStruct((B, PAIR_DEV, ROWS, 128), jnp.float32)] * 2,
        in_specs=[smem, smem, smem, anywhere, anywhere],
        out_specs=[anywhere, anywhere],
        scratch_shapes=[boxes, terms, field, padded, field, padded, padded, padded, dma, dma],
        compiler_params=pltpu.CompilerParams(vmem_limit_bytes=32 << 20),
        cost_estimate=pl.CostEstimate(flops=100_000_000, bytes_accessed=30_000_000, transcendentals=0),
        name="solve",
    )(place, pos, anchors, near, far)


def add_far_kernel(pos_ref, slot_ref, terms_ref, *refs):
    *from_groups, out_ref = refs
    out_ref[...] = jnp.zeros(out_ref.shape, jnp.float32)

    def here(p, carry):
        for s in range(PAIR_DEV):
            j = pos_ref[1, s * B + p]

            @pl.when(j < 128)
            def _(j=j, s=s):
                out_ref[j] = out_ref[j] + terms_ref[p, s]

        return carry

    lax.fori_loop(0, B, here, 0)

    def there(k, carry):
        for d, ref in enumerate(from_groups):
            at = d * KEEP + k

            @pl.when(slot_ref[2, at] == 1)
            def _(at=at, ref=ref):
                j = slot_ref[0, at]
                out_ref[j] = out_ref[j] + ref[k]

        return carry

    lax.fori_loop(0, KEEP, there, 0)


def add_far(pos, slot, terms, from_groups):
    smem, vmem = pl.BlockSpec(memory_space=pltpu.SMEM), pl.BlockSpec(memory_space=pltpu.VMEM)
    return pl.pallas_call(
        add_far_kernel,
        out_shape=jax.ShapeDtypeStruct((128, ROWS, 128), jnp.float32),
        in_specs=[smem, smem] + [vmem] * 4,
        out_specs=vmem,
        compiler_params=pltpu.CompilerParams(vmem_limit_bytes=24 << 20),
        cost_estimate=pl.CostEstimate(flops=2_000_000, bytes_accessed=10_000_000, transcendentals=0),
        name="add_far",
    )(pos, slot, terms, *from_groups)


def add_near_kernel(pos_ref, sum_ref, terms_ref, out_ref, acc):
    acc[...] = sum_ref[...]

    def here(p, carry):
        for s in range(PAIR_DEV):
            j = pos_ref[0, s * B + p]
            acc[j] = acc[j] + terms_ref[p, s]
        return carry

    lax.fori_loop(0, B, here, 0, unroll=4)
    for j in range(BLOCK):
        out_ref[:, j * 128 : (j + 1) * 128] = acc[:, j, :]


def add_near(pos, summed, terms):
    return pl.pallas_call(
        add_near_kernel,
        out_shape=jax.ShapeDtypeStruct((128, ROWS * 128), jnp.float32),
        grid=(ROWS // BLOCK,),
        in_specs=[
            pl.BlockSpec(memory_space=pltpu.SMEM),
            pl.BlockSpec((128, BLOCK, 128), lambda i: (0, i, 0)),
            pl.BlockSpec((B, PAIR_DEV, BLOCK, 128), lambda i: (0, 0, i, 0)),
        ],
        out_specs=pl.BlockSpec((128, BLOCK * 128), lambda i: (0, i)),
        scratch_shapes=[pltpu.VMEM((128, BLOCK, 128), jnp.float32)],
        compiler_params=pltpu.CompilerParams(vmem_limit_bytes=60 << 20),
        cost_estimate=pl.CostEstimate(flops=2_000_000, bytes_accessed=10_000_000, transcendentals=0),
        name="add_near",
    )(pos, summed, terms)


def deal_near_kernel(pos_ref, orb_ref, local_ref, near_ref, table):
    for j in range(BLOCK):
        table[:, j, :] = orb_ref[:, j * 128 : (j + 1) * 128]
    local_ref[...] = table[...]

    def here(p, carry):
        for s in range(PAIR_DEV):
            near_ref[p, s] = table[pos_ref[0, s * B + p]]
        return carry

    lax.fori_loop(0, B, here, 0, unroll=4)


def deal_near(pos, orbitals):
    rows = pl.BlockSpec((128, BLOCK, 128), lambda i: (0, i, 0))
    return pl.pallas_call(
        deal_near_kernel,
        out_shape=[
            jax.ShapeDtypeStruct((128, ROWS, 128), jnp.float32),
            jax.ShapeDtypeStruct((B, PAIR_DEV, ROWS, 128), jnp.float32),
        ],
        grid=(ROWS // BLOCK,),
        in_specs=[pl.BlockSpec(memory_space=pltpu.SMEM), pl.BlockSpec((128, BLOCK * 128), lambda i: (0, i))],
        out_specs=[rows, pl.BlockSpec((B, PAIR_DEV, BLOCK, 128), lambda i: (0, 0, i, 0))],
        scratch_shapes=[pltpu.VMEM((128, BLOCK, 128), jnp.float32)],
        compiler_params=pltpu.CompilerParams(vmem_limit_bytes=60 << 20),
        cost_estimate=pl.CostEstimate(flops=2_000_000, bytes_accessed=10_000_000, transcendentals=0),
        name="deal_near",
    )(pos, orbitals)


def turned(x, shift):
    groups = lax.axis_size("grp")
    return lax.ppermute(x, "grp", [(g, (g + shift) % groups) for g in range(groups)])


def far_row(pos, first, i):
    return pos[1, (i & 1) * B + (i >> 1)]


def sent_row(slot, first, i):
    return slot[0, first + i]


def used_row(slot, first, i):
    q = slot[1, first + i]
    return 2 * (q & (B - 1)) + (q >> 6)


def exchanged(planes):
    return lax.all_to_all(planes.reshape(B, PAIR_DEV, ROWS, 128), "grid", 0, 0, tiled=True)


def fitting(orbitals, anchors, place, pos, slot):
    local, near = deal_near(pos, orbitals)
    near = exchanged(near)
    sent = fetch(slot, [local], 3, KEEP, sent_row, 0, "send")
    arrived = [turned(x, d) for d, x in enumerate(sent, 1)]
    far = exchanged(*fetch(pos, [local] + arrived, 1, 2 * B, far_row, 0, "deal_far"))
    near_terms, far_terms = solve(place, pos, anchors.reshape(-1), near, far)
    far_terms = exchanged(far_terms)
    back = fetch(slot, [far_terms.reshape(2 * B, ROWS, 128)], 3, KEEP, used_row, 0, "back")
    from_groups = [turned(x, -d) for d, x in enumerate(back, 1)]
    near_terms = exchanged(near_terms)
    return add_near(pos, add_far(pos, slot, far_terms, from_groups), near_terms)


def body(orbitals, anchors, pair_slots):
    me = lax.axis_index("grp").astype(jnp.int32)[None]
    place = lax.axis_index("grid").astype(jnp.int32)[None]
    pos, slot, fits = route(me, pair_slots)
    return lax.cond(
        fits[0] == 1,
        lambda: fitting(orbitals, anchors, place, pos, slot),
        lambda: general(orbitals, anchors, pair_slots),
    )


def solution(mesh):
    return jax.shard_map(
        body,
        mesh=mesh,
        in_specs=(P("grp", "grid"), P(), P()),
        out_specs=P("grp", "grid"),
        check_vma=False,
    )
```

```python
import functools

import jax
import jax.numpy as jnp
from jax import lax
from jax.experimental import pallas as pl
from jax.experimental.pallas import tpu as pltpu
from jax.sharding import PartitionSpec as P

B = 64
PAIR_DEV = 2
ITERS = 3
ROWS = B * B // 128
KEEP = 48
UNROLL = 16


def shift_field(field, offset, extent):
    plane_size = extent * extent
    padded_x = jnp.pad(field, ((extent, extent), (0, 0)))
    moved = lax.dynamic_slice_in_dim(padded_x, extent - offset[0], extent, 0)
    padded_yz = jnp.pad(moved, ((0, 0), (plane_size, plane_size)))
    linear = offset[1] * extent + offset[2]
    moved = lax.dynamic_slice_in_dim(padded_yz, plane_size - linear, plane_size, 1)
    cells = lax.broadcasted_iota(jnp.int32, (1, plane_size), 1)
    coord_y = cells // extent - offset[1]
    coord_z = cells % extent - offset[2]
    inside = (coord_y >= 0) & (coord_y < extent) & (coord_z >= 0) & (coord_z < extent)
    return jnp.where(inside, moved, jnp.zeros_like(moved))


def operate(field, extent):
    padded_x = jnp.pad(field, ((1, 1), (0, 0)))
    beside = padded_x[2:] + padded_x[:-2]
    padded_y = jnp.pad(field, ((0, 0), (extent, extent)))
    beside = beside + padded_y[:, 2 * extent :] + padded_y[:, : -2 * extent]
    padded_z = jnp.pad(field, ((0, 0), (1, 1)))
    cells = lax.broadcasted_iota(jnp.int32, (1, field.shape[1]), 1) % extent
    upper_z = jnp.where(cells < extent - 1, padded_z[:, 2:], jnp.zeros_like(field))
    lower_z = jnp.where(cells > 0, padded_z[:, :-2], jnp.zeros_like(field))
    return 6.0 * field - beside - upper_z - lower_z


def conjugate(density, extent):
    potential = jnp.zeros_like(density)
    resid = density
    direction = density
    norm_now = jnp.sum(resid * resid)
    for turn in range(ITERS):
        image = operate(direction, extent)
        step_len = norm_now / jnp.sum(direction * image)
        potential = potential + step_len * direction
        resid = resid - step_len * image
        norm_next = jnp.sum(resid * resid)
        direction = resid + norm_next / norm_now * direction
        norm_now = norm_next
    return potential


def pair_terms(field_a, field_b, offset, extent):
    partner = shift_field(field_b, offset, extent)
    density = field_a * partner
    potential = conjugate(density, extent)
    term_a = potential * partner
    term_b = shift_field(potential * field_a, -offset, extent)
    return (term_a, term_b)


def deal_evenly(pair_slots, owner_count, each_owner):
    flat_slots = pair_slots.reshape(-1, 2)
    filled = (flat_slots[:, 0] >= 0).astype(jnp.int32)
    order = jnp.arange(flat_slots.shape[0], dtype=jnp.int32)
    position = jnp.sum(jnp.where(order[None, :] < order[:, None], filled[None, :], 0), axis=1)
    wanted = lax.broadcasted_iota(jnp.int32, (owner_count, each_owner), 1) * owner_count
    wanted = (wanted + lax.broadcasted_iota(jnp.int32, (owner_count, each_owner), 0)).reshape(-1)
    matched = (position[None, :] == wanted[:, None]) & (filled[None, :] == 1)
    picked = jnp.dot(matched.astype(jnp.int32), flat_slots)
    return picked.reshape(owner_count, each_owner, 2)


def general(orbitals, anchors, pair_slots):
    extent = B
    grid_count = lax.axis_size("grid")
    owner_count = lax.axis_size("grp") * grid_count
    group_idx = lax.axis_index("grp")
    place_idx = lax.axis_index("grid")
    assignment = deal_evenly(pair_slots, owner_count, PAIR_DEV)
    filled = assignment[..., 0] >= 0
    safe_ids = jnp.maximum(assignment, 0)
    pieces = lax.all_gather(orbitals, "grp", axis=0, tiled=True)
    group_table = lax.dynamic_slice_in_dim(safe_ids, group_idx * grid_count, grid_count, 0)
    gather_ids = jnp.transpose(group_table, (1, 2, 0))
    outgoing = pieces[gather_ids]
    arrived = lax.all_to_all(outgoing, "grid", split_axis=2, concat_axis=2, tiled=True)
    owner_idx = group_idx * grid_count + place_idx
    own_pairs = safe_ids[owner_idx]
    own_filled = filled[owner_idx]
    offsets = anchors[own_pairs[:, 1]] - anchors[own_pairs[:, 0]]

    def solve_slot(slot_item):
        boxes_pair, offset, flag = slot_item
        term_a, term_b = pair_terms(boxes_pair[0], boxes_pair[1], offset, extent)
        weight_flag = jnp.where(flag, 1.0, 0.0).astype(jnp.float32)
        return jnp.stack([term_a, term_b]) * weight_flag

    terms = lax.map(solve_slot, (arrived, offsets, own_filled))
    returned = lax.all_to_all(terms, "grid", split_axis=2, concat_axis=2, tiled=True)
    flat_terms = returned.reshape(-1, returned.shape[-1])
    summed = jax.ops.segment_sum(flat_terms, gather_ids.reshape(-1), num_segments=anchors.shape[0])
    return lax.psum_scatter(summed, "grp", scatter_dimension=0, tiled=True)


def route_kernel(me_ref, pair_ref, pos_ref, slot_ref, fits_ref):
    me = me_ref[0]
    f32, i32 = jnp.float32, jnp.int32
    groups, each = 4, 2 * B

    def col(x):
        return jnp.sum(x, axis=1, keepdims=True)

    pairs = pair_ref[...].astype(f32).T
    at = lax.broadcasted_iota(i32, pairs.shape, 1)
    columns = [col(jnp.where(at == k, pairs, 0.0)) for k in range(pairs.shape[1])]
    a = jnp.concatenate(columns[0::2], axis=0).astype(i32)
    b = jnp.concatenate(columns[1::2], axis=0).astype(i32)
    n = a.shape[0]

    before = lax.broadcasted_iota(i32, (128, 128), 0) > lax.broadcasted_iota(i32, (128, 128), 1)
    before = jnp.where(before, 1.0, 0.0).astype(jnp.bfloat16)

    def rank_in(hot):
        ranks, passed = [], jnp.zeros((1, 128), f32)
        for k in range(0, n, 128):
            part = hot[k : k + 128]
            ahead = jnp.dot(before, part.astype(jnp.bfloat16), preferred_element_type=f32) + passed
            ranks.append(col(ahead * part))
            passed = passed + jnp.sum(part, axis=0, keepdims=True)
        return jnp.concatenate(ranks, axis=0).astype(i32)

    lane = lax.broadcasted_iota(i32, (n, 128), 1)
    valid = a >= 0
    ga, gb = a >> 7, b >> 7
    low, high = jnp.minimum(ga, gb), jnp.maximum(ga, gb)
    hot = jnp.where(valid & (lane == low * groups + high), 1.0, 0.0)
    rank = rank_in(hot)

    sums = jnp.sum(hot, axis=0, keepdims=True).astype(i32)
    lane1 = lax.broadcasted_iota(i32, (1, 128), 1)
    count, up = {}, {}
    for g in range(groups):
        for h in range(g, groups):
            count[g, h] = jnp.sum(jnp.where(lane1 == g * groups + h, sums, 0))
            up[g, h] = (count[g, h] >> 1) if h > g else 0

    def loads():
        load = [0] * groups
        for (g, h), c in count.items():
            load[g] = load[g] + (c - up[g, h])
            load[h] = load[h] + up[g, h]
        return load

    load = loads()
    for g, h in count:
        if h > g:
            up[g, h] = up[g, h] + ((load[g] - load[h] + 2) >> 2)
    load = loads()
    excess = 0
    for g in range(groups - 1):
        excess = excess + load[g] - each
        up[g, g + 1] = up[g, g + 1] + excess
    fits = 1
    goes_up = jnp.zeros((1, 128), i32)
    for (g, h), c in count.items():
        if h > g:
            u = up[g, h]
            fine = (u >= 0) & (u <= KEEP) & (c - u >= 0) & (c - u <= KEEP)
            fits = jnp.where(fine, fits, 0)
            goes_up = jnp.where(lane1 == g * groups + h, u, goes_up)
    fits_ref[0] = fits

    ups = col(hot * goes_up.astype(f32)).astype(i32)
    rises = rank < ups
    group = jnp.where(rises, high, low)
    source = low + high - group
    crosses = valid & (low != high)
    hot = jnp.where(valid & (lane == group), 1.0, 0.0)
    q = rank_in(hot)
    put = (((group - source) & 3) - 1) * KEEP + jnp.where(rises, rank, rank - ups)
    near_b = ga != group
    near = jnp.where(near_b, b, a) & 127
    far = jnp.where(near_b, a, b) & 127
    table = jnp.where(crosses, 128 + put, far)

    def side(*columns):
        at = lax.broadcasted_iota(i32, (n, 8), 1)
        out = jnp.zeros((n, 8), f32)
        for k, column in enumerate(columns):
            out = jnp.where(at == k, column.astype(f32), out)
        return out.astype(jnp.bfloat16)

    def spread(columns, mask):
        hot = jnp.where(mask, 1.0, 0.0).astype(jnp.bfloat16)
        out = lax.dot_general(columns, hot, (((0,), (0,)), ((), ())), preferred_element_type=f32)
        return out.astype(i32)

    mine = valid & (group == me)
    flag = jnp.where(near_b, 1, 0)
    columns = side(near, table & 255, a & 255, b & 255, flag, table >> 8, a >> 8, b >> 8)
    got = spread(columns, mine & (lane == q))
    pos_ref[...] = got
    pos_ref[1:4] = got[1:4] + 256 * got[5:8]
    wide = lax.broadcasted_iota(i32, (n, slot_ref.shape[1]), 1)
    here = wide == put
    zero = jnp.zeros_like(a)
    slots = spread(side(far, zero, zero + 1), crosses & (source == me) & here)
    slot_ref[...] = slots + spread(side(zero, q), crosses & mine & here)


def route(me, pair_slots):
    lists = jnp.transpose(pair_slots, (1, 2, 0)).reshape(-1, pair_slots.shape[0])
    width = 128 * -(-(3 * KEEP) // 128)
    vmem, smem = pl.BlockSpec(memory_space=pltpu.VMEM), pl.BlockSpec(memory_space=pltpu.SMEM)
    return pl.pallas_call(
        route_kernel,
        out_shape=[
            jax.ShapeDtypeStruct((8, 128), jnp.int32),
            jax.ShapeDtypeStruct((8, width), jnp.int32),
            jax.ShapeDtypeStruct((1,), jnp.int32),
        ],
        in_specs=[smem, vmem],
        out_specs=[vmem, vmem, smem],
        compiler_params=pltpu.CompilerParams(vmem_limit_bytes=40 << 20),
        cost_estimate=pl.CostEstimate(flops=10_000_000, bytes_accessed=1_000_000, transcendentals=0),
        name="route",
    )(me, lists)


def fetch_kernel(row_of, first, tables, idx_ref, *refs):
    parts, (*outs, table, sem) = refs[:tables], refs[tables:]
    copies, end = [], 0
    for k, part in enumerate(parts):
        copies.append(pltpu.make_async_copy(part, table.at[pl.ds(end, part.shape[0])], sem.at[k]))
        end += part.shape[0]
    for copy in copies:
        copy.start()
    for copy in copies:
        copy.wait()
    for k, out_ref in enumerate(outs):
        count = out_ref.shape[0]

        def move(i, carry, out_ref=out_ref, k=k, count=count):
            out_ref[i] = table[row_of(idx_ref, first + k * count, i)]
            return carry

        lax.fori_loop(0, count, move, 0, unroll=4)


def fetch(idx, tables, outs, count, row_of, first, name):
    rows = sum(t.shape[0] for t in tables)
    return pl.pallas_call(
        functools.partial(fetch_kernel, row_of, first, len(tables)),
        out_shape=[jax.ShapeDtypeStruct((count, ROWS, 128), jnp.float32)] * outs,
        in_specs=[pl.BlockSpec(memory_space=pltpu.SMEM)] + [pl.BlockSpec(memory_space=pl.ANY)] * len(tables),
        out_specs=[pl.BlockSpec(memory_space=pltpu.VMEM)] * outs,
        scratch_shapes=[pltpu.VMEM((rows, ROWS, 128), jnp.float32), pltpu.SemaphoreType.DMA((len(tables),))],
        compiler_params=pltpu.CompilerParams(vmem_limit_bytes=16 << 20),
        cost_estimate=pl.CostEstimate(flops=0, bytes_accessed=(rows + count * outs) * 16384, transcendentals=0),
        name=name,
    )(idx, *tables)


def solve_pair(offset, box_a, box_b, term_a, term_b, part, dens, resid, second, third, image):
    ox, oy, oz = offset
    shape = (ROWS, 128)
    line = lax.broadcasted_iota(jnp.int32, shape, 0)
    lane = lax.broadcasted_iota(jnp.int32, shape, 1)
    cy = 2 * line + (lane >> 6)
    cz = lane & (B - 1)
    high = lane >= B
    ends = (high & (line == 0)) | (~high & (line == ROWS - 1))
    no_up, no_down = cz == B - 1, cz == 0

    def plane(ref, x):
        return ref[pl.ds(pl.multiple_of(x * ROWS, ROWS), ROWS)]

    def put(ref, x, value):
        ref[pl.ds(pl.multiple_of(x * ROWS, ROWS), ROWS)] = value

    def shifter(sy, sz):
        flat = sy * B + sz
        lines, steps = flat >> 7, flat & 127
        inside = (cy >= sy) & (cy < B + sy) & (cz >= sz) & (cz < B + sz)
        keep = lane < 128 - steps

        def shift(ref, x):
            at = x * ROWS - lines
            moved = jnp.where(keep, ref[pl.ds(at, ROWS)], ref[pl.ds(at - 1, ROWS)])
            return jnp.where(inside, pltpu.roll(moved, steps, axis=1), 0.0)

        return shift

    def apply(ref, x):
        here = plane(ref, x + 1)
        at = (x + 1) * ROWS
        other = jnp.where(high, ref[pl.ds(at - 1, ROWS)], ref[pl.ds(at + 1, ROWS)])
        other = here + jnp.where(ends, 0.0, other)
        beside = plane(ref, x) + plane(ref, x + 2) + pltpu.roll(other, B, axis=1)
        upper = jnp.where(no_up, 0.0, pltpu.roll(here, 127, axis=1))
        lower = jnp.where(no_down, 0.0, pltpu.roll(here, 1, axis=1))
        return here, 6.0 * here - beside - upper - lower

    zero = jnp.zeros(shape, jnp.float32)
    for ref in (dens, second, third):
        put(ref, 0, zero)
        put(ref, B + 1, zero)

    shift_on = shifter(oy, oz)
    shift_back = shifter(-oy, -oz)

    def begin(x, acc):
        src = x - ox
        inside = jnp.where((src >= 0) & (src < B), 1.0, 0.0)
        moved = shift_on(box_b, jnp.clip(src, 0, B - 1) + 1) * inside
        density = plane(box_a, x + 1) * moved
        put(part, x, moved)
        put(dens, x + 1, density)
        return acc + density * density

    def first(x, acc):
        here, img = apply(dens, x)
        put(image, x + 1, img)
        return acc + here * img

    norm0 = yield begin
    step0 = norm0 / (yield first)

    def rest0(x, acc):
        left = plane(dens, x + 1) - step0 * plane(image, x + 1)
        put(resid, x, left)
        return acc + left * left

    norm1 = yield rest0
    ratio0 = norm1 / norm0

    def turn1(x, acc):
        put(second, x + 1, plane(resid, x) + ratio0 * plane(dens, x + 1))
        return acc

    def again(x, acc):
        here, img = apply(second, x)
        put(image, x + 1, img)
        return acc + here * img

    yield turn1
    step1 = norm1 / (yield again)

    def rest1(x, acc):
        left = plane(resid, x) - step1 * plane(image, x + 1)
        put(resid, x, left)
        return acc + left * left

    norm2 = yield rest1
    ratio1 = norm2 / norm1

    def turn2(x, acc):
        put(third, x + 1, plane(resid, x) + ratio1 * plane(second, x + 1))
        return acc

    def last(x, acc):
        here, img = apply(third, x)
        return acc + here * img

    yield turn2
    step2 = norm2 / (yield last)

    def finish(x, acc):
        potential = step0 * plane(dens, x + 1) + step1 * plane(second, x + 1) + step2 * plane(third, x + 1)
        put(term_a, x, potential * plane(part, x))
        put(image, x + 1, potential * plane(box_a, x + 1))
        return acc

    def back(x, acc):
        src = x + ox
        inside = jnp.where((src >= 0) & (src < B), 1.0, 0.0)
        put(term_b, x, shift_back(image, jnp.clip(src, 0, B - 1) + 1) * inside)
        return acc

    yield finish
    yield back


def run_together(solvers):
    steps = [next(solver) for solver in solvers]
    zero = jnp.zeros((ROWS, 128), jnp.float32)
    while True:
        def both(x, accs, steps=tuple(steps)):
            return tuple(step(x, acc) for step, acc in zip(steps, accs))

        accs = lax.fori_loop(0, B, both, (zero,) * len(steps), unroll=UNROLL)
        sums = [jnp.sum(acc, keepdims=True) for acc in accs]
        try:
            steps = [solver.send(value) for solver, value in zip(solvers, sums)]
        except StopIteration:
            return


def pair_kernel(place_ref, pos_ref, anchor_ref, near_ref, far_ref, near_out, far_out, boxes, terms, *rest):
    *fields, sem_in, sem_out = rest

    def flat(ref):
        return ref.reshape(ref.shape[0] * ROWS, 128)

    at = [s * B + place_ref[0] for s in range(PAIR_DEV)]
    flags = [pos_ref[4, k] for k in at]

    def pulls(s):
        return [
            pltpu.make_async_copy(near_ref.at[:, s], boxes.at[s, flags[s], pl.ds(1, B)], sem_in.at[s, 0]),
            pltpu.make_async_copy(far_ref.at[:, s], boxes.at[s, 1 - flags[s], pl.ds(1, B)], sem_in.at[s, 1]),
        ]

    def pushes(s):
        return [
            pltpu.make_async_copy(terms.at[s, flags[s]], near_out.at[:, s], sem_out.at[s, 0]),
            pltpu.make_async_copy(terms.at[s, 1 - flags[s]], far_out.at[:, s], sem_out.at[s, 1]),
        ]

    for s in range(PAIR_DEV):
        for copy in pulls(s):
            copy.start()
    solvers = []
    for s in range(PAIR_DEV):
        for copy in pulls(s):
            copy.wait()
        orb_a, orb_b = pos_ref[2, at[s]], pos_ref[3, at[s]]
        offset = [anchor_ref[3 * orb_b + k] - anchor_ref[3 * orb_a + k] for k in range(3)]
        refs = [flat(ref.at[s, k]) for ref in (boxes, terms) for k in range(2)]
        solvers.append(solve_pair(offset, *refs, *[ref.at[s] for ref in fields]))
    run_together(solvers)
    for s in range(PAIR_DEV):
        for copy in pushes(s):
            copy.start()
    for s in range(PAIR_DEV):
        for copy in pushes(s):
            copy.wait()


def solve(place, pos, anchors, near, far):
    smem = pl.BlockSpec(memory_space=pltpu.SMEM)
    anywhere = pl.BlockSpec(memory_space=pl.ANY)
    field = pltpu.VMEM((PAIR_DEV, B * ROWS, 128), jnp.float32)
    padded = pltpu.VMEM((PAIR_DEV, (B + 2) * ROWS, 128), jnp.float32)
    boxes = pltpu.VMEM((PAIR_DEV, 2, B + 2, ROWS, 128), jnp.float32)
    terms = pltpu.VMEM((PAIR_DEV, 2, B, ROWS, 128), jnp.float32)
    dma = pltpu.SemaphoreType.DMA((PAIR_DEV, 2))
    return pl.pallas_call(
        pair_kernel,
        out_shape=[jax.ShapeDtypeStruct((B, PAIR_DEV, ROWS, 128), jnp.float32)] * 2,
        in_specs=[smem, smem, smem, anywhere, anywhere],
        out_specs=[anywhere, anywhere],
        scratch_shapes=[boxes, terms, field, padded, field, padded, padded, padded, dma, dma],
        compiler_params=pltpu.CompilerParams(vmem_limit_bytes=32 << 20),
        cost_estimate=pl.CostEstimate(flops=100_000_000, bytes_accessed=30_000_000, transcendentals=0),
        name="solve",
    )(place, pos, anchors, near, far)


def add_far_kernel(pos_ref, slot_ref, terms_ref, *refs):
    *from_groups, out_ref = refs
    out_ref[...] = jnp.zeros(out_ref.shape, jnp.float32)

    def here(p, carry):
        for s in range(PAIR_DEV):
            j = pos_ref[1, s * B + p]

            @pl.when(j < 128)
            def _(j=j, s=s):
                out_ref[j] = out_ref[j] + terms_ref[p, s]

        return carry

    lax.fori_loop(0, B, here, 0)

    def there(k, carry):
        for d, ref in enumerate(from_groups):
            at = d * KEEP + k

            @pl.when(slot_ref[2, at] == 1)
            def _(at=at, ref=ref):
                j = slot_ref[0, at]
                out_ref[j] = out_ref[j] + ref[k]

        return carry

    lax.fori_loop(0, KEEP, there, 0)


def add_far(pos, slot, terms, from_groups):
    smem, vmem = pl.BlockSpec(memory_space=pltpu.SMEM), pl.BlockSpec(memory_space=pltpu.VMEM)
    return pl.pallas_call(
        add_far_kernel,
        out_shape=jax.ShapeDtypeStruct((128, ROWS, 128), jnp.float32),
        in_specs=[smem, smem] + [vmem] * 4,
        out_specs=vmem,
        compiler_params=pltpu.CompilerParams(vmem_limit_bytes=24 << 20),
        cost_estimate=pl.CostEstimate(flops=2_000_000, bytes_accessed=10_000_000, transcendentals=0),
        name="add_far",
    )(pos, slot, terms, *from_groups)


def add_near_kernel(pos_ref, sum_ref, terms_ref, out_ref, terms, first, second, sem):
    copies = [
        pltpu.make_async_copy(terms_ref, terms, sem.at[0]),
        pltpu.make_async_copy(sum_ref, first, sem.at[1]),
    ]
    for copy in copies:
        copy.start()
    second[...] = jnp.zeros(second.shape, jnp.float32)
    for copy in copies:
        copy.wait()

    def here(p, carry):
        for s, total in enumerate((first, second)):
            j = pos_ref[0, s * B + p]
            total[j] = total[j] + terms[p, s]
        return carry

    lax.fori_loop(0, B, here, 0, unroll=4)
    for j in range(ROWS):
        out_ref[:, j * 128 : (j + 1) * 128] = first[:, j, :] + second[:, j, :]


def add_near(pos, summed, terms):
    anywhere = pl.BlockSpec(memory_space=pl.ANY)
    total = pltpu.VMEM((128, ROWS, 128), jnp.float32)
    return pl.pallas_call(
        add_near_kernel,
        out_shape=jax.ShapeDtypeStruct((128, ROWS * 128), jnp.float32),
        in_specs=[pl.BlockSpec(memory_space=pltpu.SMEM), anywhere, anywhere],
        out_specs=pl.BlockSpec(memory_space=pltpu.VMEM),
        scratch_shapes=[pltpu.VMEM((B, PAIR_DEV, ROWS, 128), jnp.float32), total, total, pltpu.SemaphoreType.DMA((2,))],
        compiler_params=pltpu.CompilerParams(vmem_limit_bytes=24 << 20),
        cost_estimate=pl.CostEstimate(flops=2_000_000, bytes_accessed=10_000_000, transcendentals=0),
        name="add_near",
    )(pos, summed, terms)


def deal_near_kernel(pos_ref, orb_ref, near_ref, table):
    for j in range(ROWS):
        table[:, j, :] = orb_ref[:, j * 128 : (j + 1) * 128]

    def here(p, carry):
        for s in range(PAIR_DEV):
            near_ref[p, s] = table[pos_ref[0, s * B + p]]
        return carry

    lax.fori_loop(0, B, here, 0, unroll=4)


def deal_near(pos, orbitals):
    vmem = pl.BlockSpec(memory_space=pltpu.VMEM)
    return pl.pallas_call(
        deal_near_kernel,
        out_shape=jax.ShapeDtypeStruct((B, PAIR_DEV, ROWS, 128), jnp.float32),
        in_specs=[pl.BlockSpec(memory_space=pltpu.SMEM), vmem],
        out_specs=vmem,
        scratch_shapes=[pltpu.VMEM((128, ROWS, 128), jnp.float32)],
        compiler_params=pltpu.CompilerParams(vmem_limit_bytes=60 << 20),
        cost_estimate=pl.CostEstimate(flops=2_000_000, bytes_accessed=10_000_000, transcendentals=0),
        name="deal_near",
    )(pos, orbitals)


def turned(x, shift):
    groups = lax.axis_size("grp")
    return lax.ppermute(x, "grp", [(g, (g + shift) % groups) for g in range(groups)])


def far_row(pos, first, i):
    return pos[1, (i & 1) * B + (i >> 1)]


def sent_row(slot, first, i):
    return slot[0, first + i]


def used_row(slot, first, i):
    q = slot[1, first + i]
    return 2 * (q & (B - 1)) + (q >> 6)


def exchanged(planes):
    return lax.all_to_all(planes.reshape(B, PAIR_DEV, ROWS, 128), "grid", 0, 0, tiled=True)


def fitting(orbitals, anchors, place, pos, slot):
    near = exchanged(deal_near(pos, orbitals))
    local = orbitals.reshape(128, ROWS, 128)
    sent = fetch(slot, [local], 3, KEEP, sent_row, 0, "send")
    arrived = [turned(x, d) for d, x in enumerate(sent, 1)]
    far = exchanged(*fetch(pos, [local] + arrived, 1, 2 * B, far_row, 0, "deal_far"))
    near_terms, far_terms = solve(place, pos, anchors.reshape(-1), near, far)
    far_terms = exchanged(far_terms)
    back = fetch(slot, [far_terms.reshape(2 * B, ROWS, 128)], 3, KEEP, used_row, 0, "back")
    from_groups = [turned(x, -d) for d, x in enumerate(back, 1)]
    near_terms = exchanged(near_terms)
    return add_near(pos, add_far(pos, slot, far_terms, from_groups), near_terms)


def body(orbitals, anchors, pair_slots):
    me = lax.axis_index("grp").astype(jnp.int32)[None]
    place = lax.axis_index("grid").astype(jnp.int32)[None]
    pos, slot, fits = route(me, pair_slots)
    return lax.cond(
        fits[0] == 1,
        lambda: fitting(orbitals, anchors, place, pos, slot),
        lambda: general(orbitals, anchors, pair_slots),
    )


def solution(mesh):
    return jax.shard_map(
        body,
        mesh=mesh,
        in_specs=(P("grp", "grid"), P(), P()),
        out_specs=P("grp", "grid"),
        check_vma=False,
    )
```

```python
import functools

import jax
import jax.numpy as jnp
from jax import lax
from jax.experimental import pallas as pl
from jax.experimental.pallas import tpu as pltpu
from jax.sharding import PartitionSpec as P

B = 64
PAIR_DEV = 2
ITERS = 3
ROWS = B * B // 128
KEEP = 48
UNROLL = 16
BLOCK = 16


def shift_field(field, offset, extent):
    plane_size = extent * extent
    padded_x = jnp.pad(field, ((extent, extent), (0, 0)))
    moved = lax.dynamic_slice_in_dim(padded_x, extent - offset[0], extent, 0)
    padded_yz = jnp.pad(moved, ((0, 0), (plane_size, plane_size)))
    linear = offset[1] * extent + offset[2]
    moved = lax.dynamic_slice_in_dim(padded_yz, plane_size - linear, plane_size, 1)
    cells = lax.broadcasted_iota(jnp.int32, (1, plane_size), 1)
    coord_y = cells // extent - offset[1]
    coord_z = cells % extent - offset[2]
    inside = (coord_y >= 0) & (coord_y < extent) & (coord_z >= 0) & (coord_z < extent)
    return jnp.where(inside, moved, jnp.zeros_like(moved))


def operate(field, extent):
    padded_x = jnp.pad(field, ((1, 1), (0, 0)))
    beside = padded_x[2:] + padded_x[:-2]
    padded_y = jnp.pad(field, ((0, 0), (extent, extent)))
    beside = beside + padded_y[:, 2 * extent :] + padded_y[:, : -2 * extent]
    padded_z = jnp.pad(field, ((0, 0), (1, 1)))
    cells = lax.broadcasted_iota(jnp.int32, (1, field.shape[1]), 1) % extent
    upper_z = jnp.where(cells < extent - 1, padded_z[:, 2:], jnp.zeros_like(field))
    lower_z = jnp.where(cells > 0, padded_z[:, :-2], jnp.zeros_like(field))
    return 6.0 * field - beside - upper_z - lower_z


def conjugate(density, extent):
    potential = jnp.zeros_like(density)
    resid = density
    direction = density
    norm_now = jnp.sum(resid * resid)
    for turn in range(ITERS):
        image = operate(direction, extent)
        step_len = norm_now / jnp.sum(direction * image)
        potential = potential + step_len * direction
        resid = resid - step_len * image
        norm_next = jnp.sum(resid * resid)
        direction = resid + norm_next / norm_now * direction
        norm_now = norm_next
    return potential


def pair_terms(field_a, field_b, offset, extent):
    partner = shift_field(field_b, offset, extent)
    density = field_a * partner
    potential = conjugate(density, extent)
    term_a = potential * partner
    term_b = shift_field(potential * field_a, -offset, extent)
    return (term_a, term_b)


def deal_evenly(pair_slots, owner_count, each_owner):
    flat_slots = pair_slots.reshape(-1, 2)
    filled = (flat_slots[:, 0] >= 0).astype(jnp.int32)
    order = jnp.arange(flat_slots.shape[0], dtype=jnp.int32)
    position = jnp.sum(jnp.where(order[None, :] < order[:, None], filled[None, :], 0), axis=1)
    wanted = lax.broadcasted_iota(jnp.int32, (owner_count, each_owner), 1) * owner_count
    wanted = (wanted + lax.broadcasted_iota(jnp.int32, (owner_count, each_owner), 0)).reshape(-1)
    matched = (position[None, :] == wanted[:, None]) & (filled[None, :] == 1)
    picked = jnp.dot(matched.astype(jnp.int32), flat_slots)
    return picked.reshape(owner_count, each_owner, 2)


def general(orbitals, anchors, pair_slots):
    extent = B
    grid_count = lax.axis_size("grid")
    owner_count = lax.axis_size("grp") * grid_count
    group_idx = lax.axis_index("grp")
    place_idx = lax.axis_index("grid")
    assignment = deal_evenly(pair_slots, owner_count, PAIR_DEV)
    filled = assignment[..., 0] >= 0
    safe_ids = jnp.maximum(assignment, 0)
    pieces = lax.all_gather(orbitals, "grp", axis=0, tiled=True)
    group_table = lax.dynamic_slice_in_dim(safe_ids, group_idx * grid_count, grid_count, 0)
    gather_ids = jnp.transpose(group_table, (1, 2, 0))
    outgoing = pieces[gather_ids]
    arrived = lax.all_to_all(outgoing, "grid", split_axis=2, concat_axis=2, tiled=True)
    owner_idx = group_idx * grid_count + place_idx
    own_pairs = safe_ids[owner_idx]
    own_filled = filled[owner_idx]
    offsets = anchors[own_pairs[:, 1]] - anchors[own_pairs[:, 0]]

    def solve_slot(slot_item):
        boxes_pair, offset, flag = slot_item
        term_a, term_b = pair_terms(boxes_pair[0], boxes_pair[1], offset, extent)
        weight_flag = jnp.where(flag, 1.0, 0.0).astype(jnp.float32)
        return jnp.stack([term_a, term_b]) * weight_flag

    terms = lax.map(solve_slot, (arrived, offsets, own_filled))
    returned = lax.all_to_all(terms, "grid", split_axis=2, concat_axis=2, tiled=True)
    flat_terms = returned.reshape(-1, returned.shape[-1])
    summed = jax.ops.segment_sum(flat_terms, gather_ids.reshape(-1), num_segments=anchors.shape[0])
    return lax.psum_scatter(summed, "grp", scatter_dimension=0, tiled=True)


def route_kernel(me_ref, pair_ref, pos_ref, slot_ref, fits_ref):
    me = me_ref[0]
    f32, i32 = jnp.float32, jnp.int32
    groups, each = 4, 2 * B

    def col(x):
        return jnp.sum(x, axis=1, keepdims=True)

    pairs = pair_ref[...].astype(f32).T
    at = lax.broadcasted_iota(i32, pairs.shape, 1)
    columns = [col(jnp.where(at == k, pairs, 0.0)) for k in range(pairs.shape[1])]
    a = jnp.concatenate(columns[0::2], axis=0).astype(i32)
    b = jnp.concatenate(columns[1::2], axis=0).astype(i32)
    n = a.shape[0]

    before = lax.broadcasted_iota(i32, (128, 128), 0) > lax.broadcasted_iota(i32, (128, 128), 1)
    before = jnp.where(before, 1.0, 0.0).astype(jnp.bfloat16)

    def rank_in(hot):
        ranks, passed = [], jnp.zeros((1, 128), f32)
        for k in range(0, n, 128):
            part = hot[k : k + 128]
            ahead = jnp.dot(before, part.astype(jnp.bfloat16), preferred_element_type=f32) + passed
            ranks.append(col(ahead * part))
            passed = passed + jnp.sum(part, axis=0, keepdims=True)
        return jnp.concatenate(ranks, axis=0).astype(i32)

    lane = lax.broadcasted_iota(i32, (n, 128), 1)
    valid = a >= 0
    ga, gb = a >> 7, b >> 7
    low, high = jnp.minimum(ga, gb), jnp.maximum(ga, gb)
    hot = jnp.where(valid & (lane == low * groups + high), 1.0, 0.0)
    rank = rank_in(hot)

    sums = jnp.sum(hot, axis=0, keepdims=True).astype(i32)
    lane1 = lax.broadcasted_iota(i32, (1, 128), 1)
    count, up = {}, {}
    for g in range(groups):
        for h in range(g, groups):
            count[g, h] = jnp.sum(jnp.where(lane1 == g * groups + h, sums, 0))
            up[g, h] = (count[g, h] >> 1) if h > g else 0

    def loads():
        load = [0] * groups
        for (g, h), c in count.items():
            load[g] = load[g] + (c - up[g, h])
            load[h] = load[h] + up[g, h]
        return load

    load = loads()
    for g, h in count:
        if h > g:
            up[g, h] = up[g, h] + ((load[g] - load[h] + 2) >> 2)
    load = loads()
    excess = 0
    for g in range(groups - 1):
        excess = excess + load[g] - each
        up[g, g + 1] = up[g, g + 1] + excess
    fits = 1
    goes_up = jnp.zeros((1, 128), i32)
    for (g, h), c in count.items():
        if h > g:
            u = up[g, h]
            fine = (u >= 0) & (u <= KEEP) & (c - u >= 0) & (c - u <= KEEP)
            fits = jnp.where(fine, fits, 0)
            goes_up = jnp.where(lane1 == g * groups + h, u, goes_up)
    fits_ref[0] = fits

    ups = col(hot * goes_up.astype(f32)).astype(i32)
    rises = rank < ups
    group = jnp.where(rises, high, low)
    source = low + high - group
    crosses = valid & (low != high)
    hot = jnp.where(valid & (lane == group), 1.0, 0.0)
    q = rank_in(hot)
    put = (((group - source) & 3) - 1) * KEEP + jnp.where(rises, rank, rank - ups)
    near_b = ga != group
    near = jnp.where(near_b, b, a) & 127
    far = jnp.where(near_b, a, b) & 127
    table = jnp.where(crosses, 128 + put, far)

    def side(*columns):
        at = lax.broadcasted_iota(i32, (n, 8), 1)
        out = jnp.zeros((n, 8), f32)
        for k, column in enumerate(columns):
            out = jnp.where(at == k, column.astype(f32), out)
        return out.astype(jnp.bfloat16)

    def spread(columns, mask):
        hot = jnp.where(mask, 1.0, 0.0).astype(jnp.bfloat16)
        out = lax.dot_general(columns, hot, (((0,), (0,)), ((), ())), preferred_element_type=f32)
        return out.astype(i32)

    mine = valid & (group == me)
    flag = jnp.where(near_b, 1, 0)
    columns = side(near, table & 255, a & 255, b & 255, flag, table >> 8, a >> 8, b >> 8)
    got = spread(columns, mine & (lane == q))
    pos_ref[...] = got
    pos_ref[1:4] = got[1:4] + 256 * got[5:8]
    wide = lax.broadcasted_iota(i32, (n, slot_ref.shape[1]), 1)
    here = wide == put
    zero = jnp.zeros_like(a)
    slots = spread(side(far, zero, zero + 1), crosses & (source == me) & here)
    slot_ref[...] = slots + spread(side(zero, q), crosses & mine & here)


def route(me, pair_slots):
    lists = jnp.transpose(pair_slots, (1, 2, 0)).reshape(-1, pair_slots.shape[0])
    width = 128 * -(-(3 * KEEP) // 128)
    vmem, smem = pl.BlockSpec(memory_space=pltpu.VMEM), pl.BlockSpec(memory_space=pltpu.SMEM)
    return pl.pallas_call(
        route_kernel,
        out_shape=[
            jax.ShapeDtypeStruct((8, 128), jnp.int32),
            jax.ShapeDtypeStruct((8, width), jnp.int32),
            jax.ShapeDtypeStruct((1,), jnp.int32),
        ],
        in_specs=[smem, vmem],
        out_specs=[vmem, vmem, smem],
        compiler_params=pltpu.CompilerParams(vmem_limit_bytes=40 << 20),
        cost_estimate=pl.CostEstimate(flops=10_000_000, bytes_accessed=1_000_000, transcendentals=0),
        name="route",
    )(me, lists)


def fetch_kernel(row_of, first, tables, idx_ref, *refs):
    parts, (*outs, table, sem) = refs[:tables], refs[tables:]
    copies, end = [], 0
    for k, part in enumerate(parts):
        copies.append(pltpu.make_async_copy(part, table.at[pl.ds(end, part.shape[0])], sem.at[k]))
        end += part.shape[0]
    for copy in copies:
        copy.start()
    for copy in copies:
        copy.wait()
    for k, out_ref in enumerate(outs):
        count = out_ref.shape[0]

        def move(i, carry, out_ref=out_ref, k=k, count=count):
            out_ref[i] = table[row_of(idx_ref, first + k * count, i)]
            return carry

        lax.fori_loop(0, count, move, 0, unroll=4)


def fetch(idx, tables, outs, count, row_of, first, name):
    rows = sum(t.shape[0] for t in tables)
    return pl.pallas_call(
        functools.partial(fetch_kernel, row_of, first, len(tables)),
        out_shape=[jax.ShapeDtypeStruct((count, ROWS, 128), jnp.float32)] * outs,
        in_specs=[pl.BlockSpec(memory_space=pltpu.SMEM)] + [pl.BlockSpec(memory_space=pl.ANY)] * len(tables),
        out_specs=[pl.BlockSpec(memory_space=pltpu.VMEM)] * outs,
        scratch_shapes=[pltpu.VMEM((rows, ROWS, 128), jnp.float32), pltpu.SemaphoreType.DMA((len(tables),))],
        compiler_params=pltpu.CompilerParams(vmem_limit_bytes=16 << 20),
        cost_estimate=pl.CostEstimate(flops=0, bytes_accessed=(rows + count * outs) * 16384, transcendentals=0),
        name=name,
    )(idx, *tables)


def solve_pair(offset, box_a, box_b, term_a, term_b, part, dens, resid, second, third, image):
    ox, oy, oz = offset
    shape = (ROWS, 128)
    line = lax.broadcasted_iota(jnp.int32, shape, 0)
    lane = lax.broadcasted_iota(jnp.int32, shape, 1)
    cy = 2 * line + (lane >> 6)
    cz = lane & (B - 1)
    high = lane >= B
    ends = (high & (line == 0)) | (~high & (line == ROWS - 1))
    no_up, no_down = cz == B - 1, cz == 0

    def plane(ref, x):
        return ref[pl.ds(pl.multiple_of(x * ROWS, ROWS), ROWS)]

    def put(ref, x, value):
        ref[pl.ds(pl.multiple_of(x * ROWS, ROWS), ROWS)] = value

    def shifter(sy, sz):
        flat = sy * B + sz
        lines, steps = flat >> 7, flat & 127
        inside = (cy >= sy) & (cy < B + sy) & (cz >= sz) & (cz < B + sz)
        keep = lane < 128 - steps

        def shift(ref, x):
            at = x * ROWS - lines
            moved = jnp.where(keep, ref[pl.ds(at, ROWS)], ref[pl.ds(at - 1, ROWS)])
            return jnp.where(inside, pltpu.roll(moved, steps, axis=1), 0.0)

        return shift

    def apply(ref, x):
        here = plane(ref, x + 1)
        at = (x + 1) * ROWS
        other = jnp.where(high, ref[pl.ds(at - 1, ROWS)], ref[pl.ds(at + 1, ROWS)])
        other = here + jnp.where(ends, 0.0, other)
        beside = plane(ref, x) + plane(ref, x + 2) + pltpu.roll(other, B, axis=1)
        upper = jnp.where(no_up, 0.0, pltpu.roll(here, 127, axis=1))
        lower = jnp.where(no_down, 0.0, pltpu.roll(here, 1, axis=1))
        return here, 6.0 * here - beside - upper - lower

    zero = jnp.zeros(shape, jnp.float32)
    for ref in (dens, second, third):
        put(ref, 0, zero)
        put(ref, B + 1, zero)

    shift_on = shifter(oy, oz)
    shift_back = shifter(-oy, -oz)

    def begin(x, acc):
        src = x - ox
        inside = jnp.where((src >= 0) & (src < B), 1.0, 0.0)
        moved = shift_on(box_b, jnp.clip(src, 0, B - 1) + 1) * inside
        density = plane(box_a, x + 1) * moved
        put(part, x, moved)
        put(dens, x + 1, density)
        return acc + density * density

    def first(x, acc):
        here, img = apply(dens, x)
        put(image, x + 1, img)
        return acc + here * img

    norm0 = yield begin
    step0 = norm0 / (yield first)

    def rest0(x, acc):
        left = plane(dens, x + 1) - step0 * plane(image, x + 1)
        put(resid, x, left)
        return acc + left * left

    norm1 = yield rest0
    ratio0 = norm1 / norm0

    def turn1(x, acc):
        put(second, x + 1, plane(resid, x) + ratio0 * plane(dens, x + 1))
        return acc

    def again(x, acc):
        here, img = apply(second, x)
        put(image, x + 1, img)
        return acc + here * img

    yield turn1
    step1 = norm1 / (yield again)

    def rest1(x, acc):
        left = plane(resid, x) - step1 * plane(image, x + 1)
        put(resid, x, left)
        return acc + left * left

    norm2 = yield rest1
    ratio1 = norm2 / norm1

    def turn2(x, acc):
        put(third, x + 1, plane(resid, x) + ratio1 * plane(second, x + 1))
        return acc

    def last(x, acc):
        here, img = apply(third, x)
        return acc + here * img

    yield turn2
    step2 = norm2 / (yield last)

    def finish(x, acc):
        potential = step0 * plane(dens, x + 1) + step1 * plane(second, x + 1) + step2 * plane(third, x + 1)
        put(term_a, x, potential * plane(part, x))
        put(image, x + 1, potential * plane(box_a, x + 1))
        return acc

    def back(x, acc):
        src = x + ox
        inside = jnp.where((src >= 0) & (src < B), 1.0, 0.0)
        put(term_b, x, shift_back(image, jnp.clip(src, 0, B - 1) + 1) * inside)
        return acc

    yield finish
    yield back


def run_together(solvers):
    steps = [next(solver) for solver in solvers]
    zero = jnp.zeros((ROWS, 128), jnp.float32)
    while True:
        def both(x, accs, steps=tuple(steps)):
            return tuple(step(x, acc) for step, acc in zip(steps, accs))

        accs = lax.fori_loop(0, B, both, (zero,) * len(steps), unroll=UNROLL)
        sums = [jnp.sum(acc, keepdims=True) for acc in accs]
        try:
            steps = [solver.send(value) for solver, value in zip(solvers, sums)]
        except StopIteration:
            return


def pair_kernel(place_ref, pos_ref, anchor_ref, near_ref, far_ref, near_out, far_out, boxes, terms, *rest):
    *fields, sem_in, sem_out = rest

    def flat(ref):
        return ref.reshape(ref.shape[0] * ROWS, 128)

    at = [s * B + place_ref[0] for s in range(PAIR_DEV)]
    flags = [pos_ref[4, k] for k in at]

    def pulls(s):
        return [
            pltpu.make_async_copy(near_ref.at[:, s], boxes.at[s, flags[s], pl.ds(1, B)], sem_in.at[s, 0]),
            pltpu.make_async_copy(far_ref.at[:, s], boxes.at[s, 1 - flags[s], pl.ds(1, B)], sem_in.at[s, 1]),
        ]

    def pushes(s):
        return [
            pltpu.make_async_copy(terms.at[s, flags[s]], near_out.at[:, s], sem_out.at[s, 0]),
            pltpu.make_async_copy(terms.at[s, 1 - flags[s]], far_out.at[:, s], sem_out.at[s, 1]),
        ]

    for s in range(PAIR_DEV):
        for copy in pulls(s):
            copy.start()
    solvers = []
    for s in range(PAIR_DEV):
        for copy in pulls(s):
            copy.wait()
        orb_a, orb_b = pos_ref[2, at[s]], pos_ref[3, at[s]]
        offset = [anchor_ref[3 * orb_b + k] - anchor_ref[3 * orb_a + k] for k in range(3)]
        refs = [flat(ref.at[s, k]) for ref in (boxes, terms) for k in range(2)]
        solvers.append(solve_pair(offset, *refs, *[ref.at[s] for ref in fields]))
    run_together(solvers)
    for s in range(PAIR_DEV):
        for copy in pushes(s):
            copy.start()
    for s in range(PAIR_DEV):
        for copy in pushes(s):
            copy.wait()


def solve(place, pos, anchors, near, far):
    smem = pl.BlockSpec(memory_space=pltpu.SMEM)
    anywhere = pl.BlockSpec(memory_space=pl.ANY)
    field = pltpu.VMEM((PAIR_DEV, B * ROWS, 128), jnp.float32)
    padded = pltpu.VMEM((PAIR_DEV, (B + 2) * ROWS, 128), jnp.float32)
    boxes = pltpu.VMEM((PAIR_DEV, 2, B + 2, ROWS, 128), jnp.float32)
    terms = pltpu.VMEM((PAIR_DEV, 2, B, ROWS, 128), jnp.float32)
    dma = pltpu.SemaphoreType.DMA((PAIR_DEV, 2))
    return pl.pallas_call(
        pair_kernel,
        out_shape=[jax.ShapeDtypeStruct((B, PAIR_DEV, ROWS, 128), jnp.float32)] * 2,
        in_specs=[smem, smem, smem, anywhere, anywhere],
        out_specs=[anywhere, anywhere],
        scratch_shapes=[boxes, terms, field, padded, field, padded, padded, padded, dma, dma],
        compiler_params=pltpu.CompilerParams(vmem_limit_bytes=32 << 20),
        cost_estimate=pl.CostEstimate(flops=100_000_000, bytes_accessed=30_000_000, transcendentals=0),
        name="solve",
    )(place, pos, anchors, near, far)


def add_far_kernel(pos_ref, slot_ref, terms_ref, *refs):
    *from_groups, out_ref = refs
    out_ref[...] = jnp.zeros(out_ref.shape, jnp.float32)

    def here(p, carry):
        for s in range(PAIR_DEV):
            j = pos_ref[1, s * B + p]

            @pl.when(j < 128)
            def _(j=j, s=s):
                out_ref[j] = out_ref[j] + terms_ref[p, s]

        return carry

    lax.fori_loop(0, B, here, 0)

    def there(k, carry):
        for d, ref in enumerate(from_groups):
            at = d * KEEP + k

            @pl.when(slot_ref[2, at] == 1)
            def _(at=at, ref=ref):
                j = slot_ref[0, at]
                out_ref[j] = out_ref[j] + ref[k]

        return carry

    lax.fori_loop(0, KEEP, there, 0)


def add_far(pos, slot, terms, from_groups):
    smem, vmem = pl.BlockSpec(memory_space=pltpu.SMEM), pl.BlockSpec(memory_space=pltpu.VMEM)
    return pl.pallas_call(
        add_far_kernel,
        out_shape=jax.ShapeDtypeStruct((128, ROWS, 128), jnp.float32),
        in_specs=[smem, smem] + [vmem] * 4,
        out_specs=vmem,
        compiler_params=pltpu.CompilerParams(vmem_limit_bytes=24 << 20),
        cost_estimate=pl.CostEstimate(flops=2_000_000, bytes_accessed=10_000_000, transcendentals=0),
        name="add_far",
    )(pos, slot, terms, *from_groups)


def add_near_kernel(pos_ref, sum_ref, terms_ref, out_ref, acc):
    acc[...] = sum_ref[...]

    def here(p, carry):
        for s in range(PAIR_DEV):
            j = pos_ref[0, s * B + p]
            acc[j] = acc[j] + terms_ref[p, s]
        return carry

    lax.fori_loop(0, B, here, 0, unroll=4)

    def lay_out(k, carry):
        rows = pl.ds(pl.multiple_of(k * 8, 8), 8)
        for first in range(0, BLOCK, 8):
            lines = jnp.swapaxes(acc[rows, first : first + 8], 0, 1)
            for j in range(8):
                out_ref[rows, (first + j) * 128 : (first + j + 1) * 128] = lines[j]
        return carry

    lax.fori_loop(0, acc.shape[0] // 8, lay_out, 0, unroll=2)


def add_near(pos, summed, terms):
    return pl.pallas_call(
        add_near_kernel,
        out_shape=jax.ShapeDtypeStruct((128, ROWS * 128), jnp.float32),
        grid=(ROWS // BLOCK,),
        in_specs=[
            pl.BlockSpec(memory_space=pltpu.SMEM),
            pl.BlockSpec((128, BLOCK, 128), lambda i: (0, i, 0)),
            pl.BlockSpec((B, PAIR_DEV, BLOCK, 128), lambda i: (0, 0, i, 0)),
        ],
        out_specs=pl.BlockSpec((128, BLOCK * 128), lambda i: (0, i)),
        scratch_shapes=[pltpu.VMEM((128, BLOCK, 128), jnp.float32)],
        compiler_params=pltpu.CompilerParams(vmem_limit_bytes=60 << 20),
        cost_estimate=pl.CostEstimate(flops=2_000_000, bytes_accessed=10_000_000, transcendentals=0),
        name="add_near",
    )(pos, summed, terms)


def deal_near_kernel(pos_ref, orb_ref, near_ref, table):
    def lay_out(k, carry):
        rows = pl.ds(pl.multiple_of(k * 8, 8), 8)
        for first in range(0, BLOCK, 8):
            lines = [orb_ref[rows, (first + j) * 128 : (first + j + 1) * 128] for j in range(8)]
            table[rows, first : first + 8] = jnp.swapaxes(jnp.stack(lines), 0, 1)
        return carry

    lax.fori_loop(0, table.shape[0] // 8, lay_out, 0, unroll=2)

    def here(p, carry):
        for s in range(PAIR_DEV):
            near_ref[p, s] = table[pos_ref[0, s * B + p]]
        return carry

    lax.fori_loop(0, B, here, 0, unroll=4)


def deal_near(pos, orbitals):
    return pl.pallas_call(
        deal_near_kernel,
        out_shape=jax.ShapeDtypeStruct((B, PAIR_DEV, ROWS, 128), jnp.float32),
        grid=(ROWS // BLOCK,),
        in_specs=[pl.BlockSpec(memory_space=pltpu.SMEM), pl.BlockSpec((128, BLOCK * 128), lambda i: (0, i))],
        out_specs=pl.BlockSpec((B, PAIR_DEV, BLOCK, 128), lambda i: (0, 0, i, 0)),
        scratch_shapes=[pltpu.VMEM((128, BLOCK, 128), jnp.float32)],
        compiler_params=pltpu.CompilerParams(vmem_limit_bytes=60 << 20),
        cost_estimate=pl.CostEstimate(flops=2_000_000, bytes_accessed=10_000_000, transcendentals=0),
        name="deal_near",
    )(pos, orbitals)


def turned(x, shift):
    groups = lax.axis_size("grp")
    return lax.ppermute(x, "grp", [(g, (g + shift) % groups) for g in range(groups)])


def far_row(pos, first, i):
    return pos[1, (i & 1) * B + (i >> 1)]


def sent_row(slot, first, i):
    return slot[0, first + i]


def used_row(slot, first, i):
    q = slot[1, first + i]
    return 2 * (q & (B - 1)) + (q >> 6)


def exchanged(planes):
    return lax.all_to_all(planes.reshape(B, PAIR_DEV, ROWS, 128), "grid", 0, 0, tiled=True)


def fitting(orbitals, anchors, place, pos, slot):
    near = exchanged(deal_near(pos, orbitals))
    local = orbitals.reshape(128, ROWS, 128)
    sent = fetch(slot, [local], 3, KEEP, sent_row, 0, "send")
    arrived = [turned(x, d) for d, x in enumerate(sent, 1)]
    far = exchanged(*fetch(pos, [local] + arrived, 1, 2 * B, far_row, 0, "deal_far"))
    near_terms, far_terms = solve(place, pos, anchors.reshape(-1), near, far)
    far_terms = exchanged(far_terms)
    back = fetch(slot, [far_terms.reshape(2 * B, ROWS, 128)], 3, KEEP, used_row, 0, "back")
    from_groups = [turned(x, -d) for d, x in enumerate(back, 1)]
    near_terms = exchanged(near_terms)
    return add_near(pos, add_far(pos, slot, far_terms, from_groups), near_terms)


def body(orbitals, anchors, pair_slots):
    me = lax.axis_index("grp").astype(jnp.int32)[None]
    place = lax.axis_index("grid").astype(jnp.int32)[None]
    pos, slot, fits = route(me, pair_slots)
    return lax.cond(
        fits[0] == 1,
        lambda: fitting(orbitals, anchors, place, pos, slot),
        lambda: general(orbitals, anchors, pair_slots),
    )


def solution(mesh):
    return jax.shard_map(
        body,
        mesh=mesh,
        in_specs=(P("grp", "grid"), P(), P()),
        out_specs=P("grp", "grid"),
        check_vma=False,
    )
```

```python
import functools

import jax
import jax.numpy as jnp
from jax import lax
from jax.experimental import pallas as pl
from jax.experimental.pallas import tpu as pltpu
from jax.sharding import PartitionSpec as P

B = 64
PAIR_DEV = 2
ITERS = 3
ROWS = B * B // 128
KEEP = 48
UNROLL = 16
TRIMMED = 56


def shift_field(field, offset, extent):
    plane_size = extent * extent
    padded_x = jnp.pad(field, ((extent, extent), (0, 0)))
    moved = lax.dynamic_slice_in_dim(padded_x, extent - offset[0], extent, 0)
    padded_yz = jnp.pad(moved, ((0, 0), (plane_size, plane_size)))
    linear = offset[1] * extent + offset[2]
    moved = lax.dynamic_slice_in_dim(padded_yz, plane_size - linear, plane_size, 1)
    cells = lax.broadcasted_iota(jnp.int32, (1, plane_size), 1)
    coord_y = cells // extent - offset[1]
    coord_z = cells % extent - offset[2]
    inside = (coord_y >= 0) & (coord_y < extent) & (coord_z >= 0) & (coord_z < extent)
    return jnp.where(inside, moved, jnp.zeros_like(moved))


def operate(field, extent):
    padded_x = jnp.pad(field, ((1, 1), (0, 0)))
    beside = padded_x[2:] + padded_x[:-2]
    padded_y = jnp.pad(field, ((0, 0), (extent, extent)))
    beside = beside + padded_y[:, 2 * extent :] + padded_y[:, : -2 * extent]
    padded_z = jnp.pad(field, ((0, 0), (1, 1)))
    cells = lax.broadcasted_iota(jnp.int32, (1, field.shape[1]), 1) % extent
    upper_z = jnp.where(cells < extent - 1, padded_z[:, 2:], jnp.zeros_like(field))
    lower_z = jnp.where(cells > 0, padded_z[:, :-2], jnp.zeros_like(field))
    return 6.0 * field - beside - upper_z - lower_z


def conjugate(density, extent):
    potential = jnp.zeros_like(density)
    resid = density
    direction = density
    norm_now = jnp.sum(resid * resid)
    for turn in range(ITERS):
        image = operate(direction, extent)
        step_len = norm_now / jnp.sum(direction * image)
        potential = potential + step_len * direction
        resid = resid - step_len * image
        norm_next = jnp.sum(resid * resid)
        direction = resid + norm_next / norm_now * direction
        norm_now = norm_next
    return potential


def pair_terms(field_a, field_b, offset, extent):
    partner = shift_field(field_b, offset, extent)
    density = field_a * partner
    potential = conjugate(density, extent)
    term_a = potential * partner
    term_b = shift_field(potential * field_a, -offset, extent)
    return (term_a, term_b)


def deal_evenly(pair_slots, owner_count, each_owner):
    flat_slots = pair_slots.reshape(-1, 2)
    filled = (flat_slots[:, 0] >= 0).astype(jnp.int32)
    order = jnp.arange(flat_slots.shape[0], dtype=jnp.int32)
    position = jnp.sum(jnp.where(order[None, :] < order[:, None], filled[None, :], 0), axis=1)
    wanted = lax.broadcasted_iota(jnp.int32, (owner_count, each_owner), 1) * owner_count
    wanted = (wanted + lax.broadcasted_iota(jnp.int32, (owner_count, each_owner), 0)).reshape(-1)
    matched = (position[None, :] == wanted[:, None]) & (filled[None, :] == 1)
    picked = jnp.dot(matched.astype(jnp.int32), flat_slots)
    return picked.reshape(owner_count, each_owner, 2)


def general(orbitals, anchors, pair_slots):
    extent = B
    grid_count = lax.axis_size("grid")
    owner_count = lax.axis_size("grp") * grid_count
    group_idx = lax.axis_index("grp")
    place_idx = lax.axis_index("grid")
    assignment = deal_evenly(pair_slots, owner_count, PAIR_DEV)
    filled = assignment[..., 0] >= 0
    safe_ids = jnp.maximum(assignment, 0)
    pieces = lax.all_gather(orbitals, "grp", axis=0, tiled=True)
    group_table = lax.dynamic_slice_in_dim(safe_ids, group_idx * grid_count, grid_count, 0)
    gather_ids = jnp.transpose(group_table, (1, 2, 0))
    outgoing = pieces[gather_ids]
    arrived = lax.all_to_all(outgoing, "grid", split_axis=2, concat_axis=2, tiled=True)
    owner_idx = group_idx * grid_count + place_idx
    own_pairs = safe_ids[owner_idx]
    own_filled = filled[owner_idx]
    offsets = anchors[own_pairs[:, 1]] - anchors[own_pairs[:, 0]]

    def solve_slot(slot_item):
        boxes_pair, offset, flag = slot_item
        term_a, term_b = pair_terms(boxes_pair[0], boxes_pair[1], offset, extent)
        weight_flag = jnp.where(flag, 1.0, 0.0).astype(jnp.float32)
        return jnp.stack([term_a, term_b]) * weight_flag

    terms = lax.map(solve_slot, (arrived, offsets, own_filled))
    returned = lax.all_to_all(terms, "grid", split_axis=2, concat_axis=2, tiled=True)
    flat_terms = returned.reshape(-1, returned.shape[-1])
    summed = jax.ops.segment_sum(flat_terms, gather_ids.reshape(-1), num_segments=anchors.shape[0])
    return lax.psum_scatter(summed, "grp", scatter_dimension=0, tiled=True)


def route_kernel(me_ref, pair_ref, anchor_ref, pos_ref, slot_ref, used_ref, mode_ref):
    me = me_ref[0]
    f32, i32 = jnp.float32, jnp.int32
    groups, each = 4, 2 * B

    def col(x):
        return jnp.sum(x, axis=1, keepdims=True)

    pairs = pair_ref[...].astype(f32).T
    at = lax.broadcasted_iota(i32, pairs.shape, 1)
    columns = [col(jnp.where(at == k, pairs, 0.0)) for k in range(pairs.shape[1])]
    a = jnp.concatenate(columns[0::2], axis=0).astype(i32)
    b = jnp.concatenate(columns[1::2], axis=0).astype(i32)
    n = a.shape[0]

    before = lax.broadcasted_iota(i32, (128, 128), 0) > lax.broadcasted_iota(i32, (128, 128), 1)
    before = jnp.where(before, 1.0, 0.0).astype(jnp.bfloat16)

    def earlier(width):
        i = lax.broadcasted_iota(i32, (width, width), 0)
        j = lax.broadcasted_iota(i32, (width, width), 1)
        return jnp.where(((i >> 4) == (j >> 4)) & (i < j), 1.0, 0.0)

    def sort_in(hot):
        width = hot.shape[1]
        totals = jnp.sum(hot, axis=0, keepdims=True)
        rows = jnp.broadcast_to(totals, (8, width))
        below = jnp.dot(rows, earlier(width), precision=lax.Precision.HIGHEST, preferred_element_type=f32)[0:1]
        ranks, passed = [], below
        for k in range(0, n, 128):
            part = hot[k : k + 128]
            ahead = jnp.dot(before, part.astype(jnp.bfloat16), preferred_element_type=f32) + passed
            ranks.append(col(ahead * part))
            passed = passed + jnp.sum(part, axis=0, keepdims=True)
        return jnp.concatenate(ranks, axis=0), totals, below

    lane = lax.broadcasted_iota(i32, (n, 128), 1)
    valid = a >= 0
    ga, gb = a >> 7, b >> 7
    low, high = jnp.minimum(ga, gb), jnp.maximum(ga, gb)
    anchor_y = anchor_ref[1:2].astype(f32)
    name = lax.broadcasted_iota(i32, (n, anchor_ref.shape[1]), 1)
    oy = col(jnp.where(name == b, anchor_y, 0.0) - jnp.where(name == a, anchor_y, 0.0)).astype(i32)
    spare = jnp.abs(oy) >> 1
    kinds = lax.broadcasted_iota(i32, (n, 256), 1)
    hot = jnp.where(valid & (kinds == (low * groups + high) * 16 + spare), 1.0, 0.0)
    rank, sums, _ = sort_in(hot)
    sums = sums.astype(i32)
    kind1 = lax.broadcasted_iota(i32, (1, 256), 1) >> 4
    count, up = {}, {}
    for g in range(groups):
        for h in range(g, groups):
            count[g, h] = jnp.sum(jnp.where(kind1 == g * groups + h, sums, 0))
            up[g, h] = (count[g, h] >> 1) if h > g else 0

    def loads():
        load = [0] * groups
        for (g, h), c in count.items():
            load[g] = load[g] + (c - up[g, h])
            load[h] = load[h] + up[g, h]
        return load

    load = loads()
    for g, h in count:
        if h > g:
            up[g, h] = up[g, h] + ((load[g] - load[h] + 2) >> 2)
    load = loads()
    excess = 0
    for g in range(groups - 1):
        excess = excess + load[g] - each
        up[g, g + 1] = up[g, g + 1] + excess
    fits = 1
    goes_up, there = jnp.zeros((1, 256), f32), jnp.ones((1, 256), f32)
    for (g, h), c in count.items():
        if h > g:
            u = up[g, h]
            fine = (u >= 0) & (u <= KEEP) & (c - u >= 0) & (c - u <= KEEP)
            fits = jnp.where(fine, fits, 0)
            goes_up = jnp.where(kind1 == g * groups + h, u.astype(f32), goes_up)
            there = jnp.where(kind1 == g * groups + h, jnp.maximum(c, 1).astype(f32), there)

    u, c = col(hot * goes_up), jnp.maximum(col(hot * there), 1.0)
    risen = jnp.floor((rank * u + 0.5) / c)
    rises = jnp.floor((rank * u + u + 0.5) / c) > risen
    group = jnp.where(rises, high, low)
    source = low + high - group
    crosses = valid & (low != high)
    hot = jnp.where(valid & (lane == group * 16 + spare), 1.0, 0.0)
    order, _, below = sort_in(hot)
    order = order.astype(i32)
    second = order >= B
    q = jnp.where(second, B + each - 1 - order, order)
    lane1 = lax.broadcasted_iota(i32, (1, 128), 1)
    need = (ROWS * PAIR_DEV - TRIMMED) - 1
    match = 1
    for g in range(groups):
        for j in range(need // 2 + 1):
            both = (lane1 == g * 16 + j + 1) | (lane1 == g * 16 + need - j + 1)
            match = jnp.where(jnp.sum(jnp.where(both, below, 0.0)) <= each, match, 0)
    mode_ref[0] = jnp.where(fits == 1, 1 - match, 2)

    put = (((group - source) & 3) - 1) * KEEP + jnp.where(rises, risen, rank - risen).astype(i32)
    near_b = ga != group
    near = jnp.where(near_b, b, a) & 127
    far = jnp.where(near_b, a, b) & 127
    table = jnp.where(crosses, 128 + put, far)
    spare = spare * match
    moved = jnp.where(second, spare, 0)
    from_a = jnp.where(oy > 0, spare, 0) - moved
    from_b = jnp.where(oy < 0, spare, 0) - moved
    near_from, far_from = jnp.where(near_b, from_b, from_a), jnp.where(near_b, from_a, from_b)

    def side(*columns):
        at = lax.broadcasted_iota(i32, (n, 8), 1)
        out = jnp.zeros((n, 8), f32)
        for k, column in enumerate(columns):
            out = jnp.where(at == k, column.astype(f32), out)
        return out.astype(jnp.bfloat16)

    def spread(columns, mask):
        hot = jnp.where(mask, 1.0, 0.0).astype(jnp.bfloat16)
        out = lax.dot_general(columns, hot, (((0,), (0,)), ((), ())), preferred_element_type=f32)
        return out.astype(i32)

    mine = valid & (group == me)
    flag = jnp.where(near_b, 1, 0)
    columns = side(near, table & 255, a & 255, b & 255, flag, table >> 8, a >> 8, b >> 8)
    here = mine & (lane == q)
    got = spread(columns, here)
    more = spread(side(near_from + 16, far_from + 16, spare), here)
    pos_ref[...] = got
    pos_ref[1:4] = got[1:4] + 256 * got[5:8]
    pos_ref[6:7] = pos_ref[1:2]
    pos_ref[0:1] = got[0:1] * ROWS + more[0:1] - 16
    pos_ref[1:2] = pos_ref[6:7] * ROWS + more[1:2] - 16
    pos_ref[5:6] = more[2:3]
    wide = lax.broadcasted_iota(i32, (n, slot_ref.shape[1]), 1)
    here = wide == put
    zero = jnp.zeros_like(a)
    slots = spread(side(far, zero, zero + 1, far_from + 16), crosses & (source == me) & here)
    used_ref[...] = spread(side(q & (B - 1), q >> 6, spare), crosses & mine & here)
    slot_ref[...] = slots
    slot_ref[3:4] = slots[0:1] * ROWS + slots[3:4] - 16


def route(me, pair_slots, anchors):
    lists = jnp.transpose(pair_slots, (1, 2, 0)).reshape(-1, pair_slots.shape[0])
    width = 128 * -(-(3 * KEEP) // 128)
    vmem, smem = pl.BlockSpec(memory_space=pltpu.VMEM), pl.BlockSpec(memory_space=pltpu.SMEM)
    return pl.pallas_call(
        route_kernel,
        out_shape=[
            jax.ShapeDtypeStruct((8, 128), jnp.int32),
            jax.ShapeDtypeStruct((8, width), jnp.int32),
            jax.ShapeDtypeStruct((8, width), jnp.int32),
            jax.ShapeDtypeStruct((1,), jnp.int32),
        ],
        in_specs=[smem, vmem, vmem],
        out_specs=[vmem, vmem, vmem, smem],
        compiler_params=pltpu.CompilerParams(vmem_limit_bytes=40 << 20),
        cost_estimate=pl.CostEstimate(flops=10_000_000, bytes_accessed=1_000_000, transcendentals=0),
        name="route",
    )(me, lists, jnp.transpose(anchors))


def flat(ref):
    return ref.reshape(ref.shape[0] * ROWS, 128)


def fetch_kernel(row_of, idx_ref, table_ref, *refs):
    *outs, table, sem = refs
    copy = pltpu.make_async_copy(table_ref, table, sem)
    copy.start()
    copy.wait()
    for k, out_ref in enumerate(outs):
        count = out_ref.shape[0]

        def move(i, carry, out_ref=out_ref, k=k, count=count):
            out_ref[i] = row_of(idx_ref, table, k * count + i)
            return carry

        lax.fori_loop(0, count, move, 0, unroll=4)


def fetch(idx, table, row_of, name):
    return pl.pallas_call(
        functools.partial(fetch_kernel, row_of),
        out_shape=[jax.ShapeDtypeStruct((KEEP, ROWS, 128), jnp.float32)] * 3,
        in_specs=[pl.BlockSpec(memory_space=pltpu.SMEM), pl.BlockSpec(memory_space=pl.ANY)],
        out_specs=[pl.BlockSpec(memory_space=pltpu.VMEM)] * 3,
        scratch_shapes=[pltpu.VMEM(table.shape, jnp.float32), pltpu.SemaphoreType.DMA],
        compiler_params=pltpu.CompilerParams(vmem_limit_bytes=16 << 20),
        cost_estimate=pl.CostEstimate(flops=0, bytes_accessed=8_000_000, transcendentals=0),
        name=name,
    )(idx, table)


def sent_row(idx_ref, table, i):
    return table[idx_ref[0, i]]


def line_no():
    return lax.broadcasted_iota(jnp.int32, (ROWS, 128), 0)


def its_lines(s, spare, lines):
    keep = line_no() >= spare if s else line_no() < ROWS - spare
    return jnp.where(keep, lines, 0.0)


def deal_owner(pos_ref, row, p, table, out_ref, at):
    first, second = [table[pl.ds(pos_ref[row, s * B + p] + ROWS, ROWS)] for s in range(PAIR_DEV)]
    lines = out_ref.shape[1]
    cut = lines - ROWS
    out_ref[at, :cut] = first[:cut]
    if cut < ROWS:
        shared = lax.broadcasted_iota(jnp.int32, (ROWS - cut, 128), 0) + cut < ROWS - pos_ref[5, p]
        out_ref[at, cut:ROWS] = jnp.where(shared, first[cut:], second[: ROWS - cut])
    out_ref[at, ROWS:] = second[ROWS - cut :]


def clear_ends(table):
    zero = jnp.zeros((ROWS, 128), jnp.float32)
    table[0] = zero
    table[table.shape[0] - 1] = zero


PARTS = 4


def deal_near_kernel(pos_ref, orb_ref, near_ref, table, stage, near, sem_in, sem_out):
    pulls = [
        pltpu.make_async_copy(orb_ref.at[:, pl.ds(k * 1024, 1024)], stage.at[k], sem_in.at[k]) for k in range(PARTS)
    ]
    for copy in pulls:
        copy.start()
    clear_ends(table)
    for k, copy in enumerate(pulls):
        copy.wait()

        def lay_out(i, carry, k=k):
            rows = pl.ds(pl.multiple_of(i * 8, 8), 8)
            lines = [stage[k, rows, j * 128 : (j + 1) * 128] for j in range(8)]
            table[pl.ds(i * 8 + 1, 8), k * 8 : k * 8 + 8] = jnp.swapaxes(jnp.stack(lines), 0, 1)
            return carry

        lax.fori_loop(0, 128 // 8, lay_out, 0, unroll=2)
    pushes = []
    for k in range(PARTS):

        def owner(p, carry):
            deal_owner(pos_ref, 0, p, flat(table), near, p)
            return carry

        mine = pl.ds(k * (B // PARTS), B // PARTS)
        lax.fori_loop(k * (B // PARTS), (k + 1) * (B // PARTS), owner, 0, unroll=4)
        pushes.append(pltpu.make_async_copy(near.at[mine], near_ref.at[mine], sem_out.at[k]))
        pushes[-1].start()
    for copy in pushes:
        copy.wait()


def deal_near(lines, pos, orbitals):
    anywhere = pl.BlockSpec(memory_space=pl.ANY)
    dma = pltpu.SemaphoreType.DMA((PARTS,))
    return pl.pallas_call(
        deal_near_kernel,
        out_shape=jax.ShapeDtypeStruct((B, lines, 128), jnp.float32),
        in_specs=[pl.BlockSpec(memory_space=pltpu.SMEM), anywhere],
        out_specs=anywhere,
        scratch_shapes=[
            pltpu.VMEM((130, ROWS, 128), jnp.float32),
            pltpu.VMEM((PARTS, 128, 1024), jnp.float32),
            pltpu.VMEM((B, lines, 128), jnp.float32),
            dma,
            dma,
        ],
        compiler_params=pltpu.CompilerParams(vmem_limit_bytes=60 << 20),
        cost_estimate=pl.CostEstimate(flops=2_000_000, bytes_accessed=10_000_000, transcendentals=0),
        name="deal_near",
    )(pos, orbitals)


def deal_far_kernel(pos_ref, *refs):
    *parts, far_ref, table, sem = refs
    copies, end = [], 1
    for k, part in enumerate(parts):
        copies.append(pltpu.make_async_copy(part, table.at[pl.ds(end, part.shape[0])], sem.at[k]))
        end += part.shape[0]
    for copy in copies:
        copy.start()
    clear_ends(table)
    for copy in copies:
        copy.wait()

    def owner(p, carry):
        deal_owner(pos_ref, 1, p, flat(table), far_ref, p)
        return carry

    lax.fori_loop(0, B, owner, 0, unroll=4)


def deal_far(lines, pos, parts):
    rows = sum(x.shape[0] for x in parts)
    return pl.pallas_call(
        deal_far_kernel,
        out_shape=jax.ShapeDtypeStruct((B, lines, 128), jnp.float32),
        in_specs=[pl.BlockSpec(memory_space=pltpu.SMEM)] + [pl.BlockSpec(memory_space=pl.ANY)] * len(parts),
        out_specs=pl.BlockSpec(memory_space=pltpu.VMEM),
        scratch_shapes=[pltpu.VMEM((rows + 2, ROWS, 128), jnp.float32), pltpu.SemaphoreType.DMA((len(parts),))],
        compiler_params=pltpu.CompilerParams(vmem_limit_bytes=16 << 20),
        cost_estimate=pl.CostEstimate(flops=0, bytes_accessed=12_000_000, transcendentals=0),
        name="deal_far",
    )(pos, *parts)


def solve_pair(offset, from_a, from_b, box_a, box_b, term_a, term_b, part, dens, resid, second, third, image):
    ox, oy, oz = offset
    shape = (ROWS, 128)
    line = lax.broadcasted_iota(jnp.int32, shape, 0)
    lane = lax.broadcasted_iota(jnp.int32, shape, 1)
    cy = 2 * line + (lane >> 6)
    cz = lane & (B - 1)
    high = lane >= B
    ends = (high & (line == 0)) | (~high & (line == ROWS - 1))
    no_up, no_down = cz == B - 1, cz == 0

    def plane(ref, x):
        return ref[pl.ds(pl.multiple_of(x * ROWS, ROWS), ROWS)]

    def put(ref, x, value):
        ref[pl.ds(pl.multiple_of(x * ROWS, ROWS), ROWS)] = value

    def shifter(sy, sz):
        flat = sy * B + sz
        lines, steps = flat >> 7, flat & 127
        inside = (cy >= sy) & (cy < B + sy) & (cz >= sz) & (cz < B + sz)
        keep = lane < 128 - steps

        def shift(ref, x, first):
            at = x * ROWS - lines - first
            moved = jnp.where(keep, ref[pl.ds(at, ROWS)], ref[pl.ds(at - 1, ROWS)])
            return jnp.where(inside, pltpu.roll(moved, steps, axis=1), 0.0)

        return shift

    def apply(ref, x):
        here = plane(ref, x + 1)
        at = (x + 1) * ROWS
        other = jnp.where(high, ref[pl.ds(at - 1, ROWS)], ref[pl.ds(at + 1, ROWS)])
        other = here + jnp.where(ends, 0.0, other)
        beside = plane(ref, x) + plane(ref, x + 2) + pltpu.roll(other, B, axis=1)
        upper = jnp.where(no_up, 0.0, pltpu.roll(here, 127, axis=1))
        lower = jnp.where(no_down, 0.0, pltpu.roll(here, 1, axis=1))
        return here, 6.0 * here - beside - upper - lower

    zero = jnp.zeros(shape, jnp.float32)
    for ref in (dens, second, third):
        put(ref, 0, zero)
        put(ref, B + 1, zero)

    shift_on = shifter(oy, oz)
    shift_back = shifter(-oy, -oz)

    def begin(x, acc):
        src = x - ox
        inside = jnp.where((src >= 0) & (src < B), 1.0, 0.0)
        moved = shift_on(box_b, jnp.clip(src, 0, B - 1) + 1, from_b) * inside
        density = box_a[pl.ds((x + 1) * ROWS - from_a, ROWS)] * moved
        put(part, x, moved)
        put(dens, x + 1, density)
        return acc + density * density

    def first(x, acc):
        here, img = apply(dens, x)
        put(image, x + 1, img)
        return acc + here * img

    norm0 = yield begin
    step0 = norm0 / (yield first)

    def rest0(x, acc):
        left = plane(dens, x + 1) - step0 * plane(image, x + 1)
        put(resid, x, left)
        return acc + left * left

    norm1 = yield rest0
    ratio0 = norm1 / norm0

    def turn1(x, acc):
        put(second, x + 1, plane(resid, x) + ratio0 * plane(dens, x + 1))
        return acc

    def again(x, acc):
        here, img = apply(second, x)
        put(image, x + 1, img)
        return acc + here * img

    yield turn1
    step1 = norm1 / (yield again)

    def rest1(x, acc):
        left = plane(resid, x) - step1 * plane(image, x + 1)
        put(resid, x, left)
        return acc + left * left

    norm2 = yield rest1
    ratio1 = norm2 / norm1

    def turn2(x, acc):
        put(third, x + 1, plane(resid, x) + ratio1 * plane(second, x + 1))
        return acc

    def last(x, acc):
        here, img = apply(third, x)
        return acc + here * img

    yield turn2
    step2 = norm2 / (yield last)

    def finish(x, acc):
        potential = step0 * plane(dens, x + 1) + step1 * plane(second, x + 1) + step2 * plane(third, x + 1)
        here = pl.ds((x + 1) * ROWS - from_a, ROWS)
        term_a[here] = potential * plane(part, x)
        put(image, x + 1, potential * box_a[here])
        return acc

    def back(x, acc):
        src = x + ox
        inside = jnp.where((src >= 0) & (src < B), 1.0, 0.0)
        term_b[pl.ds((x + 1) * ROWS - from_b, ROWS)] = shift_back(image, jnp.clip(src, 0, B - 1) + 1, 0) * inside
        return acc

    yield finish
    yield back


def run_together(solvers):
    steps = [next(solver) for solver in solvers]
    zero = jnp.zeros((ROWS, 128), jnp.float32)
    while True:
        def both(x, accs, steps=tuple(steps)):
            return tuple(step(x, acc) for step, acc in zip(steps, accs))

        accs = lax.fori_loop(0, B, both, (zero,) * len(steps), unroll=UNROLL)
        sums = [jnp.sum(acc, keepdims=True) for acc in accs]
        try:
            steps = [solver.send(value) for solver, value in zip(solvers, sums)]
        except StopIteration:
            return


def pair_kernel(place_ref, pos_ref, anchor_ref, near_ref, far_ref, near_out, far_out, boxes, terms, *rest):
    *fields, sem = rest
    lines = near_ref.shape[1]
    cut = lines - ROWS
    at = [s * B + place_ref[0] for s in range(PAIR_DEV)]
    flags = [pos_ref[4, k] for k in at]
    copies = []
    for s in range(PAIR_DEV):
        for k, ref in enumerate((near_ref, far_ref)):
            which = 1 - flags[s] if k else flags[s]
            source = ref.at[:, pl.ds(s * cut, ROWS)]
            copies.append(pltpu.make_async_copy(source, boxes.at[s, which, pl.ds(1, B)], sem.at[s, k]))
    for copy in copies:
        copy.start()
    for s in range(PAIR_DEV):
        for k in range(2):
            clear_ends(boxes.at[s, k])
    for copy in copies:
        copy.wait()
    solvers = []
    for s in range(PAIR_DEV):
        orb_a, orb_b = pos_ref[2, at[s]], pos_ref[3, at[s]]
        offset = [anchor_ref[3 * orb_b + k] - anchor_ref[3 * orb_a + k] for k in range(3)]
        spare = pos_ref[5, at[s]]
        moved = spare if s else 0
        from_a = jnp.where(offset[1] > 0, spare, 0) - moved
        from_b = jnp.where(offset[1] < 0, spare, 0) - moved
        refs = [flat(ref.at[s, k]) for ref in (boxes, terms) for k in range(2)]
        solvers.append(solve_pair(offset, from_a, from_b, *refs, *[ref.at[s] for ref in fields]))
    run_together(solvers)

    def together(x, carry):
        for k, out in enumerate((near_out, far_out)):
            first, second = [terms[s, 1 - flags[s] if k else flags[s], x + 1] for s in range(PAIR_DEV)]
            out[x, :cut] = first[:cut]
            if cut < ROWS:
                low = its_lines(0, pos_ref[5, at[0]], first)[cut:]
                out[x, cut:ROWS] = low + its_lines(1, pos_ref[5, at[1]], second)[: ROWS - cut]
            out[x, ROWS:] = second[ROWS - cut :]
        return carry

    lax.fori_loop(0, B, together, 0, unroll=4)


def solve(place, pos, anchors, near, far):
    smem, vmem = pl.BlockSpec(memory_space=pltpu.SMEM), pl.BlockSpec(memory_space=pltpu.VMEM)
    anywhere = pl.BlockSpec(memory_space=pl.ANY)
    field = pltpu.VMEM((PAIR_DEV, B * ROWS, 128), jnp.float32)
    padded = pltpu.VMEM((PAIR_DEV, (B + 2) * ROWS, 128), jnp.float32)
    boxes = pltpu.VMEM((PAIR_DEV, 2, B + 2, ROWS, 128), jnp.float32)
    return pl.pallas_call(
        pair_kernel,
        out_shape=[jax.ShapeDtypeStruct(near.shape, jnp.float32)] * 2,
        in_specs=[smem, smem, smem, anywhere, anywhere],
        out_specs=[vmem, vmem],
        scratch_shapes=[
            boxes, boxes, field, padded, field, padded, padded, padded,
            pltpu.SemaphoreType.DMA((PAIR_DEV, 2)),
        ],
        compiler_params=pltpu.CompilerParams(vmem_limit_bytes=40 << 20),
        cost_estimate=pl.CostEstimate(flops=100_000_000, bytes_accessed=30_000_000, transcendentals=0),
        name="solve",
    )(place, pos, anchors, near, far)


def add_lines(total, line, lines):
    here = pl.ds(line + ROWS, ROWS)
    total[here] = total[here] + lines


def add_far_kernel(pos_ref, slot_ref, terms_ref, *refs):
    *from_groups, out_ref = refs
    out_ref[...] = jnp.zeros(out_ref.shape, jnp.float32)
    total = flat(out_ref)
    cut = terms_ref.shape[1] - ROWS

    def here(p, carry):
        for s in range(PAIR_DEV):
            q = s * B + p

            @pl.when(pos_ref[6, q] < 128)
            def _(q=q, s=s):
                lines = terms_ref[p, s * cut : s * cut + ROWS]
                add_lines(total, pos_ref[1, q], its_lines(s, pos_ref[5, q], lines))

        return carry

    lax.fori_loop(0, B, here, 0)

    def there(k, carry):
        for d, ref in enumerate(from_groups):
            at = d * KEEP + k

            @pl.when(slot_ref[2, at] == 1)
            def _(at=at, ref=ref):
                add_lines(total, slot_ref[3, at], ref[k])

        return carry

    lax.fori_loop(0, KEEP, there, 0)


def add_far(pos, slot, terms, from_groups):
    smem, vmem = pl.BlockSpec(memory_space=pltpu.SMEM), pl.BlockSpec(memory_space=pltpu.VMEM)
    return pl.pallas_call(
        add_far_kernel,
        out_shape=jax.ShapeDtypeStruct((130, ROWS, 128), jnp.float32),
        in_specs=[smem, smem] + [vmem] * 4,
        out_specs=vmem,
        compiler_params=pltpu.CompilerParams(vmem_limit_bytes=24 << 20),
        cost_estimate=pl.CostEstimate(flops=2_000_000, bytes_accessed=10_000_000, transcendentals=0),
        name="add_far",
    )(pos, slot, terms, *from_groups)


def add_near_kernel(pos_ref, sum_ref, terms_ref, out_ref, acc, terms, stage, sem_sum, sem_in, sem_out):
    cut = terms.shape[1] - ROWS
    copies = [pltpu.make_async_copy(sum_ref, acc, sem_sum)]
    for k in range(PARTS):
        mine = pl.ds(k * (B // PARTS), B // PARTS)
        copies.append(pltpu.make_async_copy(terms_ref.at[mine], terms.at[mine], sem_in.at[k]))
    for copy in copies:
        copy.start()
    copies[0].wait()
    for k in range(PARTS):
        copies[k + 1].wait()

        def here(p, carry):
            for s in range(PAIR_DEV):
                q = s * B + p
                lines = terms[p, s * cut : s * cut + ROWS]
                add_lines(flat(acc), pos_ref[0, q], its_lines(s, pos_ref[5, q], lines))
            return carry

        lax.fori_loop(k * (B // PARTS), (k + 1) * (B // PARTS), here, 0, unroll=2)
    pushes = []
    for k in range(PARTS):

        def lay_out(i, carry, k=k):
            rows = pl.ds(pl.multiple_of(i * 8, 8), 8)
            lines = jnp.swapaxes(acc[pl.ds(i * 8 + 1, 8), k * 8 : k * 8 + 8], 0, 1)
            for j in range(8):
                stage[k, rows, j * 128 : (j + 1) * 128] = lines[j]
            return carry

        lax.fori_loop(0, 128 // 8, lay_out, 0, unroll=2)
        pushes.append(pltpu.make_async_copy(stage.at[k], out_ref.at[:, pl.ds(k * 1024, 1024)], sem_out.at[k]))
        pushes[-1].start()
    for copy in pushes:
        copy.wait()


def add_near(pos, summed, terms):
    anywhere = pl.BlockSpec(memory_space=pl.ANY)
    dma = pltpu.SemaphoreType.DMA((PARTS,))
    return pl.pallas_call(
        add_near_kernel,
        out_shape=jax.ShapeDtypeStruct((128, ROWS * 128), jnp.float32),
        in_specs=[pl.BlockSpec(memory_space=pltpu.SMEM), anywhere, anywhere],
        out_specs=anywhere,
        scratch_shapes=[
            pltpu.VMEM((130, ROWS, 128), jnp.float32),
            pltpu.VMEM(terms.shape, jnp.float32),
            pltpu.VMEM((PARTS, 128, 1024), jnp.float32),
            pltpu.SemaphoreType.DMA,
            dma,
            dma,
        ],
        compiler_params=pltpu.CompilerParams(vmem_limit_bytes=60 << 20),
        cost_estimate=pl.CostEstimate(flops=2_000_000, bytes_accessed=10_000_000, transcendentals=0),
        name="add_near",
    )(pos, summed, terms)


def turned(x, shift):
    groups = lax.axis_size("grp")
    return lax.ppermute(x, "grp", [(g, (g + shift) % groups) for g in range(groups)])


def exchanged(planes):
    return lax.all_to_all(planes, "grid", 0, 0, tiled=True)


def fitting(lines, orbitals, anchors, place, pos, slot, used):
    def used_row(used_ref, table, i):
        p, s, spare = used_ref[0, i], used_ref[1, i], used_ref[2, i]
        plane = table[p, pl.ds(pl.multiple_of(s * (lines - ROWS), 8), ROWS)]
        keep = (line_no() >= s * spare) & (line_no() < ROWS - (1 - s) * spare)
        return jnp.where(keep, plane, 0.0)

    near = exchanged(deal_near(lines, pos, orbitals))
    local = orbitals.reshape(128, ROWS, 128)
    arrived = [turned(x, d) for d, x in enumerate(fetch(slot, local, sent_row, "send"), 1)]
    far = exchanged(deal_far(lines, pos, [local] + arrived))
    near_terms, far_terms = solve(place, pos, anchors.reshape(-1), near, far)
    far_terms = exchanged(far_terms)
    from_groups = [turned(x, -d) for d, x in enumerate(fetch(used, far_terms, used_row, "back"), 1)]
    near_terms = exchanged(near_terms)
    return add_near(pos, add_far(pos, slot, far_terms, from_groups), near_terms)


def body(orbitals, anchors, pair_slots):
    me = lax.axis_index("grp").astype(jnp.int32)[None]
    place = lax.axis_index("grid").astype(jnp.int32)[None]
    pos, slot, used, mode = route(me, pair_slots, anchors)
    return lax.switch(
        mode[0],
        [
            lambda: fitting(TRIMMED, orbitals, anchors, place, pos, slot, used),
            lambda: fitting(PAIR_DEV * ROWS, orbitals, anchors, place, pos, slot, used),
            lambda: general(orbitals, anchors, pair_slots),
        ],
    )


def solution(mesh):
    return jax.shard_map(
        body,
        mesh=mesh,
        in_specs=(P("grp", "grid"), P(), P()),
        out_specs=P("grp", "grid"),
        check_vma=False,
    )
```

```python
import functools

import jax
import jax.numpy as jnp
from jax import lax
from jax.experimental import pallas as pl
from jax.experimental.pallas import tpu as pltpu
from jax.sharding import PartitionSpec as P

B = 64
PAIR_DEV = 2
ITERS = 3
ROWS = B * B // 128
KEEP = 48
UNROLL = 16
TRIMMED = 56


def deal_evenly(pair_slots, owner_count, each_owner):
    flat_slots = pair_slots.reshape(-1, 2)
    filled = (flat_slots[:, 0] >= 0).astype(jnp.int32)
    order = jnp.arange(flat_slots.shape[0], dtype=jnp.int32)
    position = jnp.sum(jnp.where(order[None, :] < order[:, None], filled[None, :], 0), axis=1)
    wanted = lax.broadcasted_iota(jnp.int32, (owner_count, each_owner), 1) * owner_count
    wanted = (wanted + lax.broadcasted_iota(jnp.int32, (owner_count, each_owner), 0)).reshape(-1)
    matched = (position[None, :] == wanted[:, None]) & (filled[None, :] == 1)
    picked = jnp.dot(matched.astype(jnp.int32), flat_slots)
    return picked.reshape(owner_count, each_owner, 2)


def route_kernel(me_ref, pair_ref, anchor_ref, pos_ref, slot_ref, used_ref, fits_ref):
    me = me_ref[0]
    f32, i32 = jnp.float32, jnp.int32
    groups, each = 4, 2 * B

    def col(x):
        return jnp.sum(x, axis=1, keepdims=True)

    pairs = pair_ref[...].astype(f32).T
    at = lax.broadcasted_iota(i32, pairs.shape, 1)
    columns = [col(jnp.where(at == k, pairs, 0.0)) for k in range(pairs.shape[1])]
    a = jnp.concatenate(columns[0::2], axis=0).astype(i32)
    b = jnp.concatenate(columns[1::2], axis=0).astype(i32)
    n = a.shape[0]

    before = lax.broadcasted_iota(i32, (128, 128), 0) > lax.broadcasted_iota(i32, (128, 128), 1)
    before = jnp.where(before, 1.0, 0.0).astype(jnp.bfloat16)

    def earlier(width):
        i = lax.broadcasted_iota(i32, (width, width), 0)
        j = lax.broadcasted_iota(i32, (width, width), 1)
        return jnp.where(((i >> 4) == (j >> 4)) & (i < j), 1.0, 0.0)

    def sort_in(hot):
        width = hot.shape[1]
        totals = jnp.sum(hot, axis=0, keepdims=True)
        rows = jnp.broadcast_to(totals, (8, width))
        below = jnp.dot(rows, earlier(width), precision=lax.Precision.HIGHEST, preferred_element_type=f32)[0:1]
        ranks, passed = [], below
        for k in range(0, n, 128):
            part = hot[k : k + 128]
            ahead = jnp.dot(before, part.astype(jnp.bfloat16), preferred_element_type=f32) + passed
            ranks.append(col(ahead * part))
            passed = passed + jnp.sum(part, axis=0, keepdims=True)
        return jnp.concatenate(ranks, axis=0), totals, below

    lane = lax.broadcasted_iota(i32, (n, 128), 1)
    valid = a >= 0
    ga, gb = a >> 7, b >> 7
    low, high = jnp.minimum(ga, gb), jnp.maximum(ga, gb)
    anchor_y = anchor_ref[1:2].astype(f32)
    name = lax.broadcasted_iota(i32, (n, anchor_ref.shape[1]), 1)
    oy = col(jnp.where(name == b, anchor_y, 0.0) - jnp.where(name == a, anchor_y, 0.0)).astype(i32)
    spare = jnp.abs(oy) >> 1
    kinds = lax.broadcasted_iota(i32, (n, 256), 1)
    hot = jnp.where(valid & (kinds == (low * groups + high) * 16 + spare), 1.0, 0.0)
    rank, sums, _ = sort_in(hot)
    sums = sums.astype(i32)
    kind1 = lax.broadcasted_iota(i32, (1, 256), 1) >> 4
    count, up = {}, {}
    for g in range(groups):
        for h in range(g, groups):
            count[g, h] = jnp.sum(jnp.where(kind1 == g * groups + h, sums, 0))
            up[g, h] = (count[g, h] >> 1) if h > g else 0

    def loads():
        load = [0] * groups
        for (g, h), c in count.items():
            load[g] = load[g] + (c - up[g, h])
            load[h] = load[h] + up[g, h]
        return load

    load = loads()
    for g, h in count:
        if h > g:
            up[g, h] = up[g, h] + ((load[g] - load[h] + 2) >> 2)
    load = loads()
    excess = 0
    for g in range(groups - 1):
        excess = excess + load[g] - each
        up[g, g + 1] = up[g, g + 1] + excess
    need = (ROWS * PAIR_DEV - TRIMMED) - 1
    fits = 1
    goes_up, there = jnp.zeros((1, 256), f32), jnp.ones((1, 256), f32)
    for (g, h), c in count.items():
        if h > g:
            u = up[g, h]
            fine = (u >= 0) & (u <= KEEP) & (c - u >= 0) & (c - u <= KEEP)
            fits = jnp.where(fine, fits, 0)
            goes_up = jnp.where(kind1 == g * groups + h, u.astype(f32), goes_up)
            there = jnp.where(kind1 == g * groups + h, jnp.maximum(c, 1).astype(f32), there)

    key1 = lax.broadcasted_iota(i32, (1, 256), 1) & 15
    weight = jnp.where(key1 <= need // 2, 1, 0) + jnp.where(key1 <= need // 2 + 1, 1, 0)
    small = {t: jnp.sum(jnp.where(kind1 == t[0] * groups + t[1], sums * weight, 0)).astype(f32) for t in count}
    share = goes_up / there
    surplus = jnp.zeros((1, 256), f32)
    for g in range(groups):
        held = jnp.zeros((1, 256), f32)
        for (low_g, high_g), amount in small.items():
            if low_g == high_g:
                held = held + (amount if low_g == g else 0.0)
            elif g in (low_g, high_g):
                part = jnp.sum(jnp.where((kind1 == low_g * groups + high_g) & (key1 == 0), share, 0.0))
                held = held + amount * (part if high_g == g else 1.0 - part)
        surplus = surplus + jnp.where((kind1 >> 2) == g, held, 0.0) - jnp.where((kind1 & 3) == g, held, 0.0)
    bend = surplus / (2.0 * jnp.maximum(goes_up, 1.0))
    most = jnp.minimum(there / jnp.maximum(goes_up, 1.0) - 1.0, 1.0)
    bend = jnp.clip(bend, -0.98 * most, 0.98 * most)
    u, c, bend = col(hot * goes_up), jnp.maximum(col(hot * there), 1.0), col(hot * bend)

    def risen_at(r):
        x = r / c
        return jnp.where(r >= c, u, jnp.clip(jnp.floor(u * (x + bend * x * (1.0 - x)) + 0.5 / c), 0.0, u))

    risen = risen_at(rank)
    rises = risen_at(rank + 1.0) > risen
    group = jnp.where(rises, high, low)
    source = low + high - group
    crosses = valid & (low != high)
    hot = jnp.where(valid & (lane == group * 16 + spare), 1.0, 0.0)
    order, keyed, below = sort_in(hot)
    order = order.astype(i32)
    second = order >= B
    q = jnp.where(second, B + each - 1 - order, order)
    lane1 = lax.broadcasted_iota(i32, (1, 128), 1)
    match = 1
    for g in range(groups):
        fits = jnp.where(jnp.sum(jnp.where((lane1 >> 4) == g, keyed, 0.0)) == each, fits, 0)
        for j in range(need // 2 + 1):
            both = (lane1 == g * 16 + j + 1) | (lane1 == g * 16 + need - j + 1)
            match = jnp.where(jnp.sum(jnp.where(both, below, 0.0)) <= each, match, 0)
    fits_ref[0] = fits * match

    put = (((group - source) & 3) - 1) * KEEP + jnp.where(rises, risen, rank - risen).astype(i32)
    near_b = ga != group
    near = jnp.where(near_b, b, a) & 127
    far = jnp.where(near_b, a, b) & 127
    table = jnp.where(crosses, 128 + put, far)
    moved = jnp.where(second, spare, 0)
    from_a = jnp.where(oy > 0, spare, 0) - moved
    from_b = jnp.where(oy < 0, spare, 0) - moved
    near_from, far_from = jnp.where(near_b, from_b, from_a), jnp.where(near_b, from_a, from_b)

    def side(*columns):
        at = lax.broadcasted_iota(i32, (n, 8), 1)
        out = jnp.zeros((n, 8), f32)
        for k, column in enumerate(columns):
            out = jnp.where(at == k, column.astype(f32), out)
        return out.astype(jnp.bfloat16)

    def spread(columns, mask):
        hot = jnp.where(mask, 1.0, 0.0).astype(jnp.bfloat16)
        out = lax.dot_general(columns, hot, (((0,), (0,)), ((), ())), preferred_element_type=f32)
        return out.astype(i32)

    mine = valid & (group == me)
    flag = jnp.where(near_b, 1, 0)
    columns = side(near, table & 255, a & 255, b & 255, flag, table >> 8, a >> 8, b >> 8)
    here = mine & (lane == q)
    got = spread(columns, here)
    more = spread(side(near_from + 16, far_from + 16, spare), here)
    pos_ref[...] = got
    pos_ref[1:4] = got[1:4] + 256 * got[5:8]
    pos_ref[6:7] = pos_ref[1:2]
    pos_ref[0:1] = got[0:1] * ROWS + more[0:1] - 16
    pos_ref[1:2] = pos_ref[6:7] * ROWS + more[1:2] - 16
    pos_ref[5:6] = more[2:3]
    wide = lax.broadcasted_iota(i32, (n, slot_ref.shape[1]), 1)
    here = wide == put
    zero = jnp.zeros_like(a)
    slots = spread(side(far, zero, zero + 1, far_from + 16), crosses & (source == me) & here)
    used_ref[...] = spread(side(q & (B - 1), q >> 6, spare), crosses & mine & here)
    slot_ref[...] = slots
    slot_ref[3:4] = slots[0:1] * ROWS + slots[3:4] - 16


def route(me, pair_slots, anchors):
    lists = jnp.transpose(pair_slots, (1, 2, 0)).reshape(-1, pair_slots.shape[0])
    width = 128 * -(-(3 * KEEP) // 128)
    vmem, smem = pl.BlockSpec(memory_space=pltpu.VMEM), pl.BlockSpec(memory_space=pltpu.SMEM)
    return pl.pallas_call(
        route_kernel,
        out_shape=[
            jax.ShapeDtypeStruct((8, 128), jnp.int32),
            jax.ShapeDtypeStruct((8, width), jnp.int32),
            jax.ShapeDtypeStruct((8, width), jnp.int32),
            jax.ShapeDtypeStruct((1,), jnp.int32),
        ],
        in_specs=[smem, vmem, vmem],
        out_specs=[vmem, vmem, vmem, smem],
        compiler_params=pltpu.CompilerParams(vmem_limit_bytes=40 << 20),
        cost_estimate=pl.CostEstimate(flops=10_000_000, bytes_accessed=1_000_000, transcendentals=0),
        name="route",
    )(me, lists, jnp.transpose(anchors))


def flat(ref):
    return ref.reshape(ref.shape[0] * ROWS, 128)


def fetch_kernel(row_of, idx_ref, table_ref, *refs):
    *outs, table, sem = refs
    copy = pltpu.make_async_copy(table_ref, table, sem)
    copy.start()
    copy.wait()
    for k, out_ref in enumerate(outs):
        count = out_ref.shape[0]

        def move(i, carry, out_ref=out_ref, k=k, count=count):
            out_ref[i] = row_of(idx_ref, table, k * count + i)
            return carry

        lax.fori_loop(0, count, move, 0, unroll=4)


def fetch(idx, table, row_of, name):
    return pl.pallas_call(
        functools.partial(fetch_kernel, row_of),
        out_shape=[jax.ShapeDtypeStruct((KEEP, ROWS, 128), jnp.float32)] * 3,
        in_specs=[pl.BlockSpec(memory_space=pltpu.SMEM), pl.BlockSpec(memory_space=pl.ANY)],
        out_specs=[pl.BlockSpec(memory_space=pltpu.VMEM)] * 3,
        scratch_shapes=[pltpu.VMEM(table.shape, jnp.float32), pltpu.SemaphoreType.DMA],
        compiler_params=pltpu.CompilerParams(vmem_limit_bytes=16 << 20),
        cost_estimate=pl.CostEstimate(flops=0, bytes_accessed=8_000_000, transcendentals=0),
        name=name,
    )(idx, table)


def sent_row(idx_ref, table, i):
    return table[idx_ref[0, i]]


def line_no():
    return lax.broadcasted_iota(jnp.int32, (ROWS, 128), 0)


def its_lines(s, spare, lines):
    keep = line_no() >= spare if s else line_no() < ROWS - spare
    return jnp.where(keep, lines, 0.0)


def deal_owner(pos_ref, row, p, table, out_ref, at):
    first, second = [table[pl.ds(pos_ref[row, s * B + p] + ROWS, ROWS)] for s in range(PAIR_DEV)]
    lines = out_ref.shape[1]
    cut = lines - ROWS
    out_ref[at, :cut] = first[:cut]
    if cut < ROWS:
        shared = lax.broadcasted_iota(jnp.int32, (ROWS - cut, 128), 0) + cut < ROWS - pos_ref[5, p]
        out_ref[at, cut:ROWS] = jnp.where(shared, first[cut:], second[: ROWS - cut])
    out_ref[at, ROWS:] = second[ROWS - cut :]


def clear_ends(table):
    zero = jnp.zeros((ROWS, 128), jnp.float32)
    table[0] = zero
    table[table.shape[0] - 1] = zero


PARTS = 4


def deal_near_kernel(pos_ref, orb_ref, near_ref, table, stage, near, sem_in, sem_out):
    pulls = [
        pltpu.make_async_copy(orb_ref.at[:, pl.ds(k * 1024, 1024)], stage.at[k], sem_in.at[k]) for k in range(PARTS)
    ]
    for copy in pulls:
        copy.start()
    clear_ends(table)
    for k, copy in enumerate(pulls):
        copy.wait()

        def lay_out(i, carry, k=k):
            rows = pl.ds(pl.multiple_of(i * 8, 8), 8)
            lines = [stage[k, rows, j * 128 : (j + 1) * 128] for j in range(8)]
            table[pl.ds(i * 8 + 1, 8), k * 8 : k * 8 + 8] = jnp.swapaxes(jnp.stack(lines), 0, 1)
            return carry

        lax.fori_loop(0, 128 // 8, lay_out, 0, unroll=2)
    pushes = []
    for k in range(PARTS):

        def owner(p, carry):
            deal_owner(pos_ref, 0, p, flat(table), near, p)
            return carry

        mine = pl.ds(k * (B // PARTS), B // PARTS)
        lax.fori_loop(k * (B // PARTS), (k + 1) * (B // PARTS), owner, 0, unroll=4)
        pushes.append(pltpu.make_async_copy(near.at[mine], near_ref.at[mine], sem_out.at[k]))
        pushes[-1].start()
    for copy in pushes:
        copy.wait()


def deal_near(lines, pos, orbitals):
    anywhere = pl.BlockSpec(memory_space=pl.ANY)
    dma = pltpu.SemaphoreType.DMA((PARTS,))
    return pl.pallas_call(
        deal_near_kernel,
        out_shape=jax.ShapeDtypeStruct((B, lines, 128), jnp.float32),
        in_specs=[pl.BlockSpec(memory_space=pltpu.SMEM), anywhere],
        out_specs=anywhere,
        scratch_shapes=[
            pltpu.VMEM((130, ROWS, 128), jnp.float32),
            pltpu.VMEM((PARTS, 128, 1024), jnp.float32),
            pltpu.VMEM((B, lines, 128), jnp.float32),
            dma,
            dma,
        ],
        compiler_params=pltpu.CompilerParams(vmem_limit_bytes=60 << 20),
        cost_estimate=pl.CostEstimate(flops=2_000_000, bytes_accessed=10_000_000, transcendentals=0),
        name="deal_near",
    )(pos, orbitals)


def deal_far_kernel(row, pos_ref, *refs):
    *parts, far_ref, table, sem = refs
    copies, end = [], 1
    for k, part in enumerate(parts):
        copies.append(pltpu.make_async_copy(part, table.at[pl.ds(end, part.shape[0])], sem.at[k]))
        end += part.shape[0]
    for copy in copies:
        copy.start()
    clear_ends(table)
    for copy in copies:
        copy.wait()

    def owner(p, carry):
        deal_owner(pos_ref, row, p, flat(table), far_ref, p)
        return carry

    lax.fori_loop(0, B, owner, 0, unroll=4)


def deal_far(lines, row, pos, parts):
    rows = sum(x.shape[0] for x in parts)
    return pl.pallas_call(
        functools.partial(deal_far_kernel, row),
        out_shape=jax.ShapeDtypeStruct((B, lines, 128), jnp.float32),
        in_specs=[pl.BlockSpec(memory_space=pltpu.SMEM)] + [pl.BlockSpec(memory_space=pl.ANY)] * len(parts),
        out_specs=pl.BlockSpec(memory_space=pltpu.VMEM),
        scratch_shapes=[pltpu.VMEM((rows + 2, ROWS, 128), jnp.float32), pltpu.SemaphoreType.DMA((len(parts),))],
        compiler_params=pltpu.CompilerParams(vmem_limit_bytes=32 << 20),
        cost_estimate=pl.CostEstimate(flops=0, bytes_accessed=12_000_000, transcendentals=0),
        name="deal_far",
    )(pos, *parts)


def solve_pair(offset, from_a, from_b, box_a, box_b, term_a, term_b, part, dens, resid, second, third, image):
    ox, oy, oz = offset
    shape = (ROWS, 128)
    line = lax.broadcasted_iota(jnp.int32, shape, 0)
    lane = lax.broadcasted_iota(jnp.int32, shape, 1)
    cy = 2 * line + (lane >> 6)
    cz = lane & (B - 1)
    high = lane >= B
    ends = (high & (line == 0)) | (~high & (line == ROWS - 1))
    no_up, no_down = cz == B - 1, cz == 0

    def plane(ref, x):
        return ref[pl.ds(pl.multiple_of(x * ROWS, ROWS), ROWS)]

    def put(ref, x, value):
        ref[pl.ds(pl.multiple_of(x * ROWS, ROWS), ROWS)] = value

    def shifter(sy, sz):
        flat = sy * B + sz
        lines, steps = flat >> 7, flat & 127
        inside = (cy >= sy) & (cy < B + sy) & (cz >= sz) & (cz < B + sz)
        keep = lane < 128 - steps

        def shift(ref, x, first):
            at = x * ROWS - lines - first
            moved = jnp.where(keep, ref[pl.ds(at, ROWS)], ref[pl.ds(at - 1, ROWS)])
            return jnp.where(inside, pltpu.roll(moved, steps, axis=1), 0.0)

        return shift

    def apply(ref, x):
        here = plane(ref, x + 1)
        at = (x + 1) * ROWS
        other = jnp.where(high, ref[pl.ds(at - 1, ROWS)], ref[pl.ds(at + 1, ROWS)])
        other = here + jnp.where(ends, 0.0, other)
        beside = plane(ref, x) + plane(ref, x + 2) + pltpu.roll(other, B, axis=1)
        upper = jnp.where(no_up, 0.0, pltpu.roll(here, 127, axis=1))
        lower = jnp.where(no_down, 0.0, pltpu.roll(here, 1, axis=1))
        return here, 6.0 * here - beside - upper - lower

    zero = jnp.zeros(shape, jnp.float32)
    for ref in (dens, second, third):
        put(ref, 0, zero)
        put(ref, B + 1, zero)

    shift_on = shifter(oy, oz)
    shift_back = shifter(-oy, -oz)

    def begin(x, acc):
        src = x - ox
        inside = jnp.where((src >= 0) & (src < B), 1.0, 0.0)
        moved = shift_on(box_b, jnp.clip(src, 0, B - 1) + 1, from_b) * inside
        density = box_a[pl.ds((x + 1) * ROWS - from_a, ROWS)] * moved
        put(part, x, moved)
        put(dens, x + 1, density)
        return acc + density * density

    def first(x, acc):
        here, img = apply(dens, x)
        put(image, x + 1, img)
        return acc + here * img

    norm0 = yield begin
    step0 = norm0 / (yield first)

    def rest0(x, acc):
        left = plane(dens, x + 1) - step0 * plane(image, x + 1)
        put(resid, x, left)
        return acc + left * left

    norm1 = yield rest0
    ratio0 = norm1 / norm0

    def turn1(x, acc):
        put(second, x + 1, plane(resid, x) + ratio0 * plane(dens, x + 1))
        return acc

    def again(x, acc):
        here, img = apply(second, x)
        put(image, x + 1, img)
        return acc + here * img

    yield turn1
    step1 = norm1 / (yield again)

    def rest1(x, acc):
        left = plane(resid, x) - step1 * plane(image, x + 1)
        put(resid, x, left)
        return acc + left * left

    norm2 = yield rest1
    ratio1 = norm2 / norm1

    def turn2(x, acc):
        put(third, x + 1, plane(resid, x) + ratio1 * plane(second, x + 1))
        return acc

    def last(x, acc):
        here, img = apply(third, x)
        return acc + here * img

    yield turn2
    step2 = norm2 / (yield last)

    def finish(x, acc):
        potential = step0 * plane(dens, x + 1) + step1 * plane(second, x + 1) + step2 * plane(third, x + 1)
        here = pl.ds((x + 1) * ROWS - from_a, ROWS)
        term_a[here] = potential * plane(part, x)
        put(image, x + 1, potential * box_a[here])
        return acc

    def back(x, acc):
        src = x + ox
        inside = jnp.where((src >= 0) & (src < B), 1.0, 0.0)
        term_b[pl.ds((x + 1) * ROWS - from_b, ROWS)] = shift_back(image, jnp.clip(src, 0, B - 1) + 1, 0) * inside
        return acc

    yield finish
    yield back


def run_together(solvers, unroll):
    steps = [next(solver) for solver in solvers]
    zero = jnp.zeros((ROWS, 128), jnp.float32)
    while True:
        def both(x, accs, steps=tuple(steps)):
            return tuple(step(x, acc) for step, acc in zip(steps, accs))

        accs = lax.fori_loop(0, B, both, (zero,) * len(steps), unroll=unroll)
        sums = [jnp.sum(acc, keepdims=True) for acc in accs]
        try:
            steps = [solver.send(value) for solver, value in zip(solvers, sums)]
        except StopIteration:
            return


def pair_kernel(place_ref, pos_ref, anchor_ref, near_ref, far_ref, near_out, far_out, boxes, terms, *rest):
    *fields, sem = rest
    lines = near_ref.shape[1]
    cut = lines - ROWS
    at = [s * B + place_ref[0] for s in range(PAIR_DEV)]
    flags = [pos_ref[4, k] for k in at]
    copies = []
    for s in range(PAIR_DEV):
        for k, ref in enumerate((near_ref, far_ref)):
            which = 1 - flags[s] if k else flags[s]
            source = ref.at[:, pl.ds(s * cut, ROWS)]
            copies.append(pltpu.make_async_copy(source, boxes.at[s, which, pl.ds(1, B)], sem.at[s, k]))
    for copy in copies:
        copy.start()
    for s in range(PAIR_DEV):
        for k in range(2):
            clear_ends(boxes.at[s, k])
    for copy in copies:
        copy.wait()
    solvers = []
    for s in range(PAIR_DEV):
        orb_a, orb_b = pos_ref[2, at[s]], pos_ref[3, at[s]]
        offset = [anchor_ref[3 * orb_b + k] - anchor_ref[3 * orb_a + k] for k in range(3)]
        spare = pos_ref[5, at[s]]
        moved = spare if s else 0
        from_a = jnp.where(offset[1] > 0, spare, 0) - moved
        from_b = jnp.where(offset[1] < 0, spare, 0) - moved
        refs = [flat(ref.at[s, k]) for ref in (boxes, terms) for k in range(2)]
        solvers.append(solve_pair(offset, from_a, from_b, *refs, *[ref.at[s] for ref in fields]))
    run_together(solvers, UNROLL if cut < ROWS else 1)

    def together(x, carry):
        for k, out in enumerate((near_out, far_out)):
            first, second = [terms[s, 1 - flags[s] if k else flags[s], x + 1] for s in range(PAIR_DEV)]
            out[x, :cut] = first[:cut]
            if cut < ROWS:
                low = its_lines(0, pos_ref[5, at[0]], first)[cut:]
                out[x, cut:ROWS] = low + its_lines(1, pos_ref[5, at[1]], second)[: ROWS - cut]
            out[x, ROWS:] = second[ROWS - cut :]
        return carry

    lax.fori_loop(0, B, together, 0, unroll=4)


def solve(place, pos, anchors, near, far):
    smem, vmem = pl.BlockSpec(memory_space=pltpu.SMEM), pl.BlockSpec(memory_space=pltpu.VMEM)
    anywhere = pl.BlockSpec(memory_space=pl.ANY)
    field = pltpu.VMEM((PAIR_DEV, B * ROWS, 128), jnp.float32)
    padded = pltpu.VMEM((PAIR_DEV, (B + 2) * ROWS, 128), jnp.float32)
    boxes = pltpu.VMEM((PAIR_DEV, 2, B + 2, ROWS, 128), jnp.float32)
    return pl.pallas_call(
        pair_kernel,
        out_shape=[jax.ShapeDtypeStruct(near.shape, jnp.float32)] * 2,
        in_specs=[smem, smem, smem, anywhere, anywhere],
        out_specs=[vmem, vmem],
        scratch_shapes=[
            boxes, boxes, field, padded, field, padded, padded, padded,
            pltpu.SemaphoreType.DMA((PAIR_DEV, 2)),
        ],
        compiler_params=pltpu.CompilerParams(vmem_limit_bytes=40 << 20),
        cost_estimate=pl.CostEstimate(flops=100_000_000, bytes_accessed=30_000_000, transcendentals=0),
        name="solve",
    )(place, pos, anchors, near, far)


def add_lines(total, line, lines):
    here = pl.ds(line + ROWS, ROWS)
    total[here] = total[here] + lines


def add_far_kernel(pos_ref, slot_ref, terms_ref, *refs):
    *from_groups, out_ref = refs
    out_ref[...] = jnp.zeros(out_ref.shape, jnp.float32)
    total = flat(out_ref)
    cut = terms_ref.shape[1] - ROWS

    def here(p, carry):
        for s in range(PAIR_DEV):
            q = s * B + p

            @pl.when(pos_ref[6, q] < 128)
            def _(q=q, s=s):
                lines = terms_ref[p, s * cut : s * cut + ROWS]
                add_lines(total, pos_ref[1, q], its_lines(s, pos_ref[5, q], lines))

        return carry

    lax.fori_loop(0, B, here, 0)

    def there(k, carry):
        for d, ref in enumerate(from_groups):
            at = d * KEEP + k

            @pl.when(slot_ref[2, at] == 1)
            def _(at=at, ref=ref):
                add_lines(total, slot_ref[3, at], ref[k])

        return carry

    lax.fori_loop(0, KEEP, there, 0)


def add_far(pos, slot, terms, from_groups):
    smem, vmem = pl.BlockSpec(memory_space=pltpu.SMEM), pl.BlockSpec(memory_space=pltpu.VMEM)
    return pl.pallas_call(
        add_far_kernel,
        out_shape=jax.ShapeDtypeStruct((130, ROWS, 128), jnp.float32),
        in_specs=[smem, smem] + [vmem] * 4,
        out_specs=vmem,
        compiler_params=pltpu.CompilerParams(vmem_limit_bytes=24 << 20),
        cost_estimate=pl.CostEstimate(flops=2_000_000, bytes_accessed=10_000_000, transcendentals=0),
        name="add_far",
    )(pos, slot, terms, *from_groups)


def add_near_kernel(pos_ref, sum_ref, terms_ref, out_ref, acc, terms, stage, sem_sum, sem_in, sem_out):
    cut = terms.shape[1] - ROWS
    copies = [pltpu.make_async_copy(sum_ref, acc, sem_sum)]
    for k in range(PARTS):
        mine = pl.ds(k * (B // PARTS), B // PARTS)
        copies.append(pltpu.make_async_copy(terms_ref.at[mine], terms.at[mine], sem_in.at[k]))
    for copy in copies:
        copy.start()
    copies[0].wait()
    for k in range(PARTS):
        copies[k + 1].wait()

        def here(p, carry):
            for s in range(PAIR_DEV):
                q = s * B + p
                lines = terms[p, s * cut : s * cut + ROWS]
                add_lines(flat(acc), pos_ref[0, q], its_lines(s, pos_ref[5, q], lines))
            return carry

        lax.fori_loop(k * (B // PARTS), (k + 1) * (B // PARTS), here, 0, unroll=2)
    pushes = []
    for k in range(PARTS):

        def lay_out(i, carry, k=k):
            rows = pl.ds(pl.multiple_of(i * 8, 8), 8)
            lines = jnp.swapaxes(acc[pl.ds(i * 8 + 1, 8), k * 8 : k * 8 + 8], 0, 1)
            for j in range(8):
                stage[k, rows, j * 128 : (j + 1) * 128] = lines[j]
            return carry

        lax.fori_loop(0, 128 // 8, lay_out, 0, unroll=2)
        pushes.append(pltpu.make_async_copy(stage.at[k], out_ref.at[:, pl.ds(k * 1024, 1024)], sem_out.at[k]))
        pushes[-1].start()
    for copy in pushes:
        copy.wait()


def add_near(pos, summed, terms):
    anywhere = pl.BlockSpec(memory_space=pl.ANY)
    dma = pltpu.SemaphoreType.DMA((PARTS,))
    return pl.pallas_call(
        add_near_kernel,
        out_shape=jax.ShapeDtypeStruct((128, ROWS * 128), jnp.float32),
        in_specs=[pl.BlockSpec(memory_space=pltpu.SMEM), anywhere, anywhere],
        out_specs=anywhere,
        scratch_shapes=[
            pltpu.VMEM((130, ROWS, 128), jnp.float32),
            pltpu.VMEM(terms.shape, jnp.float32),
            pltpu.VMEM((PARTS, 128, 1024), jnp.float32),
            pltpu.SemaphoreType.DMA,
            dma,
            dma,
        ],
        compiler_params=pltpu.CompilerParams(vmem_limit_bytes=60 << 20),
        cost_estimate=pl.CostEstimate(flops=2_000_000, bytes_accessed=10_000_000, transcendentals=0),
        name="add_near",
    )(pos, summed, terms)


def turned(x, shift):
    groups = lax.axis_size("grp")
    return lax.ppermute(x, "grp", [(g, (g + shift) % groups) for g in range(groups)])


def exchanged(planes):
    return lax.all_to_all(planes, "grid", 0, 0, tiled=True)


def fitting(orbitals, anchors, place, pos, slot, used):
    def used_row(used_ref, table, i):
        p, s, spare = used_ref[0, i], used_ref[1, i], used_ref[2, i]
        plane = table[p, pl.ds(pl.multiple_of(s * (TRIMMED - ROWS), 8), ROWS)]
        keep = (line_no() >= s * spare) & (line_no() < ROWS - (1 - s) * spare)
        return jnp.where(keep, plane, 0.0)

    near = exchanged(deal_near(TRIMMED, pos, orbitals))
    local = orbitals.reshape(128, ROWS, 128)
    arrived = [turned(x, d) for d, x in enumerate(fetch(slot, local, sent_row, "send"), 1)]
    far = exchanged(deal_far(TRIMMED, 1, pos, [local] + arrived))
    near_terms, far_terms = solve(place, pos, anchors.reshape(-1), near, far)
    far_terms = exchanged(far_terms)
    from_groups = [turned(x, -d) for d, x in enumerate(fetch(used, far_terms, used_row, "back"), 1)]
    near_terms = exchanged(near_terms)
    return add_near(pos, add_far(pos, slot, far_terms, from_groups), near_terms)


def add_all_kernel(pos_ref, terms_ref, out_ref):
    out_ref[...] = jnp.zeros(out_ref.shape, jnp.float32)
    total = flat(out_ref)

    def here(p, carry):
        for s in range(PAIR_DEV):
            for k in range(2):
                at = (k * PAIR_DEV + s) * ROWS
                add_lines(total, pos_ref[k, s * B + p], terms_ref[p, at : at + ROWS])
        return carry

    lax.fori_loop(0, B, here, 0)


def add_all(pos, terms, count):
    return pl.pallas_call(
        add_all_kernel,
        out_shape=jax.ShapeDtypeStruct((count + 2, ROWS, 128), jnp.float32),
        in_specs=[pl.BlockSpec(memory_space=pltpu.SMEM), pl.BlockSpec(memory_space=pltpu.VMEM)],
        out_specs=pl.BlockSpec(memory_space=pltpu.VMEM),
        compiler_params=pltpu.CompilerParams(vmem_limit_bytes=32 << 20),
        cost_estimate=pl.CostEstimate(flops=2_000_000, bytes_accessed=10_000_000, transcendentals=0),
        name="add_all",
    )(pos, terms)


def general(orbitals, anchors, pair_slots, place):
    groups, grid_count = lax.axis_size("grp"), lax.axis_size("grid")
    me, rows = lax.axis_index("grp"), orbitals.shape[0]
    dealt = deal_evenly(pair_slots, groups * grid_count, PAIR_DEV)
    own = lax.dynamic_slice_in_dim(dealt, me * grid_count, grid_count, 0)
    own = jnp.maximum(jnp.transpose(own, (2, 1, 0)).reshape(2, PAIR_DEV * grid_count), 0)
    pos = jnp.concatenate([own * ROWS, own, jnp.zeros((4, own.shape[1]), jnp.int32)])
    round_trip = [turned(orbitals, d) for d in (3, 2, 1)] + [orbitals]
    pieces = lax.dynamic_slice_in_dim(jnp.concatenate(round_trip * 2), (3 - me) * rows, groups * rows, 0)
    table = pieces.reshape(-1, ROWS, 128)
    lines = PAIR_DEV * ROWS
    both = jnp.concatenate([deal_far(lines, k, pos, [table]) for k in range(2)], axis=1)

    def solve_both(both):
        return jnp.concatenate(solve(place, pos, anchors.reshape(-1), both[:, :lines], both[:, lines:]), axis=1)

    def there_and_back(step, both):
        return lax.cond(step == 0, solve_both, lambda x: x, exchanged(both))

    summed = add_all(pos, lax.fori_loop(0, 2, there_and_back, both), table.shape[0])
    blocks = [lax.dynamic_slice_in_dim(summed, ((me + d) & 3) * rows + 1, rows, 0) for d in range(4)]
    return (blocks[0] + sum(turned(blocks[d], d) for d in (1, 2, 3))).reshape(orbitals.shape)


def body(orbitals, anchors, pair_slots):
    me = lax.axis_index("grp").astype(jnp.int32)[None]
    place = lax.axis_index("grid").astype(jnp.int32)[None]
    pos, slot, used, fits = route(me, pair_slots, anchors)
    return lax.cond(
        fits[0] == 1,
        lambda: fitting(orbitals, anchors, place, pos, slot, used),
        lambda: general(orbitals, anchors, pair_slots, place),
    )


def solution(mesh):
    return jax.shard_map(
        body,
        mesh=mesh,
        in_specs=(P("grp", "grid"), P(), P()),
        out_specs=P("grp", "grid"),
        check_vma=False,
    )
```

```python
import functools

import jax
import jax.numpy as jnp
from jax import lax
from jax.experimental import pallas as pl
from jax.experimental.pallas import tpu as pltpu
from jax.sharding import PartitionSpec as P

B = 64
PAIR_DEV = 2
ITERS = 3
ROWS = B * B // 128
KEEP = 48
UNROLL = 16
TRIMMED = 56


def deal_evenly(pair_slots, owner_count, each_owner):
    flat_slots = pair_slots.reshape(-1, 2)
    filled = (flat_slots[:, 0] >= 0).astype(jnp.int32)
    order = jnp.arange(flat_slots.shape[0], dtype=jnp.int32)
    position = jnp.sum(jnp.where(order[None, :] < order[:, None], filled[None, :], 0), axis=1)
    wanted = lax.broadcasted_iota(jnp.int32, (owner_count, each_owner), 1) * owner_count
    wanted = (wanted + lax.broadcasted_iota(jnp.int32, (owner_count, each_owner), 0)).reshape(-1)
    matched = (position[None, :] == wanted[:, None]) & (filled[None, :] == 1)
    picked = jnp.dot(matched.astype(jnp.int32), flat_slots)
    return picked.reshape(owner_count, each_owner, 2)


def route_kernel(me_ref, pair_ref, anchor_ref, pos_ref, slot_ref, used_ref, mode_ref):
    me = me_ref[0]
    f32, i32 = jnp.float32, jnp.int32
    groups, each = 4, 2 * B

    def col(x):
        return jnp.sum(x, axis=1, keepdims=True)

    pairs = pair_ref[...].astype(f32).T
    at = lax.broadcasted_iota(i32, pairs.shape, 1)
    columns = [col(jnp.where(at == k, pairs, 0.0)) for k in range(pairs.shape[1])]
    a = jnp.concatenate(columns[0::2], axis=0).astype(i32)
    b = jnp.concatenate(columns[1::2], axis=0).astype(i32)
    n = a.shape[0]

    before = lax.broadcasted_iota(i32, (128, 128), 0) > lax.broadcasted_iota(i32, (128, 128), 1)
    before = jnp.where(before, 1.0, 0.0).astype(jnp.bfloat16)

    def sort_in(hot):
        width = hot.shape[1]
        totals = jnp.sum(hot, axis=0, keepdims=True)
        key = lax.broadcasted_iota(i32, (8, width), 1) & 15
        running = jnp.broadcast_to(totals, (8, width))
        for step in (1, 2, 4, 8):
            running = running + jnp.where(key >= step, pltpu.roll(running, step, axis=1), 0.0)
        below = running[0:1] - totals
        ranks, passed = [], below
        for k in range(0, n, 128):
            part = hot[k : k + 128]
            ahead = jnp.dot(before, part.astype(jnp.bfloat16), preferred_element_type=f32) + passed
            ranks.append(col(ahead * part))
            passed = passed + jnp.sum(part, axis=0, keepdims=True)
        return jnp.concatenate(ranks, axis=0), totals, below

    lane = lax.broadcasted_iota(i32, (n, 128), 1)
    valid = a >= 0
    ga, gb = a >> 7, b >> 7
    low, high = jnp.minimum(ga, gb), jnp.maximum(ga, gb)
    anchor_y = anchor_ref[1:2].astype(f32)
    name = lax.broadcasted_iota(i32, (n, anchor_ref.shape[1]), 1)
    oy = col(jnp.where(name == b, anchor_y, 0.0) - jnp.where(name == a, anchor_y, 0.0)).astype(i32)
    spare = jnp.abs(oy) >> 1
    kinds = lax.broadcasted_iota(i32, (n, 256), 1)
    hot = jnp.where(valid & (kinds == (low * groups + high) * 16 + spare), 1.0, 0.0)
    rank, sums, _ = sort_in(hot)
    sums = sums.astype(i32)
    kind1 = lax.broadcasted_iota(i32, (1, 256), 1) >> 4
    count, up = {}, {}
    for g in range(groups):
        for h in range(g, groups):
            count[g, h] = jnp.sum(jnp.where(kind1 == g * groups + h, sums, 0))
            up[g, h] = (count[g, h] >> 1) if h > g else 0

    def loads():
        load = [0] * groups
        for (g, h), c in count.items():
            load[g] = load[g] + (c - up[g, h])
            load[h] = load[h] + up[g, h]
        return load

    load = loads()
    for g, h in count:
        if h > g:
            up[g, h] = up[g, h] + ((load[g] - load[h] + 2) >> 2)
    load = loads()
    excess = 0
    for g in range(groups - 1):
        excess = excess + load[g] - each
        up[g, g + 1] = up[g, g + 1] + excess
    need = (ROWS * PAIR_DEV - TRIMMED) - 1
    fits = 1
    goes_up, there = jnp.zeros((1, 256), f32), jnp.ones((1, 256), f32)
    for (g, h), c in count.items():
        if h > g:
            u = up[g, h]
            fine = (u >= 0) & (u <= KEEP) & (c - u >= 0) & (c - u <= KEEP)
            fits = jnp.where(fine, fits, 0)
            goes_up = jnp.where(kind1 == g * groups + h, u.astype(f32), goes_up)
            there = jnp.where(kind1 == g * groups + h, jnp.maximum(c, 1).astype(f32), there)

    key1 = lax.broadcasted_iota(i32, (1, 256), 1) & 15
    weight = jnp.where(key1 <= need // 2, 1, 0) + jnp.where(key1 <= need // 2 + 1, 1, 0)
    small = {t: jnp.sum(jnp.where(kind1 == t[0] * groups + t[1], sums * weight, 0)).astype(f32) for t in count}
    share = goes_up / there
    surplus = jnp.zeros((1, 256), f32)
    for g in range(groups):
        held = jnp.zeros((1, 256), f32)
        for (low_g, high_g), amount in small.items():
            if low_g == high_g:
                held = held + (amount if low_g == g else 0.0)
            elif g in (low_g, high_g):
                part = jnp.sum(jnp.where((kind1 == low_g * groups + high_g) & (key1 == 0), share, 0.0))
                held = held + amount * (part if high_g == g else 1.0 - part)
        surplus = surplus + jnp.where((kind1 >> 2) == g, held, 0.0) - jnp.where((kind1 & 3) == g, held, 0.0)
    bend = surplus / (2.0 * jnp.maximum(goes_up, 1.0))
    most = jnp.minimum(there / jnp.maximum(goes_up, 1.0) - 1.0, 1.0)
    bend = jnp.clip(bend, -0.98 * most, 0.98 * most)
    u, c, bend = col(hot * goes_up), jnp.maximum(col(hot * there), 1.0), col(hot * bend)

    def risen_at(r):
        x = r / c
        return jnp.where(r >= c, u, jnp.clip(jnp.floor(u * (x + bend * x * (1.0 - x)) + 0.5 / c), 0.0, u))

    risen = risen_at(rank)
    rises = risen_at(rank + 1.0) > risen
    group = jnp.where(rises, high, low)
    source = low + high - group
    crosses = valid & (low != high)
    hot = jnp.where(valid & (lane == group * 16 + spare), 1.0, 0.0)
    order, keyed, below = sort_in(hot)
    order = order.astype(i32)
    second = order >= B
    q = jnp.where(second, B + each - 1 - order, order)
    lane1 = lax.broadcasted_iota(i32, (1, 128), 1)
    match = 1
    for g in range(groups):
        fits = jnp.where(jnp.sum(jnp.where((lane1 >> 4) == g, keyed, 0.0)) == each, fits, 0)
        for j in range(need // 2 + 1):
            both = (lane1 == g * 16 + j + 1) | (lane1 == g * 16 + need - j + 1)
            match = jnp.where(jnp.sum(jnp.where(both, below, 0.0)) <= each, match, 0)
    mode_ref[0] = jnp.where(fits == 1, 1 - match, 2)

    put = (((group - source) & 3) - 1) * KEEP + jnp.where(rises, risen, rank - risen).astype(i32)
    near_b = ga != group
    near = jnp.where(near_b, b, a) & 127
    far = jnp.where(near_b, a, b) & 127
    table = jnp.where(crosses, 128 + put, far)
    spare = spare * match
    moved = jnp.where(second, spare, 0)
    from_a = jnp.where(oy > 0, spare, 0) - moved
    from_b = jnp.where(oy < 0, spare, 0) - moved
    near_from, far_from = jnp.where(near_b, from_b, from_a), jnp.where(near_b, from_a, from_b)

    def side(*columns):
        at = lax.broadcasted_iota(i32, (n, 8), 1)
        out = jnp.zeros((n, 8), f32)
        for k, column in enumerate(columns):
            out = jnp.where(at == k, column.astype(f32), out)
        return out.astype(jnp.bfloat16)

    def spread(columns, mask):
        hot = jnp.where(mask, 1.0, 0.0).astype(jnp.bfloat16)
        out = lax.dot_general(columns, hot, (((0,), (0,)), ((), ())), preferred_element_type=f32)
        return out.astype(i32)

    mine = valid & (group == me)
    flag = jnp.where(near_b, 1, 0)
    columns = side(near, table & 255, a & 255, b & 255, flag, table >> 8, a >> 8, b >> 8)
    here = mine & (lane == q)
    got = spread(columns, here)
    more = spread(side(near_from + 16, far_from + 16, spare), here)
    pos_ref[...] = got
    pos_ref[1:4] = got[1:4] + 256 * got[5:8]
    pos_ref[6:7] = pos_ref[1:2]
    pos_ref[0:1] = got[0:1] * ROWS + more[0:1] - 16
    pos_ref[1:2] = pos_ref[6:7] * ROWS + more[1:2] - 16
    pos_ref[5:6] = more[2:3]
    wide = lax.broadcasted_iota(i32, (n, slot_ref.shape[1]), 1)
    here = wide == put
    zero = jnp.zeros_like(a)
    slots = spread(side(far, zero, zero + 1, far_from + 16), crosses & (source == me) & here)
    used_ref[...] = spread(side(q & (B - 1), q >> 6, spare), crosses & mine & here)
    slot_ref[...] = slots
    slot_ref[3:4] = slots[0:1] * ROWS + slots[3:4] - 16


def route(me, pair_slots, anchors):
    lists = jnp.transpose(pair_slots, (1, 2, 0)).reshape(-1, pair_slots.shape[0])
    width = 128 * -(-(3 * KEEP) // 128)
    vmem, smem = pl.BlockSpec(memory_space=pltpu.VMEM), pl.BlockSpec(memory_space=pltpu.SMEM)
    return pl.pallas_call(
        route_kernel,
        out_shape=[
            jax.ShapeDtypeStruct((8, 128), jnp.int32),
            jax.ShapeDtypeStruct((8, width), jnp.int32),
            jax.ShapeDtypeStruct((8, width), jnp.int32),
            jax.ShapeDtypeStruct((1,), jnp.int32),
        ],
        in_specs=[smem, vmem, vmem],
        out_specs=[vmem, vmem, vmem, smem],
        compiler_params=pltpu.CompilerParams(vmem_limit_bytes=40 << 20),
        cost_estimate=pl.CostEstimate(flops=10_000_000, bytes_accessed=1_000_000, transcendentals=0),
        name="route",
    )(me, lists, jnp.transpose(anchors))


def flat(ref):
    return ref.reshape(ref.shape[0] * ROWS, 128)


def fetch_kernel(row_of, idx_ref, table_ref, *refs):
    *outs, table, sem = refs
    copy = pltpu.make_async_copy(table_ref, table, sem)
    copy.start()
    copy.wait()
    for k, out_ref in enumerate(outs):
        count = out_ref.shape[0]

        def move(i, carry, out_ref=out_ref, k=k, count=count):
            out_ref[i] = row_of(idx_ref, table, k * count + i)
            return carry

        lax.fori_loop(0, count, move, 0, unroll=4)


def fetch(idx, table, row_of, name):
    return pl.pallas_call(
        functools.partial(fetch_kernel, row_of),
        out_shape=[jax.ShapeDtypeStruct((KEEP, ROWS, 128), jnp.float32)] * 3,
        in_specs=[pl.BlockSpec(memory_space=pltpu.SMEM), pl.BlockSpec(memory_space=pl.ANY)],
        out_specs=[pl.BlockSpec(memory_space=pltpu.VMEM)] * 3,
        scratch_shapes=[pltpu.VMEM(table.shape, jnp.float32), pltpu.SemaphoreType.DMA],
        compiler_params=pltpu.CompilerParams(vmem_limit_bytes=16 << 20),
        cost_estimate=pl.CostEstimate(flops=0, bytes_accessed=8_000_000, transcendentals=0),
        name=name,
    )(idx, table)


def sent_row(idx_ref, table, i):
    return table[idx_ref[0, i]]


def line_no():
    return lax.broadcasted_iota(jnp.int32, (ROWS, 128), 0)


def its_lines(s, spare, lines):
    keep = line_no() >= spare if s else line_no() < ROWS - spare
    return jnp.where(keep, lines, 0.0)


def deal_owner(pos_ref, row, p, table, out_ref, at):
    first, second = [table[pl.ds(pos_ref[row, s * B + p] + ROWS, ROWS)] for s in range(PAIR_DEV)]
    lines = out_ref.shape[1]
    cut = lines - ROWS
    out_ref[at, :cut] = first[:cut]
    if cut < ROWS:
        shared = lax.broadcasted_iota(jnp.int32, (ROWS - cut, 128), 0) + cut < ROWS - pos_ref[5, p]
        out_ref[at, cut:ROWS] = jnp.where(shared, first[cut:], second[: ROWS - cut])
    out_ref[at, ROWS:] = second[ROWS - cut :]


def clear_ends(table):
    zero = jnp.zeros((ROWS, 128), jnp.float32)
    table[0] = zero
    table[table.shape[0] - 1] = zero


PARTS = 4


def deal_near_kernel(pos_ref, orb_ref, near_ref, table, stage, near, sem_in, sem_out):
    pulls = [
        pltpu.make_async_copy(orb_ref.at[:, pl.ds(k * 1024, 1024)], stage.at[k], sem_in.at[k]) for k in range(PARTS)
    ]
    for copy in pulls:
        copy.start()
    clear_ends(table)
    for k, copy in enumerate(pulls):
        copy.wait()

        def lay_out(i, carry, k=k):
            rows = pl.ds(pl.multiple_of(i * 8, 8), 8)
            lines = [stage[k, rows, j * 128 : (j + 1) * 128] for j in range(8)]
            table[pl.ds(i * 8 + 1, 8), k * 8 : k * 8 + 8] = jnp.swapaxes(jnp.stack(lines), 0, 1)
            return carry

        lax.fori_loop(0, 128 // 8, lay_out, 0, unroll=2)
    pushes = []
    for k in range(PARTS):

        def owner(p, carry):
            deal_owner(pos_ref, 0, p, flat(table), near, p)
            return carry

        mine = pl.ds(k * (B // PARTS), B // PARTS)
        lax.fori_loop(k * (B // PARTS), (k + 1) * (B // PARTS), owner, 0, unroll=4)
        pushes.append(pltpu.make_async_copy(near.at[mine], near_ref.at[mine], sem_out.at[k]))
        pushes[-1].start()
    for copy in pushes:
        copy.wait()


def deal_near(lines, pos, orbitals):
    anywhere = pl.BlockSpec(memory_space=pl.ANY)
    dma = pltpu.SemaphoreType.DMA((PARTS,))
    return pl.pallas_call(
        deal_near_kernel,
        out_shape=jax.ShapeDtypeStruct((B, lines, 128), jnp.float32),
        in_specs=[pl.BlockSpec(memory_space=pltpu.SMEM), anywhere],
        out_specs=anywhere,
        scratch_shapes=[
            pltpu.VMEM((130, ROWS, 128), jnp.float32),
            pltpu.VMEM((PARTS, 128, 1024), jnp.float32),
            pltpu.VMEM((B, lines, 128), jnp.float32),
            dma,
            dma,
        ],
        compiler_params=pltpu.CompilerParams(vmem_limit_bytes=60 << 20),
        cost_estimate=pl.CostEstimate(flops=2_000_000, bytes_accessed=10_000_000, transcendentals=0),
        name="deal_near",
    )(pos, orbitals)


def deal_far_kernel(row, pos_ref, *refs):
    *parts, far_ref, table, sem = refs
    copies, end = [], 1
    for k, part in enumerate(parts):
        copies.append(pltpu.make_async_copy(part, table.at[pl.ds(end, part.shape[0])], sem.at[k]))
        end += part.shape[0]
    for copy in copies:
        copy.start()
    clear_ends(table)
    for copy in copies:
        copy.wait()

    def owner(p, carry):
        deal_owner(pos_ref, row, p, flat(table), far_ref, p)
        return carry

    lax.fori_loop(0, B, owner, 0, unroll=4)


def deal_far(lines, row, pos, parts):
    rows = sum(x.shape[0] for x in parts)
    return pl.pallas_call(
        functools.partial(deal_far_kernel, row),
        out_shape=jax.ShapeDtypeStruct((B, lines, 128), jnp.float32),
        in_specs=[pl.BlockSpec(memory_space=pltpu.SMEM)] + [pl.BlockSpec(memory_space=pl.ANY)] * len(parts),
        out_specs=pl.BlockSpec(memory_space=pltpu.VMEM),
        scratch_shapes=[pltpu.VMEM((rows + 2, ROWS, 128), jnp.float32), pltpu.SemaphoreType.DMA((len(parts),))],
        compiler_params=pltpu.CompilerParams(vmem_limit_bytes=32 << 20),
        cost_estimate=pl.CostEstimate(flops=0, bytes_accessed=12_000_000, transcendentals=0),
        name="deal_far",
    )(pos, *parts)


def solve_pair(offset, from_a, from_b, box_a, box_b, term_a, term_b, part, dens, resid, second, third, image):
    ox, oy, oz = offset
    shape = (ROWS, 128)
    line = lax.broadcasted_iota(jnp.int32, shape, 0)
    lane = lax.broadcasted_iota(jnp.int32, shape, 1)
    cy = 2 * line + (lane >> 6)
    cz = lane & (B - 1)
    high = lane >= B
    ends = (high & (line == 0)) | (~high & (line == ROWS - 1))
    no_up, no_down = cz == B - 1, cz == 0

    def plane(ref, x):
        return ref[pl.ds(pl.multiple_of(x * ROWS, ROWS), ROWS)]

    def put(ref, x, value):
        ref[pl.ds(pl.multiple_of(x * ROWS, ROWS), ROWS)] = value

    def shifter(sy, sz):
        flat = sy * B + sz
        lines, steps = flat >> 7, flat & 127
        inside = (cy >= sy) & (cy < B + sy) & (cz >= sz) & (cz < B + sz)
        keep = lane < 128 - steps

        def shift(ref, x, first):
            at = x * ROWS - lines - first
            moved = jnp.where(keep, ref[pl.ds(at, ROWS)], ref[pl.ds(at - 1, ROWS)])
            return jnp.where(inside, pltpu.roll(moved, steps, axis=1), 0.0)

        return shift

    def apply(ref, x):
        here = plane(ref, x + 1)
        at = (x + 1) * ROWS
        other = jnp.where(high, ref[pl.ds(at - 1, ROWS)], ref[pl.ds(at + 1, ROWS)])
        other = here + jnp.where(ends, 0.0, other)
        beside = plane(ref, x) + plane(ref, x + 2) + pltpu.roll(other, B, axis=1)
        upper = jnp.where(no_up, 0.0, pltpu.roll(here, 127, axis=1))
        lower = jnp.where(no_down, 0.0, pltpu.roll(here, 1, axis=1))
        return here, 6.0 * here - beside - upper - lower

    zero = jnp.zeros(shape, jnp.float32)
    for ref in (dens, second, third):
        put(ref, 0, zero)
        put(ref, B + 1, zero)

    shift_on = shifter(oy, oz)
    shift_back = shifter(-oy, -oz)

    def begin(x, acc):
        src = x - ox
        inside = jnp.where((src >= 0) & (src < B), 1.0, 0.0)
        moved = shift_on(box_b, jnp.clip(src, 0, B - 1) + 1, from_b) * inside
        density = box_a[pl.ds((x + 1) * ROWS - from_a, ROWS)] * moved
        put(part, x, moved)
        put(dens, x + 1, density)
        return acc + density * density

    def first(x, acc):
        here, img = apply(dens, x)
        put(image, x + 1, img)
        return acc + here * img

    norm0 = yield begin
    step0 = norm0 / (yield first)

    def rest0(x, acc):
        left = plane(dens, x + 1) - step0 * plane(image, x + 1)
        put(resid, x, left)
        return acc + left * left

    norm1 = yield rest0
    ratio0 = norm1 / norm0

    def turn1(x, acc):
        put(second, x + 1, plane(resid, x) + ratio0 * plane(dens, x + 1))
        return acc

    def again(x, acc):
        here, img = apply(second, x)
        put(image, x + 1, img)
        return acc + here * img

    yield turn1
    step1 = norm1 / (yield again)

    def rest1(x, acc):
        left = plane(resid, x) - step1 * plane(image, x + 1)
        put(resid, x, left)
        return acc + left * left

    norm2 = yield rest1
    ratio1 = norm2 / norm1

    def turn2(x, acc):
        put(third, x + 1, plane(resid, x) + ratio1 * plane(second, x + 1))
        return acc

    def last(x, acc):
        here, img = apply(third, x)
        return acc + here * img

    yield turn2
    step2 = norm2 / (yield last)

    def finish(x, acc):
        potential = step0 * plane(dens, x + 1) + step1 * plane(second, x + 1) + step2 * plane(third, x + 1)
        here = pl.ds((x + 1) * ROWS - from_a, ROWS)
        term_a[here] = potential * plane(part, x)
        put(image, x + 1, potential * box_a[here])
        return acc

    def back(x, acc):
        src = x + ox
        inside = jnp.where((src >= 0) & (src < B), 1.0, 0.0)
        term_b[pl.ds((x + 1) * ROWS - from_b, ROWS)] = shift_back(image, jnp.clip(src, 0, B - 1) + 1, 0) * inside
        return acc

    yield finish
    yield back


def run_together(solvers, unroll):
    steps = [next(solver) for solver in solvers]
    zero = jnp.zeros((ROWS, 128), jnp.float32)
    while True:
        def both(x, accs, steps=tuple(steps)):
            return tuple(step(x, acc) for step, acc in zip(steps, accs))

        accs = lax.fori_loop(0, B, both, (zero,) * len(steps), unroll=unroll)
        sums = [jnp.sum(acc, keepdims=True) for acc in accs]
        try:
            steps = [solver.send(value) for solver, value in zip(solvers, sums)]
        except StopIteration:
            return


def pair_kernel(place_ref, pos_ref, anchor_ref, near_ref, far_ref, near_out, far_out, boxes, terms, *rest):
    *fields, sem = rest
    lines = near_ref.shape[1]
    cut = lines - ROWS
    at = [s * B + place_ref[0] for s in range(PAIR_DEV)]
    flags = [pos_ref[4, k] for k in at]
    copies = []
    for s in range(PAIR_DEV):
        for k, ref in enumerate((near_ref, far_ref)):
            which = 1 - flags[s] if k else flags[s]
            source = ref.at[:, pl.ds(s * cut, ROWS)]
            copies.append(pltpu.make_async_copy(source, boxes.at[s, which, pl.ds(1, B)], sem.at[s, k]))
    for copy in copies:
        copy.start()
    for s in range(PAIR_DEV):
        for k in range(2):
            clear_ends(boxes.at[s, k])
    for copy in copies:
        copy.wait()
    solvers = []
    for s in range(PAIR_DEV):
        orb_a, orb_b = pos_ref[2, at[s]], pos_ref[3, at[s]]
        offset = [anchor_ref[3 * orb_b + k] - anchor_ref[3 * orb_a + k] for k in range(3)]
        spare = pos_ref[5, at[s]]
        moved = spare if s else 0
        from_a = jnp.where(offset[1] > 0, spare, 0) - moved
        from_b = jnp.where(offset[1] < 0, spare, 0) - moved
        refs = [flat(ref.at[s, k]) for ref in (boxes, terms) for k in range(2)]
        solvers.append(solve_pair(offset, from_a, from_b, *refs, *[ref.at[s] for ref in fields]))
    run_together(solvers, UNROLL if cut < ROWS else 1)

    def together(x, carry):
        for k, out in enumerate((near_out, far_out)):
            first, second = [terms[s, 1 - flags[s] if k else flags[s], x + 1] for s in range(PAIR_DEV)]
            out[x, :cut] = first[:cut]
            if cut < ROWS:
                low = its_lines(0, pos_ref[5, at[0]], first)[cut:]
                out[x, cut:ROWS] = low + its_lines(1, pos_ref[5, at[1]], second)[: ROWS - cut]
            out[x, ROWS:] = second[ROWS - cut :]
        return carry

    lax.fori_loop(0, B, together, 0, unroll=4)


def solve(place, pos, anchors, near, far):
    smem, vmem = pl.BlockSpec(memory_space=pltpu.SMEM), pl.BlockSpec(memory_space=pltpu.VMEM)
    anywhere = pl.BlockSpec(memory_space=pl.ANY)
    field = pltpu.VMEM((PAIR_DEV, B * ROWS, 128), jnp.float32)
    padded = pltpu.VMEM((PAIR_DEV, (B + 2) * ROWS, 128), jnp.float32)
    boxes = pltpu.VMEM((PAIR_DEV, 2, B + 2, ROWS, 128), jnp.float32)
    return pl.pallas_call(
        pair_kernel,
        out_shape=[jax.ShapeDtypeStruct(near.shape, jnp.float32)] * 2,
        in_specs=[smem, smem, smem, anywhere, anywhere],
        out_specs=[vmem, vmem],
        scratch_shapes=[
            boxes, boxes, field, padded, field, padded, padded, padded,
            pltpu.SemaphoreType.DMA((PAIR_DEV, 2)),
        ],
        compiler_params=pltpu.CompilerParams(vmem_limit_bytes=40 << 20),
        cost_estimate=pl.CostEstimate(flops=100_000_000, bytes_accessed=30_000_000, transcendentals=0),
        name="solve",
    )(place, pos, anchors, near, far)


def add_lines(total, line, lines):
    here = pl.ds(line + ROWS, ROWS)
    total[here] = total[here] + lines


def add_far_kernel(pos_ref, terms_ref, out_ref):
    out_ref[...] = jnp.zeros(out_ref.shape, jnp.float32)
    total = flat(out_ref)
    cut = terms_ref.shape[1] - ROWS

    def here(p, carry):
        for s in range(PAIR_DEV):
            q = s * B + p

            @pl.when(pos_ref[6, q] < 128)
            def _(q=q, s=s):
                lines = terms_ref[p, s * cut : s * cut + ROWS]
                add_lines(total, pos_ref[1, q], its_lines(s, pos_ref[5, q], lines))

        return carry

    lax.fori_loop(0, B, here, 0)


def add_far(pos, terms):
    smem, vmem = pl.BlockSpec(memory_space=pltpu.SMEM), pl.BlockSpec(memory_space=pltpu.VMEM)
    return pl.pallas_call(
        add_far_kernel,
        out_shape=jax.ShapeDtypeStruct((130, ROWS, 128), jnp.float32),
        in_specs=[smem, vmem],
        out_specs=vmem,
        compiler_params=pltpu.CompilerParams(vmem_limit_bytes=24 << 20),
        cost_estimate=pl.CostEstimate(flops=2_000_000, bytes_accessed=4_000_000, transcendentals=0),
        name="add_far",
    )(pos, terms)


def add_arrived_kernel(slot_ref, sum_ref, *refs):
    *from_groups, out_ref, sem = refs
    copy = pltpu.make_async_copy(sum_ref, out_ref, sem)
    copy.start()
    copy.wait()
    total = flat(out_ref)

    def there(k, carry):
        for d, ref in enumerate(from_groups):
            at = d * KEEP + k

            @pl.when(slot_ref[2, at] == 1)
            def _(at=at, ref=ref):
                add_lines(total, slot_ref[3, at], ref[k])

        return carry

    lax.fori_loop(0, KEEP, there, 0)


def add_arrived(slot, summed, from_groups):
    smem, vmem = pl.BlockSpec(memory_space=pltpu.SMEM), pl.BlockSpec(memory_space=pltpu.VMEM)
    return pl.pallas_call(
        add_arrived_kernel,
        out_shape=jax.ShapeDtypeStruct(summed.shape, jnp.float32),
        in_specs=[smem, pl.BlockSpec(memory_space=pl.ANY)] + [vmem] * 3,
        out_specs=vmem,
        scratch_shapes=[pltpu.SemaphoreType.DMA],
        compiler_params=pltpu.CompilerParams(vmem_limit_bytes=24 << 20),
        cost_estimate=pl.CostEstimate(flops=2_000_000, bytes_accessed=6_000_000, transcendentals=0),
        name="add_arrived",
    )(slot, summed, *from_groups)


def add_near_kernel(pos_ref, sum_ref, terms_ref, out_ref, acc, terms, stage, sem_sum, sem_in, sem_out):
    cut = terms.shape[1] - ROWS
    copies = [pltpu.make_async_copy(sum_ref, acc, sem_sum)]
    for k in range(PARTS):
        mine = pl.ds(k * (B // PARTS), B // PARTS)
        copies.append(pltpu.make_async_copy(terms_ref.at[mine], terms.at[mine], sem_in.at[k]))
    for copy in copies:
        copy.start()
    copies[0].wait()
    for k in range(PARTS):
        copies[k + 1].wait()

        def here(p, carry):
            for s in range(PAIR_DEV):
                q = s * B + p
                lines = terms[p, s * cut : s * cut + ROWS]
                add_lines(flat(acc), pos_ref[0, q], its_lines(s, pos_ref[5, q], lines))
            return carry

        lax.fori_loop(k * (B // PARTS), (k + 1) * (B // PARTS), here, 0, unroll=2)
    pushes = []
    for k in range(PARTS):

        def lay_out(i, carry, k=k):
            rows = pl.ds(pl.multiple_of(i * 8, 8), 8)
            lines = jnp.swapaxes(acc[pl.ds(i * 8 + 1, 8), k * 8 : k * 8 + 8], 0, 1)
            for j in range(8):
                stage[k, rows, j * 128 : (j + 1) * 128] = lines[j]
            return carry

        lax.fori_loop(0, 128 // 8, lay_out, 0, unroll=2)
        pushes.append(pltpu.make_async_copy(stage.at[k], out_ref.at[:, pl.ds(k * 1024, 1024)], sem_out.at[k]))
        pushes[-1].start()
    for copy in pushes:
        copy.wait()


def add_near(pos, summed, terms):
    anywhere = pl.BlockSpec(memory_space=pl.ANY)
    dma = pltpu.SemaphoreType.DMA((PARTS,))
    return pl.pallas_call(
        add_near_kernel,
        out_shape=jax.ShapeDtypeStruct((128, ROWS * 128), jnp.float32),
        in_specs=[pl.BlockSpec(memory_space=pltpu.SMEM), anywhere, anywhere],
        out_specs=anywhere,
        scratch_shapes=[
            pltpu.VMEM((130, ROWS, 128), jnp.float32),
            pltpu.VMEM(terms.shape, jnp.float32),
            pltpu.VMEM((PARTS, 128, 1024), jnp.float32),
            pltpu.SemaphoreType.DMA,
            dma,
            dma,
        ],
        compiler_params=pltpu.CompilerParams(vmem_limit_bytes=60 << 20),
        cost_estimate=pl.CostEstimate(flops=2_000_000, bytes_accessed=10_000_000, transcendentals=0),
        name="add_near",
    )(pos, summed, terms)


def turned(x, shift):
    groups = lax.axis_size("grp")
    return lax.ppermute(x, "grp", [(g, (g + shift) % groups) for g in range(groups)])


def exchanged(planes):
    return lax.all_to_all(planes, "grid", 0, 0, tiled=True)


def there_and_back(place, pos, anchors, both):
    lines = both.shape[1] // 2

    def solve_both(both):
        return jnp.concatenate(solve(place, pos, anchors, both[:, :lines], both[:, lines:]), axis=1)

    def step(k, both):
        return lax.cond(k == 0, solve_both, lambda x: x, exchanged(both))

    return lax.fori_loop(0, 2, step, both)


def fitting(lines, orbitals, anchors, place, pos, slot, used):
    def used_row(used_ref, table, i):
        p, s, spare = used_ref[0, i], used_ref[1, i], used_ref[2, i]
        plane = table[p, pl.ds(pl.multiple_of(s * (lines - ROWS), 8), ROWS)]
        keep = (line_no() >= s * spare) & (line_no() < ROWS - (1 - s) * spare)
        return jnp.where(keep, plane, 0.0)

    trimmed = lines == TRIMMED
    near = deal_near(lines, pos, orbitals)
    if trimmed:
        near = exchanged(near)
    local = orbitals.reshape(128, ROWS, 128)
    arrived = [turned(x, d) for d, x in enumerate(fetch(slot, local, sent_row, "send"), 1)]
    far = deal_far(lines, 1, pos, [local] + arrived)
    if trimmed:
        near_terms, far_terms = solve(place, pos, anchors.reshape(-1), near, exchanged(far))
        far_terms = exchanged(far_terms)
    else:
        both = there_and_back(place, pos, anchors.reshape(-1), jnp.concatenate([near, far], axis=1))
        near_terms, far_terms = both[:, :lines], both[:, lines:]
    from_groups = [turned(x, -d) for d, x in enumerate(fetch(used, far_terms, used_row, "back"), 1)]
    summed = add_far(pos, far_terms)
    if trimmed:
        near_terms = exchanged(near_terms)
    return add_near(pos, add_arrived(slot, summed, from_groups), near_terms)


def add_all_kernel(pos_ref, terms_ref, out_ref):
    out_ref[...] = jnp.zeros(out_ref.shape, jnp.float32)
    total = flat(out_ref)

    def here(p, carry):
        for s in range(PAIR_DEV):
            for k in range(2):
                at = (k * PAIR_DEV + s) * ROWS
                add_lines(total, pos_ref[k, s * B + p], terms_ref[p, at : at + ROWS])
        return carry

    lax.fori_loop(0, B, here, 0)


def add_all(pos, terms, count):
    return pl.pallas_call(
        add_all_kernel,
        out_shape=jax.ShapeDtypeStruct((count + 2, ROWS, 128), jnp.float32),
        in_specs=[pl.BlockSpec(memory_space=pltpu.SMEM), pl.BlockSpec(memory_space=pltpu.VMEM)],
        out_specs=pl.BlockSpec(memory_space=pltpu.VMEM),
        compiler_params=pltpu.CompilerParams(vmem_limit_bytes=32 << 20),
        cost_estimate=pl.CostEstimate(flops=2_000_000, bytes_accessed=10_000_000, transcendentals=0),
        name="add_all",
    )(pos, terms)


def general(orbitals, anchors, pair_slots, place):
    groups, grid_count = lax.axis_size("grp"), lax.axis_size("grid")
    me, rows = lax.axis_index("grp"), orbitals.shape[0]
    dealt = deal_evenly(pair_slots, groups * grid_count, PAIR_DEV)
    own = lax.dynamic_slice_in_dim(dealt, me * grid_count, grid_count, 0)
    own = jnp.maximum(jnp.transpose(own, (2, 1, 0)).reshape(2, PAIR_DEV * grid_count), 0)
    pos = jnp.concatenate([own * ROWS, own, jnp.zeros((4, own.shape[1]), jnp.int32)])
    round_trip = [turned(orbitals, d) for d in (3, 2, 1)] + [orbitals]
    pieces = lax.dynamic_slice_in_dim(jnp.concatenate(round_trip * 2), (3 - me) * rows, groups * rows, 0)
    table = pieces.reshape(-1, ROWS, 128)
    both = jnp.concatenate([deal_far(PAIR_DEV * ROWS, k, pos, [table]) for k in range(2)], axis=1)

    terms = there_and_back(place, pos, anchors.reshape(-1), both)
    summed = add_all(pos, terms, table.shape[0])
    blocks = [lax.dynamic_slice_in_dim(summed, ((me + d) & 3) * rows + 1, rows, 0) for d in range(4)]
    return (blocks[0] + sum(turned(blocks[d], d) for d in (1, 2, 3))).reshape(orbitals.shape)


def body(orbitals, anchors, pair_slots):
    me = lax.axis_index("grp").astype(jnp.int32)[None]
    place = lax.axis_index("grid").astype(jnp.int32)[None]
    pos, slot, used, mode = route(me, pair_slots, anchors)
    return lax.switch(
        mode[0],
        [
            lambda: fitting(TRIMMED, orbitals, anchors, place, pos, slot, used),
            lambda: fitting(PAIR_DEV * ROWS, orbitals, anchors, place, pos, slot, used),
            lambda: general(orbitals, anchors, pair_slots, place),
        ],
    )


def solution(mesh):
    return jax.shard_map(
        body,
        mesh=mesh,
        in_specs=(P("grp", "grid"), P(), P()),
        out_specs=P("grp", "grid"),
        check_vma=False,
    )
```

```python
import functools

import jax
import jax.numpy as jnp
from jax import lax
from jax.experimental import pallas as pl
from jax.experimental.pallas import tpu as pltpu
from jax.sharding import PartitionSpec as P

B = 64
PAIR_DEV = 2
ITERS = 3
ROWS = B * B // 128
KEEP = 48
UNROLL = 16
TRIMMED = 56


def deal_evenly(pair_slots, owner_count, each_owner):
    flat_slots = pair_slots.reshape(-1, 2)
    filled = (flat_slots[:, 0] >= 0).astype(jnp.int32)
    order = jnp.arange(flat_slots.shape[0], dtype=jnp.int32)
    position = jnp.sum(jnp.where(order[None, :] < order[:, None], filled[None, :], 0), axis=1)
    wanted = lax.broadcasted_iota(jnp.int32, (owner_count, each_owner), 1) * owner_count
    wanted = (wanted + lax.broadcasted_iota(jnp.int32, (owner_count, each_owner), 0)).reshape(-1)
    matched = (position[None, :] == wanted[:, None]) & (filled[None, :] == 1)
    picked = jnp.dot(matched.astype(jnp.int32), flat_slots)
    return picked.reshape(owner_count, each_owner, 2)


def route_kernel(me_ref, pair_ref, anchor_ref, pos_ref, slot_ref, used_ref, mode_ref):
    me = me_ref[0]
    f32, i32 = jnp.float32, jnp.int32
    groups, each = 4, 2 * B

    def col(x):
        return jnp.sum(x, axis=1, keepdims=True)

    pairs = pair_ref[...].astype(f32).T
    at = lax.broadcasted_iota(i32, pairs.shape, 1)
    columns = [col(jnp.where(at == k, pairs, 0.0)) for k in range(pairs.shape[1])]
    a = jnp.concatenate(columns[0::2], axis=0).astype(i32)
    b = jnp.concatenate(columns[1::2], axis=0).astype(i32)
    n = a.shape[0]

    before = lax.broadcasted_iota(i32, (128, 128), 0) > lax.broadcasted_iota(i32, (128, 128), 1)
    before = jnp.where(before, 1.0, 0.0).astype(jnp.bfloat16)

    def sort_in(hot):
        width = hot.shape[1]
        totals = jnp.sum(hot, axis=0, keepdims=True)
        key = lax.broadcasted_iota(i32, (8, width), 1) & 15
        running = jnp.broadcast_to(totals, (8, width))
        for step in (1, 2, 4, 8):
            running = running + jnp.where(key >= step, pltpu.roll(running, step, axis=1), 0.0)
        below = running[0:1] - totals
        ranks, passed = [], below
        for k in range(0, n, 128):
            part = hot[k : k + 128]
            ahead = jnp.dot(before, part.astype(jnp.bfloat16), preferred_element_type=f32) + passed
            ranks.append(col(ahead * part))
            passed = passed + jnp.sum(part, axis=0, keepdims=True)
        return jnp.concatenate(ranks, axis=0), totals, below

    lane = lax.broadcasted_iota(i32, (n, 128), 1)
    valid = a >= 0
    ga, gb = a >> 7, b >> 7
    low, high = jnp.minimum(ga, gb), jnp.maximum(ga, gb)
    anchor_y = anchor_ref[1:2].astype(f32)
    name = lax.broadcasted_iota(i32, (n, anchor_ref.shape[1]), 1)
    oy = col(jnp.where(name == b, anchor_y, 0.0) - jnp.where(name == a, anchor_y, 0.0)).astype(i32)
    spare = jnp.abs(oy) >> 1
    kinds = lax.broadcasted_iota(i32, (n, 256), 1)
    hot = jnp.where(valid & (kinds == (low * groups + high) * 16 + spare), 1.0, 0.0)
    rank, sums, _ = sort_in(hot)
    sums = sums.astype(i32)
    kind1 = lax.broadcasted_iota(i32, (1, 256), 1) >> 4
    count, up = {}, {}
    for g in range(groups):
        for h in range(g, groups):
            count[g, h] = jnp.sum(jnp.where(kind1 == g * groups + h, sums, 0))
            up[g, h] = (count[g, h] >> 1) if h > g else 0

    def loads():
        load = [0] * groups
        for (g, h), c in count.items():
            load[g] = load[g] + (c - up[g, h])
            load[h] = load[h] + up[g, h]
        return load

    load = loads()
    for g, h in count:
        if h > g:
            up[g, h] = up[g, h] + ((load[g] - load[h] + 2) >> 2)
    load = loads()
    excess = 0
    for g in range(groups - 1):
        excess = excess + load[g] - each
        up[g, g + 1] = up[g, g + 1] + excess
    need = (ROWS * PAIR_DEV - TRIMMED) - 1
    fits = 1
    goes_up, there = jnp.zeros((1, 256), f32), jnp.ones((1, 256), f32)
    for (g, h), c in count.items():
        if h > g:
            u = up[g, h]
            fine = (u >= 0) & (u <= KEEP) & (c - u >= 0) & (c - u <= KEEP)
            fits = jnp.where(fine, fits, 0)
            goes_up = jnp.where(kind1 == g * groups + h, u.astype(f32), goes_up)
            there = jnp.where(kind1 == g * groups + h, jnp.maximum(c, 1).astype(f32), there)

    key1 = lax.broadcasted_iota(i32, (1, 256), 1) & 15
    weight = jnp.where(key1 <= need // 2, 1, 0) + jnp.where(key1 <= need // 2 + 1, 1, 0)
    small = {t: jnp.sum(jnp.where(kind1 == t[0] * groups + t[1], sums * weight, 0)).astype(f32) for t in count}
    share = goes_up / there
    surplus = jnp.zeros((1, 256), f32)
    for g in range(groups):
        held = jnp.zeros((1, 256), f32)
        for (low_g, high_g), amount in small.items():
            if low_g == high_g:
                held = held + (amount if low_g == g else 0.0)
            elif g in (low_g, high_g):
                part = jnp.sum(jnp.where((kind1 == low_g * groups + high_g) & (key1 == 0), share, 0.0))
                held = held + amount * (part if high_g == g else 1.0 - part)
        surplus = surplus + jnp.where((kind1 >> 2) == g, held, 0.0) - jnp.where((kind1 & 3) == g, held, 0.0)
    bend = surplus / (2.0 * jnp.maximum(goes_up, 1.0))
    most = jnp.minimum(there / jnp.maximum(goes_up, 1.0) - 1.0, 1.0)
    bend = jnp.clip(bend, -0.98 * most, 0.98 * most)
    u, c, bend = col(hot * goes_up), jnp.maximum(col(hot * there), 1.0), col(hot * bend)

    def risen_at(r):
        x = r / c
        return jnp.where(r >= c, u, jnp.clip(jnp.floor(u * (x + bend * x * (1.0 - x)) + 0.5 / c), 0.0, u))

    risen = risen_at(rank)
    rises = risen_at(rank + 1.0) > risen
    group = jnp.where(rises, high, low)
    source = low + high - group
    crosses = valid & (low != high)
    hot = jnp.where(valid & (lane == group * 16 + spare), 1.0, 0.0)
    order, keyed, below = sort_in(hot)
    order = order.astype(i32)
    second = order >= B
    q = jnp.where(second, B + each - 1 - order, order)
    lane1 = lax.broadcasted_iota(i32, (1, 128), 1)
    match = 1
    for g in range(groups):
        fits = jnp.where(jnp.sum(jnp.where((lane1 >> 4) == g, keyed, 0.0)) == each, fits, 0)
        for j in range(need // 2 + 1):
            both = (lane1 == g * 16 + j + 1) | (lane1 == g * 16 + need - j + 1)
            match = jnp.where(jnp.sum(jnp.where(both, below, 0.0)) <= each, match, 0)
    mode_ref[0] = jnp.where(fits == 1, 1 - match, 2)

    put = (((group - source) & 3) - 1) * KEEP + jnp.where(rises, risen, rank - risen).astype(i32)
    near_b = ga != group
    near = jnp.where(near_b, b, a) & 127
    far = jnp.where(near_b, a, b) & 127
    table = jnp.where(crosses, 128 + put, far)
    spare = spare * match
    moved = jnp.where(second, spare, 0)
    from_a = jnp.where(oy > 0, spare, 0) - moved
    from_b = jnp.where(oy < 0, spare, 0) - moved
    near_from, far_from = jnp.where(near_b, from_b, from_a), jnp.where(near_b, from_a, from_b)

    def side(*columns):
        at = lax.broadcasted_iota(i32, (n, 8), 1)
        out = jnp.zeros((n, 8), f32)
        for k, column in enumerate(columns):
            out = jnp.where(at == k, column.astype(f32), out)
        return out.astype(jnp.bfloat16)

    def spread(columns, mask):
        hot = jnp.where(mask, 1.0, 0.0).astype(jnp.bfloat16)
        out = lax.dot_general(columns, hot, (((0,), (0,)), ((), ())), preferred_element_type=f32)
        return out.astype(i32)

    mine = valid & (group == me)
    flag = jnp.where(near_b, 1, 0)
    columns = side(near, table & 255, a & 255, b & 255, flag, table >> 8, a >> 8, b >> 8)
    here = mine & (lane == q)
    got = spread(columns, here)
    more = spread(side(near_from + 16, far_from + 16, spare), here)
    pos_ref[...] = got
    pos_ref[1:4] = got[1:4] + 256 * got[5:8]
    pos_ref[6:7] = pos_ref[1:2]
    pos_ref[0:1] = got[0:1] * ROWS + more[0:1] - 16
    pos_ref[1:2] = pos_ref[6:7] * ROWS + more[1:2] - 16
    pos_ref[5:6] = more[2:3]
    wide = lax.broadcasted_iota(i32, (n, slot_ref.shape[1]), 1)
    here = wide == put
    zero = jnp.zeros_like(a)
    slots = spread(side(far, zero, zero + 1, far_from + 16), crosses & (source == me) & here)
    used_ref[...] = spread(side(q & (B - 1), q >> 6, spare), crosses & mine & here)
    slot_ref[...] = slots
    slot_ref[3:4] = slots[0:1] * ROWS + slots[3:4] - 16


def route(me, pair_slots, anchors):
    lists = jnp.transpose(pair_slots, (1, 2, 0)).reshape(-1, pair_slots.shape[0])
    width = 128 * -(-(3 * KEEP) // 128)
    vmem, smem = pl.BlockSpec(memory_space=pltpu.VMEM), pl.BlockSpec(memory_space=pltpu.SMEM)
    return pl.pallas_call(
        route_kernel,
        out_shape=[
            jax.ShapeDtypeStruct((8, 128), jnp.int32),
            jax.ShapeDtypeStruct((8, width), jnp.int32),
            jax.ShapeDtypeStruct((8, width), jnp.int32),
            jax.ShapeDtypeStruct((1,), jnp.int32),
        ],
        in_specs=[smem, vmem, vmem],
        out_specs=[vmem, vmem, vmem, smem],
        compiler_params=pltpu.CompilerParams(vmem_limit_bytes=40 << 20),
        cost_estimate=pl.CostEstimate(flops=10_000_000, bytes_accessed=1_000_000, transcendentals=0),
        name="route",
    )(me, lists, jnp.transpose(anchors))


def flat(ref):
    return ref.reshape(ref.shape[0] * ROWS, 128)


def fetch_kernel(row_of, idx_ref, table_ref, *refs):
    *outs, table, sem = refs
    copy = pltpu.make_async_copy(table_ref, table, sem)
    copy.start()
    copy.wait()
    for k, out_ref in enumerate(outs):
        count = out_ref.shape[0]

        def move(i, carry, out_ref=out_ref, k=k, count=count):
            out_ref[i] = row_of(idx_ref, table, k * count + i)
            return carry

        lax.fori_loop(0, count, move, 0, unroll=4)


def fetch(idx, table, row_of, name):
    return pl.pallas_call(
        functools.partial(fetch_kernel, row_of),
        out_shape=[jax.ShapeDtypeStruct((KEEP, ROWS, 128), jnp.float32)] * 3,
        in_specs=[pl.BlockSpec(memory_space=pltpu.SMEM), pl.BlockSpec(memory_space=pl.ANY)],
        out_specs=[pl.BlockSpec(memory_space=pltpu.VMEM)] * 3,
        scratch_shapes=[pltpu.VMEM(table.shape, jnp.float32), pltpu.SemaphoreType.DMA],
        compiler_params=pltpu.CompilerParams(vmem_limit_bytes=16 << 20),
        cost_estimate=pl.CostEstimate(flops=0, bytes_accessed=8_000_000, transcendentals=0),
        name=name,
    )(idx, table)


def sent_row(idx_ref, table, i):
    return table[idx_ref[0, i]]


def line_no():
    return lax.broadcasted_iota(jnp.int32, (ROWS, 128), 0)


def its_lines(s, spare, lines):
    keep = line_no() >= spare if s else line_no() < ROWS - spare
    return jnp.where(keep, lines, 0.0)


def deal_owner(pos_ref, row, p, table, out_ref, at):
    first, second = [table[pl.ds(pos_ref[row, s * B + p] + ROWS, ROWS)] for s in range(PAIR_DEV)]
    lines = out_ref.shape[1]
    cut = lines - ROWS
    out_ref[at, :cut] = first[:cut]
    if cut < ROWS:
        shared = lax.broadcasted_iota(jnp.int32, (ROWS - cut, 128), 0) + cut < ROWS - pos_ref[5, p]
        out_ref[at, cut:ROWS] = jnp.where(shared, first[cut:], second[: ROWS - cut])
    out_ref[at, ROWS:] = second[ROWS - cut :]


def clear_ends(table):
    zero = jnp.zeros((ROWS, 128), jnp.float32)
    table[0] = zero
    table[table.shape[0] - 1] = zero


PARTS = 4


def deal_near_kernel(pos_ref, orb_ref, near_ref, table, stage, near, sem_in, sem_out):
    pulls = [
        pltpu.make_async_copy(orb_ref.at[:, pl.ds(k * 1024, 1024)], stage.at[k], sem_in.at[k]) for k in range(PARTS)
    ]
    for copy in pulls:
        copy.start()
    clear_ends(table)
    for k, copy in enumerate(pulls):
        copy.wait()

        def lay_out(i, carry, k=k):
            rows = pl.ds(pl.multiple_of(i * 8, 8), 8)
            lines = [stage[k, rows, j * 128 : (j + 1) * 128] for j in range(8)]
            table[pl.ds(i * 8 + 1, 8), k * 8 : k * 8 + 8] = jnp.swapaxes(jnp.stack(lines), 0, 1)
            return carry

        lax.fori_loop(0, 128 // 8, lay_out, 0, unroll=2)
    pushes = []
    for k in range(PARTS):

        def owner(p, carry):
            deal_owner(pos_ref, 0, p, flat(table), near, p)
            return carry

        mine = pl.ds(k * (B // PARTS), B // PARTS)
        lax.fori_loop(k * (B // PARTS), (k + 1) * (B // PARTS), owner, 0, unroll=4)
        pushes.append(pltpu.make_async_copy(near.at[mine], near_ref.at[mine], sem_out.at[k]))
        pushes[-1].start()
    for copy in pushes:
        copy.wait()


def deal_near(lines, pos, orbitals):
    anywhere = pl.BlockSpec(memory_space=pl.ANY)
    dma = pltpu.SemaphoreType.DMA((PARTS,))
    return pl.pallas_call(
        deal_near_kernel,
        out_shape=jax.ShapeDtypeStruct((B, lines, 128), jnp.float32),
        in_specs=[pl.BlockSpec(memory_space=pltpu.SMEM), anywhere],
        out_specs=anywhere,
        scratch_shapes=[
            pltpu.VMEM((130, ROWS, 128), jnp.float32),
            pltpu.VMEM((PARTS, 128, 1024), jnp.float32),
            pltpu.VMEM((B, lines, 128), jnp.float32),
            dma,
            dma,
        ],
        compiler_params=pltpu.CompilerParams(vmem_limit_bytes=60 << 20),
        cost_estimate=pl.CostEstimate(flops=2_000_000, bytes_accessed=10_000_000, transcendentals=0),
        name="deal_near",
    )(pos, orbitals)


def deal_far_kernel(row, pos_ref, *refs):
    *parts, far_ref, table, sem = refs
    copies, end = [], 1
    for k, part in enumerate(parts):
        copies.append(pltpu.make_async_copy(part, table.at[pl.ds(end, part.shape[0])], sem.at[k]))
        end += part.shape[0]
    for copy in copies:
        copy.start()
    clear_ends(table)
    for copy in copies:
        copy.wait()

    def owner(p, carry):
        deal_owner(pos_ref, row, p, flat(table), far_ref, p)
        return carry

    lax.fori_loop(0, B, owner, 0, unroll=4)


def deal_far(lines, row, pos, parts):
    rows = sum(x.shape[0] for x in parts)
    return pl.pallas_call(
        functools.partial(deal_far_kernel, row),
        out_shape=jax.ShapeDtypeStruct((B, lines, 128), jnp.float32),
        in_specs=[pl.BlockSpec(memory_space=pltpu.SMEM)] + [pl.BlockSpec(memory_space=pl.ANY)] * len(parts),
        out_specs=pl.BlockSpec(memory_space=pltpu.VMEM),
        scratch_shapes=[pltpu.VMEM((rows + 2, ROWS, 128), jnp.float32), pltpu.SemaphoreType.DMA((len(parts),))],
        compiler_params=pltpu.CompilerParams(vmem_limit_bytes=63 << 20),
        cost_estimate=pl.CostEstimate(flops=0, bytes_accessed=12_000_000, transcendentals=0),
        name="deal_far",
    )(pos, *parts)


def solve_pair(offset, from_a, from_b, box_a, box_b, term_a, term_b, part, dens, resid, second, third, image):
    ox, oy, oz = offset
    shape = (ROWS, 128)
    line = lax.broadcasted_iota(jnp.int32, shape, 0)
    lane = lax.broadcasted_iota(jnp.int32, shape, 1)
    cy = 2 * line + (lane >> 6)
    cz = lane & (B - 1)
    high = lane >= B
    ends = (high & (line == 0)) | (~high & (line == ROWS - 1))
    no_up, no_down = cz == B - 1, cz == 0

    def plane(ref, x):
        return ref[pl.ds(pl.multiple_of(x * ROWS, ROWS), ROWS)]

    def put(ref, x, value):
        ref[pl.ds(pl.multiple_of(x * ROWS, ROWS), ROWS)] = value

    def shifter(sy, sz):
        flat = sy * B + sz
        lines, steps = flat >> 7, flat & 127
        inside = (cy >= sy) & (cy < B + sy) & (cz >= sz) & (cz < B + sz)
        keep = lane < 128 - steps

        def shift(ref, x, first):
            at = x * ROWS - lines - first
            moved = jnp.where(keep, ref[pl.ds(at, ROWS)], ref[pl.ds(at - 1, ROWS)])
            return jnp.where(inside, pltpu.roll(moved, steps, axis=1), 0.0)

        return shift

    def apply(ref, x):
        here = plane(ref, x + 1)
        at = (x + 1) * ROWS
        other = jnp.where(high, ref[pl.ds(at - 1, ROWS)], ref[pl.ds(at + 1, ROWS)])
        other = here + jnp.where(ends, 0.0, other)
        beside = plane(ref, x) + plane(ref, x + 2) + pltpu.roll(other, B, axis=1)
        upper = jnp.where(no_up, 0.0, pltpu.roll(here, 127, axis=1))
        lower = jnp.where(no_down, 0.0, pltpu.roll(here, 1, axis=1))
        return here, 6.0 * here - beside - upper - lower

    zero = jnp.zeros(shape, jnp.float32)
    for ref in (dens, second, third):
        put(ref, 0, zero)
        put(ref, B + 1, zero)

    shift_on = shifter(oy, oz)
    shift_back = shifter(-oy, -oz)

    def begin(x, acc):
        src = x - ox
        inside = jnp.where((src >= 0) & (src < B), 1.0, 0.0)
        moved = shift_on(box_b, jnp.clip(src, 0, B - 1) + 1, from_b) * inside
        density = box_a[pl.ds((x + 1) * ROWS - from_a, ROWS)] * moved
        put(part, x, moved)
        put(dens, x + 1, density)
        return acc + density * density

    def first(x, acc):
        here, img = apply(dens, x)
        put(image, x + 1, img)
        return acc + here * img

    norm0 = yield begin
    step0 = norm0 / (yield first)

    def rest0(x, acc):
        left = plane(dens, x + 1) - step0 * plane(image, x + 1)
        put(resid, x, left)
        return acc + left * left

    norm1 = yield rest0
    ratio0 = norm1 / norm0

    def turn1(x, acc):
        put(second, x + 1, plane(resid, x) + ratio0 * plane(dens, x + 1))
        return acc

    def again(x, acc):
        here, img = apply(second, x)
        put(image, x + 1, img)
        return acc + here * img

    yield turn1
    step1 = norm1 / (yield again)

    def rest1(x, acc):
        left = plane(resid, x) - step1 * plane(image, x + 1)
        put(resid, x, left)
        return acc + left * left

    norm2 = yield rest1
    ratio1 = norm2 / norm1

    def turn2(x, acc):
        put(third, x + 1, plane(resid, x) + ratio1 * plane(second, x + 1))
        return acc

    def last(x, acc):
        here, img = apply(third, x)
        return acc + here * img

    yield turn2
    step2 = norm2 / (yield last)

    def finish(x, acc):
        potential = step0 * plane(dens, x + 1) + step1 * plane(second, x + 1) + step2 * plane(third, x + 1)
        here = pl.ds((x + 1) * ROWS - from_a, ROWS)
        term_a[here] = potential * plane(part, x)
        put(image, x + 1, potential * box_a[here])
        return acc

    def back(x, acc):
        src = x + ox
        inside = jnp.where((src >= 0) & (src < B), 1.0, 0.0)
        term_b[pl.ds((x + 1) * ROWS - from_b, ROWS)] = shift_back(image, jnp.clip(src, 0, B - 1) + 1, 0) * inside
        return acc

    yield finish
    yield back


def run_together(solvers, unroll):
    steps = [next(solver) for solver in solvers]
    zero = jnp.zeros((ROWS, 128), jnp.float32)
    while True:
        def both(x, accs, steps=tuple(steps)):
            return tuple(step(x, acc) for step, acc in zip(steps, accs))

        accs = lax.fori_loop(0, B, both, (zero,) * len(steps), unroll=unroll)
        sums = [jnp.sum(acc, keepdims=True) for acc in accs]
        try:
            steps = [solver.send(value) for solver, value in zip(solvers, sums)]
        except StopIteration:
            return


def pair_kernel(place_ref, pos_ref, anchor_ref, near_ref, far_ref, near_out, far_out, boxes, terms, *rest):
    *fields, sem = rest
    lines = near_ref.shape[1]
    cut = lines - ROWS
    at = [s * B + place_ref[0] for s in range(PAIR_DEV)]
    flags = [pos_ref[4, k] for k in at]
    copies = []
    for s in range(PAIR_DEV):
        for k, ref in enumerate((near_ref, far_ref)):
            which = 1 - flags[s] if k else flags[s]
            source = ref.at[:, pl.ds(s * cut, ROWS)]
            copies.append(pltpu.make_async_copy(source, boxes.at[s, which, pl.ds(1, B)], sem.at[s, k]))
    for copy in copies:
        copy.start()
    for s in range(PAIR_DEV):
        for k in range(2):
            clear_ends(boxes.at[s, k])
    for copy in copies:
        copy.wait()
    solvers = []
    for s in range(PAIR_DEV):
        orb_a, orb_b = pos_ref[2, at[s]], pos_ref[3, at[s]]
        offset = [anchor_ref[3 * orb_b + k] - anchor_ref[3 * orb_a + k] for k in range(3)]
        spare = pos_ref[5, at[s]]
        moved = spare if s else 0
        from_a = jnp.where(offset[1] > 0, spare, 0) - moved
        from_b = jnp.where(offset[1] < 0, spare, 0) - moved
        refs = [flat(ref.at[s, k]) for ref in (boxes, terms) for k in range(2)]
        solvers.append(solve_pair(offset, from_a, from_b, *refs, *[ref.at[s] for ref in fields]))
    run_together(solvers, UNROLL if cut < ROWS else 1)

    def together(x, carry):
        for k, out in enumerate((near_out, far_out)):
            first, second = [terms[s, 1 - flags[s] if k else flags[s], x + 1] for s in range(PAIR_DEV)]
            out[x, :cut] = first[:cut]
            if cut < ROWS:
                low = its_lines(0, pos_ref[5, at[0]], first)[cut:]
                out[x, cut:ROWS] = low + its_lines(1, pos_ref[5, at[1]], second)[: ROWS - cut]
            out[x, ROWS:] = second[ROWS - cut :]
        return carry

    lax.fori_loop(0, B, together, 0, unroll=4)


def solve(place, pos, anchors, near, far):
    smem, vmem = pl.BlockSpec(memory_space=pltpu.SMEM), pl.BlockSpec(memory_space=pltpu.VMEM)
    anywhere = pl.BlockSpec(memory_space=pl.ANY)
    field = pltpu.VMEM((PAIR_DEV, B * ROWS, 128), jnp.float32)
    padded = pltpu.VMEM((PAIR_DEV, (B + 2) * ROWS, 128), jnp.float32)
    boxes = pltpu.VMEM((PAIR_DEV, 2, B + 2, ROWS, 128), jnp.float32)
    return pl.pallas_call(
        pair_kernel,
        out_shape=[jax.ShapeDtypeStruct(near.shape, jnp.float32)] * 2,
        in_specs=[smem, smem, smem, anywhere, anywhere],
        out_specs=[vmem, vmem],
        scratch_shapes=[
            boxes, boxes, field, padded, field, padded, padded, padded,
            pltpu.SemaphoreType.DMA((PAIR_DEV, 2)),
        ],
        compiler_params=pltpu.CompilerParams(vmem_limit_bytes=40 << 20),
        cost_estimate=pl.CostEstimate(flops=100_000_000, bytes_accessed=30_000_000, transcendentals=0),
        name="solve",
    )(place, pos, anchors, near, far)


def add_lines(total, line, lines):
    here = pl.ds(line + ROWS, ROWS)
    total[here] = total[here] + lines


def add_far_kernel(pos_ref, terms_ref, out_ref):
    out_ref[...] = jnp.zeros(out_ref.shape, jnp.float32)
    total = flat(out_ref)
    cut = terms_ref.shape[1] - ROWS

    def here(p, carry):
        for s in range(PAIR_DEV):
            q = s * B + p

            @pl.when(pos_ref[6, q] < 128)
            def _(q=q, s=s):
                lines = terms_ref[p, s * cut : s * cut + ROWS]
                add_lines(total, pos_ref[1, q], its_lines(s, pos_ref[5, q], lines))

        return carry

    lax.fori_loop(0, B, here, 0)


def add_far(pos, terms):
    smem, vmem = pl.BlockSpec(memory_space=pltpu.SMEM), pl.BlockSpec(memory_space=pltpu.VMEM)
    return pl.pallas_call(
        add_far_kernel,
        out_shape=jax.ShapeDtypeStruct((130, ROWS, 128), jnp.float32),
        in_specs=[smem, vmem],
        out_specs=vmem,
        compiler_params=pltpu.CompilerParams(vmem_limit_bytes=24 << 20),
        cost_estimate=pl.CostEstimate(flops=2_000_000, bytes_accessed=4_000_000, transcendentals=0),
        name="add_far",
    )(pos, terms)


def add_arrived_kernel(slot_ref, sum_ref, *refs):
    *from_groups, out_ref, sem = refs
    copy = pltpu.make_async_copy(sum_ref, out_ref, sem)
    copy.start()
    copy.wait()
    total = flat(out_ref)

    def there(k, carry):
        for d, ref in enumerate(from_groups):
            at = d * KEEP + k

            @pl.when(slot_ref[2, at] == 1)
            def _(at=at, ref=ref):
                add_lines(total, slot_ref[3, at], ref[k])

        return carry

    lax.fori_loop(0, KEEP, there, 0)


def add_arrived(slot, summed, from_groups):
    smem, vmem = pl.BlockSpec(memory_space=pltpu.SMEM), pl.BlockSpec(memory_space=pltpu.VMEM)
    return pl.pallas_call(
        add_arrived_kernel,
        out_shape=jax.ShapeDtypeStruct(summed.shape, jnp.float32),
        in_specs=[smem, pl.BlockSpec(memory_space=pl.ANY)] + [vmem] * 3,
        out_specs=vmem,
        scratch_shapes=[pltpu.SemaphoreType.DMA],
        compiler_params=pltpu.CompilerParams(vmem_limit_bytes=63 << 20),
        cost_estimate=pl.CostEstimate(flops=2_000_000, bytes_accessed=6_000_000, transcendentals=0),
        name="add_arrived",
    )(slot, summed, *from_groups)


def add_near_kernel(pos_ref, sum_ref, terms_ref, out_ref, acc, terms, stage, sem_sum, sem_in, sem_out):
    cut = terms.shape[1] - ROWS
    copies = [pltpu.make_async_copy(sum_ref, acc, sem_sum)]
    for k in range(PARTS):
        mine = pl.ds(k * (B // PARTS), B // PARTS)
        copies.append(pltpu.make_async_copy(terms_ref.at[mine], terms.at[mine], sem_in.at[k]))
    for copy in copies:
        copy.start()
    copies[0].wait()
    for k in range(PARTS):
        copies[k + 1].wait()

        def here(p, carry):
            for s in range(PAIR_DEV):
                q = s * B + p
                lines = terms[p, s * cut : s * cut + ROWS]
                add_lines(flat(acc), pos_ref[0, q], its_lines(s, pos_ref[5, q], lines))
            return carry

        lax.fori_loop(k * (B // PARTS), (k + 1) * (B // PARTS), here, 0, unroll=2)
    pushes = []
    for k in range(PARTS):

        def lay_out(i, carry, k=k):
            rows = pl.ds(pl.multiple_of(i * 8, 8), 8)
            lines = jnp.swapaxes(acc[pl.ds(i * 8 + 1, 8), k * 8 : k * 8 + 8], 0, 1)
            for j in range(8):
                stage[k, rows, j * 128 : (j + 1) * 128] = lines[j]
            return carry

        lax.fori_loop(0, 128 // 8, lay_out, 0, unroll=2)
        pushes.append(pltpu.make_async_copy(stage.at[k], out_ref.at[:, pl.ds(k * 1024, 1024)], sem_out.at[k]))
        pushes[-1].start()
    for copy in pushes:
        copy.wait()


def add_near(pos, summed, terms):
    anywhere = pl.BlockSpec(memory_space=pl.ANY)
    dma = pltpu.SemaphoreType.DMA((PARTS,))
    return pl.pallas_call(
        add_near_kernel,
        out_shape=jax.ShapeDtypeStruct((128, ROWS * 128), jnp.float32),
        in_specs=[pl.BlockSpec(memory_space=pltpu.SMEM), anywhere, anywhere],
        out_specs=anywhere,
        scratch_shapes=[
            pltpu.VMEM((130, ROWS, 128), jnp.float32),
            pltpu.VMEM(terms.shape, jnp.float32),
            pltpu.VMEM((PARTS, 128, 1024), jnp.float32),
            pltpu.SemaphoreType.DMA,
            dma,
            dma,
        ],
        compiler_params=pltpu.CompilerParams(vmem_limit_bytes=63 << 20),
        cost_estimate=pl.CostEstimate(flops=2_000_000, bytes_accessed=10_000_000, transcendentals=0),
        name="add_near",
    )(pos, summed, terms)


def turned(x, shift):
    groups = lax.axis_size("grp")
    return lax.ppermute(x, "grp", [(g, (g + shift) % groups) for g in range(groups)])


def exchanged(planes):
    return lax.all_to_all(planes, "grid", 0, 0, tiled=True)


def there_and_back(place, pos, anchors, both):
    lines = both.shape[1] // 2

    def solve_both(both):
        return jnp.concatenate(solve(place, pos, anchors, both[:, :lines], both[:, lines:]), axis=1)

    def step(k, both):
        return lax.cond(k == 0, solve_both, lambda x: x, exchanged(both))

    return lax.fori_loop(0, 2, step, both)


def fitting(lines, orbitals, anchors, place, pos, slot, used):
    def used_row(used_ref, table, i):
        p, s, spare = used_ref[0, i], used_ref[1, i], used_ref[2, i]
        plane = table[p, pl.ds(pl.multiple_of(s * (lines - ROWS), 8), ROWS)]
        keep = (line_no() >= s * spare) & (line_no() < ROWS - (1 - s) * spare)
        return jnp.where(keep, plane, 0.0)

    trimmed = lines == TRIMMED
    near = deal_near(lines, pos, orbitals)
    if trimmed:
        near = exchanged(near)
    local = orbitals.reshape(128, ROWS, 128)
    arrived = [turned(x, d) for d, x in enumerate(fetch(slot, local, sent_row, "send"), 1)]
    far = deal_far(lines, 1, pos, [local] + arrived)
    if trimmed:
        near_terms, far_terms = solve(place, pos, anchors.reshape(-1), near, exchanged(far))
        far_terms = exchanged(far_terms)
    else:
        both = there_and_back(place, pos, anchors.reshape(-1), jnp.concatenate([near, far], axis=1))
        near_terms, far_terms = both[:, :lines], both[:, lines:]
    from_groups = [turned(x, -d) for d, x in enumerate(fetch(used, far_terms, used_row, "back"), 1)]
    summed = add_far(pos, far_terms)
    if trimmed:
        near_terms = exchanged(near_terms)
    return add_near(pos, add_arrived(slot, summed, from_groups), near_terms)


def add_all_kernel(pos_ref, terms_ref, out_ref):
    out_ref[...] = jnp.zeros(out_ref.shape, jnp.float32)
    total = flat(out_ref)

    def here(p, carry):
        for s in range(PAIR_DEV):
            for k in range(2):
                at = (k * PAIR_DEV + s) * ROWS
                add_lines(total, pos_ref[k, s * B + p], terms_ref[p, at : at + ROWS])
        return carry

    lax.fori_loop(0, B, here, 0)


def add_all(pos, terms, count):
    return pl.pallas_call(
        add_all_kernel,
        out_shape=jax.ShapeDtypeStruct((count + 2, ROWS, 128), jnp.float32),
        in_specs=[pl.BlockSpec(memory_space=pltpu.SMEM), pl.BlockSpec(memory_space=pltpu.VMEM)],
        out_specs=pl.BlockSpec(memory_space=pltpu.VMEM),
        compiler_params=pltpu.CompilerParams(vmem_limit_bytes=32 << 20),
        cost_estimate=pl.CostEstimate(flops=2_000_000, bytes_accessed=10_000_000, transcendentals=0),
        name="add_all",
    )(pos, terms)


def general(orbitals, anchors, pair_slots, place):
    groups, grid_count = lax.axis_size("grp"), lax.axis_size("grid")
    me, rows = lax.axis_index("grp"), orbitals.shape[0]
    dealt = deal_evenly(pair_slots, groups * grid_count, PAIR_DEV)
    own = lax.dynamic_slice_in_dim(dealt, me * grid_count, grid_count, 0)
    own = jnp.maximum(jnp.transpose(own, (2, 1, 0)).reshape(2, PAIR_DEV * grid_count), 0)
    pos = jnp.concatenate([own * ROWS, own, jnp.zeros((4, own.shape[1]), jnp.int32)])
    round_trip = [turned(orbitals, d) for d in (3, 2, 1)] + [orbitals]
    pieces = lax.dynamic_slice_in_dim(jnp.concatenate(round_trip * 2), (3 - me) * rows, groups * rows, 0)
    table = pieces.reshape(-1, ROWS, 128)
    both = jnp.concatenate([deal_far(PAIR_DEV * ROWS, k, pos, [table]) for k in range(2)], axis=1)

    terms = there_and_back(place, pos, anchors.reshape(-1), both)
    summed = add_all(pos, terms, table.shape[0])
    blocks = [lax.dynamic_slice_in_dim(summed, ((me + d) & 3) * rows + 1, rows, 0) for d in range(4)]
    return (blocks[0] + sum(turned(blocks[d], d) for d in (1, 2, 3))).reshape(orbitals.shape)


def body(orbitals, anchors, pair_slots):
    me = lax.axis_index("grp").astype(jnp.int32)[None]
    place = lax.axis_index("grid").astype(jnp.int32)[None]
    pos, slot, used, mode = route(me, pair_slots, anchors)

    def other():
        return lax.cond(
            mode[0] == 1,
            lambda: fitting(PAIR_DEV * ROWS, orbitals, anchors, place, pos, slot, used),
            lambda: general(orbitals, anchors, pair_slots, place),
        )

    return lax.cond(mode[0] == 0, lambda: fitting(TRIMMED, orbitals, anchors, place, pos, slot, used), other)


def solution(mesh):
    return jax.shard_map(
        body,
        mesh=mesh,
        in_specs=(P("grp", "grid"), P(), P()),
        out_specs=P("grp", "grid"),
        check_vma=False,
    )
```

```python
import functools

import jax
import jax.numpy as jnp
from jax import lax
from jax.experimental import pallas as pl
from jax.experimental.pallas import tpu as pltpu
from jax.sharding import PartitionSpec as P

B = 64
PAIR_DEV = 2
ITERS = 3
ROWS = B * B // 128
KEEP = 48
UNROLL = 16
TRIMMED = 56


def deal_evenly(pair_slots, owner_count, each_owner):
    flat_slots = pair_slots.reshape(-1, 2)
    filled = (flat_slots[:, 0] >= 0).astype(jnp.int32)
    order = jnp.arange(flat_slots.shape[0], dtype=jnp.int32)
    position = jnp.sum(jnp.where(order[None, :] < order[:, None], filled[None, :], 0), axis=1)
    wanted = lax.broadcasted_iota(jnp.int32, (owner_count, each_owner), 1) * owner_count
    wanted = (wanted + lax.broadcasted_iota(jnp.int32, (owner_count, each_owner), 0)).reshape(-1)
    matched = (position[None, :] == wanted[:, None]) & (filled[None, :] == 1)
    picked = jnp.dot(matched.astype(jnp.int32), flat_slots)
    return picked.reshape(owner_count, each_owner, 2)


def route_kernel(me_ref, pair_ref, anchor_ref, pos_ref, slot_ref, used_ref, mode_ref):
    me = me_ref[0]
    f32, i32 = jnp.float32, jnp.int32
    groups, each = 4, 2 * B

    def col(x):
        return jnp.sum(x, axis=1, keepdims=True)

    pairs = pair_ref[...].astype(f32).T
    at = lax.broadcasted_iota(i32, pairs.shape, 1)
    columns = [col(jnp.where(at == k, pairs, 0.0)) for k in range(pairs.shape[1])]
    a = jnp.concatenate(columns[0::2], axis=0).astype(i32)
    b = jnp.concatenate(columns[1::2], axis=0).astype(i32)
    n = a.shape[0]

    before = lax.broadcasted_iota(i32, (128, 128), 0) > lax.broadcasted_iota(i32, (128, 128), 1)
    before = jnp.where(before, 1.0, 0.0).astype(jnp.bfloat16)

    def sort_in(hot):
        width = hot.shape[1]
        totals = jnp.sum(hot, axis=0, keepdims=True)
        key = lax.broadcasted_iota(i32, (8, width), 1) & 15
        running = jnp.broadcast_to(totals, (8, width))
        for step in (1, 2, 4, 8):
            running = running + jnp.where(key >= step, pltpu.roll(running, step, axis=1), 0.0)
        below = running[0:1] - totals
        ranks, passed = [], below
        for k in range(0, n, 128):
            part = hot[k : k + 128]
            ahead = jnp.dot(before, part.astype(jnp.bfloat16), preferred_element_type=f32) + passed
            ranks.append(col(ahead * part))
            passed = passed + jnp.sum(part, axis=0, keepdims=True)
        return jnp.concatenate(ranks, axis=0), totals, below

    lane = lax.broadcasted_iota(i32, (n, 128), 1)
    valid = a >= 0
    ga, gb = a >> 7, b >> 7
    low, high = jnp.minimum(ga, gb), jnp.maximum(ga, gb)
    anchor_y = anchor_ref[1:2].astype(f32)
    name = lax.broadcasted_iota(i32, (n, anchor_ref.shape[1]), 1)
    oy = col(jnp.where(name == b, anchor_y, 0.0) - jnp.where(name == a, anchor_y, 0.0)).astype(i32)
    spare = jnp.abs(oy) >> 1
    kinds = lax.broadcasted_iota(i32, (n, 256), 1)
    hot = jnp.where(valid & (kinds == (low * groups + high) * 16 + spare), 1.0, 0.0)
    rank, sums, _ = sort_in(hot)
    sums = sums.astype(i32)
    kind1 = lax.broadcasted_iota(i32, (1, 256), 1) >> 4
    count, up = {}, {}
    for g in range(groups):
        for h in range(g, groups):
            count[g, h] = jnp.sum(jnp.where(kind1 == g * groups + h, sums, 0))
            up[g, h] = (count[g, h] >> 1) if h > g else 0

    def loads():
        load = [0] * groups
        for (g, h), c in count.items():
            load[g] = load[g] + (c - up[g, h])
            load[h] = load[h] + up[g, h]
        return load

    load = loads()
    for g, h in count:
        if h > g:
            up[g, h] = up[g, h] + ((load[g] - load[h] + 2) >> 2)
    load = loads()
    excess = 0
    for g in range(groups - 1):
        excess = excess + load[g] - each
        up[g, g + 1] = up[g, g + 1] + excess
    need = (ROWS * PAIR_DEV - TRIMMED) - 1
    fits = 1
    goes_up, there = jnp.zeros((1, 256), f32), jnp.ones((1, 256), f32)
    for (g, h), c in count.items():
        if h > g:
            u = up[g, h]
            fine = (u >= 0) & (u <= KEEP) & (c - u >= 0) & (c - u <= KEEP)
            fits = jnp.where(fine, fits, 0)
            goes_up = jnp.where(kind1 == g * groups + h, u.astype(f32), goes_up)
            there = jnp.where(kind1 == g * groups + h, jnp.maximum(c, 1).astype(f32), there)

    key1 = lax.broadcasted_iota(i32, (1, 256), 1) & 15
    weight = jnp.where(key1 <= need // 2, 1, 0) + jnp.where(key1 <= need // 2 + 1, 1, 0)
    small = {t: jnp.sum(jnp.where(kind1 == t[0] * groups + t[1], sums * weight, 0)).astype(f32) for t in count}
    share = goes_up / there
    surplus = jnp.zeros((1, 256), f32)
    for g in range(groups):
        held = jnp.zeros((1, 256), f32)
        for (low_g, high_g), amount in small.items():
            if low_g == high_g:
                held = held + (amount if low_g == g else 0.0)
            elif g in (low_g, high_g):
                part = jnp.sum(jnp.where((kind1 == low_g * groups + high_g) & (key1 == 0), share, 0.0))
                held = held + amount * (part if high_g == g else 1.0 - part)
        surplus = surplus + jnp.where((kind1 >> 2) == g, held, 0.0) - jnp.where((kind1 & 3) == g, held, 0.0)
    bend = surplus / (2.0 * jnp.maximum(goes_up, 1.0))
    most = jnp.minimum(there / jnp.maximum(goes_up, 1.0) - 1.0, 1.0)
    bend = jnp.clip(bend, -0.98 * most, 0.98 * most)
    u, c, bend = col(hot * goes_up), jnp.maximum(col(hot * there), 1.0), col(hot * bend)

    def risen_at(r):
        x = r / c
        return jnp.where(r >= c, u, jnp.clip(jnp.floor(u * (x + bend * x * (1.0 - x)) + 0.5 / c), 0.0, u))

    risen = risen_at(rank)
    rises = risen_at(rank + 1.0) > risen
    group = jnp.where(rises, high, low)
    source = low + high - group
    crosses = valid & (low != high)
    hot = jnp.where(valid & (lane == group * 16 + spare), 1.0, 0.0)
    order, keyed, below = sort_in(hot)
    order = order.astype(i32)
    second = order >= B
    q = jnp.where(second, B + each - 1 - order, order)
    lane1 = lax.broadcasted_iota(i32, (1, 128), 1)
    match = 1
    for g in range(groups):
        fits = jnp.where(jnp.sum(jnp.where((lane1 >> 4) == g, keyed, 0.0)) == each, fits, 0)
        for j in range(need // 2 + 1):
            both = (lane1 == g * 16 + j + 1) | (lane1 == g * 16 + need - j + 1)
            match = jnp.where(jnp.sum(jnp.where(both, below, 0.0)) <= each, match, 0)
    mode_ref[0] = jnp.where(fits == 1, 1 - match, 2)

    put = (((group - source) & 3) - 1) * KEEP + jnp.where(rises, risen, rank - risen).astype(i32)
    near_b = ga != group
    near = jnp.where(near_b, b, a) & 127
    far = jnp.where(near_b, a, b) & 127
    table = jnp.where(crosses, 128 + put, far)
    spare = spare * match
    moved = jnp.where(second, spare, 0)
    from_a = jnp.where(oy > 0, spare, 0) - moved
    from_b = jnp.where(oy < 0, spare, 0) - moved
    near_from, far_from = jnp.where(near_b, from_b, from_a), jnp.where(near_b, from_a, from_b)

    def side(*columns):
        at = lax.broadcasted_iota(i32, (n, 8), 1)
        out = jnp.zeros((n, 8), f32)
        for k, column in enumerate(columns):
            out = jnp.where(at == k, column.astype(f32), out)
        return out.astype(jnp.bfloat16)

    def spread(columns, mask):
        hot = jnp.where(mask, 1.0, 0.0).astype(jnp.bfloat16)
        out = lax.dot_general(columns, hot, (((0,), (0,)), ((), ())), preferred_element_type=f32)
        return out.astype(i32)

    mine = valid & (group == me)
    flag = jnp.where(near_b, 1, 0)
    columns = side(near, table & 255, a & 255, b & 255, flag, table >> 8, a >> 8, b >> 8)
    here = mine & (lane == q)
    got = spread(columns, here)
    more = spread(side(near_from + 16, far_from + 16, spare), here)
    pos_ref[...] = got
    pos_ref[1:4] = got[1:4] + 256 * got[5:8]
    pos_ref[6:7] = pos_ref[1:2]
    pos_ref[0:1] = got[0:1] * ROWS + more[0:1] - 16
    pos_ref[1:2] = pos_ref[6:7] * ROWS + more[1:2] - 16
    pos_ref[5:6] = more[2:3]
    wide = lax.broadcasted_iota(i32, (n, slot_ref.shape[1]), 1)
    here = wide == put
    zero = jnp.zeros_like(a)
    slots = spread(side(far, zero, zero + 1, far_from + 16), crosses & (source == me) & here)
    used_ref[...] = spread(side(q & (B - 1), q >> 6, spare), crosses & mine & here)
    slot_ref[...] = slots
    slot_ref[3:4] = slots[0:1] * ROWS + slots[3:4] - 16


def route(me, pair_slots, anchors):
    lists = jnp.transpose(pair_slots, (1, 2, 0)).reshape(-1, pair_slots.shape[0])
    width = 128 * -(-(3 * KEEP) // 128)
    vmem, smem = pl.BlockSpec(memory_space=pltpu.VMEM), pl.BlockSpec(memory_space=pltpu.SMEM)
    return pl.pallas_call(
        route_kernel,
        out_shape=[
            jax.ShapeDtypeStruct((8, 128), jnp.int32),
            jax.ShapeDtypeStruct((8, width), jnp.int32),
            jax.ShapeDtypeStruct((8, width), jnp.int32),
            jax.ShapeDtypeStruct((1,), jnp.int32),
        ],
        in_specs=[smem, vmem, vmem],
        out_specs=[vmem, vmem, vmem, smem],
        compiler_params=pltpu.CompilerParams(vmem_limit_bytes=40 << 20),
        cost_estimate=pl.CostEstimate(flops=10_000_000, bytes_accessed=1_000_000, transcendentals=0),
        name="route",
    )(me, lists, jnp.transpose(anchors))


def flat(ref):
    return ref.reshape(ref.shape[0] * ROWS, 128)


def fetch_kernel(row_of, idx_ref, table_ref, *refs):
    *outs, table, sem = refs
    copy = pltpu.make_async_copy(table_ref, table, sem)
    copy.start()
    copy.wait()
    for k, out_ref in enumerate(outs):
        count = out_ref.shape[0]

        def move(i, carry, out_ref=out_ref, k=k, count=count):
            out_ref[i] = row_of(idx_ref, table, k * count + i)
            return carry

        lax.fori_loop(0, count, move, 0, unroll=4)


def fetch(idx, table, row_of, name):
    return pl.pallas_call(
        functools.partial(fetch_kernel, row_of),
        out_shape=[jax.ShapeDtypeStruct((KEEP, ROWS, 128), jnp.float32)] * 3,
        in_specs=[pl.BlockSpec(memory_space=pltpu.SMEM), pl.BlockSpec(memory_space=pl.ANY)],
        out_specs=[pl.BlockSpec(memory_space=pltpu.VMEM)] * 3,
        scratch_shapes=[pltpu.VMEM(table.shape, jnp.float32), pltpu.SemaphoreType.DMA],
        compiler_params=pltpu.CompilerParams(vmem_limit_bytes=16 << 20),
        cost_estimate=pl.CostEstimate(flops=0, bytes_accessed=8_000_000, transcendentals=0),
        name=name,
    )(idx, table)


def sent_row(idx_ref, table, i):
    return table[idx_ref[0, i]]


def line_no():
    return lax.broadcasted_iota(jnp.int32, (ROWS, 128), 0)


def its_lines(s, spare, lines):
    keep = line_no() >= spare if s else line_no() < ROWS - spare
    return jnp.where(keep, lines, 0.0)


def deal_owner(pos_ref, row, p, table, out_ref, at):
    first, second = [table[pl.ds(pos_ref[row, s * B + p] + ROWS, ROWS)] for s in range(PAIR_DEV)]
    lines = out_ref.shape[1]
    cut = lines - ROWS
    out_ref[at, :cut] = first[:cut]
    if cut < ROWS:
        shared = lax.broadcasted_iota(jnp.int32, (ROWS - cut, 128), 0) + cut < ROWS - pos_ref[5, p]
        out_ref[at, cut:ROWS] = jnp.where(shared, first[cut:], second[: ROWS - cut])
    out_ref[at, ROWS:] = second[ROWS - cut :]


def clear_ends(table):
    zero = jnp.zeros((ROWS, 128), jnp.float32)
    table[0] = zero
    table[table.shape[0] - 1] = zero


PARTS = 4


def deal_near_kernel(pos_ref, orb_ref, near_ref, table, stage, near, sem_in, sem_out):
    pulls = [
        pltpu.make_async_copy(orb_ref.at[:, pl.ds(k * 1024, 1024)], stage.at[k], sem_in.at[k]) for k in range(PARTS)
    ]
    for copy in pulls:
        copy.start()
    clear_ends(table)
    for k, copy in enumerate(pulls):
        copy.wait()

        def lay_out(i, carry, k=k):
            rows = pl.ds(pl.multiple_of(i * 8, 8), 8)
            lines = [stage[k, rows, j * 128 : (j + 1) * 128] for j in range(8)]
            table[pl.ds(i * 8 + 1, 8), k * 8 : k * 8 + 8] = jnp.swapaxes(jnp.stack(lines), 0, 1)
            return carry

        lax.fori_loop(0, 128 // 8, lay_out, 0, unroll=2)
    pushes = []
    for k in range(PARTS):

        def owner(p, carry):
            deal_owner(pos_ref, 0, p, flat(table), near, p)
            return carry

        mine = pl.ds(k * (B // PARTS), B // PARTS)
        lax.fori_loop(k * (B // PARTS), (k + 1) * (B // PARTS), owner, 0, unroll=4)
        pushes.append(pltpu.make_async_copy(near.at[mine], near_ref.at[mine], sem_out.at[k]))
        pushes[-1].start()
    for copy in pushes:
        copy.wait()


def deal_near(lines, pos, orbitals):
    anywhere = pl.BlockSpec(memory_space=pl.ANY)
    dma = pltpu.SemaphoreType.DMA((PARTS,))
    return pl.pallas_call(
        deal_near_kernel,
        out_shape=jax.ShapeDtypeStruct((B, lines, 128), jnp.float32),
        in_specs=[pl.BlockSpec(memory_space=pltpu.SMEM), anywhere],
        out_specs=anywhere,
        scratch_shapes=[
            pltpu.VMEM((130, ROWS, 128), jnp.float32),
            pltpu.VMEM((PARTS, 128, 1024), jnp.float32),
            pltpu.VMEM((B, lines, 128), jnp.float32),
            dma,
            dma,
        ],
        compiler_params=pltpu.CompilerParams(vmem_limit_bytes=60 << 20),
        cost_estimate=pl.CostEstimate(flops=2_000_000, bytes_accessed=10_000_000, transcendentals=0),
        name="deal_near",
    )(pos, orbitals)


def deal_far_kernel(row, pos_ref, *refs):
    *parts, far_ref, table, sem = refs
    copies, end = [], 1
    for k, part in enumerate(parts):
        copies.append(pltpu.make_async_copy(part, table.at[pl.ds(end, part.shape[0])], sem.at[k]))
        end += part.shape[0]
    for copy in copies:
        copy.start()
    clear_ends(table)
    for copy in copies:
        copy.wait()

    def owner(p, carry):
        deal_owner(pos_ref, row, p, flat(table), far_ref, p)
        return carry

    lax.fori_loop(0, B, owner, 0, unroll=4)


def deal_far(lines, row, pos, parts):
    rows = sum(x.shape[0] for x in parts)
    return pl.pallas_call(
        functools.partial(deal_far_kernel, row),
        out_shape=jax.ShapeDtypeStruct((B, lines, 128), jnp.float32),
        in_specs=[pl.BlockSpec(memory_space=pltpu.SMEM)] + [pl.BlockSpec(memory_space=pl.ANY)] * len(parts),
        out_specs=pl.BlockSpec(memory_space=pltpu.VMEM),
        scratch_shapes=[pltpu.VMEM((rows + 2, ROWS, 128), jnp.float32), pltpu.SemaphoreType.DMA((len(parts),))],
        compiler_params=pltpu.CompilerParams(vmem_limit_bytes=32 << 20),
        cost_estimate=pl.CostEstimate(flops=0, bytes_accessed=12_000_000, transcendentals=0),
        name="deal_far",
    )(pos, *parts)


def solve_pair(offset, from_a, from_b, box_a, box_b, term_a, term_b, part, dens, resid, second, third, image):
    ox, oy, oz = offset
    shape = (ROWS, 128)
    line = lax.broadcasted_iota(jnp.int32, shape, 0)
    lane = lax.broadcasted_iota(jnp.int32, shape, 1)
    cy = 2 * line + (lane >> 6)
    cz = lane & (B - 1)
    high = lane >= B
    ends = (high & (line == 0)) | (~high & (line == ROWS - 1))
    no_up, no_down = cz == B - 1, cz == 0

    def plane(ref, x):
        return ref[pl.ds(pl.multiple_of(x * ROWS, ROWS), ROWS)]

    def put(ref, x, value):
        ref[pl.ds(pl.multiple_of(x * ROWS, ROWS), ROWS)] = value

    def shifter(sy, sz):
        flat = sy * B + sz
        lines, steps = flat >> 7, flat & 127
        inside = (cy >= sy) & (cy < B + sy) & (cz >= sz) & (cz < B + sz)
        keep = lane < 128 - steps

        def shift(ref, x, first):
            at = x * ROWS - lines - first
            moved = jnp.where(keep, ref[pl.ds(at, ROWS)], ref[pl.ds(at - 1, ROWS)])
            return jnp.where(inside, pltpu.roll(moved, steps, axis=1), 0.0)

        return shift

    def apply(ref, x):
        here = plane(ref, x + 1)
        at = (x + 1) * ROWS
        other = jnp.where(high, ref[pl.ds(at - 1, ROWS)], ref[pl.ds(at + 1, ROWS)])
        other = here + jnp.where(ends, 0.0, other)
        beside = plane(ref, x) + plane(ref, x + 2) + pltpu.roll(other, B, axis=1)
        upper = jnp.where(no_up, 0.0, pltpu.roll(here, 127, axis=1))
        lower = jnp.where(no_down, 0.0, pltpu.roll(here, 1, axis=1))
        return here, 6.0 * here - beside - upper - lower

    zero = jnp.zeros(shape, jnp.float32)
    for ref in (dens, second, third):
        put(ref, 0, zero)
        put(ref, B + 1, zero)

    shift_on = shifter(oy, oz)
    shift_back = shifter(-oy, -oz)

    def begin(x, acc):
        src = x - ox
        inside = jnp.where((src >= 0) & (src < B), 1.0, 0.0)
        moved = shift_on(box_b, jnp.clip(src, 0, B - 1) + 1, from_b) * inside
        density = box_a[pl.ds((x + 1) * ROWS - from_a, ROWS)] * moved
        put(part, x, moved)
        put(dens, x + 1, density)
        return acc + density * density

    def first(x, acc):
        here, img = apply(dens, x)
        put(image, x + 1, img)
        return acc + here * img

    norm0 = yield begin
    step0 = norm0 / (yield first)

    def rest0(x, acc):
        left = plane(dens, x + 1) - step0 * plane(image, x + 1)
        put(resid, x, left)
        return acc + left * left

    norm1 = yield rest0
    ratio0 = norm1 / norm0

    def turn1(x, acc):
        put(second, x + 1, plane(resid, x) + ratio0 * plane(dens, x + 1))
        return acc

    def again(x, acc):
        here, img = apply(second, x)
        put(image, x + 1, img)
        return acc + here * img

    yield turn1
    step1 = norm1 / (yield again)

    def rest1(x, acc):
        left = plane(resid, x) - step1 * plane(image, x + 1)
        put(resid, x, left)
        return acc + left * left

    norm2 = yield rest1
    ratio1 = norm2 / norm1

    def turn2(x, acc):
        put(third, x + 1, plane(resid, x) + ratio1 * plane(second, x + 1))
        return acc

    def last(x, acc):
        here, img = apply(third, x)
        return acc + here * img

    yield turn2
    step2 = norm2 / (yield last)

    def finish(x, acc):
        potential = step0 * plane(dens, x + 1) + step1 * plane(second, x + 1) + step2 * plane(third, x + 1)
        here = pl.ds((x + 1) * ROWS - from_a, ROWS)
        term_a[here] = potential * plane(part, x)
        put(image, x + 1, potential * box_a[here])
        return acc

    def back(x, acc):
        src = x + ox
        inside = jnp.where((src >= 0) & (src < B), 1.0, 0.0)
        term_b[pl.ds((x + 1) * ROWS - from_b, ROWS)] = shift_back(image, jnp.clip(src, 0, B - 1) + 1, 0) * inside
        return acc

    yield finish
    yield back


def run_together(solvers, unroll):
    steps = [next(solver) for solver in solvers]
    zero = jnp.zeros((ROWS, 128), jnp.float32)
    while True:
        def both(x, accs, steps=tuple(steps)):
            return tuple(step(x, acc) for step, acc in zip(steps, accs))

        accs = lax.fori_loop(0, B, both, (zero,) * len(steps), unroll=unroll)
        sums = [jnp.sum(acc, keepdims=True) for acc in accs]
        try:
            steps = [solver.send(value) for solver, value in zip(solvers, sums)]
        except StopIteration:
            return


def pair_kernel(place_ref, pos_ref, anchor_ref, near_ref, far_ref, near_out, far_out, boxes, terms, *rest):
    *fields, sem = rest
    lines = near_ref.shape[1]
    cut = lines - ROWS
    at = [s * B + place_ref[0] for s in range(PAIR_DEV)]
    flags = [pos_ref[4, k] for k in at]
    copies = []
    for s in range(PAIR_DEV):
        for k, ref in enumerate((near_ref, far_ref)):
            which = 1 - flags[s] if k else flags[s]
            source = ref.at[:, pl.ds(s * cut, ROWS)]
            copies.append(pltpu.make_async_copy(source, boxes.at[s, which, pl.ds(1, B)], sem.at[s, k]))
    for copy in copies:
        copy.start()
    for s in range(PAIR_DEV):
        for k in range(2):
            clear_ends(boxes.at[s, k])
    for copy in copies:
        copy.wait()
    solvers = []
    for s in range(PAIR_DEV):
        orb_a, orb_b = pos_ref[2, at[s]], pos_ref[3, at[s]]
        offset = [anchor_ref[3 * orb_b + k] - anchor_ref[3 * orb_a + k] for k in range(3)]
        spare = pos_ref[5, at[s]]
        moved = spare if s else 0
        from_a = jnp.where(offset[1] > 0, spare, 0) - moved
        from_b = jnp.where(offset[1] < 0, spare, 0) - moved
        refs = [flat(ref.at[s, k]) for ref in (boxes, terms) for k in range(2)]
        solvers.append(solve_pair(offset, from_a, from_b, *refs, *[ref.at[s] for ref in fields]))
    run_together(solvers, UNROLL if cut < ROWS else 1)

    def together(x, carry):
        for k, out in enumerate((near_out, far_out)):
            first, second = [terms[s, 1 - flags[s] if k else flags[s], x + 1] for s in range(PAIR_DEV)]
            out[x, :cut] = first[:cut]
            if cut < ROWS:
                low = its_lines(0, pos_ref[5, at[0]], first)[cut:]
                out[x, cut:ROWS] = low + its_lines(1, pos_ref[5, at[1]], second)[: ROWS - cut]
            out[x, ROWS:] = second[ROWS - cut :]
        return carry

    lax.fori_loop(0, B, together, 0, unroll=4)


def solve(place, pos, anchors, near, far):
    smem, vmem = pl.BlockSpec(memory_space=pltpu.SMEM), pl.BlockSpec(memory_space=pltpu.VMEM)
    anywhere = pl.BlockSpec(memory_space=pl.ANY)
    field = pltpu.VMEM((PAIR_DEV, B * ROWS, 128), jnp.float32)
    padded = pltpu.VMEM((PAIR_DEV, (B + 2) * ROWS, 128), jnp.float32)
    boxes = pltpu.VMEM((PAIR_DEV, 2, B + 2, ROWS, 128), jnp.float32)
    return pl.pallas_call(
        pair_kernel,
        out_shape=[jax.ShapeDtypeStruct(near.shape, jnp.float32)] * 2,
        in_specs=[smem, smem, smem, anywhere, anywhere],
        out_specs=[vmem, vmem],
        scratch_shapes=[
            boxes, boxes, field, padded, field, padded, padded, padded,
            pltpu.SemaphoreType.DMA((PAIR_DEV, 2)),
        ],
        compiler_params=pltpu.CompilerParams(vmem_limit_bytes=40 << 20),
        cost_estimate=pl.CostEstimate(flops=100_000_000, bytes_accessed=30_000_000, transcendentals=0),
        name="solve",
    )(place, pos, anchors, near, far)


def add_lines(total, line, lines):
    here = pl.ds(line + ROWS, ROWS)
    total[here] = total[here] + lines


def add_far_kernel(pos_ref, terms_ref, out_ref):
    out_ref[...] = jnp.zeros(out_ref.shape, jnp.float32)
    total = flat(out_ref)
    cut = terms_ref.shape[1] - ROWS

    def here(p, carry):
        for s in range(PAIR_DEV):
            q = s * B + p

            @pl.when(pos_ref[6, q] < 128)
            def _(q=q, s=s):
                lines = terms_ref[p, s * cut : s * cut + ROWS]
                add_lines(total, pos_ref[1, q], its_lines(s, pos_ref[5, q], lines))

        return carry

    lax.fori_loop(0, B, here, 0)


def add_far(pos, terms):
    smem, vmem = pl.BlockSpec(memory_space=pltpu.SMEM), pl.BlockSpec(memory_space=pltpu.VMEM)
    return pl.pallas_call(
        add_far_kernel,
        out_shape=jax.ShapeDtypeStruct((130, ROWS, 128), jnp.float32),
        in_specs=[smem, vmem],
        out_specs=vmem,
        compiler_params=pltpu.CompilerParams(vmem_limit_bytes=24 << 20),
        cost_estimate=pl.CostEstimate(flops=2_000_000, bytes_accessed=4_000_000, transcendentals=0),
        name="add_far",
    )(pos, terms)


def add_arrived_kernel(slot_ref, sum_ref, *refs):
    *from_groups, out_ref, sem = refs
    copy = pltpu.make_async_copy(sum_ref, out_ref, sem)
    copy.start()
    copy.wait()
    total = flat(out_ref)

    def there(k, carry):
        for d, ref in enumerate(from_groups):
            at = d * KEEP + k

            @pl.when(slot_ref[2, at] == 1)
            def _(at=at, ref=ref):
                add_lines(total, slot_ref[3, at], ref[k])

        return carry

    lax.fori_loop(0, KEEP, there, 0)


def add_arrived(slot, summed, from_groups):
    smem, vmem = pl.BlockSpec(memory_space=pltpu.SMEM), pl.BlockSpec(memory_space=pltpu.VMEM)
    return pl.pallas_call(
        add_arrived_kernel,
        out_shape=jax.ShapeDtypeStruct(summed.shape, jnp.float32),
        in_specs=[smem, pl.BlockSpec(memory_space=pl.ANY)] + [vmem] * 3,
        out_specs=vmem,
        scratch_shapes=[pltpu.SemaphoreType.DMA],
        compiler_params=pltpu.CompilerParams(vmem_limit_bytes=24 << 20),
        cost_estimate=pl.CostEstimate(flops=2_000_000, bytes_accessed=6_000_000, transcendentals=0),
        name="add_arrived",
    )(slot, summed, *from_groups)


def add_near_kernel(pos_ref, sum_ref, terms_ref, out_ref, acc, terms, stage, sem_sum, sem_in, sem_out):
    cut = terms.shape[1] - ROWS
    copies = [pltpu.make_async_copy(sum_ref, acc, sem_sum)]
    for k in range(PARTS):
        mine = pl.ds(k * (B // PARTS), B // PARTS)
        copies.append(pltpu.make_async_copy(terms_ref.at[mine], terms.at[mine], sem_in.at[k]))
    for copy in copies:
        copy.start()
    copies[0].wait()
    for k in range(PARTS):
        copies[k + 1].wait()

        def here(p, carry):
            for s in range(PAIR_DEV):
                q = s * B + p
                lines = terms[p, s * cut : s * cut + ROWS]
                add_lines(flat(acc), pos_ref[0, q], its_lines(s, pos_ref[5, q], lines))
            return carry

        lax.fori_loop(k * (B // PARTS), (k + 1) * (B // PARTS), here, 0, unroll=2)
    pushes = []
    for k in range(PARTS):

        def lay_out(i, carry, k=k):
            rows = pl.ds(pl.multiple_of(i * 8, 8), 8)
            lines = jnp.swapaxes(acc[pl.ds(i * 8 + 1, 8), k * 8 : k * 8 + 8], 0, 1)
            for j in range(8):
                stage[k, rows, j * 128 : (j + 1) * 128] = lines[j]
            return carry

        lax.fori_loop(0, 128 // 8, lay_out, 0, unroll=2)
        pushes.append(pltpu.make_async_copy(stage.at[k], out_ref.at[:, pl.ds(k * 1024, 1024)], sem_out.at[k]))
        pushes[-1].start()
    for copy in pushes:
        copy.wait()


def add_near(pos, summed, terms):
    anywhere = pl.BlockSpec(memory_space=pl.ANY)
    dma = pltpu.SemaphoreType.DMA((PARTS,))
    return pl.pallas_call(
        add_near_kernel,
        out_shape=jax.ShapeDtypeStruct((128, ROWS * 128), jnp.float32),
        in_specs=[pl.BlockSpec(memory_space=pltpu.SMEM), anywhere, anywhere],
        out_specs=anywhere,
        scratch_shapes=[
            pltpu.VMEM((130, ROWS, 128), jnp.float32),
            pltpu.VMEM(terms.shape, jnp.float32),
            pltpu.VMEM((PARTS, 128, 1024), jnp.float32),
            pltpu.SemaphoreType.DMA,
            dma,
            dma,
        ],
        compiler_params=pltpu.CompilerParams(vmem_limit_bytes=63 << 20),
        cost_estimate=pl.CostEstimate(flops=2_000_000, bytes_accessed=10_000_000, transcendentals=0),
        name="add_near",
    )(pos, summed, terms)


def turned(x, shift):
    groups = lax.axis_size("grp")
    return lax.ppermute(x, "grp", [(g, (g + shift) % groups) for g in range(groups)])


def exchanged(planes):
    return lax.all_to_all(planes, "grid", 0, 0, tiled=True)


def there_and_back(place, pos, anchors, both):
    lines = both.shape[1] // 2

    def solve_both(both):
        return jnp.concatenate(solve(place, pos, anchors, both[:, :lines], both[:, lines:]), axis=1)

    def step(k, both):
        return lax.cond(k == 0, solve_both, lambda x: x, exchanged(both))

    return lax.fori_loop(0, 2, step, both)


def fitting(lines, orbitals, anchors, place, pos, slot, used):
    def used_row(used_ref, table, i):
        p, s, spare = used_ref[0, i], used_ref[1, i], used_ref[2, i]
        plane = table[p, pl.ds(pl.multiple_of(s * (lines - ROWS), 8), ROWS)]
        keep = (line_no() >= s * spare) & (line_no() < ROWS - (1 - s) * spare)
        return jnp.where(keep, plane, 0.0)

    trimmed = lines == TRIMMED
    near = deal_near(lines, pos, orbitals)
    if trimmed:
        near = exchanged(near)
    local = orbitals.reshape(128, ROWS, 128)
    arrived = [turned(x, d) for d, x in enumerate(fetch(slot, local, sent_row, "send"), 1)]
    far = deal_far(lines, 1, pos, [local] + arrived)
    if trimmed:
        near_terms, far_terms = solve(place, pos, anchors.reshape(-1), near, exchanged(far))
        far_terms = exchanged(far_terms)
    else:
        both = there_and_back(place, pos, anchors.reshape(-1), jnp.concatenate([near, far], axis=1))
        near_terms, far_terms = both[:, :lines], both[:, lines:]
    from_groups = [turned(x, -d) for d, x in enumerate(fetch(used, far_terms, used_row, "back"), 1)]
    summed = add_far(pos, far_terms)
    if trimmed:
        near_terms = exchanged(near_terms)
    return add_near(pos, add_arrived(slot, summed, from_groups), near_terms)


def add_all_kernel(pos_ref, terms_ref, out_ref):
    out_ref[...] = jnp.zeros(out_ref.shape, jnp.float32)
    total = flat(out_ref)

    def here(p, carry):
        for s in range(PAIR_DEV):
            for k in range(2):
                at = (k * PAIR_DEV + s) * ROWS
                add_lines(total, pos_ref[k, s * B + p], terms_ref[p, at : at + ROWS])
        return carry

    lax.fori_loop(0, B, here, 0)


def add_all(pos, terms, count):
    return pl.pallas_call(
        add_all_kernel,
        out_shape=jax.ShapeDtypeStruct((count + 2, ROWS, 128), jnp.float32),
        in_specs=[pl.BlockSpec(memory_space=pltpu.SMEM), pl.BlockSpec(memory_space=pltpu.VMEM)],
        out_specs=pl.BlockSpec(memory_space=pltpu.VMEM),
        compiler_params=pltpu.CompilerParams(vmem_limit_bytes=32 << 20),
        cost_estimate=pl.CostEstimate(flops=2_000_000, bytes_accessed=10_000_000, transcendentals=0),
        name="add_all",
    )(pos, terms)


def general(orbitals, anchors, pair_slots, place):
    groups, grid_count = lax.axis_size("grp"), lax.axis_size("grid")
    me, rows = lax.axis_index("grp"), orbitals.shape[0]
    dealt = deal_evenly(pair_slots, groups * grid_count, PAIR_DEV)
    own = lax.dynamic_slice_in_dim(dealt, me * grid_count, grid_count, 0)
    own = jnp.maximum(jnp.transpose(own, (2, 1, 0)).reshape(2, PAIR_DEV * grid_count), 0)
    pos = jnp.concatenate([own * ROWS, own, jnp.zeros((4, own.shape[1]), jnp.int32)])
    round_trip = [turned(orbitals, d) for d in (3, 2, 1)] + [orbitals]
    pieces = lax.dynamic_slice_in_dim(jnp.concatenate(round_trip * 2), (3 - me) * rows, groups * rows, 0)
    table = pieces.reshape(-1, ROWS, 128)
    both = jnp.concatenate([deal_far(PAIR_DEV * ROWS, k, pos, [table]) for k in range(2)], axis=1)

    terms = there_and_back(place, pos, anchors.reshape(-1), both)
    summed = add_all(pos, terms, table.shape[0])
    blocks = [lax.dynamic_slice_in_dim(summed, ((me + d) & 3) * rows + 1, rows, 0) for d in range(4)]
    return (blocks[0] + sum(turned(blocks[d], d) for d in (1, 2, 3))).reshape(orbitals.shape)


def body(orbitals, anchors, pair_slots):
    me = lax.axis_index("grp").astype(jnp.int32)[None]
    place = lax.axis_index("grid").astype(jnp.int32)[None]
    pos, slot, used, mode = route(me, pair_slots, anchors)

    def other():
        return lax.cond(
            mode[0] == 1,
            lambda: fitting(PAIR_DEV * ROWS, orbitals, anchors, place, pos, slot, used),
            lambda: general(orbitals, anchors, pair_slots, place),
        )

    return lax.cond(mode[0] == 0, lambda: fitting(TRIMMED, orbitals, anchors, place, pos, slot, used), other)


def solution(mesh):
    return jax.shard_map(
        body,
        mesh=mesh,
        in_specs=(P("grp", "grid"), P(), P()),
        out_specs=P("grp", "grid"),
        check_vma=False,
    )
```

```python
import functools

import jax
import jax.numpy as jnp
from jax import lax
from jax.experimental import pallas as pl
from jax.experimental.pallas import tpu as pltpu
from jax.sharding import PartitionSpec as P

B = 64
PAIR_DEV = 2
ITERS = 3
ROWS = B * B // 128
KEEP = 48
UNROLL = 32
TRIMMED = 56


def deal_evenly(pair_slots, owner_count, each_owner):
    flat_slots = pair_slots.reshape(-1, 2)
    filled = (flat_slots[:, 0] >= 0).astype(jnp.int32)
    order = jnp.arange(flat_slots.shape[0], dtype=jnp.int32)
    position = jnp.sum(jnp.where(order[None, :] < order[:, None], filled[None, :], 0), axis=1)
    wanted = lax.broadcasted_iota(jnp.int32, (owner_count, each_owner), 1) * owner_count
    wanted = (wanted + lax.broadcasted_iota(jnp.int32, (owner_count, each_owner), 0)).reshape(-1)
    matched = (position[None, :] == wanted[:, None]) & (filled[None, :] == 1)
    picked = jnp.dot(matched.astype(jnp.int32), flat_slots)
    return picked.reshape(owner_count, each_owner, 2)


def route_kernel(me_ref, pair_ref, anchor_ref, pos_ref, slot_ref, used_ref, mode_ref):
    me = me_ref[0]
    f32, i32 = jnp.float32, jnp.int32
    groups, each = 4, 2 * B

    def col(x):
        return jnp.sum(x, axis=1, keepdims=True)

    pairs = pair_ref[...].astype(f32).T
    at = lax.broadcasted_iota(i32, pairs.shape, 1)
    columns = [col(jnp.where(at == k, pairs, 0.0)) for k in range(pairs.shape[1])]
    a = jnp.concatenate(columns[0::2], axis=0).astype(i32)
    b = jnp.concatenate(columns[1::2], axis=0).astype(i32)
    n = a.shape[0]

    before = lax.broadcasted_iota(i32, (128, 128), 0) > lax.broadcasted_iota(i32, (128, 128), 1)
    before = jnp.where(before, 1.0, 0.0).astype(jnp.bfloat16)

    def sort_in(hot):
        width = hot.shape[1]
        totals = jnp.sum(hot, axis=0, keepdims=True)
        key = lax.broadcasted_iota(i32, (8, width), 1) & 15
        running = jnp.broadcast_to(totals, (8, width))
        for step in (1, 2, 4, 8):
            running = running + jnp.where(key >= step, pltpu.roll(running, step, axis=1), 0.0)
        below = running[0:1] - totals
        ranks, passed = [], below
        for k in range(0, n, 128):
            part = hot[k : k + 128]
            ahead = jnp.dot(before, part.astype(jnp.bfloat16), preferred_element_type=f32) + passed
            ranks.append(col(ahead * part))
            passed = passed + jnp.sum(part, axis=0, keepdims=True)
        return jnp.concatenate(ranks, axis=0), totals, below

    lane = lax.broadcasted_iota(i32, (n, 128), 1)
    valid = a >= 0
    ga, gb = a >> 7, b >> 7
    low, high = jnp.minimum(ga, gb), jnp.maximum(ga, gb)
    anchor_y = anchor_ref[1:2].astype(f32)
    name = lax.broadcasted_iota(i32, (n, anchor_ref.shape[1]), 1)
    oy = col(jnp.where(name == b, anchor_y, 0.0) - jnp.where(name == a, anchor_y, 0.0)).astype(i32)
    spare = jnp.abs(oy) >> 1
    kinds = lax.broadcasted_iota(i32, (n, 256), 1)
    hot = jnp.where(valid & (kinds == (low * groups + high) * 16 + spare), 1.0, 0.0)
    rank, sums, _ = sort_in(hot)
    sums = sums.astype(i32)
    kind1 = lax.broadcasted_iota(i32, (1, 256), 1) >> 4
    count, up = {}, {}
    for g in range(groups):
        for h in range(g, groups):
            count[g, h] = jnp.sum(jnp.where(kind1 == g * groups + h, sums, 0))
            up[g, h] = (count[g, h] >> 1) if h > g else 0

    def loads():
        load = [0] * groups
        for (g, h), c in count.items():
            load[g] = load[g] + (c - up[g, h])
            load[h] = load[h] + up[g, h]
        return load

    load = loads()
    for g, h in count:
        if h > g:
            up[g, h] = up[g, h] + ((load[g] - load[h] + 2) >> 2)
    load = loads()
    excess = 0
    for g in range(groups - 1):
        excess = excess + load[g] - each
        up[g, g + 1] = up[g, g + 1] + excess
    need = (ROWS * PAIR_DEV - TRIMMED) - 1
    fits = 1
    goes_up, there = jnp.zeros((1, 256), f32), jnp.ones((1, 256), f32)
    for (g, h), c in count.items():
        if h > g:
            u = up[g, h]
            fine = (u >= 0) & (u <= KEEP) & (c - u >= 0) & (c - u <= KEEP)
            fits = jnp.where(fine, fits, 0)
            goes_up = jnp.where(kind1 == g * groups + h, u.astype(f32), goes_up)
            there = jnp.where(kind1 == g * groups + h, jnp.maximum(c, 1).astype(f32), there)

    key1 = lax.broadcasted_iota(i32, (1, 256), 1) & 15
    weight = jnp.where(key1 <= need // 2, 1, 0) + jnp.where(key1 <= need // 2 + 1, 1, 0)
    small = {t: jnp.sum(jnp.where(kind1 == t[0] * groups + t[1], sums * weight, 0)).astype(f32) for t in count}
    share = goes_up / there
    surplus = jnp.zeros((1, 256), f32)
    for g in range(groups):
        held = jnp.zeros((1, 256), f32)
        for (low_g, high_g), amount in small.items():
            if low_g == high_g:
                held = held + (amount if low_g == g else 0.0)
            elif g in (low_g, high_g):
                part = jnp.sum(jnp.where((kind1 == low_g * groups + high_g) & (key1 == 0), share, 0.0))
                held = held + amount * (part if high_g == g else 1.0 - part)
        surplus = surplus + jnp.where((kind1 >> 2) == g, held, 0.0) - jnp.where((kind1 & 3) == g, held, 0.0)
    bend = surplus / (2.0 * jnp.maximum(goes_up, 1.0))
    most = jnp.minimum(there / jnp.maximum(goes_up, 1.0) - 1.0, 1.0)
    bend = jnp.clip(bend, -0.98 * most, 0.98 * most)
    u, c, bend = col(hot * goes_up), jnp.maximum(col(hot * there), 1.0), col(hot * bend)

    def risen_at(r):
        x = r / c
        return jnp.where(r >= c, u, jnp.clip(jnp.floor(u * (x + bend * x * (1.0 - x)) + 0.5 / c), 0.0, u))

    risen = risen_at(rank)
    rises = risen_at(rank + 1.0) > risen
    group = jnp.where(rises, high, low)
    source = low + high - group
    crosses = valid & (low != high)
    hot = jnp.where(valid & (lane == group * 16 + spare), 1.0, 0.0)
    order, keyed, below = sort_in(hot)
    order = order.astype(i32)
    second = order >= B
    q = jnp.where(second, B + each - 1 - order, order)
    lane1 = lax.broadcasted_iota(i32, (1, 128), 1)
    match = 1
    for g in range(groups):
        fits = jnp.where(jnp.sum(jnp.where((lane1 >> 4) == g, keyed, 0.0)) == each, fits, 0)
        for j in range(need // 2 + 1):
            both = (lane1 == g * 16 + j + 1) | (lane1 == g * 16 + need - j + 1)
            match = jnp.where(jnp.sum(jnp.where(both, below, 0.0)) <= each, match, 0)
    mode_ref[0] = jnp.where(fits == 1, 1 - match, 2)

    put = (((group - source) & 3) - 1) * KEEP + jnp.where(rises, risen, rank - risen).astype(i32)
    near_b = ga != group
    near = jnp.where(near_b, b, a) & 127
    far = jnp.where(near_b, a, b) & 127
    table = jnp.where(crosses, 128 + put, far)
    spare = spare * match
    moved = jnp.where(second, spare, 0)
    from_a = jnp.where(oy > 0, spare, 0) - moved
    from_b = jnp.where(oy < 0, spare, 0) - moved
    near_from, far_from = jnp.where(near_b, from_b, from_a), jnp.where(near_b, from_a, from_b)

    def side(*columns):
        at = lax.broadcasted_iota(i32, (n, 8), 1)
        out = jnp.zeros((n, 8), f32)
        for k, column in enumerate(columns):
            out = jnp.where(at == k, column.astype(f32), out)
        return out.astype(jnp.bfloat16)

    def spread(columns, mask):
        hot = jnp.where(mask, 1.0, 0.0).astype(jnp.bfloat16)
        out = lax.dot_general(columns, hot, (((0,), (0,)), ((), ())), preferred_element_type=f32)
        return out.astype(i32)

    mine = valid & (group == me)
    flag = jnp.where(near_b, 1, 0)
    columns = side(near, table & 255, a & 255, b & 255, flag, table >> 8, a >> 8, b >> 8)
    here = mine & (lane == q)
    got = spread(columns, here)
    more = spread(side(near_from + 16, far_from + 16, spare), here)
    pos_ref[...] = got
    pos_ref[1:4] = got[1:4] + 256 * got[5:8]
    pos_ref[6:7] = pos_ref[1:2]
    pos_ref[0:1] = got[0:1] * ROWS + more[0:1] - 16
    pos_ref[1:2] = pos_ref[6:7] * ROWS + more[1:2] - 16
    pos_ref[5:6] = more[2:3]
    wide = lax.broadcasted_iota(i32, (n, slot_ref.shape[1]), 1)
    here = wide == put
    zero = jnp.zeros_like(a)
    slots = spread(side(far, zero, zero + 1, far_from + 16), crosses & (source == me) & here)
    used_ref[...] = spread(side(q & (B - 1), q >> 6, spare), crosses & mine & here)
    slot_ref[...] = slots
    slot_ref[3:4] = slots[0:1] * ROWS + slots[3:4] - 16


def route(me, pair_slots, anchors):
    lists = jnp.transpose(pair_slots, (1, 2, 0)).reshape(-1, pair_slots.shape[0])
    width = 128 * -(-(3 * KEEP) // 128)
    vmem, smem = pl.BlockSpec(memory_space=pltpu.VMEM), pl.BlockSpec(memory_space=pltpu.SMEM)
    return pl.pallas_call(
        route_kernel,
        out_shape=[
            jax.ShapeDtypeStruct((8, 128), jnp.int32),
            jax.ShapeDtypeStruct((8, width), jnp.int32),
            jax.ShapeDtypeStruct((8, width), jnp.int32),
            jax.ShapeDtypeStruct((1,), jnp.int32),
        ],
        in_specs=[smem, vmem, vmem],
        out_specs=[vmem, vmem, vmem, smem],
        compiler_params=pltpu.CompilerParams(vmem_limit_bytes=40 << 20),
        cost_estimate=pl.CostEstimate(flops=10_000_000, bytes_accessed=1_000_000, transcendentals=0),
        name="route",
    )(me, lists, jnp.transpose(anchors))


def flat(ref):
    return ref.reshape(ref.shape[0] * ROWS, 128)


def fetch_kernel(row_of, idx_ref, table_ref, *refs):
    *outs, table, sem = refs
    copy = pltpu.make_async_copy(table_ref, table, sem)
    copy.start()
    copy.wait()
    for k, out_ref in enumerate(outs):
        count = out_ref.shape[0]

        def move(i, carry, out_ref=out_ref, k=k, count=count):
            out_ref[i] = row_of(idx_ref, table, k * count + i)
            return carry

        lax.fori_loop(0, count, move, 0, unroll=4)


def fetch(idx, table, row_of, name):
    return pl.pallas_call(
        functools.partial(fetch_kernel, row_of),
        out_shape=[jax.ShapeDtypeStruct((KEEP, ROWS, 128), jnp.float32)] * 3,
        in_specs=[pl.BlockSpec(memory_space=pltpu.SMEM), pl.BlockSpec(memory_space=pl.ANY)],
        out_specs=[pl.BlockSpec(memory_space=pltpu.VMEM)] * 3,
        scratch_shapes=[pltpu.VMEM(table.shape, jnp.float32), pltpu.SemaphoreType.DMA],
        compiler_params=pltpu.CompilerParams(vmem_limit_bytes=16 << 20),
        cost_estimate=pl.CostEstimate(flops=0, bytes_accessed=8_000_000, transcendentals=0),
        name=name,
    )(idx, table)


def sent_row(idx_ref, table, i):
    return table[idx_ref[0, i]]


def line_no():
    return lax.broadcasted_iota(jnp.int32, (ROWS, 128), 0)


def its_lines(s, spare, lines):
    keep = line_no() >= spare if s else line_no() < ROWS - spare
    return jnp.where(keep, lines, 0.0)


def deal_owner(pos_ref, row, p, table, out_ref, at):
    first, second = [table[pl.ds(pos_ref[row, s * B + p] + ROWS, ROWS)] for s in range(PAIR_DEV)]
    lines = out_ref.shape[1]
    cut = lines - ROWS
    out_ref[at, :cut] = first[:cut]
    if cut < ROWS:
        shared = lax.broadcasted_iota(jnp.int32, (ROWS - cut, 128), 0) + cut < ROWS - pos_ref[5, p]
        out_ref[at, cut:ROWS] = jnp.where(shared, first[cut:], second[: ROWS - cut])
    out_ref[at, ROWS:] = second[ROWS - cut :]


def clear_ends(table):
    zero = jnp.zeros((ROWS, 128), jnp.float32)
    table[0] = zero
    table[table.shape[0] - 1] = zero


PARTS = 4


def deal_near_kernel(pos_ref, orb_ref, near_ref, table, stage, near, sem_in, sem_out):
    pulls = [
        pltpu.make_async_copy(orb_ref.at[:, pl.ds(k * 1024, 1024)], stage.at[k], sem_in.at[k]) for k in range(PARTS)
    ]
    for copy in pulls:
        copy.start()
    clear_ends(table)
    for k, copy in enumerate(pulls):
        copy.wait()

        def lay_out(i, carry, k=k):
            rows = pl.ds(pl.multiple_of(i * 8, 8), 8)
            lines = [stage[k, rows, j * 128 : (j + 1) * 128] for j in range(8)]
            table[pl.ds(i * 8 + 1, 8), k * 8 : k * 8 + 8] = jnp.swapaxes(jnp.stack(lines), 0, 1)
            return carry

        lax.fori_loop(0, 128 // 8, lay_out, 0, unroll=2)
    pushes = []
    for k in range(PARTS):

        def owner(p, carry):
            deal_owner(pos_ref, 0, p, flat(table), near, p)
            return carry

        mine = pl.ds(k * (B // PARTS), B // PARTS)
        lax.fori_loop(k * (B // PARTS), (k + 1) * (B // PARTS), owner, 0, unroll=4)
        pushes.append(pltpu.make_async_copy(near.at[mine], near_ref.at[mine], sem_out.at[k]))
        pushes[-1].start()
    for copy in pushes:
        copy.wait()


def deal_near(lines, pos, orbitals):
    anywhere = pl.BlockSpec(memory_space=pl.ANY)
    dma = pltpu.SemaphoreType.DMA((PARTS,))
    return pl.pallas_call(
        deal_near_kernel,
        out_shape=jax.ShapeDtypeStruct((B, lines, 128), jnp.float32),
        in_specs=[pl.BlockSpec(memory_space=pltpu.SMEM), anywhere],
        out_specs=anywhere,
        scratch_shapes=[
            pltpu.VMEM((130, ROWS, 128), jnp.float32),
            pltpu.VMEM((PARTS, 128, 1024), jnp.float32),
            pltpu.VMEM((B, lines, 128), jnp.float32),
            dma,
            dma,
        ],
        compiler_params=pltpu.CompilerParams(vmem_limit_bytes=60 << 20),
        cost_estimate=pl.CostEstimate(flops=2_000_000, bytes_accessed=10_000_000, transcendentals=0),
        name="deal_near",
    )(pos, orbitals)


def deal_far_kernel(row, pos_ref, *refs):
    *parts, far_ref, table, sem = refs
    copies, end = [], 1
    for k, part in enumerate(parts):
        copies.append(pltpu.make_async_copy(part, table.at[pl.ds(end, part.shape[0])], sem.at[k]))
        end += part.shape[0]
    for copy in copies:
        copy.start()
    clear_ends(table)
    for copy in copies:
        copy.wait()

    def owner(p, carry):
        deal_owner(pos_ref, row, p, flat(table), far_ref, p)
        return carry

    lax.fori_loop(0, B, owner, 0, unroll=4)


def deal_far(lines, row, pos, parts):
    rows = sum(x.shape[0] for x in parts)
    return pl.pallas_call(
        functools.partial(deal_far_kernel, row),
        out_shape=jax.ShapeDtypeStruct((B, lines, 128), jnp.float32),
        in_specs=[pl.BlockSpec(memory_space=pltpu.SMEM)] + [pl.BlockSpec(memory_space=pl.ANY)] * len(parts),
        out_specs=pl.BlockSpec(memory_space=pltpu.VMEM),
        scratch_shapes=[pltpu.VMEM((rows + 2, ROWS, 128), jnp.float32), pltpu.SemaphoreType.DMA((len(parts),))],
        compiler_params=pltpu.CompilerParams(vmem_limit_bytes=32 << 20),
        cost_estimate=pl.CostEstimate(flops=0, bytes_accessed=12_000_000, transcendentals=0),
        name="deal_far",
    )(pos, *parts)


def solve_pair(offset, from_a, from_b, box_a, box_b, term_a, term_b, part, dens, resid, second, third, image):
    ox, oy, oz = offset
    shape = (ROWS, 128)
    line = lax.broadcasted_iota(jnp.int32, shape, 0)
    lane = lax.broadcasted_iota(jnp.int32, shape, 1)
    cy = 2 * line + (lane >> 6)
    cz = lane & (B - 1)
    high = lane >= B
    ends = (high & (line == 0)) | (~high & (line == ROWS - 1))
    no_up, no_down = cz == B - 1, cz == 0

    def plane(ref, x):
        return ref[pl.ds(pl.multiple_of(x * ROWS, ROWS), ROWS)]

    def put(ref, x, value):
        ref[pl.ds(pl.multiple_of(x * ROWS, ROWS), ROWS)] = value

    def shifter(sy, sz):
        flat = sy * B + sz
        lines, steps = flat >> 7, flat & 127
        inside = (cy >= sy) & (cy < B + sy) & (cz >= sz) & (cz < B + sz)
        keep = lane < 128 - steps

        def shift(ref, x, first):
            at = x * ROWS - lines - first
            moved = jnp.where(keep, ref[pl.ds(at, ROWS)], ref[pl.ds(at - 1, ROWS)])
            return jnp.where(inside, pltpu.roll(moved, steps, axis=1), 0.0)

        return shift

    def apply(ref, x):
        here = plane(ref, x + 1)
        at = (x + 1) * ROWS
        other = jnp.where(high, ref[pl.ds(at - 1, ROWS)], ref[pl.ds(at + 1, ROWS)])
        other = here + jnp.where(ends, 0.0, other)
        beside = plane(ref, x) + plane(ref, x + 2) + pltpu.roll(other, B, axis=1)
        upper = jnp.where(no_up, 0.0, pltpu.roll(here, 127, axis=1))
        lower = jnp.where(no_down, 0.0, pltpu.roll(here, 1, axis=1))
        return here, 6.0 * here - beside - upper - lower

    zero = jnp.zeros(shape, jnp.float32)
    for ref in (dens, second, third):
        put(ref, 0, zero)
        put(ref, B + 1, zero)

    shift_on = shifter(oy, oz)
    shift_back = shifter(-oy, -oz)

    def begin(x, acc):
        src = x - ox
        inside = jnp.where((src >= 0) & (src < B), 1.0, 0.0)
        moved = shift_on(box_b, jnp.clip(src, 0, B - 1) + 1, from_b) * inside
        density = box_a[pl.ds((x + 1) * ROWS - from_a, ROWS)] * moved
        put(part, x, moved)
        put(dens, x + 1, density)
        return acc + density * density

    def first(x, acc):
        here, img = apply(dens, x)
        put(image, x + 1, img)
        return acc + here * img

    norm0 = yield begin
    step0 = norm0 / (yield first)

    def rest0(x, acc):
        left = plane(dens, x + 1) - step0 * plane(image, x + 1)
        put(resid, x, left)
        return acc + left * left

    norm1 = yield rest0
    ratio0 = norm1 / norm0

    def turn1(x, acc):
        put(second, x + 1, plane(resid, x) + ratio0 * plane(dens, x + 1))
        return acc

    def again(x, acc):
        here, img = apply(second, x)
        put(image, x + 1, img)
        return acc + here * img

    yield turn1
    step1 = norm1 / (yield again)

    def rest1(x, acc):
        left = plane(resid, x) - step1 * plane(image, x + 1)
        put(resid, x, left)
        return acc + left * left

    norm2 = yield rest1
    ratio1 = norm2 / norm1

    def turn2(x, acc):
        put(third, x + 1, plane(resid, x) + ratio1 * plane(second, x + 1))
        return acc

    def last(x, acc):
        here, img = apply(third, x)
        return acc + here * img

    yield turn2
    step2 = norm2 / (yield last)

    def finish(x, acc):
        potential = step0 * plane(dens, x + 1) + step1 * plane(second, x + 1) + step2 * plane(third, x + 1)
        here = pl.ds((x + 1) * ROWS - from_a, ROWS)
        term_a[here] = potential * plane(part, x)
        put(image, x + 1, potential * box_a[here])
        return acc

    def back(x, acc):
        src = x + ox
        inside = jnp.where((src >= 0) & (src < B), 1.0, 0.0)
        term_b[pl.ds((x + 1) * ROWS - from_b, ROWS)] = shift_back(image, jnp.clip(src, 0, B - 1) + 1, 0) * inside
        return acc

    yield finish
    yield back


def run_together(solvers, unroll):
    steps = [next(solver) for solver in solvers]
    zero = jnp.zeros((ROWS, 128), jnp.float32)
    while True:
        def both(x, accs, steps=tuple(steps)):
            return tuple(step(x, acc) for step, acc in zip(steps, accs))

        accs = lax.fori_loop(0, B, both, (zero,) * len(steps), unroll=unroll)
        sums = [jnp.sum(acc, keepdims=True) for acc in accs]
        try:
            steps = [solver.send(value) for solver, value in zip(solvers, sums)]
        except StopIteration:
            return


def pair_kernel(place_ref, pos_ref, anchor_ref, near_ref, far_ref, near_out, far_out, boxes, terms, *rest):
    *fields, sem = rest
    lines = near_ref.shape[1]
    cut = lines - ROWS
    at = [s * B + place_ref[0] for s in range(PAIR_DEV)]
    flags = [pos_ref[4, k] for k in at]
    copies = []
    for s in range(PAIR_DEV):
        for k, ref in enumerate((near_ref, far_ref)):
            which = 1 - flags[s] if k else flags[s]
            source = ref.at[:, pl.ds(s * cut, ROWS)]
            copies.append(pltpu.make_async_copy(source, boxes.at[s, which, pl.ds(1, B)], sem.at[s, k]))
    for copy in copies:
        copy.start()
    for s in range(PAIR_DEV):
        for k in range(2):
            clear_ends(boxes.at[s, k])
    for copy in copies:
        copy.wait()
    solvers = []
    for s in range(PAIR_DEV):
        orb_a, orb_b = pos_ref[2, at[s]], pos_ref[3, at[s]]
        offset = [anchor_ref[3 * orb_b + k] - anchor_ref[3 * orb_a + k] for k in range(3)]
        spare = pos_ref[5, at[s]]
        moved = spare if s else 0
        from_a = jnp.where(offset[1] > 0, spare, 0) - moved
        from_b = jnp.where(offset[1] < 0, spare, 0) - moved
        refs = [flat(ref.at[s, k]) for ref in (boxes, terms) for k in range(2)]
        solvers.append(solve_pair(offset, from_a, from_b, *refs, *[ref.at[s] for ref in fields]))
    run_together(solvers, UNROLL if cut < ROWS else 1)

    def together(x, carry):
        for k, out in enumerate((near_out, far_out)):
            first, second = [terms[s, 1 - flags[s] if k else flags[s], x + 1] for s in range(PAIR_DEV)]
            out[x, :cut] = first[:cut]
            if cut < ROWS:
                low = its_lines(0, pos_ref[5, at[0]], first)[cut:]
                out[x, cut:ROWS] = low + its_lines(1, pos_ref[5, at[1]], second)[: ROWS - cut]
            out[x, ROWS:] = second[ROWS - cut :]
        return carry

    lax.fori_loop(0, B, together, 0, unroll=4)


def solve(place, pos, anchors, near, far):
    smem, vmem = pl.BlockSpec(memory_space=pltpu.SMEM), pl.BlockSpec(memory_space=pltpu.VMEM)
    anywhere = pl.BlockSpec(memory_space=pl.ANY)
    field = pltpu.VMEM((PAIR_DEV, B * ROWS, 128), jnp.float32)
    padded = pltpu.VMEM((PAIR_DEV, (B + 2) * ROWS, 128), jnp.float32)
    boxes = pltpu.VMEM((PAIR_DEV, 2, B + 2, ROWS, 128), jnp.float32)
    return pl.pallas_call(
        pair_kernel,
        out_shape=[jax.ShapeDtypeStruct(near.shape, jnp.float32)] * 2,
        in_specs=[smem, smem, smem, anywhere, anywhere],
        out_specs=[vmem, vmem],
        scratch_shapes=[
            boxes, boxes, field, padded, field, padded, padded, padded,
            pltpu.SemaphoreType.DMA((PAIR_DEV, 2)),
        ],
        compiler_params=pltpu.CompilerParams(vmem_limit_bytes=40 << 20),
        cost_estimate=pl.CostEstimate(flops=100_000_000, bytes_accessed=30_000_000, transcendentals=0),
        name="solve",
    )(place, pos, anchors, near, far)


def add_lines(total, line, lines):
    here = pl.ds(line + ROWS, ROWS)
    total[here] = total[here] + lines


def add_far_kernel(pos_ref, terms_ref, out_ref):
    out_ref[...] = jnp.zeros(out_ref.shape, jnp.float32)
    total = flat(out_ref)
    cut = terms_ref.shape[1] - ROWS

    def here(p, carry):
        for s in range(PAIR_DEV):
            q = s * B + p

            @pl.when(pos_ref[6, q] < 128)
            def _(q=q, s=s):
                lines = terms_ref[p, s * cut : s * cut + ROWS]
                add_lines(total, pos_ref[1, q], its_lines(s, pos_ref[5, q], lines))

        return carry

    lax.fori_loop(0, B, here, 0)


def add_far(pos, terms):
    smem, vmem = pl.BlockSpec(memory_space=pltpu.SMEM), pl.BlockSpec(memory_space=pltpu.VMEM)
    return pl.pallas_call(
        add_far_kernel,
        out_shape=jax.ShapeDtypeStruct((130, ROWS, 128), jnp.float32),
        in_specs=[smem, vmem],
        out_specs=vmem,
        compiler_params=pltpu.CompilerParams(vmem_limit_bytes=24 << 20),
        cost_estimate=pl.CostEstimate(flops=2_000_000, bytes_accessed=4_000_000, transcendentals=0),
        name="add_far",
    )(pos, terms)


def add_arrived_kernel(slot_ref, sum_ref, *refs):
    *from_groups, out_ref, sem = refs
    copy = pltpu.make_async_copy(sum_ref, out_ref, sem)
    copy.start()
    copy.wait()
    total = flat(out_ref)

    def there(k, carry):
        for d, ref in enumerate(from_groups):
            at = d * KEEP + k
            add_lines(total, slot_ref[3, at], jnp.where(slot_ref[2, at] == 1, ref[k], 0.0))
        return carry

    lax.fori_loop(0, KEEP, there, 0, unroll=2)


def add_arrived(slot, summed, from_groups):
    smem, vmem = pl.BlockSpec(memory_space=pltpu.SMEM), pl.BlockSpec(memory_space=pltpu.VMEM)
    return pl.pallas_call(
        add_arrived_kernel,
        out_shape=jax.ShapeDtypeStruct(summed.shape, jnp.float32),
        in_specs=[smem, pl.BlockSpec(memory_space=pl.ANY)] + [vmem] * 3,
        out_specs=vmem,
        scratch_shapes=[pltpu.SemaphoreType.DMA],
        compiler_params=pltpu.CompilerParams(vmem_limit_bytes=24 << 20),
        cost_estimate=pl.CostEstimate(flops=2_000_000, bytes_accessed=6_000_000, transcendentals=0),
        name="add_arrived",
    )(slot, summed, *from_groups)


def add_near_kernel(pos_ref, sum_ref, terms_ref, out_ref, acc, terms, stage, sem_sum, sem_in, sem_out):
    cut = terms.shape[1] - ROWS
    copies = [pltpu.make_async_copy(sum_ref, acc, sem_sum)]
    for k in range(PARTS):
        mine = pl.ds(k * (B // PARTS), B // PARTS)
        copies.append(pltpu.make_async_copy(terms_ref.at[mine], terms.at[mine], sem_in.at[k]))
    for copy in copies:
        copy.start()
    copies[0].wait()
    for k in range(PARTS):
        copies[k + 1].wait()

        def here(p, carry):
            for s in range(PAIR_DEV):
                q = s * B + p
                lines = terms[p, s * cut : s * cut + ROWS]
                add_lines(flat(acc), pos_ref[0, q], its_lines(s, pos_ref[5, q], lines))
            return carry

        lax.fori_loop(k * (B // PARTS), (k + 1) * (B // PARTS), here, 0, unroll=2)
    pushes = []
    for k in range(PARTS):

        def lay_out(i, carry, k=k):
            rows = pl.ds(pl.multiple_of(i * 8, 8), 8)
            lines = jnp.swapaxes(acc[pl.ds(i * 8 + 1, 8), k * 8 : k * 8 + 8], 0, 1)
            for j in range(8):
                stage[k, rows, j * 128 : (j + 1) * 128] = lines[j]
            return carry

        lax.fori_loop(0, 128 // 8, lay_out, 0, unroll=2)
        pushes.append(pltpu.make_async_copy(stage.at[k], out_ref.at[:, pl.ds(k * 1024, 1024)], sem_out.at[k]))
        pushes[-1].start()
    for copy in pushes:
        copy.wait()


def add_near(pos, summed, terms):
    anywhere = pl.BlockSpec(memory_space=pl.ANY)
    dma = pltpu.SemaphoreType.DMA((PARTS,))
    return pl.pallas_call(
        add_near_kernel,
        out_shape=jax.ShapeDtypeStruct((128, ROWS * 128), jnp.float32),
        in_specs=[pl.BlockSpec(memory_space=pltpu.SMEM), anywhere, anywhere],
        out_specs=anywhere,
        scratch_shapes=[
            pltpu.VMEM((130, ROWS, 128), jnp.float32),
            pltpu.VMEM(terms.shape, jnp.float32),
            pltpu.VMEM((PARTS, 128, 1024), jnp.float32),
            pltpu.SemaphoreType.DMA,
            dma,
            dma,
        ],
        compiler_params=pltpu.CompilerParams(vmem_limit_bytes=63 << 20),
        cost_estimate=pl.CostEstimate(flops=2_000_000, bytes_accessed=10_000_000, transcendentals=0),
        name="add_near",
    )(pos, summed, terms)


def turned(x, shift):
    groups = lax.axis_size("grp")
    return lax.ppermute(x, "grp", [(g, (g + shift) % groups) for g in range(groups)])


def exchanged(planes):
    return lax.all_to_all(planes, "grid", 0, 0, tiled=True)


def there_and_back(place, pos, anchors, both):
    lines = both.shape[1] // 2

    def solve_both(both):
        return jnp.concatenate(solve(place, pos, anchors, both[:, :lines], both[:, lines:]), axis=1)

    def step(k, both):
        return lax.cond(k == 0, solve_both, lambda x: x, exchanged(both))

    return lax.fori_loop(0, 2, step, both)


def fitting(lines, orbitals, anchors, place, pos, slot, used):
    def used_row(used_ref, table, i):
        p, s, spare = used_ref[0, i], used_ref[1, i], used_ref[2, i]
        plane = table[p, pl.ds(pl.multiple_of(s * (lines - ROWS), 8), ROWS)]
        keep = (line_no() >= s * spare) & (line_no() < ROWS - (1 - s) * spare)
        return jnp.where(keep, plane, 0.0)

    trimmed = lines == TRIMMED
    near = deal_near(lines, pos, orbitals)
    if trimmed:
        near = exchanged(near)
    local = orbitals.reshape(128, ROWS, 128)
    arrived = [turned(x, d) for d, x in enumerate(fetch(slot, local, sent_row, "send"), 1)]
    far = deal_far(lines, 1, pos, [local] + arrived)
    if trimmed:
        near_terms, far_terms = solve(place, pos, anchors.reshape(-1), near, exchanged(far))
        far_terms = exchanged(far_terms)
    else:
        both = there_and_back(place, pos, anchors.reshape(-1), jnp.concatenate([near, far], axis=1))
        near_terms, far_terms = both[:, :lines], both[:, lines:]
    from_groups = [turned(x, -d) for d, x in enumerate(fetch(used, far_terms, used_row, "back"), 1)]
    summed = add_far(pos, far_terms)
    if trimmed:
        near_terms = exchanged(near_terms)
    return add_near(pos, add_arrived(slot, summed, from_groups), near_terms)


def add_all_kernel(pos_ref, terms_ref, out_ref):
    out_ref[...] = jnp.zeros(out_ref.shape, jnp.float32)
    total = flat(out_ref)

    def here(p, carry):
        for s in range(PAIR_DEV):
            for k in range(2):
                at = (k * PAIR_DEV + s) * ROWS
                add_lines(total, pos_ref[k, s * B + p], terms_ref[p, at : at + ROWS])
        return carry

    lax.fori_loop(0, B, here, 0)


def add_all(pos, terms, count):
    return pl.pallas_call(
        add_all_kernel,
        out_shape=jax.ShapeDtypeStruct((count + 2, ROWS, 128), jnp.float32),
        in_specs=[pl.BlockSpec(memory_space=pltpu.SMEM), pl.BlockSpec(memory_space=pltpu.VMEM)],
        out_specs=pl.BlockSpec(memory_space=pltpu.VMEM),
        compiler_params=pltpu.CompilerParams(vmem_limit_bytes=32 << 20),
        cost_estimate=pl.CostEstimate(flops=2_000_000, bytes_accessed=10_000_000, transcendentals=0),
        name="add_all",
    )(pos, terms)


def general(orbitals, anchors, pair_slots, place):
    groups, grid_count = lax.axis_size("grp"), lax.axis_size("grid")
    me, rows = lax.axis_index("grp"), orbitals.shape[0]
    dealt = deal_evenly(pair_slots, groups * grid_count, PAIR_DEV)
    own = lax.dynamic_slice_in_dim(dealt, me * grid_count, grid_count, 0)
    own = jnp.maximum(jnp.transpose(own, (2, 1, 0)).reshape(2, PAIR_DEV * grid_count), 0)
    pos = jnp.concatenate([own * ROWS, own, jnp.zeros((4, own.shape[1]), jnp.int32)])
    round_trip = [turned(orbitals, d) for d in (3, 2, 1)] + [orbitals]
    pieces = lax.dynamic_slice_in_dim(jnp.concatenate(round_trip * 2), (3 - me) * rows, groups * rows, 0)
    table = pieces.reshape(-1, ROWS, 128)
    both = jnp.concatenate([deal_far(PAIR_DEV * ROWS, k, pos, [table]) for k in range(2)], axis=1)

    terms = there_and_back(place, pos, anchors.reshape(-1), both)
    summed = add_all(pos, terms, table.shape[0])
    blocks = [lax.dynamic_slice_in_dim(summed, ((me + d) & 3) * rows + 1, rows, 0) for d in range(4)]
    return (blocks[0] + sum(turned(blocks[d], d) for d in (1, 2, 3))).reshape(orbitals.shape)


def body(orbitals, anchors, pair_slots):
    me = lax.axis_index("grp").astype(jnp.int32)[None]
    place = lax.axis_index("grid").astype(jnp.int32)[None]
    pos, slot, used, mode = route(me, pair_slots, anchors)

    def other():
        return lax.cond(
            mode[0] == 1,
            lambda: fitting(PAIR_DEV * ROWS, orbitals, anchors, place, pos, slot, used),
            lambda: general(orbitals, anchors, pair_slots, place),
        )

    return lax.cond(mode[0] == 0, lambda: fitting(TRIMMED, orbitals, anchors, place, pos, slot, used), other)


def solution(mesh):
    return jax.shard_map(
        body,
        mesh=mesh,
        in_specs=(P("grp", "grid"), P(), P()),
        out_specs=P("grp", "grid"),
        check_vma=False,
    )
```

```python
import functools

import jax
import jax.numpy as jnp
from jax import lax
from jax.experimental import pallas as pl
from jax.experimental.pallas import tpu as pltpu
from jax.sharding import PartitionSpec as P

B = 64
PAIR_DEV = 2
ITERS = 3
ROWS = B * B // 128
KEEP = 48
UNROLL = 32
TRIMMED = 56


def deal_evenly(pair_slots, owner_count, each_owner):
    flat_slots = pair_slots.reshape(-1, 2)
    filled = (flat_slots[:, 0] >= 0).astype(jnp.int32)
    order = jnp.arange(flat_slots.shape[0], dtype=jnp.int32)
    position = jnp.sum(jnp.where(order[None, :] < order[:, None], filled[None, :], 0), axis=1)
    wanted = lax.broadcasted_iota(jnp.int32, (owner_count, each_owner), 1) * owner_count
    wanted = (wanted + lax.broadcasted_iota(jnp.int32, (owner_count, each_owner), 0)).reshape(-1)
    matched = (position[None, :] == wanted[:, None]) & (filled[None, :] == 1)
    picked = jnp.dot(matched.astype(jnp.int32), flat_slots)
    return picked.reshape(owner_count, each_owner, 2)


def route_kernel(me_ref, pair_ref, anchor_ref, pos_ref, slot_ref, used_ref, mode_ref):
    me = me_ref[0]
    f32, i32 = jnp.float32, jnp.int32
    groups, each = 4, 2 * B

    def col(x):
        return jnp.sum(x, axis=1, keepdims=True)

    pairs = pair_ref[...].astype(f32).T
    at = lax.broadcasted_iota(i32, pairs.shape, 1)
    columns = [col(jnp.where(at == k, pairs, 0.0)) for k in range(pairs.shape[1])]
    a = jnp.concatenate(columns[0::2], axis=0).astype(i32)
    b = jnp.concatenate(columns[1::2], axis=0).astype(i32)
    n = a.shape[0]

    before = lax.broadcasted_iota(i32, (128, 128), 0) > lax.broadcasted_iota(i32, (128, 128), 1)
    before = jnp.where(before, 1.0, 0.0).astype(jnp.bfloat16)

    def sort_in(hot):
        width = hot.shape[1]
        totals = jnp.sum(hot, axis=0, keepdims=True)
        key = lax.broadcasted_iota(i32, (8, width), 1) & 15
        running = jnp.broadcast_to(totals, (8, width))
        for step in (1, 2, 4, 8):
            running = running + jnp.where(key >= step, pltpu.roll(running, step, axis=1), 0.0)
        below = running[0:1] - totals
        ranks, passed = [], below
        for k in range(0, n, 128):
            part = hot[k : k + 128]
            ahead = jnp.dot(before, part.astype(jnp.bfloat16), preferred_element_type=f32) + passed
            ranks.append(col(ahead * part))
            passed = passed + jnp.sum(part, axis=0, keepdims=True)
        return jnp.concatenate(ranks, axis=0), totals, below

    lane = lax.broadcasted_iota(i32, (n, 128), 1)
    valid = a >= 0
    ga, gb = a >> 7, b >> 7
    low, high = jnp.minimum(ga, gb), jnp.maximum(ga, gb)
    anchor_y = anchor_ref[1:2].astype(f32)
    name = lax.broadcasted_iota(i32, (n, anchor_ref.shape[1]), 1)
    oy = col(jnp.where(name == b, anchor_y, 0.0) - jnp.where(name == a, anchor_y, 0.0)).astype(i32)
    spare = jnp.abs(oy) >> 1
    kinds = lax.broadcasted_iota(i32, (n, 256), 1)
    hot = jnp.where(valid & (kinds == (low * groups + high) * 16 + spare), 1.0, 0.0)
    rank, sums, _ = sort_in(hot)
    sums = sums.astype(i32)
    kind1 = lax.broadcasted_iota(i32, (1, 256), 1) >> 4
    count, up = {}, {}
    for g in range(groups):
        for h in range(g, groups):
            count[g, h] = jnp.sum(jnp.where(kind1 == g * groups + h, sums, 0))
            up[g, h] = (count[g, h] >> 1) if h > g else 0

    def loads():
        load = [0] * groups
        for (g, h), c in count.items():
            load[g] = load[g] + (c - up[g, h])
            load[h] = load[h] + up[g, h]
        return load

    load = loads()
    for g, h in count:
        if h > g:
            up[g, h] = up[g, h] + ((load[g] - load[h] + 2) >> 2)
    load = loads()
    excess = 0
    for g in range(groups - 1):
        excess = excess + load[g] - each
        up[g, g + 1] = up[g, g + 1] + excess
    need = (ROWS * PAIR_DEV - TRIMMED) - 1
    fits = 1
    goes_up, there = jnp.zeros((1, 256), f32), jnp.ones((1, 256), f32)
    for (g, h), c in count.items():
        if h > g:
            u = up[g, h]
            fine = (u >= 0) & (u <= KEEP) & (c - u >= 0) & (c - u <= KEEP)
            fits = jnp.where(fine, fits, 0)
            goes_up = jnp.where(kind1 == g * groups + h, u.astype(f32), goes_up)
            there = jnp.where(kind1 == g * groups + h, jnp.maximum(c, 1).astype(f32), there)

    key1 = lax.broadcasted_iota(i32, (1, 256), 1) & 15
    weight = jnp.where(key1 <= need // 2, 1, 0) + jnp.where(key1 <= need // 2 + 1, 1, 0)
    small = {t: jnp.sum(jnp.where(kind1 == t[0] * groups + t[1], sums * weight, 0)).astype(f32) for t in count}
    share = goes_up / there
    surplus = jnp.zeros((1, 256), f32)
    for g in range(groups):
        held = jnp.zeros((1, 256), f32)
        for (low_g, high_g), amount in small.items():
            if low_g == high_g:
                held = held + (amount if low_g == g else 0.0)
            elif g in (low_g, high_g):
                part = jnp.sum(jnp.where((kind1 == low_g * groups + high_g) & (key1 == 0), share, 0.0))
                held = held + amount * (part if high_g == g else 1.0 - part)
        surplus = surplus + jnp.where((kind1 >> 2) == g, held, 0.0) - jnp.where((kind1 & 3) == g, held, 0.0)
    bend = surplus / (2.0 * jnp.maximum(goes_up, 1.0))
    most = jnp.minimum(there / jnp.maximum(goes_up, 1.0) - 1.0, 1.0)
    bend = jnp.clip(bend, -0.98 * most, 0.98 * most)
    u, c, bend = col(hot * goes_up), jnp.maximum(col(hot * there), 1.0), col(hot * bend)

    def risen_at(r):
        x = r / c
        return jnp.where(r >= c, u, jnp.clip(jnp.floor(u * (x + bend * x * (1.0 - x)) + 0.5 / c), 0.0, u))

    risen = risen_at(rank)
    rises = risen_at(rank + 1.0) > risen
    group = jnp.where(rises, high, low)
    source = low + high - group
    crosses = valid & (low != high)
    hot = jnp.where(valid & (lane == group * 16 + spare), 1.0, 0.0)
    order, keyed, below = sort_in(hot)
    order = order.astype(i32)
    second = order >= B
    q = jnp.where(second, B + each - 1 - order, order)
    lane1 = lax.broadcasted_iota(i32, (1, 128), 1)
    match = 1
    for g in range(groups):
        fits = jnp.where(jnp.sum(jnp.where((lane1 >> 4) == g, keyed, 0.0)) == each, fits, 0)
        for j in range(need // 2 + 1):
            both = (lane1 == g * 16 + j + 1) | (lane1 == g * 16 + need - j + 1)
            match = jnp.where(jnp.sum(jnp.where(both, below, 0.0)) <= each, match, 0)
    mode_ref[0] = jnp.where(fits == 1, 1 - match, 2)

    put = (((group - source) & 3) - 1) * KEEP + jnp.where(rises, risen, rank - risen).astype(i32)
    near_b = ga != group
    near = jnp.where(near_b, b, a) & 127
    far = jnp.where(near_b, a, b) & 127
    table = jnp.where(crosses, 128 + put, far)
    spare = spare * match
    moved = jnp.where(second, spare, 0)
    from_a = jnp.where(oy > 0, spare, 0) - moved
    from_b = jnp.where(oy < 0, spare, 0) - moved
    near_from, far_from = jnp.where(near_b, from_b, from_a), jnp.where(near_b, from_a, from_b)

    def side(*columns):
        at = lax.broadcasted_iota(i32, (n, 8), 1)
        out = jnp.zeros((n, 8), f32)
        for k, column in enumerate(columns):
            out = jnp.where(at == k, column.astype(f32), out)
        return out.astype(jnp.bfloat16)

    def spread(columns, mask):
        hot = jnp.where(mask, 1.0, 0.0).astype(jnp.bfloat16)
        out = lax.dot_general(columns, hot, (((0,), (0,)), ((), ())), preferred_element_type=f32)
        return out.astype(i32)

    mine = valid & (group == me)
    flag = jnp.where(near_b, 1, 0)
    columns = side(near, table & 255, a & 255, b & 255, flag, table >> 8, a >> 8, b >> 8)
    here = mine & (lane == q)
    got = spread(columns, here)
    more = spread(side(near_from + 16, far_from + 16, spare), here)
    pos_ref[...] = got
    pos_ref[1:4] = got[1:4] + 256 * got[5:8]
    pos_ref[6:7] = pos_ref[1:2]
    pos_ref[0:1] = got[0:1] * ROWS + more[0:1] - 16
    pos_ref[1:2] = pos_ref[6:7] * ROWS + more[1:2] - 16
    pos_ref[5:6] = more[2:3]
    wide = lax.broadcasted_iota(i32, (n, slot_ref.shape[1]), 1)
    here = wide == put
    zero = jnp.zeros_like(a)
    slots = spread(side(far, zero, zero + 1, far_from + 16), crosses & (source == me) & here)
    used_ref[...] = spread(side(q & (B - 1), q >> 6, spare), crosses & mine & here)
    slot_ref[...] = slots
    slot_ref[3:4] = slots[0:1] * ROWS + slots[3:4] - 16


def route(me, pair_slots, anchors):
    lists = jnp.transpose(pair_slots, (1, 2, 0)).reshape(-1, pair_slots.shape[0])
    width = 128 * -(-(3 * KEEP) // 128)
    vmem, smem = pl.BlockSpec(memory_space=pltpu.VMEM), pl.BlockSpec(memory_space=pltpu.SMEM)
    return pl.pallas_call(
        route_kernel,
        out_shape=[
            jax.ShapeDtypeStruct((8, 128), jnp.int32),
            jax.ShapeDtypeStruct((8, width), jnp.int32),
            jax.ShapeDtypeStruct((8, width), jnp.int32),
            jax.ShapeDtypeStruct((1,), jnp.int32),
        ],
        in_specs=[smem, vmem, vmem],
        out_specs=[vmem, vmem, vmem, smem],
        compiler_params=pltpu.CompilerParams(vmem_limit_bytes=40 << 20),
        cost_estimate=pl.CostEstimate(flops=10_000_000, bytes_accessed=1_000_000, transcendentals=0),
        name="route",
    )(me, lists, jnp.transpose(anchors))


def flat(ref):
    return ref.reshape(ref.shape[0] * ROWS, 128)


def fetch_kernel(row_of, idx_ref, table_ref, *refs):
    *outs, table, sem = refs
    copy = pltpu.make_async_copy(table_ref, table, sem)
    copy.start()
    copy.wait()
    for k, out_ref in enumerate(outs):
        count = out_ref.shape[0]

        def move(i, carry, out_ref=out_ref, k=k, count=count):
            out_ref[i] = row_of(idx_ref, table, k * count + i)
            return carry

        lax.fori_loop(0, count, move, 0, unroll=4)


def fetch(idx, table, row_of, name):
    return pl.pallas_call(
        functools.partial(fetch_kernel, row_of),
        out_shape=[jax.ShapeDtypeStruct((KEEP, ROWS, 128), jnp.float32)] * 3,
        in_specs=[pl.BlockSpec(memory_space=pltpu.SMEM), pl.BlockSpec(memory_space=pl.ANY)],
        out_specs=[pl.BlockSpec(memory_space=pltpu.VMEM)] * 3,
        scratch_shapes=[pltpu.VMEM(table.shape, jnp.float32), pltpu.SemaphoreType.DMA],
        compiler_params=pltpu.CompilerParams(vmem_limit_bytes=16 << 20),
        cost_estimate=pl.CostEstimate(flops=0, bytes_accessed=8_000_000, transcendentals=0),
        name=name,
    )(idx, table)


def sent_row(idx_ref, table, i):
    return table[idx_ref[0, i]]


def line_no():
    return lax.broadcasted_iota(jnp.int32, (ROWS, 128), 0)


def its_lines(s, spare, lines):
    keep = line_no() >= spare if s else line_no() < ROWS - spare
    return jnp.where(keep, lines, 0.0)


def deal_owner(pos_ref, row, p, table, out_ref, at):
    first, second = [table[pl.ds(pos_ref[row, s * B + p] + ROWS, ROWS)] for s in range(PAIR_DEV)]
    lines = out_ref.shape[1]
    cut = lines - ROWS
    out_ref[at, :cut] = first[:cut]
    if cut < ROWS:
        shared = lax.broadcasted_iota(jnp.int32, (ROWS - cut, 128), 0) + cut < ROWS - pos_ref[5, p]
        out_ref[at, cut:ROWS] = jnp.where(shared, first[cut:], second[: ROWS - cut])
    out_ref[at, ROWS:] = second[ROWS - cut :]


def clear_ends(table):
    zero = jnp.zeros((ROWS, 128), jnp.float32)
    table[0] = zero
    table[table.shape[0] - 1] = zero


PARTS = 4


def deal_near_kernel(pos_ref, orb_ref, near_ref, table, stage, near, sem_in, sem_out):
    pulls = [
        pltpu.make_async_copy(orb_ref.at[:, pl.ds(k * 1024, 1024)], stage.at[k], sem_in.at[k]) for k in range(PARTS)
    ]
    for copy in pulls:
        copy.start()
    clear_ends(table)
    for k, copy in enumerate(pulls):
        copy.wait()

        def lay_out(i, carry, k=k):
            rows = pl.ds(pl.multiple_of(i * 8, 8), 8)
            lines = [stage[k, rows, j * 128 : (j + 1) * 128] for j in range(8)]
            table[pl.ds(i * 8 + 1, 8), k * 8 : k * 8 + 8] = jnp.swapaxes(jnp.stack(lines), 0, 1)
            return carry

        lax.fori_loop(0, 128 // 8, lay_out, 0, unroll=4)
    pushes = []
    for k in range(PARTS):

        def owner(p, carry):
            deal_owner(pos_ref, 0, p, flat(table), near, p)
            return carry

        mine = pl.ds(k * (B // PARTS), B // PARTS)
        lax.fori_loop(k * (B // PARTS), (k + 1) * (B // PARTS), owner, 0, unroll=4)
        pushes.append(pltpu.make_async_copy(near.at[mine], near_ref.at[mine], sem_out.at[k]))
        pushes[-1].start()
    for copy in pushes:
        copy.wait()


def deal_near(lines, pos, orbitals):
    anywhere = pl.BlockSpec(memory_space=pl.ANY)
    dma = pltpu.SemaphoreType.DMA((PARTS,))
    return pl.pallas_call(
        deal_near_kernel,
        out_shape=jax.ShapeDtypeStruct((B, lines, 128), jnp.float32),
        in_specs=[pl.BlockSpec(memory_space=pltpu.SMEM), anywhere],
        out_specs=anywhere,
        scratch_shapes=[
            pltpu.VMEM((130, ROWS, 128), jnp.float32),
            pltpu.VMEM((PARTS, 128, 1024), jnp.float32),
            pltpu.VMEM((B, lines, 128), jnp.float32),
            dma,
            dma,
        ],
        compiler_params=pltpu.CompilerParams(vmem_limit_bytes=60 << 20),
        cost_estimate=pl.CostEstimate(flops=2_000_000, bytes_accessed=10_000_000, transcendentals=0),
        name="deal_near",
    )(pos, orbitals)


def deal_far_kernel(row, pos_ref, *refs):
    *parts, far_ref, table, sem = refs
    copies, end = [], 1
    for k, part in enumerate(parts):
        copies.append(pltpu.make_async_copy(part, table.at[pl.ds(end, part.shape[0])], sem.at[k]))
        end += part.shape[0]
    for copy in copies:
        copy.start()
    clear_ends(table)
    for copy in copies:
        copy.wait()

    def owner(p, carry):
        deal_owner(pos_ref, row, p, flat(table), far_ref, p)
        return carry

    lax.fori_loop(0, B, owner, 0, unroll=4)


def deal_far(lines, row, pos, parts):
    rows = sum(x.shape[0] for x in parts)
    return pl.pallas_call(
        functools.partial(deal_far_kernel, row),
        out_shape=jax.ShapeDtypeStruct((B, lines, 128), jnp.float32),
        in_specs=[pl.BlockSpec(memory_space=pltpu.SMEM)] + [pl.BlockSpec(memory_space=pl.ANY)] * len(parts),
        out_specs=pl.BlockSpec(memory_space=pltpu.VMEM),
        scratch_shapes=[pltpu.VMEM((rows + 2, ROWS, 128), jnp.float32), pltpu.SemaphoreType.DMA((len(parts),))],
        compiler_params=pltpu.CompilerParams(vmem_limit_bytes=32 << 20),
        cost_estimate=pl.CostEstimate(flops=0, bytes_accessed=12_000_000, transcendentals=0),
        name="deal_far",
    )(pos, *parts)


def solve_pair(offset, from_a, from_b, box_a, box_b, term_a, term_b, part, dens, resid, second, third, image):
    ox, oy, oz = offset
    shape = (ROWS, 128)
    line = lax.broadcasted_iota(jnp.int32, shape, 0)
    lane = lax.broadcasted_iota(jnp.int32, shape, 1)
    cy = 2 * line + (lane >> 6)
    cz = lane & (B - 1)
    high = lane >= B
    ends = (high & (line == 0)) | (~high & (line == ROWS - 1))
    no_up, no_down = cz == B - 1, cz == 0

    def plane(ref, x):
        return ref[pl.ds(pl.multiple_of(x * ROWS, ROWS), ROWS)]

    def put(ref, x, value):
        ref[pl.ds(pl.multiple_of(x * ROWS, ROWS), ROWS)] = value

    def shifter(sy, sz):
        flat = sy * B + sz
        lines, steps = flat >> 7, flat & 127
        inside = (cy >= sy) & (cy < B + sy) & (cz >= sz) & (cz < B + sz)
        keep = lane < 128 - steps

        def shift(ref, x, first):
            at = x * ROWS - lines - first
            moved = jnp.where(keep, ref[pl.ds(at, ROWS)], ref[pl.ds(at - 1, ROWS)])
            return jnp.where(inside, pltpu.roll(moved, steps, axis=1), 0.0)

        return shift

    def apply(ref, x):
        here = plane(ref, x + 1)
        at = (x + 1) * ROWS
        other = jnp.where(high, ref[pl.ds(at - 1, ROWS)], ref[pl.ds(at + 1, ROWS)])
        other = here + jnp.where(ends, 0.0, other)
        beside = plane(ref, x) + plane(ref, x + 2) + pltpu.roll(other, B, axis=1)
        upper = jnp.where(no_up, 0.0, pltpu.roll(here, 127, axis=1))
        lower = jnp.where(no_down, 0.0, pltpu.roll(here, 1, axis=1))
        return here, 6.0 * here - beside - upper - lower

    zero = jnp.zeros(shape, jnp.float32)
    for ref in (dens, second, third):
        put(ref, 0, zero)
        put(ref, B + 1, zero)

    shift_on = shifter(oy, oz)
    shift_back = shifter(-oy, -oz)

    def begin(x, acc):
        src = x - ox
        inside = jnp.where((src >= 0) & (src < B), 1.0, 0.0)
        moved = shift_on(box_b, jnp.clip(src, 0, B - 1) + 1, from_b) * inside
        density = box_a[pl.ds((x + 1) * ROWS - from_a, ROWS)] * moved
        put(part, x, moved)
        put(dens, x + 1, density)
        return acc + density * density

    def first(x, acc):
        here, img = apply(dens, x)
        put(image, x + 1, img)
        return acc + here * img

    norm0 = yield begin
    step0 = norm0 / (yield first)

    def rest0(x, acc):
        left = plane(dens, x + 1) - step0 * plane(image, x + 1)
        put(resid, x, left)
        return acc + left * left

    norm1 = yield rest0
    ratio0 = norm1 / norm0

    def turn1(x, acc):
        put(second, x + 1, plane(resid, x) + ratio0 * plane(dens, x + 1))
        return acc

    def again(x, acc):
        here, img = apply(second, x)
        put(image, x + 1, img)
        return acc + here * img

    yield turn1
    step1 = norm1 / (yield again)

    def rest1(x, acc):
        left = plane(resid, x) - step1 * plane(image, x + 1)
        put(resid, x, left)
        return acc + left * left

    norm2 = yield rest1
    ratio1 = norm2 / norm1

    def turn2(x, acc):
        put(third, x + 1, plane(resid, x) + ratio1 * plane(second, x + 1))
        return acc

    def last(x, acc):
        here, img = apply(third, x)
        return acc + here * img

    yield turn2
    step2 = norm2 / (yield last)

    def finish(x, acc):
        potential = step0 * plane(dens, x + 1) + step1 * plane(second, x + 1) + step2 * plane(third, x + 1)
        here = pl.ds((x + 1) * ROWS - from_a, ROWS)
        term_a[here] = potential * plane(part, x)
        put(image, x + 1, potential * box_a[here])
        return acc

    def back(x, acc):
        src = x + ox
        inside = jnp.where((src >= 0) & (src < B), 1.0, 0.0)
        term_b[pl.ds((x + 1) * ROWS - from_b, ROWS)] = shift_back(image, jnp.clip(src, 0, B - 1) + 1, 0) * inside
        return acc

    yield finish
    yield back


def run_together(solvers, unroll):
    steps = [next(solver) for solver in solvers]
    zero = jnp.zeros((ROWS, 128), jnp.float32)
    while True:
        def both(x, accs, steps=tuple(steps)):
            return tuple(step(x, acc) for step, acc in zip(steps, accs))

        accs = lax.fori_loop(0, B, both, (zero,) * len(steps), unroll=unroll)
        sums = [jnp.sum(acc, keepdims=True) for acc in accs]
        try:
            steps = [solver.send(value) for solver, value in zip(solvers, sums)]
        except StopIteration:
            return


def pair_kernel(place_ref, pos_ref, anchor_ref, near_ref, far_ref, near_out, far_out, boxes, terms, *rest):
    *fields, sem = rest
    lines = near_ref.shape[1]
    cut = lines - ROWS
    at = [s * B + place_ref[0] for s in range(PAIR_DEV)]
    flags = [pos_ref[4, k] for k in at]
    copies = []
    for s in range(PAIR_DEV):
        for k, ref in enumerate((near_ref, far_ref)):
            which = 1 - flags[s] if k else flags[s]
            source = ref.at[:, pl.ds(s * cut, ROWS)]
            copies.append(pltpu.make_async_copy(source, boxes.at[s, which, pl.ds(1, B)], sem.at[s, k]))
    for copy in copies:
        copy.start()
    for s in range(PAIR_DEV):
        for k in range(2):
            clear_ends(boxes.at[s, k])
    for copy in copies:
        copy.wait()
    solvers = []
    for s in range(PAIR_DEV):
        orb_a, orb_b = pos_ref[2, at[s]], pos_ref[3, at[s]]
        offset = [anchor_ref[3 * orb_b + k] - anchor_ref[3 * orb_a + k] for k in range(3)]
        spare = pos_ref[5, at[s]]
        moved = spare if s else 0
        from_a = jnp.where(offset[1] > 0, spare, 0) - moved
        from_b = jnp.where(offset[1] < 0, spare, 0) - moved
        refs = [flat(ref.at[s, k]) for ref in (boxes, terms) for k in range(2)]
        solvers.append(solve_pair(offset, from_a, from_b, *refs, *[ref.at[s] for ref in fields]))
    run_together(solvers, UNROLL if cut < ROWS else 1)

    def together(x, carry):
        for k, out in enumerate((near_out, far_out)):
            first, second = [terms[s, 1 - flags[s] if k else flags[s], x + 1] for s in range(PAIR_DEV)]
            out[x, :cut] = first[:cut]
            if cut < ROWS:
                low = its_lines(0, pos_ref[5, at[0]], first)[cut:]
                out[x, cut:ROWS] = low + its_lines(1, pos_ref[5, at[1]], second)[: ROWS - cut]
            out[x, ROWS:] = second[ROWS - cut :]
        return carry

    lax.fori_loop(0, B, together, 0, unroll=4)


def solve(place, pos, anchors, near, far):
    smem, vmem = pl.BlockSpec(memory_space=pltpu.SMEM), pl.BlockSpec(memory_space=pltpu.VMEM)
    anywhere = pl.BlockSpec(memory_space=pl.ANY)
    field = pltpu.VMEM((PAIR_DEV, B * ROWS, 128), jnp.float32)
    padded = pltpu.VMEM((PAIR_DEV, (B + 2) * ROWS, 128), jnp.float32)
    boxes = pltpu.VMEM((PAIR_DEV, 2, B + 2, ROWS, 128), jnp.float32)
    return pl.pallas_call(
        pair_kernel,
        out_shape=[jax.ShapeDtypeStruct(near.shape, jnp.float32)] * 2,
        in_specs=[smem, smem, smem, anywhere, anywhere],
        out_specs=[vmem, vmem],
        scratch_shapes=[
            boxes, boxes, field, padded, field, padded, padded, padded,
            pltpu.SemaphoreType.DMA((PAIR_DEV, 2)),
        ],
        compiler_params=pltpu.CompilerParams(vmem_limit_bytes=40 << 20),
        cost_estimate=pl.CostEstimate(flops=100_000_000, bytes_accessed=30_000_000, transcendentals=0),
        name="solve",
    )(place, pos, anchors, near, far)


def add_lines(total, line, lines):
    here = pl.ds(line + ROWS, ROWS)
    total[here] = total[here] + lines


def add_far_kernel(pos_ref, terms_ref, out_ref):
    out_ref[...] = jnp.zeros(out_ref.shape, jnp.float32)
    total = flat(out_ref)
    cut = terms_ref.shape[1] - ROWS

    def here(p, carry):
        for s in range(PAIR_DEV):
            q = s * B + p

            @pl.when(pos_ref[6, q] < 128)
            def _(q=q, s=s):
                lines = terms_ref[p, s * cut : s * cut + ROWS]
                add_lines(total, pos_ref[1, q], its_lines(s, pos_ref[5, q], lines))

        return carry

    lax.fori_loop(0, B, here, 0)


def add_far(pos, terms):
    smem, vmem = pl.BlockSpec(memory_space=pltpu.SMEM), pl.BlockSpec(memory_space=pltpu.VMEM)
    return pl.pallas_call(
        add_far_kernel,
        out_shape=jax.ShapeDtypeStruct((130, ROWS, 128), jnp.float32),
        in_specs=[smem, vmem],
        out_specs=vmem,
        compiler_params=pltpu.CompilerParams(vmem_limit_bytes=24 << 20),
        cost_estimate=pl.CostEstimate(flops=2_000_000, bytes_accessed=4_000_000, transcendentals=0),
        name="add_far",
    )(pos, terms)


def add_arrived_kernel(slot_ref, sum_ref, *refs):
    *from_groups, out_ref, sem = refs
    copy = pltpu.make_async_copy(sum_ref, out_ref, sem)
    copy.start()
    copy.wait()
    total = flat(out_ref)

    def there(k, carry):
        for d, ref in enumerate(from_groups):
            at = d * KEEP + k
            add_lines(total, slot_ref[3, at], jnp.where(slot_ref[2, at] == 1, ref[k], 0.0))
        return carry

    lax.fori_loop(0, KEEP, there, 0, unroll=2)


def add_arrived(slot, summed, from_groups):
    smem, vmem = pl.BlockSpec(memory_space=pltpu.SMEM), pl.BlockSpec(memory_space=pltpu.VMEM)
    return pl.pallas_call(
        add_arrived_kernel,
        out_shape=jax.ShapeDtypeStruct(summed.shape, jnp.float32),
        in_specs=[smem, pl.BlockSpec(memory_space=pl.ANY)] + [vmem] * 3,
        out_specs=vmem,
        scratch_shapes=[pltpu.SemaphoreType.DMA],
        compiler_params=pltpu.CompilerParams(vmem_limit_bytes=24 << 20),
        cost_estimate=pl.CostEstimate(flops=2_000_000, bytes_accessed=6_000_000, transcendentals=0),
        name="add_arrived",
    )(slot, summed, *from_groups)


def add_near_kernel(pos_ref, sum_ref, terms_ref, out_ref, acc, terms, stage, sem_sum, sem_in, sem_out):
    cut = terms.shape[1] - ROWS
    copies = [pltpu.make_async_copy(sum_ref, acc, sem_sum)]
    for k in range(PARTS):
        mine = pl.ds(k * (B // PARTS), B // PARTS)
        copies.append(pltpu.make_async_copy(terms_ref.at[mine], terms.at[mine], sem_in.at[k]))
    for copy in copies:
        copy.start()
    copies[0].wait()
    for k in range(PARTS):
        copies[k + 1].wait()

        def here(p, carry):
            for s in range(PAIR_DEV):
                q = s * B + p
                lines = terms[p, s * cut : s * cut + ROWS]
                add_lines(flat(acc), pos_ref[0, q], its_lines(s, pos_ref[5, q], lines))
            return carry

        lax.fori_loop(k * (B // PARTS), (k + 1) * (B // PARTS), here, 0, unroll=8)
    pushes = []
    for k in range(PARTS):

        def lay_out(i, carry, k=k):
            rows = pl.ds(pl.multiple_of(i * 8, 8), 8)
            lines = jnp.swapaxes(acc[pl.ds(i * 8 + 1, 8), k * 8 : k * 8 + 8], 0, 1)
            for j in range(8):
                stage[k, rows, j * 128 : (j + 1) * 128] = lines[j]
            return carry

        lax.fori_loop(0, 128 // 8, lay_out, 0, unroll=4)
        pushes.append(pltpu.make_async_copy(stage.at[k], out_ref.at[:, pl.ds(k * 1024, 1024)], sem_out.at[k]))
        pushes[-1].start()
    for copy in pushes:
        copy.wait()


def add_near(pos, summed, terms):
    anywhere = pl.BlockSpec(memory_space=pl.ANY)
    dma = pltpu.SemaphoreType.DMA((PARTS,))
    return pl.pallas_call(
        add_near_kernel,
        out_shape=jax.ShapeDtypeStruct((128, ROWS * 128), jnp.float32),
        in_specs=[pl.BlockSpec(memory_space=pltpu.SMEM), anywhere, anywhere],
        out_specs=anywhere,
        scratch_shapes=[
            pltpu.VMEM((130, ROWS, 128), jnp.float32),
            pltpu.VMEM(terms.shape, jnp.float32),
            pltpu.VMEM((PARTS, 128, 1024), jnp.float32),
            pltpu.SemaphoreType.DMA,
            dma,
            dma,
        ],
        compiler_params=pltpu.CompilerParams(vmem_limit_bytes=63 << 20),
        cost_estimate=pl.CostEstimate(flops=2_000_000, bytes_accessed=10_000_000, transcendentals=0),
        name="add_near",
    )(pos, summed, terms)


def turned(x, shift):
    groups = lax.axis_size("grp")
    return lax.ppermute(x, "grp", [(g, (g + shift) % groups) for g in range(groups)])


def exchanged(planes):
    return lax.all_to_all(planes, "grid", 0, 0, tiled=True)


def there_and_back(place, pos, anchors, both):
    lines = both.shape[1] // 2

    def solve_both(both):
        return jnp.concatenate(solve(place, pos, anchors, both[:, :lines], both[:, lines:]), axis=1)

    def step(k, both):
        return lax.cond(k == 0, solve_both, lambda x: x, exchanged(both))

    return lax.fori_loop(0, 2, step, both)


def fitting(lines, orbitals, anchors, place, pos, slot, used):
    def used_row(used_ref, table, i):
        p, s, spare = used_ref[0, i], used_ref[1, i], used_ref[2, i]
        plane = table[p, pl.ds(pl.multiple_of(s * (lines - ROWS), 8), ROWS)]
        keep = (line_no() >= s * spare) & (line_no() < ROWS - (1 - s) * spare)
        return jnp.where(keep, plane, 0.0)

    trimmed = lines == TRIMMED
    near = deal_near(lines, pos, orbitals)
    if trimmed:
        near = exchanged(near)
    local = orbitals.reshape(128, ROWS, 128)
    arrived = [turned(x, d) for d, x in enumerate(fetch(slot, local, sent_row, "send"), 1)]
    far = deal_far(lines, 1, pos, [local] + arrived)
    if trimmed:
        near_terms, far_terms = solve(place, pos, anchors.reshape(-1), near, exchanged(far))
        far_terms = exchanged(far_terms)
    else:
        both = there_and_back(place, pos, anchors.reshape(-1), jnp.concatenate([near, far], axis=1))
        near_terms, far_terms = both[:, :lines], both[:, lines:]
    from_groups = [turned(x, -d) for d, x in enumerate(fetch(used, far_terms, used_row, "back"), 1)]
    summed = add_far(pos, far_terms)
    if trimmed:
        near_terms = exchanged(near_terms)
    return add_near(pos, add_arrived(slot, summed, from_groups), near_terms)


def add_all_kernel(pos_ref, terms_ref, out_ref):
    out_ref[...] = jnp.zeros(out_ref.shape, jnp.float32)
    total = flat(out_ref)

    def here(p, carry):
        for s in range(PAIR_DEV):
            for k in range(2):
                at = (k * PAIR_DEV + s) * ROWS
                add_lines(total, pos_ref[k, s * B + p], terms_ref[p, at : at + ROWS])
        return carry

    lax.fori_loop(0, B, here, 0)


def add_all(pos, terms, count):
    return pl.pallas_call(
        add_all_kernel,
        out_shape=jax.ShapeDtypeStruct((count + 2, ROWS, 128), jnp.float32),
        in_specs=[pl.BlockSpec(memory_space=pltpu.SMEM), pl.BlockSpec(memory_space=pltpu.VMEM)],
        out_specs=pl.BlockSpec(memory_space=pltpu.VMEM),
        compiler_params=pltpu.CompilerParams(vmem_limit_bytes=32 << 20),
        cost_estimate=pl.CostEstimate(flops=2_000_000, bytes_accessed=10_000_000, transcendentals=0),
        name="add_all",
    )(pos, terms)


def general(orbitals, anchors, pair_slots, place):
    groups, grid_count = lax.axis_size("grp"), lax.axis_size("grid")
    me, rows = lax.axis_index("grp"), orbitals.shape[0]
    dealt = deal_evenly(pair_slots, groups * grid_count, PAIR_DEV)
    own = lax.dynamic_slice_in_dim(dealt, me * grid_count, grid_count, 0)
    own = jnp.maximum(jnp.transpose(own, (2, 1, 0)).reshape(2, PAIR_DEV * grid_count), 0)
    pos = jnp.concatenate([own * ROWS, own, jnp.zeros((4, own.shape[1]), jnp.int32)])
    round_trip = [turned(orbitals, d) for d in (3, 2, 1)] + [orbitals]
    pieces = lax.dynamic_slice_in_dim(jnp.concatenate(round_trip * 2), (3 - me) * rows, groups * rows, 0)
    table = pieces.reshape(-1, ROWS, 128)
    both = jnp.concatenate([deal_far(PAIR_DEV * ROWS, k, pos, [table]) for k in range(2)], axis=1)

    terms = there_and_back(place, pos, anchors.reshape(-1), both)
    summed = add_all(pos, terms, table.shape[0])
    blocks = [lax.dynamic_slice_in_dim(summed, ((me + d) & 3) * rows + 1, rows, 0) for d in range(4)]
    return (blocks[0] + sum(turned(blocks[d], d) for d in (1, 2, 3))).reshape(orbitals.shape)


def body(orbitals, anchors, pair_slots):
    me = lax.axis_index("grp").astype(jnp.int32)[None]
    place = lax.axis_index("grid").astype(jnp.int32)[None]
    pos, slot, used, mode = route(me, pair_slots, anchors)

    def other():
        return lax.cond(
            mode[0] == 1,
            lambda: fitting(PAIR_DEV * ROWS, orbitals, anchors, place, pos, slot, used),
            lambda: general(orbitals, anchors, pair_slots, place),
        )

    return lax.cond(mode[0] == 0, lambda: fitting(TRIMMED, orbitals, anchors, place, pos, slot, used), other)


def solution(mesh):
    return jax.shard_map(
        body,
        mesh=mesh,
        in_specs=(P("grp", "grid"), P(), P()),
        out_specs=P("grp", "grid"),
        check_vma=False,
    )
```
